32 devices in a mesh: fsdp: 2 (over x), context: 4 (over z), tensor: 4 (over y, core).
Axes of the slice: x: 2, y: 2, z: 4, core: 2. Of those that a mesh axis runs over, the one named last changes fastest.
Arguments:
- tokens: bfloat16 [8, 2048, 1024], P('fsdp', 'context'), may hold values from -6 to 6
- cotangent: bfloat16 [8, 2048, 1024], P('fsdp', 'context'), may hold values from -6 to 6
- teacher: bfloat16 [8, 2048, 1024], P('fsdp', 'context'), may hold values from -6 to 6
- valid_mask: int32 [8, 2048], P('fsdp', 'context'), may hold values from 0 to 1, as said below
- segment_ids: int32 [8, 2048], P('fsdp'), may hold values from 0 to 3, as said below
- ln1_gain: bfloat16 [1024], P('fsdp'), may hold values from 0.099609375 to 1.8984375
- ln1_bias: bfloat16 [1024], P('fsdp'), may hold values from -2 to 2
- w_qkv: bfloat16 [3, 1024, 1024], P(None, 'fsdp', 'tensor'), may hold values from -0.1875 to 0.1875
- b_qv: bfloat16 [2, 16, 64], P(None, 'tensor', 'fsdp'), may hold values from -2 to 2
- w_out: bfloat16 [1024, 1024], P('tensor', 'fsdp'), may hold values from -0.75 to 0.75
- b_out: bfloat16 [1024], P('fsdp'), may hold values from -2 to 2
- ln2_gain: bfloat16 [1024], P('fsdp'), may hold values from 0.099609375 to 1.8984375
- ln2_bias: bfloat16 [1024], P('fsdp'), may hold values from -2 to 2
- w_fc1: bfloat16 [1024, 4096], P('fsdp', 'tensor'), may hold values from -0.1875 to 0.1875
- b_fc1: bfloat16 [16, 256], P('tensor', 'fsdp'), may hold values from -2 to 2
- w_fc2: bfloat16 [4096, 1024], P('tensor', 'fsdp'), may hold values from -0.09375 to 0.09375
- b_fc2: bfloat16 [1024], P('fsdp'), may hold values from -2 to 2
Outputs:
- output: bfloat16 [8, 2048, 1024], P('fsdp', 'context')
- loss: float32 [], replicated
- input_grad: bfloat16 [8, 2048, 1024], P('fsdp', 'context')
- grad_ln1_gain: float32 [1024], P('fsdp')
- grad_ln1_bias: float32 [1024], P('fsdp')
- grad_w_qkv: float32 [3, 1024, 1024], P(None, 'fsdp', 'tensor')
- grad_b_qv: float32 [2, 16, 64], P(None, 'tensor', 'fsdp')
- grad_w_out: float32 [1024, 1024], P('tensor', 'fsdp')
- grad_b_out: float32 [1024], P('fsdp')
- grad_ln2_gain: float32 [1024], P('fsdp')
- grad_ln2_bias: float32 [1024], P('fsdp')
- grad_w_fc1: float32 [1024, 4096], P('fsdp', 'tensor')
- grad_b_fc1: float32 [16, 256], P('tensor', 'fsdp')
- grad_w_fc2: float32 [4096, 1024], P('tensor', 'fsdp')
- grad_b_fc2: float32 [1024], P('fsdp')
The draws below stay inside these ranges and needn't reach their ends.
Inputs may be any that keep to these rules, and one draw needn't show every extreme that they name: `valid_mask`: the first token of every sequence is valid. `segment_ids`: never falls along a sequence. Among the 4 sequences of one index of fsdp exactly one is a single document.
All inputs are finite; a program needn't handle non-finite values.
Results may differ from the reference program's by a relative error of at most 0.015.
Values may be sent and summed in bfloat16 or wider, within the bound.
A program may use at most 256 MiB of HBM per device.

```python
import math
import jax
import jax.numpy as jnp
from jax import lax

D = 1024
HEADS = 16
HD = 64
FF = 4096
LEN = 2048
SEQ_GRP = 4
WINDOW = 1024
SEQS = 8
TOKENS = 16384


def draw_valid_mask(key, part):
    key = jax.random.fold_in(key, 11)
    index = jnp.arange(SEQS * LEN, dtype=jnp.int32).reshape(SEQS, LEN)
    level = 20 + 60 * index // (SEQS * LEN)
    roll = jax.random.randint(key, (SEQS, LEN), 0, 100, dtype=jnp.int32)
    marks = (roll < level).astype(jnp.int32)
    first = jnp.arange(LEN, dtype=jnp.int32)[None, :] == 0
    return jnp.where(first, 1, marks).astype(jnp.int32)


def draw_segment_ids(key, part):
    key = jax.random.fold_in(key, 7)
    key_cuts, key_whole = jax.random.split(key)
    cuts = jax.random.randint(key_cuts, (SEQS, 3), 1, LEN, dtype=jnp.int32)
    position = jnp.arange(LEN, dtype=jnp.int32)
    numbers = jnp.sum((position[None, :, None] >= cuts[:, None, :]).astype(jnp.int32), axis=-1)
    chosen = jax.random.randint(key_whole, (SEQS // SEQ_GRP,), 0, SEQ_GRP, dtype=jnp.int32)
    single = jnp.arange(SEQS, dtype=jnp.int32) % SEQ_GRP == jnp.repeat(chosen, SEQ_GRP)
    return jnp.where(single[:, None], 0, numbers).astype(jnp.int32)


def block_levels(key, extent, shards, smallest, largest):
    def one(dim, shards_of):
        heights = jax.random.uniform(jax.random.fold_in(jax.random.fold_in(key, 6), dim), (shards_of,), jnp.float32, smallest / len(shards), largest / len(shards))
        return jnp.repeat(jnp.exp(heights), extent[dim] // shards_of).reshape((-1,) + (1,) * (len(extent) - dim - 1))

    level = one(*shards[0])
    for cut in shards[1:]:
        level = level * one(*cut)
    return level


def noise(own_key, dims, scale, limit, cuts=(), kind=jnp.bfloat16):
    array = jax.random.normal(own_key, dims, jnp.float32) * scale
    if len(cuts) > 0:
        array = block_levels(own_key, dims, cuts, -0.22, 0.18) * array
    return jnp.clip(array, min=-limit, max=limit).astype(kind)


def setup_inputs(seed: int = 0) -> dict:
    seeds = jax.random.split(jax.random.key(seed), 18)
    tokens = noise(seeds[0], (SEQS, LEN, D), 1.0, 6.0, ((0, 2), (1, 4)))
    cotangent = noise(seeds[1], (SEQS, LEN, D), 1.0, 6.0, ((0, 2), (1, 4)))
    teacher = noise(seeds[2], (SEQS, LEN, D), 1.0, 6.0, ((0, 2), (1, 4)))
    valid_mask = draw_valid_mask(jax.random.fold_in(seeds[17], 71), 0)
    segment_ids = draw_segment_ids(jax.random.fold_in(seeds[17], 71), 0)
    ln1_gain = jnp.clip(1.0 + 0.18 * jax.random.normal(seeds[5], (D,), jnp.float32), 0.099609375, 1.8984375).astype(jnp.bfloat16)
    ln1_bias = noise(seeds[6], (D,), 0.3, 2.0, ((0, 2),))
    w_qkv = noise(seeds[7], (3, D, D), D ** -0.5, 0.1875, ((1, 2), (2, 4)))
    b_qv = noise(seeds[8], (2, HEADS, HD), 0.3, 2.0, ((1, 4), (2, 2)))
    w_out = noise(seeds[9], (D, D), (D // 16) ** -0.5, 0.75, ((0, 4), (1, 2)))
    b_out = noise(seeds[10], (D,), 0.3, 2.0, ((0, 2),))
    ln2_gain = jnp.clip(1.0 + 0.18 * jax.random.normal(seeds[11], (D,), jnp.float32), 0.099609375, 1.8984375).astype(jnp.bfloat16)
    ln2_bias = noise(seeds[12], (D,), 0.3, 2.0, ((0, 2),))
    w_fc1 = noise(seeds[13], (D, FF), D ** -0.5, 0.1875, ((0, 2), (1, 4)))
    b_fc1 = noise(seeds[14], (HEADS, FF // HEADS), 0.3, 2.0, ((0, 4), (1, 2)))
    w_fc2 = noise(seeds[15], (FF, D), FF ** -0.5, 0.09375, ((0, 4), (1, 2)))
    b_fc2 = noise(seeds[16], (D,), 0.3, 2.0, ((0, 2),))
    return {"tokens": tokens, "cotangent": cotangent, "teacher": teacher, "valid_mask": valid_mask, "segment_ids": segment_ids, "ln1_gain": ln1_gain, "ln1_bias": ln1_bias, "w_qkv": w_qkv, "b_qv": b_qv, "w_out": w_out, "b_out": b_out, "ln2_gain": ln2_gain, "ln2_bias": ln2_bias, "w_fc1": w_fc1, "b_fc1": b_fc1, "w_fc2": w_fc2, "b_fc2": b_fc2}


EPSILON = 1e-05
MASKED = -1e+30
HIGH = lax.Precision.HIGHEST

@jax.custom_vjp
def low(v):
    return lax.optimization_barrier(v.astype(jnp.bfloat16)).astype(jnp.float32)

@jax.custom_vjp
def low_back(v):
    return v

def low_keep(v):
    return (low(v), None)

def low_pass(kept, grad):
    return (grad,)

def back_keep(v):
    return (v, None)

def back_low(kept, grad):
    return (low(grad),)
low.defvjp(low_keep, low_pass)
low_back.defvjp(back_keep, back_low)

def rounded(values):
    return low(low_back(values))

def norm_rows(values, gain, shift):
    center = values - lax.optimization_barrier(jnp.mean(values, axis=-1, keepdims=True))
    spread = lax.optimization_barrier(jnp.mean(center * center, axis=-1, keepdims=True))
    return center * lax.rsqrt(spread + EPSILON) * gain + shift

def gelu_tanh(values):
    return 0.5 * values * (1.0 + jnp.tanh(0.7978845608028654 * (values + 0.044715 * values * values * values)))

def matmul(left, right):
    return jnp.dot(left, right, precision=HIGH)

def attend(query, keys, values, segments):
    block = min(512, LEN)
    span = block + WINDOW
    heads_query = query.reshape(LEN, HEADS, HD)
    padded_keys = jnp.pad(keys.reshape(LEN, HEADS, HD), ((WINDOW, 0), (0, 0), (0, 0)))
    padded_values = jnp.pad(values.reshape(LEN, HEADS, HD), ((WINDOW, 0), (0, 0), (0, 0)))
    padded_seg = jnp.concatenate([jnp.full((WINDOW,), -1, jnp.int32), segments.astype(jnp.int32)])
    scale = 1.0 / math.sqrt(HD)

    def one_block(start):
        query_block = lax.dynamic_slice_in_dim(heads_query, start, block, 0)
        key_block = lax.dynamic_slice_in_dim(padded_keys, start, span, 0)
        value_block = lax.dynamic_slice_in_dim(padded_values, start, span, 0)
        query_seg = lax.dynamic_slice_in_dim(segments.astype(jnp.int32), start, block, 0)
        key_seg = lax.dynamic_slice_in_dim(padded_seg, start, span, 0)
        query_pos = start + jnp.arange(block, dtype=jnp.int32)
        key_pos = start - WINDOW + jnp.arange(span, dtype=jnp.int32)
        distance = query_pos[:, None] - key_pos[None, :]
        allowed = (distance >= 0) & (distance < WINDOW) & (query_seg[:, None] == key_seg[None, :])
        scores = jnp.einsum('qhe,khe->hqk', query_block, key_block, precision=HIGH) * scale
        scores = low_back(scores)
        scores = jnp.where(allowed[None], scores, MASKED)
        top = lax.optimization_barrier(jnp.max(scores, axis=-1, keepdims=True))
        weights = jnp.exp(scores - top)
        probs = weights / lax.optimization_barrier(jnp.sum(weights, axis=-1, keepdims=True))
        mixed = jnp.einsum('hqk,khe->qhe', low(probs), value_block, precision=HIGH)
        return mixed.reshape(block, HEADS * HD)
    starts = jnp.arange(LEN // block, dtype=jnp.int32) * block
    return lax.map(jax.checkpoint(one_block), starts).reshape(LEN, D)

def forward(resid_in, params, segments, teacher_rows, mask_rows, count):
    gain_one, bias_one, weight_qkv, bias_qv, weight_out, bias_out, gain_two, bias_two, weight_up, bias_up, weight_down, bias_down = params
    normed_one = low(norm_rows(resid_in, gain_one, bias_one))
    query = rounded(matmul(normed_one, weight_qkv[0]) + bias_qv[0].reshape(D))
    key_proj = rounded(matmul(normed_one, weight_qkv[1]))
    value_proj = rounded(matmul(normed_one, weight_qkv[2]) + bias_qv[1].reshape(D))
    count_seqs = resid_in.shape[0] // LEN
    pieces = []
    for index in range(count_seqs):
        lower = index * LEN
        pieces.append(attend(query[lower:lower + LEN], key_proj[lower:lower + LEN], value_proj[lower:lower + LEN], segments[index]))
    attended = rounded(jnp.concatenate(pieces, axis=0))
    middle = resid_in + low_back(matmul(attended, weight_out)) + bias_out
    normed_two = low(norm_rows(middle, gain_two, bias_two))
    hidden = low_back(matmul(normed_two, weight_up) + bias_up.reshape(FF))
    activated = low(gelu_tanh(hidden))
    block = middle + low_back(matmul(activated, weight_down)) + bias_down
    difference = block - teacher_rows
    part_loss = jnp.sum(mask_rows * lax.optimization_barrier(jnp.sum(difference * difference, axis=-1))) / (2.0 * D * count)
    return (block, part_loss)

def reference(tokens, cotangent, teacher, valid_mask, segment_ids, ln1_gain, ln1_bias, w_qkv, b_qv, w_out, b_out, ln2_gain, ln2_bias, w_fc1, b_fc1, w_fc2, b_fc2):
    params = tuple((item.astype(jnp.float32) for item in (ln1_gain, ln1_bias, w_qkv, b_qv, w_out, b_out, ln2_gain, ln2_bias, w_fc1, b_fc1, w_fc2, b_fc2)))
    count = jnp.sum(valid_mask.astype(jnp.float32))
    pairs = SEQS // 2
    span = 2 * LEN
    stacked = (tokens.astype(jnp.float32).reshape(pairs, span, D), cotangent.astype(jnp.float32).reshape(pairs, span, D), teacher.astype(jnp.float32).reshape(pairs, span, D), valid_mask.astype(jnp.float32).reshape(pairs, span), segment_ids.astype(jnp.int32).reshape(pairs, 2, LEN))
    zeros = tuple((jnp.zeros_like(item) for item in params))

    def step(carry, item):
        total_loss, sums = carry
        block_in, block_cot, block_teacher, block_mask, block_seg = item

        def run(values, weights):
            return forward(values, weights, block_seg, block_teacher, block_mask, count)
        (block_out, part_loss), pull = jax.vjp(run, block_in, params)
        grad_in, grad_params = pull((block_cot, jnp.full((), float(TOKENS * D), part_loss.dtype)))
        sums = jax.tree.map(lambda first, second: first + second, sums, grad_params)
        return ((total_loss + part_loss, sums), (block_out.astype(jnp.bfloat16), grad_in.astype(jnp.bfloat16)))
    (loss, grads), (outputs, grad_inputs) = lax.scan(step, (jnp.zeros((), jnp.float32), zeros), stacked)
    return (outputs.reshape(SEQS, LEN, D), loss, grad_inputs.reshape(SEQS, LEN, D), grads[0], grads[1], grads[2], grads[3], grads[4], grads[5], grads[6], grads[7], grads[8], grads[9], grads[10], grads[11])
```

```python
import functools
import math

import jax
import jax.numpy as jnp
from jax import lax
from jax.experimental import pallas as pl
from jax.experimental.pallas import tpu as pltpu
from jax.sharding import PartitionSpec as P

MESH = pl.DeviceIdType.MESH
BF = jnp.bfloat16
F32 = jnp.float32
D = 1024
HD = 64
WINDOW = 1024
EPSILON = 1e-05
MASKED = -1e30
QUARTER = 128
HALF = 256


def matmul(left, right, over_left, over_right):
    dims = (((over_left,), (over_right,)), ((), ()))
    return lax.dot_general(left, right, dims, preferred_element_type=F32)


def norm_parts(values):
    mean = jnp.mean(values, axis=-1, keepdims=True)
    center = values - mean
    spread = jnp.mean(center * center, axis=-1, keepdims=True)
    inverse = lax.rsqrt(spread + EPSILON)
    return center * inverse, inverse


def column_sum(values):
    return jnp.sum(values, axis=0, keepdims=True)


def mid_kernel(
    nf,
    att,
    wout_s,
    wfc1_s,
    wfc2_s,
    tokens,
    teacher,
    cot,
    vec,
    mask,
    out_h,
    gmix_h,
    gmid_h,
    gfc1,
    gfc2,
    small,
    wout,
    wfc1,
    wfc2,
    ag,
    act,
    slope,
    send,
    recv_c,
    send_y,
    recv_y,
    mid,
    gblk,
    tok_q,
    tea_q,
    cot_q,
    tea_b,
    cot_b,
    maskc,
    w_send,
    w_recv,
    w_loc,
    sems,
    q_sems,
    in_sems,
    out_sem,
    res_sem,
):
    me_f, me_z, me_t = (
        lax.axis_index("fsdp"),
        lax.axis_index("context"),
        lax.axis_index("tensor"),
    )
    me_y, me_c = me_t // 2, me_t % 2
    mate_c = (me_f, me_z, me_t + 1 - 2 * me_c)
    mate_y = (me_f, me_z, (me_t + 2) % 4)
    mine = (2 * me_c + me_y) * QUARTER
    over_y = (2 * me_c + 1 - me_y) * QUARTER

    def rows(start, size=QUARTER):
        return pl.ds(pl.multiple_of(start, QUARTER), size)

    barrier = pltpu.get_barrier_semaphore()
    peers = [(lax.rem(me_f + j, nf), me_z, me_t) for j in range(1, nf)]
    for peer in [mate_c, mate_y] + peers:
        pl.semaphore_signal(barrier, inc=1, device_id=peer, device_id_type=MESH)
    pl.semaphore_wait(barrier, 1 + nf)

    fs = wout_s.shape[1]
    own = pl.ds(pl.multiple_of(me_f * fs, fs), fs)
    places = (
        (wout_s, wout.at[:, own]),
        (wfc1_s, wfc1.at[own, :]),
        (wfc2_s, wfc2.at[:, own]),
    )

    def weight_copy(i, j):
        return pltpu.make_async_remote_copy(
            places[i][0],
            places[i][1],
            w_send.at[i, j],
            w_recv.at[i, j],
            device_id=peers[j],
            device_id_type=MESH,
        )

    for i in range(3):
        for j in range(nf - 1):
            weight_copy(i, j).start()
        pltpu.make_async_copy(places[i][0], places[i][1], w_loc.at[i]).start()

    def weight_wait(i):
        pltpu.make_async_copy(places[i][0], places[i][1], w_loc.at[i]).wait()
        for j in range(nf - 1):
            weight_copy(i, j).wait()

    quarters = ((tokens, tok_q), (teacher, tea_q), (cot, cot_q))
    for i, (source, target) in enumerate(quarters):
        pltpu.make_async_copy(source.at[:, rows(mine), :], target, q_sems.at[i]).start()

    def block_copies(s):
        slot = lax.rem(s, 2)
        return (
            pltpu.make_async_copy(teacher.at[s], tea_b.at[slot], in_sems.at[0, slot]),
            pltpu.make_async_copy(cot.at[s], cot_b.at[slot], in_sems.at[1, slot]),
        )

    turned = jnp.transpose(mask[...])
    for s in range(4):
        maskc[s] = turned[:, s : s + 1]
    small[...] = jnp.zeros_like(small)

    RSC, RSY, AGY, AGO, AGF = range(5)

    def remote(src, dst, which, s, mate):
        return pltpu.make_async_remote_copy(
            src,
            dst,
            sems.at[which, 0, s],
            sems.at[which, 1, s],
            device_id=mate,
            device_id_type=MESH,
        )

    def rs_core(s):
        half = rows((1 - me_c) * HALF, HALF)
        return remote(send.at[s, half], recv_c.at[s], RSC, s, mate_c)

    def rs_y(s):
        return remote(send_y.at[s], recv_y.at[s], RSY, s, mate_y)

    def ag_y(k, s):
        return remote(ag.at[k, s, rows(mine)], ag.at[k, s, rows(mine)], AGY, s, mate_y)

    def ag_own(k, s):
        return remote(ag.at[k, s, rows(mine)], ag.at[k, s, rows(mine)], AGO, s, mate_c)

    def ag_forward(k, s):
        return remote(ag.at[k, s, rows(over_y)], ag.at[k, s, rows(over_y)], AGF, s, mate_c)

    def step_q(s):
        rs_core(s).wait()
        send_y[s] = (
            send[s, rows(over_y)].astype(F32)
            + recv_c[s, rows((1 - me_y) * QUARTER)].astype(F32)
        ).astype(BF)
        rs_y(s).start()

    def total(s):
        rs_y(s).wait()
        return (
            send[s, rows(mine)].astype(F32)
            + recv_c[s, rows(me_y * QUARTER)].astype(F32)
            + recv_y[s].astype(F32)
        )

    def step_r(k, s):
        summed = total(s)
        if k == 0:
            middle = tok_q[s].astype(F32) + summed + vec[0:1, :]
            mid[s] = middle
            xhat, _ = norm_parts(middle)
            ag[0, s, rows(mine)] = (xhat * vec[1:2, :] + vec[2:3, :]).astype(BF)
        elif k == 1:
            block = mid[s] + summed + vec[4:5, :]
            ag[1, s, rows(mine)] = block.astype(BF)
            masks = maskc[s, rows(mine)]
            difference = block - tea_q[s].astype(F32)
            masked = masks * difference
            small[5:6, :] += column_sum(masked * difference)
            grad = cot_q[s].astype(F32) + masked * vec[5:6, :]
            gblk[s] = grad
            small[0:1, :] += column_sum(grad)
        else:
            grad_normed = summed
            xhat, inverse = norm_parts(mid[s])
            small[1:2, :] += column_sum(grad_normed * xhat)
            small[2:3, :] += column_sum(grad_normed)
            e = grad_normed * vec[1:2, :]
            grad = gblk[s] + inverse * (
                e
                - jnp.mean(e, axis=-1, keepdims=True)
                - xhat * jnp.mean(e * xhat, axis=-1, keepdims=True)
            )
            gblk[s] = grad
            small[3:4, :] += column_sum(grad)
            ag[2, s, rows(mine)] = grad.astype(BF)
        ag_y(k, s).start()
        ag_own(k, s).start()

    def step_t(k, s):
        ag_y(k, s).wait()
        ag_forward(k, s).start()

    def step_u(k, s):
        ag_own(k, s).wait()
        ag_forward(k, s).wait()

    def step_p(k, s):
        if k == 0:
            start = pl.multiple_of(s * 512, 512)
            send[s] = matmul(att[pl.ds(start, 512), :], wout[...], 1, 0).astype(BF)
        elif k == 1:
            for part in range(2):
                here = pl.ds(part * 256, 256)
                h = matmul(ag[0, s, here], wfc1[...], 1, 0) + vec[3:4, :]
                t = jnp.tanh(0.7978845608028654 * (h + 0.044715 * h * h * h))
                act[s, here] = (0.5 * h * (1.0 + t)).astype(BF)
                slope[s, here] = (
                    0.5 * (1.0 + t)
                    + 0.5 * h * (1.0 - t * t) * (0.7978845608028654 * (1.0 + 0.134145 * h * h))
                ).astype(BF)
            send[s] = matmul(act[s], wfc2[...], 1, 0).astype(BF)
        else:
            slot = lax.rem(s, 2)
            out = pltpu.make_async_copy(ag.at[1, s], out_h.at[s], out_sem)
            out.start()
            for copy in block_copies(s):
                copy.wait()

            @pl.when(s < 3)
            def _():
                for copy in block_copies(s + 1):
                    copy.start()

            out.wait()
            for part in range(2):
                here = pl.ds(part * 256, 256)
                difference = ag[1, s, here].astype(F32) - tea_b[slot, here].astype(F32)
                scaled = maskc[s, here] * vec[5:6, :]
                down = (cot_b[slot, here].astype(F32) + scaled * difference).astype(BF)
                ag[1, s, here] = down
                up = matmul(down, wfc2[...], 1, 1) * slope[s, here].astype(F32)
                rounded = up.astype(BF)
                slope[s, here] = rounded
                small[4:5, :] += column_sum(rounded.astype(F32))
            send[s] = matmul(slope[s], wfc1[...], 1, 1).astype(BF)
        rs_core(s).start()

    weight_wait(0)
    for i, (source, target) in enumerate(quarters):
        pltpu.make_async_copy(source.at[:, rows(mine), :], target, q_sems.at[i]).wait()

    for k in range(3):
        if k == 1:
            for copy in block_copies(0):
                copy.start()

        def tick(s, carry, k=k):
            if k == 0:

                @pl.when(s >= 3)
                def _():
                    step_t(0, s - 3)

                @pl.when(s >= 2)
                def _():
                    step_r(0, s - 2)

                @pl.when(s >= 1)
                def _():
                    step_q(s - 1)

                step_p(0, s)
            else:

                @pl.when(s >= 3)
                def _():
                    step_t(k, s - 3)

                @pl.when(s < 3)
                def _():
                    step_t(k - 1, s + 1)

                @pl.when(s >= 2)
                def _():
                    step_r(k, s - 2)

                @pl.when(s < 2)
                def _():
                    step_r(k - 1, s + 2)

                step_q(lax.rem(s + 3, 4))
                step_u(k - 1, s)
                if k == 1:

                    @pl.when(s == 0)
                    def _():
                        weight_wait(1)
                        weight_wait(2)

                step_p(k, s)
            return carry

        lax.fori_loop(0, 4, tick, 0)

    step_t(2, 1)
    step_r(2, 2)
    step_q(3)
    deep = lambda ref: ref.reshape(2048, 1024)
    gfc2[...] = matmul(deep(act)[...], deep(ag.at[1])[...], 0, 0).astype(BF)
    step_t(2, 2)
    step_r(2, 3)
    gfc1[...] = matmul(deep(ag.at[0])[...], deep(slope)[...], 0, 0).astype(BF)
    step_t(2, 3)
    for s in range(4):
        step_u(2, s)
    copies = (
        pltpu.make_async_copy(ag.at[2], gmix_h, res_sem.at[0]),
        pltpu.make_async_copy(gblk, gmid_h, res_sem.at[1]),
    )
    for copy in copies:
        copy.start()
    for copy in copies:
        copy.wait()


def mid_call(nf, att, wout_s, wfc1_s, wfc2_s, tokens, teacher, cot, vec, mask):
    anys = pl.BlockSpec(memory_space=pl.ANY)
    vmem = pl.BlockSpec(memory_space=pltpu.VMEM)
    dma = pltpu.SemaphoreType.DMA
    big = lambda *lead: pltpu.VMEM((*lead, 512, 1024), BF)
    return pl.pallas_call(
        functools.partial(mid_kernel, nf),
        out_shape=(
            jax.ShapeDtypeStruct((4, 512, 1024), BF),
            jax.ShapeDtypeStruct((4, 512, 1024), BF),
            jax.ShapeDtypeStruct((4, QUARTER, 1024), F32),
            jax.ShapeDtypeStruct((1024, 1024), BF),
            jax.ShapeDtypeStruct((1024, 1024), BF),
            jax.ShapeDtypeStruct((8, 1024), F32),
        ),
        in_specs=[vmem, anys, anys, anys, anys, anys, anys, vmem, vmem],
        out_specs=(anys, anys, anys, vmem, vmem, vmem),
        scratch_shapes=[
            pltpu.VMEM((256, 1024), BF),
            pltpu.VMEM((1024, 1024), BF),
            pltpu.VMEM((1024, 1024), BF),
            big(3, 4),
            big(4),
            big(4),
            big(4),
            pltpu.VMEM((4, HALF, 1024), BF),
            pltpu.VMEM((4, QUARTER, 1024), BF),
            pltpu.VMEM((4, QUARTER, 1024), BF),
            pltpu.VMEM((4, QUARTER, 1024), F32),
            pltpu.VMEM((4, QUARTER, 1024), F32),
            pltpu.VMEM((4, QUARTER, 1024), BF),
            pltpu.VMEM((4, QUARTER, 1024), BF),
            pltpu.VMEM((4, QUARTER, 1024), BF),
            big(2),
            big(2),
            pltpu.VMEM((4, 512, 1), F32),
            dma((3, nf - 1)),
            dma((3, nf - 1)),
            dma((3,)),
            dma((5, 2, 4)),
            dma((3,)),
            dma((2, 2)),
            dma,
            dma((2,)),
        ],
        compiler_params=pltpu.CompilerParams(
            collective_id=1, has_side_effects=True, vmem_limit_bytes=62 * 2**20
        ),
        cost_estimate=pl.CostEstimate(
            flops=2 * 2048 * 1024 * 1024 * 7, bytes_accessed=30 * 2**20, transcendentals=0
        ),
        name="mid",
    )(att, wout_s, wfc1_s, wfc2_s, tokens, teacher, cot, vec, mask)


def passed_along(block, axis, distance):
    devices = range(lax.axis_size(axis))
    route = [(i - distance, i) for i in devices if i - distance in devices]
    return lax.ppermute(block, axis, route)


def norm_rows(values, gain, shift):
    center = values - jnp.mean(values, axis=-1, keepdims=True)
    spread = jnp.mean(center * center, axis=-1, keepdims=True)
    return center * lax.rsqrt(spread + EPSILON) * gain + shift


def gelu_tanh(values):
    return (
        0.5
        * values
        * (1.0 + jnp.tanh(0.7978845608028654 * (values + 0.044715 * values * values * values)))
    )


def masked_scores(query_one, keys_one, allowed_one, scale):
    scores = (
        jnp.einsum("qhe,khe->hqk", query_one, keys_one, preferred_element_type=jnp.float32) * scale
    )
    return jnp.where(allowed_one[None], scores, MASKED)


def row_total(term):
    return lax.psum(term.astype(jnp.bfloat16), "tensor").astype(jnp.float32)


def local(
    tokens,
    cotangent,
    teacher,
    valid_mask,
    segment_ids,
    ln1_gain,
    ln1_bias,
    w_qkv,
    b_qv,
    w_out,
    b_out,
    ln2_gain,
    ln2_bias,
    w_fc1,
    b_fc1,
    w_fc2,
    b_fc2,
):
    (
        gain_one,
        bias_one,
        weight_qkv,
        bias_qv,
        weight_out,
        bias_out,
        gain_two,
        bias_two,
        weight_up,
        bias_up,
        weight_down,
        bias_down,
    ) = (
        lax.all_gather(ln1_gain, "fsdp", axis=0, tiled=True),
        lax.all_gather(ln1_bias, "fsdp", axis=0, tiled=True),
        lax.all_gather(w_qkv, "fsdp", axis=1, tiled=True),
        lax.all_gather(b_qv, "fsdp", axis=2, tiled=True),
        lax.all_gather(w_out, "fsdp", axis=1, tiled=True),
        lax.all_gather(b_out, "fsdp", axis=0, tiled=True),
        lax.all_gather(ln2_gain, "fsdp", axis=0, tiled=True),
        lax.all_gather(ln2_bias, "fsdp", axis=0, tiled=True),
        lax.all_gather(w_fc1, "fsdp", axis=0, tiled=True),
        lax.all_gather(b_fc1, "fsdp", axis=1, tiled=True),
        lax.all_gather(w_fc2, "fsdp", axis=1, tiled=True),
        lax.all_gather(b_fc2, "fsdp", axis=0, tiled=True),
    )
    seqs, group, width = tokens.shape
    rows = seqs * group
    local_width = weight_qkv.shape[2]
    heads_here = local_width // HD
    scale = 1.0 / math.sqrt(HD)
    gain_one = gain_one.astype(jnp.float32)
    bias_one = bias_one.astype(jnp.float32)
    gain_two = gain_two.astype(jnp.float32)
    bias_two = bias_two.astype(jnp.float32)
    bias_out = bias_out.astype(jnp.float32)
    bias_down = bias_down.astype(jnp.float32)
    bias_up = bias_up.astype(jnp.float32).reshape(-1)
    qv_bias = bias_qv.astype(jnp.float32).reshape(2, local_width)
    resid_in = tokens.astype(jnp.float32).reshape(rows, width)
    normed_one = norm_rows(resid_in, gain_one, bias_one).astype(jnp.bfloat16)
    projected = jnp.einsum(
        "rd,tde->tre", normed_one, weight_qkv, preferred_element_type=jnp.float32
    )
    query = (projected[0] + qv_bias[0]).astype(jnp.bfloat16).reshape(seqs, group, heads_here, HD)
    key_proj = projected[1].astype(jnp.bfloat16).reshape(seqs, group, heads_here, HD)
    value_proj = (
        (projected[2] + qv_bias[1]).astype(jnp.bfloat16).reshape(seqs, group, heads_here, HD)
    )
    near_keys, near_values = passed_along((key_proj, value_proj), "context", 1)
    far_keys, far_values = passed_along((key_proj, value_proj), "context", 2)
    keys_all = jnp.concatenate([far_keys, near_keys, key_proj], axis=1)
    values_all = jnp.concatenate([far_values, near_values, value_proj], axis=1)
    place = lax.axis_index("context")
    query_pos = place * group + jnp.arange(group, dtype=jnp.int32)
    key_pos = (place - 2) * group + jnp.arange(3 * group, dtype=jnp.int32)
    padded_seg = jnp.concatenate([jnp.full((seqs, 2 * group), -1, jnp.int32), segment_ids], axis=1)
    key_seg = lax.dynamic_slice_in_dim(padded_seg, place * group, 3 * group, 1)
    query_seg = lax.dynamic_slice_in_dim(segment_ids, place * group, group, 1)
    distance = query_pos[:, None] - key_pos[None, :]
    allowed = ((distance >= 0) & (distance < WINDOW))[None] & (
        query_seg[:, :, None] == key_seg[:, None, :]
    )

    def attend_one(items):
        query_one, keys_one, values_one, allowed_one = items
        scores = masked_scores(query_one, keys_one, allowed_one, scale)
        top = jnp.max(scores, axis=-1, keepdims=True)
        weights = jnp.exp(scores - top)
        total = jnp.sum(weights, axis=-1, keepdims=True)
        probs = (weights / total).astype(jnp.bfloat16)
        mixed = jnp.einsum("hqk,khe->qhe", probs, values_one, preferred_element_type=jnp.float32)
        return (mixed, top + jnp.log(total))

    mixed, log_total = lax.map(attend_one, (query, keys_all, values_all, allowed))
    attended = mixed.reshape(rows, local_width).astype(jnp.bfloat16)
    mask_f = jnp.concatenate([valid_mask, jnp.zeros_like(valid_mask)], axis=0).astype(jnp.float32)
    count = lax.psum(jnp.sum(mask_f), ("fsdp", "context"))
    tokens_all = rows * lax.axis_size("fsdp") * lax.axis_size("context")
    zero = jnp.zeros_like(bias_out)
    vec = jnp.stack(
        [bias_out, gain_two, bias_two, bias_up, bias_down, zero + tokens_all / count, zero, zero]
    )
    nf = lax.axis_size("fsdp")
    output, grad_mix, grad_middle, grad_w_fc1, grad_w_fc2, small = mid_call(
        nf, attended, w_out, w_fc1, w_fc2, tokens, teacher, cotangent, vec, mask_f
    )
    place_t = lax.axis_index("tensor")
    place_q = 2 * (place_t % 2) + place_t // 2
    summed = lax.psum(jnp.stack([small[0], small[1], small[2], small[3], small[5]]), ("tensor",))
    loss = lax.psum(jnp.sum(summed[4]), ("fsdp", "context")) / (2.0 * D * count)
    grad_b_fc2, grad_ln2_gain, grad_ln2_bias, grad_b_out = summed[0], summed[1], summed[2], summed[3]
    grad_b_fc1 = small[4].reshape(b_fc1.shape[0], -1)
    grad_mix = grad_mix.reshape(rows, width)
    grad_middle = lax.all_gather(grad_middle, "tensor", axis=0)
    grad_middle = grad_middle[jnp.array([0, 2, 1, 3])].transpose(1, 0, 2, 3).reshape(rows, width)
    grad_w_out = jnp.einsum("re,rd->ed", attended, grad_mix, preferred_element_type=jnp.float32)
    grad_attended = jnp.einsum(
        "rd,ed->re", grad_mix, weight_out, preferred_element_type=jnp.float32
    )
    grad_attended = grad_attended.astype(jnp.bfloat16).reshape(seqs, group, heads_here, HD)

    def attend_back(items):
        query_one, keys_one, values_one, allowed_one, log_one, grad_one = items
        scores = masked_scores(query_one, keys_one, allowed_one, scale)
        probs = jnp.exp(scores - log_one)
        dprobs = jnp.einsum(
            "qhe,khe->hqk", grad_one, values_one, preferred_element_type=jnp.float32
        )
        weighted = jnp.sum(probs * dprobs, axis=-1, keepdims=True)
        grad_scores = (probs * (dprobs - weighted)).astype(jnp.bfloat16)
        grad_query = (
            jnp.einsum("hqk,khe->qhe", grad_scores, keys_one, preferred_element_type=jnp.float32)
            * scale
        )
        grad_key = (
            jnp.einsum("hqk,qhe->khe", grad_scores, query_one, preferred_element_type=jnp.float32)
            * scale
        )
        grad_value = jnp.einsum(
            "hqk,qhe->khe", probs.astype(jnp.bfloat16), grad_one, preferred_element_type=jnp.float32
        )
        return (grad_query, grad_key, grad_value)

    grad_query, grad_keys_all, grad_values_all = lax.map(
        attend_back, (query, keys_all, values_all, allowed, log_total, grad_attended)
    )
    from_near = (
        passed_along(
            grad_keys_all[:, group : 2 * group].astype(jnp.bfloat16), "context", -1
        ).astype(jnp.float32),
        passed_along(
            grad_values_all[:, group : 2 * group].astype(jnp.bfloat16), "context", -1
        ).astype(jnp.float32),
    )
    from_far = (
        passed_along(grad_keys_all[:, :group].astype(jnp.bfloat16), "context", -2).astype(
            jnp.float32
        ),
        passed_along(grad_values_all[:, :group].astype(jnp.bfloat16), "context", -2).astype(
            jnp.float32
        ),
    )
    grad_key = (grad_keys_all[:, 2 * group :] + from_near[0] + from_far[0]).astype(jnp.bfloat16)
    grad_value = (grad_values_all[:, 2 * group :] + from_near[1] + from_far[1]).astype(jnp.bfloat16)
    grad_query = grad_query.astype(jnp.bfloat16)
    grad_proj = jnp.stack(
        [
            grad_query.reshape(rows, local_width),
            grad_key.reshape(rows, local_width),
            grad_value.reshape(rows, local_width),
        ]
    )
    grad_w_qkv = jnp.einsum(
        "rd,tre->tde", normed_one, grad_proj, preferred_element_type=jnp.float32
    )
    grad_b_qv = jnp.stack(
        [
            jnp.sum(grad_proj[0], axis=0, dtype=jnp.float32),
            jnp.sum(grad_proj[2], axis=0, dtype=jnp.float32),
        ]
    ).reshape(2, heads_here, HD)
    first_term = jnp.einsum(
        "tre,tde->rd", grad_proj, weight_qkv, preferred_element_type=jnp.float32
    )
    _, first_pull = jax.vjp(norm_rows, resid_in, gain_one, bias_one)
    grad_in_norm, grad_ln1_gain, grad_ln1_bias = first_pull(row_total(first_term))
    input_grad = (grad_middle + grad_in_norm).astype(jnp.bfloat16).reshape(seqs, group, width)
    gradients = (
        grad_ln1_gain,
        grad_ln1_bias,
        grad_w_qkv,
        grad_b_qv,
        grad_w_out,
        grad_b_out,
        grad_ln2_gain,
        grad_ln2_bias,
        grad_w_fc1,
        grad_b_fc1,
        grad_w_fc2,
        grad_b_fc2,
    )
    owned = (
        lax.psum_scatter(
            gradients[0].astype(jnp.bfloat16), "fsdp", scatter_dimension=0, tiled=True
        ).astype(jnp.float32),
        lax.psum_scatter(
            gradients[1].astype(jnp.bfloat16), "fsdp", scatter_dimension=0, tiled=True
        ).astype(jnp.float32),
        lax.psum_scatter(
            gradients[2].astype(jnp.bfloat16), "fsdp", scatter_dimension=1, tiled=True
        ).astype(jnp.float32),
        lax.psum_scatter(
            gradients[3].astype(jnp.bfloat16), "fsdp", scatter_dimension=2, tiled=True
        ).astype(jnp.float32),
        lax.psum_scatter(
            gradients[4].astype(jnp.bfloat16), "fsdp", scatter_dimension=1, tiled=True
        ).astype(jnp.float32),
        lax.psum_scatter(
            gradients[5].astype(jnp.bfloat16), "fsdp", scatter_dimension=0, tiled=True
        ).astype(jnp.float32),
        lax.psum_scatter(
            gradients[6].astype(jnp.bfloat16), "fsdp", scatter_dimension=0, tiled=True
        ).astype(jnp.float32),
        lax.psum_scatter(
            gradients[7].astype(jnp.bfloat16), "fsdp", scatter_dimension=0, tiled=True
        ).astype(jnp.float32),
        lax.psum_scatter(
            gradients[8].astype(jnp.bfloat16), "fsdp", scatter_dimension=0, tiled=True
        ).astype(jnp.float32),
        lax.psum_scatter(
            gradients[9].astype(jnp.bfloat16), "fsdp", scatter_dimension=1, tiled=True
        ).astype(jnp.float32),
        lax.psum_scatter(
            gradients[10].astype(jnp.bfloat16), "fsdp", scatter_dimension=1, tiled=True
        ).astype(jnp.float32),
        lax.psum_scatter(
            gradients[11].astype(jnp.bfloat16), "fsdp", scatter_dimension=0, tiled=True
        ).astype(jnp.float32),
    )
    owned = (
        lax.psum(owned[0].astype(jnp.bfloat16), "context").astype(jnp.float32),
        lax.psum(owned[1].astype(jnp.bfloat16), "context").astype(jnp.float32),
        lax.psum(owned[2].astype(jnp.bfloat16), "context").astype(jnp.float32),
        lax.psum(owned[3].astype(jnp.bfloat16), "context").astype(jnp.float32),
        lax.psum(owned[4].astype(jnp.bfloat16), "context").astype(jnp.float32),
        lax.psum(owned[5].astype(jnp.bfloat16), "context").astype(jnp.float32),
        lax.psum(owned[6].astype(jnp.bfloat16), "context").astype(jnp.float32),
        lax.psum(owned[7].astype(jnp.bfloat16), "context").astype(jnp.float32),
        lax.psum(owned[8].astype(jnp.bfloat16), "context").astype(jnp.float32),
        lax.psum(owned[9].astype(jnp.bfloat16), "context").astype(jnp.float32),
        lax.psum(owned[10].astype(jnp.bfloat16), "context").astype(jnp.float32),
        lax.psum(owned[11].astype(jnp.bfloat16), "context").astype(jnp.float32),
    )
    return (
        output,
        loss,
        input_grad,
        owned[0],
        owned[1],
        owned[2],
        owned[3],
        owned[4],
        owned[5],
        owned[6],
        owned[7],
        owned[8],
        owned[9],
        owned[10],
        owned[11],
    )


def solution(mesh):
    return jax.shard_map(
        local,
        mesh=mesh,
        in_specs=(
            P("fsdp", "context", None),
            P("fsdp", "context", None),
            P("fsdp", "context", None),
            P("fsdp", "context"),
            P("fsdp", None),
            P("fsdp"),
            P("fsdp"),
            P(None, "fsdp", "tensor"),
            P(None, "tensor", "fsdp"),
            P("tensor", "fsdp"),
            P("fsdp"),
            P("fsdp"),
            P("fsdp"),
            P("fsdp", "tensor"),
            P("tensor", "fsdp"),
            P("tensor", "fsdp"),
            P("fsdp"),
        ),
        out_specs=(
            P("fsdp", "context", None),
            P(),
            P("fsdp", "context", None),
            P("fsdp"),
            P("fsdp"),
            P(None, "fsdp", "tensor"),
            P(None, "tensor", "fsdp"),
            P("tensor", "fsdp"),
            P("fsdp"),
            P("fsdp"),
            P("fsdp"),
            P("fsdp", "tensor"),
            P("tensor", "fsdp"),
            P("tensor", "fsdp"),
            P("fsdp"),
        ),
        check_vma=False,
    )
```

```python
import functools
import math

import jax
import jax.numpy as jnp
from jax import lax
from jax.experimental import pallas as pl
from jax.experimental.pallas import tpu as pltpu
from jax.sharding import PartitionSpec as P

MESH = pl.DeviceIdType.MESH
BF = jnp.bfloat16
F32 = jnp.float32
D = 1024
HD = 64
WINDOW = 1024
EPSILON = 1e-05
MASKED = -1e30
SEQS = 4
GROUP = 512
QUARTER = 128
HALF = 256
SPAN = 1280
LOCAL = 256


def matmul(left, right, over_left, over_right):
    dims = (((over_left,), (over_right,)), ((), ()))
    return lax.dot_general(left, right, dims, preferred_element_type=F32)


def norm_parts(values):
    mean = jnp.mean(values, axis=-1, keepdims=True)
    center = values - mean
    spread = jnp.mean(center * center, axis=-1, keepdims=True)
    inverse = lax.rsqrt(spread + EPSILON)
    return center * inverse, inverse


def norm_back(grad_normed, xhat, inverse, gain):
    e = grad_normed * gain
    return inverse * (
        e
        - jnp.mean(e, axis=-1, keepdims=True)
        - xhat * jnp.mean(e * xhat, axis=-1, keepdims=True)
    )


def column_sum(values):
    return jnp.sum(values, axis=0, keepdims=True)


def aligned(start, size, unit=128):
    return pl.ds(pl.multiple_of(start, unit), size)


def allowed_bias(query_seg, key_seg):
    ahead = lax.broadcasted_iota(jnp.int32, (HALF, SPAN), 1) - lax.broadcasted_iota(
        jnp.int32, (HALF, SPAN), 0
    )
    allowed = (ahead > 0) & (ahead <= WINDOW) & (query_seg == key_seg)
    return jnp.where(allowed, 0.0, MASKED)


class Place:
    def __init__(self, nf):
        self.nf = nf
        self.f = lax.axis_index("fsdp")
        self.z = lax.axis_index("context")
        self.t = lax.axis_index("tensor")
        self.y, self.c = self.t // 2, lax.rem(self.t, 2)
        self.mate_c = (self.f, self.z, self.t + 1 - 2 * self.c)
        self.mate_y = (self.f, self.z, lax.rem(self.t + 2, 4))
        self.mine = (2 * self.c + self.y) * QUARTER
        self.over_y = (2 * self.c + 1 - self.y) * QUARTER
        self.peers_f = [(lax.rem(self.f + j, nf), self.z, self.t) for j in range(1, nf)]
        self.peers_z = [(self.f, lax.rem(self.z + j, 4), self.t) for j in range(1, 4)]
        self.up = (self.f, lax.rem(self.z + 1, 4), self.t)
        self.down = (self.f, lax.rem(self.z + 3, 4), self.t)

    def barrier(self):
        semaphore = pltpu.get_barrier_semaphore()
        everyone = [self.mate_c, self.mate_y] + self.peers_f + self.peers_z
        for peer in everyone:
            pl.semaphore_signal(semaphore, inc=1, device_id=peer, device_id_type=MESH)
        pl.semaphore_wait(semaphore, len(everyone))


def remote(src, dst, pair, mate):
    return pltpu.make_async_remote_copy(
        src, dst, pair[0], pair[1], device_id=mate, device_id_type=MESH
    )


class Ring:
    def __init__(self, at, send, recv_c, send_y, recv_y, sems):
        self.at, self.send, self.recv_c = at, send, recv_c
        self.send_y, self.recv_y, self.sems = send_y, recv_y, sems

    def pair(self, which, s):
        return self.sems.at[which, 0, s], self.sems.at[which, 1, s]

    def rs_core(self, s):
        half = aligned((1 - self.at.c) * HALF, HALF)
        return remote(self.send.at[s, half], self.recv_c.at[s], self.pair(0, s), self.at.mate_c)

    def rs_y(self, s):
        return remote(self.send_y.at[s], self.recv_y.at[s], self.pair(1, s), self.at.mate_y)

    def back_y(self, src, dst, s):
        return remote(
            src, dst.at[s, aligned(self.at.mine, QUARTER)], self.pair(2, s), self.at.mate_y
        )

    def back_own(self, src, dst, s):
        return remote(
            src, dst.at[s, aligned(self.at.mine, QUARTER)], self.pair(3, s), self.at.mate_c
        )

    def back_over(self, dst, s):
        there = dst.at[s, aligned(self.at.over_y, QUARTER)]
        return remote(there, there, self.pair(4, s), self.at.mate_c)

    def step_q(self, s):
        self.rs_core(s).wait()
        self.send_y[s] = (
            self.send[s, aligned(self.at.over_y, QUARTER)].astype(F32)
            + self.recv_c[s, aligned((1 - self.at.y) * QUARTER, QUARTER)].astype(F32)
        ).astype(BF)
        self.rs_y(s).start()

    def total(self, s):
        self.rs_y(s).wait()
        return (
            self.send[s, aligned(self.at.mine, QUARTER)].astype(F32)
            + self.recv_c[s, aligned(self.at.y * QUARTER, QUARTER)].astype(F32)
            + self.recv_y[s].astype(F32)
        )

    def spread(self, src, dst, s):
        self.back_y(src, dst, s).start()
        self.back_own(src, dst, s).start()

    def step_t(self, src, dst, s):
        self.back_y(src, dst, s).wait()
        self.back_over(dst, s).start()

    def step_u(self, src, dst, s):
        self.back_own(src, dst, s).wait()
        self.back_over(dst, s).wait()


def front_kernel(
    nf,
    wqkv_s,
    wout_s,
    wfc1_s,
    wfc2_s,
    tokens,
    teacher,
    cot,
    vec,
    mask,
    segs,
    out_h,
    gmix_h,
    gmid_h,
    gfc1,
    gfc2,
    small,
    att,
    q,
    kv_h,
    lse,
    n1_h,
    wqkv_h,
    wout_h,
    wqkv,
    wout,
    wfc1,
    wfc2,
    n2,
    blk,
    act,
    slope,
    send,
    recv_c,
    send_y,
    recv_y,
    mid,
    gblk,
    tok_q,
    tea_q,
    cot_q,
    stage,
    segk,
    bias,
    kv,
    cnt,
    w_send,
    w_recv,
    w_loc,
    ring_sems,
    q_sems,
    in_sems,
    n1_sem,
    out_sem,
    mix_sem,
    near_sems,
    far_sems,
    cz_sems,
    cf_sems,
    res_sem,
    keep_sem,
):
    at = Place(nf)
    at.barrier()
    ring = Ring(at, send, recv_c, send_y, recv_y, ring_sems)
    mine = aligned(at.mine, QUARTER)

    fs = wout_s.shape[1]
    own = aligned(at.f * fs, fs)
    places = (
        (wqkv_s, wqkv.at[:, own, :]),
        (wout_s, wout.at[:, own]),
        (wfc1_s, wfc1.at[own, :]),
        (wfc2_s, wfc2.at[:, own]),
    )

    def weight_copy(i, j):
        pair = (w_send.at[i, j], w_recv.at[i, j])
        return remote(places[i][0], places[i][1], pair, at.peers_f[j])

    def weight_start(i):
        for j in range(nf - 1):
            weight_copy(i, j).start()
        pltpu.make_async_copy(places[i][0], places[i][1], w_loc.at[i]).start()

    def weight_wait(i):
        pltpu.make_async_copy(places[i][0], places[i][1], w_loc.at[i]).wait()
        for j in range(nf - 1):
            weight_copy(i, j).wait()

    weight_start(0)

    def token_copy(s):
        slot = lax.rem(s, 2)
        return pltpu.make_async_copy(tokens.at[s], stage.at[slot], in_sems.at[slot])

    token_copy(0).start()
    quarters = ((tokens, tok_q), (teacher, tea_q), (cot, cot_q))
    for i, (source, target) in enumerate(quarters):
        pltpu.make_async_copy(source.at[:, mine, :], target, q_sems.at[i]).start()

    masks = mask[...]
    cnt[0] = jnp.broadcast_to(jnp.sum(masks, keepdims=True), (8, 128))

    def count_z(j):
        pair = (cz_sems.at[0, j], cz_sems.at[1, j])
        return remote(cnt.at[0], cnt.at[1 + j], pair, at.peers_z[j])

    def count_f(j):
        pair = (cf_sems.at[0, j], cf_sems.at[1, j])
        return remote(cnt.at[4], cnt.at[5 + j], pair, at.peers_f[j])

    for j in range(3):
        count_z(j).start()

    turned = jnp.transpose(masks)
    segk[...] = jnp.full(segk.shape, -1.0, F32)
    segk[0:4, 1024:3072] = segs[...].astype(F32)
    seg_turned = jnp.transpose(segk[:, aligned(1024 + at.z * GROUP, GROUP)])
    column = lax.broadcasted_iota(jnp.int32, (1, 128), 1)
    for s in range(SEQS):
        lse[s] = jnp.where(column == 4, turned[:, s : s + 1], seg_turned[:, s : s + 1])
    small[...] = jnp.zeros_like(small)
    @pl.when(at.z < 2)
    def _():
        def clear(s, carry):
            kv[s, 0] = jnp.zeros((GROUP, 2 * LOCAL), BF)
            return carry

        lax.fori_loop(0, SEQS, clear, 0)

    @pl.when(at.z < 1)
    def _():
        def clear(s, carry):
            kv[s, 1] = jnp.zeros((GROUP, 2 * LOCAL), BF)
            return carry

        lax.fori_loop(0, SEQS, clear, 0)

    def near_copy(s):
        return remote(
            kv.at[s, 2], kv.at[s, 1], (near_sems.at[0, s], near_sems.at[1, s]), at.up
        )

    def far_copy(s):
        return remote(kv.at[s, 1], kv.at[s, 0], (far_sems.at[0, s], far_sems.at[1, s]), at.up)

    def norm_copy(s):
        return pltpu.make_async_copy(act.at[s], n1_h.at[s], n1_sem.at[s])

    def step_norm(s, carry):
        token_copy(s).wait()

        @pl.when(s < 3)
        def _():
            token_copy(s + 1).start()

        for part in range(2):
            here = pl.ds(part * 256, 256)
            xhat, _ = norm_parts(stage[lax.rem(s, 2), here].astype(F32))
            act[s, here] = (xhat * vec[5:6, :] + vec[6:7, :]).astype(BF)
        norm_copy(s).start()
        return carry

    def step_a(s, carry):
        normed = act[s]
        q[s] = ((matmul(normed, wqkv[0], 1, 0) + vec[7:8, 0:256]) * 0.125).astype(BF)
        kv[s, 2, :, 0:LOCAL] = matmul(normed, wqkv[1], 1, 0).astype(BF)
        kv[s, 2, :, LOCAL:] = (matmul(normed, wqkv[2], 1, 0) + vec[7:8, 256:512]).astype(BF)

        @pl.when(at.z < 3)
        def _():
            near_copy(s).start()

        return carry

    lax.fori_loop(0, SEQS, step_norm, 0)
    weight_wait(0)
    lax.fori_loop(0, SEQS, step_a, 0)
    for i in range(1, 4):
        weight_start(i)
    for j in range(3):
        count_z(j).wait()
    cnt[4] = cnt[0] + cnt[1] + cnt[2] + cnt[3]
    for j in range(nf - 1):
        count_f(j).start()
    for i, (source, target) in enumerate(quarters):
        pltpu.make_async_copy(source.at[:, mine, :], target, q_sems.at[i]).wait()
    for s in range(SEQS):
        norm_copy(s).wait()
    for j in range(nf - 1):
        count_f(j).wait()
    total_count = cnt[4]
    for j in range(nf - 1):
        total_count = total_count + cnt[5 + j]
    small[6:7, 0:128] = total_count[0:1, :]
    cnt[0] = (SEQS * GROUP * nf * 4) / total_count

    def factor():
        return cnt[0, 0:1, 0:1]

    def block_copies(s):
        return (
            pltpu.make_async_copy(teacher.at[s], stage.at[0], in_sems.at[0]),
            pltpu.make_async_copy(cot.at[s], stage.at[1], in_sems.at[1]),
        )

    for copy in block_copies(0):
        copy.start()

    def kv_out(s):
        return pltpu.make_async_copy(kv.at[s], kv_h.at[s], res_sem.at[s])

    def mix_copy(s):
        return pltpu.make_async_copy(tok_q.at[s], gmix_h.at[s, mine], mix_sem.at[s])

    def ends(k, s):
        if k == 2:
            return tok_q.at[s], gmix_h
        target = (n2, blk)[k]
        return target.at[s, mine], target

    def step_r(k, s):
        summed = ring.total(s)
        if k == 0:
            middle = tok_q[s].astype(F32) + summed + vec[0:1, :]
            mid[s] = middle
            xhat, _ = norm_parts(middle)
            n2[s, mine] = (xhat * vec[1:2, :] + vec[2:3, :]).astype(BF)
        elif k == 1:
            block = mid[s] + summed + vec[4:5, :]
            blk[s, mine] = block.astype(BF)
            difference = block - tea_q[s].astype(F32)
            masked = lse[s, mine, 4:5] * difference
            small[5:6, :] += column_sum(masked * difference)
            grad = cot_q[s].astype(F32) + masked * factor()
            gblk[s] = grad
            small[0:1, :] += column_sum(grad)
        else:
            xhat, inverse = norm_parts(mid[s])
            small[1:2, :] += column_sum(summed * xhat)
            small[2:3, :] += column_sum(summed)
            grad = gblk[s] + norm_back(summed, xhat, inverse, vec[1:2, :])
            gblk[s] = grad
            small[3:4, :] += column_sum(grad)
            tok_q[s] = grad.astype(BF)
            mix_copy(s).start()
        ring.spread(*ends(k, s), s)

    def halo(s):
        @pl.when(at.z > 0)
        def _():
            near_copy(s).wait_recv()

        @pl.when((at.z > 0) & (at.z < 3))
        def _():
            far_copy(s).start()

    def step_p0(s):
        @pl.when(at.z < 3)
        def _():
            near_copy(s).wait_send()

        @pl.when((at.z > 0) & (at.z < 3))
        def _():
            far_copy(s).wait_send()

        @pl.when(at.z > 1)
        def _():
            far_copy(s).wait_recv()

        kv_out(s).start()
        lane = lax.broadcasted_iota(jnp.int32, (1, LOCAL), 1) // HD
        slot = lax.broadcasted_iota(jnp.int32, (1, 128), 1)
        keys = kv.at[s].reshape(3 * GROUP, 2 * LOCAL)
        here_segs = segk.at[:, aligned(at.z * GROUP, 3 * GROUP)]
        which = lax.broadcasted_iota(jnp.int32, (8, SPAN), 0) == s

        def block(b, carry):
            start = pl.multiple_of(b * HALF, HALF)
            here = pl.ds(start, HALF)
            span = pl.ds(start, SPAN)
            seg_row = jnp.sum(
                jnp.where(which, here_segs[:, span], 0.0), axis=0, keepdims=True
            )
            columns = lse[s, here]
            bias[...] = allowed_bias(columns[:, 5:6], seg_row)
            query = q[s, here]
            k_block = keys[span, 0:LOCAL]
            v_block = keys[span, LOCAL:]
            mixed = jnp.zeros((HALF, LOCAL), F32)
            logs = columns
            for h in range(LOCAL // HD):
                one = jnp.where(lane == h, query, jnp.zeros_like(query))
                scores = matmul(one, k_block, 1, 1) + bias[...]
                top = jnp.max(scores, axis=-1, keepdims=True)
                weights = jnp.exp(scores - top)
                whole = jnp.sum(weights, axis=-1, keepdims=True)
                part = matmul(weights.astype(BF), v_block, 1, 0) / whole
                mixed = jnp.where(lane == h, part, mixed)
                logs = jnp.where(slot == h, top + jnp.log(whole), logs)
            att[s, here] = mixed.astype(BF)
            lse[s, here] = logs
            return carry

        lax.fori_loop(0, 2, block, 0)
        send[s] = matmul(att[s], wout[...], 1, 0).astype(BF)
        ring.rs_core(s).start()

    def step_p1(s):
        ring.step_u(*ends(0, s), s)
        for part in range(2):
            here = pl.ds(part * 256, 256)
            h = matmul(n2[s, here], wfc1[...], 1, 0) + vec[3:4, :]
            t = jnp.tanh(0.7978845608028654 * (h + 0.044715 * h * h * h))
            act[s, here] = (0.5 * h * (1.0 + t)).astype(BF)
            slope[s, here] = (
                0.5 * (1.0 + t)
                + 0.5 * h * (1.0 - t * t) * (0.7978845608028654 * (1.0 + 0.134145 * h * h))
            ).astype(BF)
        send[s] = matmul(act[s], wfc2[...], 1, 0).astype(BF)
        ring.rs_core(s).start()

    def step_p2(s):
        ring.step_u(*ends(1, s), s)
        out = pltpu.make_async_copy(blk.at[s], out_h.at[s], out_sem)
        out.start()
        for copy in block_copies(s):
            copy.wait()
        out.wait()
        for part in range(2):
            here = pl.ds(part * 256, 256)
            difference = blk[s, here].astype(F32) - stage[0, here].astype(F32)
            scaled = lse[s, here, 4:5] * factor()
            down = (stage[1, here].astype(F32) + scaled * difference).astype(BF)
            blk[s, here] = down
            up = matmul(down, wfc2[...], 1, 1) * slope[s, here].astype(F32)
            rounded = up.astype(BF)
            slope[s, here] = rounded
            small[4:5, :] += column_sum(rounded.astype(F32))

        @pl.when(s < 3)
        def _():
            for copy in block_copies(s + 1):
                copy.start()

        send[s] = matmul(slope[s], wfc1[...], 1, 1).astype(BF)
        ring.rs_core(s).start()

    steps_p = (step_p0, step_p1, step_p2)

    def inside(s, action):
        @pl.when((s >= 0) & (s < SEQS))
        def _():
            action(s)

    halo(0)

    def wave(m, carry):
        for k in range(3):
            for lag in (3, 2):
                kind = (k - lag) % 3
                s = m + (k - lag - kind) // 3 - kind
                if lag == 3:
                    inside(s, lambda s: ring.step_t(*ends(kind, s), s))
                else:
                    inside(s, lambda s: step_r(kind, s))
            if k == 0:
                inside(m + 1, halo)

                @pl.when(m == 0)
                def _():
                    weight_wait(1)

            if k == 1:

                @pl.when(m == 1)
                def _():
                    weight_wait(2)
                    weight_wait(3)

            inside(m - k, steps_p[k])
            inside(m - k, ring.step_q)
        return carry

    lax.fori_loop(0, 7, wave, 0)
    deep = lambda ref: ref.reshape(SEQS * GROUP, 1024)
    last = pltpu.make_async_copy(gblk, gmid_h, out_sem)
    last.start()
    kept = (
        pltpu.make_async_copy(wqkv, wqkv_h, keep_sem.at[0]),
        pltpu.make_async_copy(wout, wout_h, keep_sem.at[1]),
    )
    for copy in kept:
        copy.start()
    deep(send)[0:1024, :] = matmul(deep(act)[...], deep(blk)[...], 0, 0).astype(BF)
    down_out = pltpu.make_async_copy(deep(send).at[0:1024], gfc2, in_sems.at[0])
    down_out.start()
    deep(send)[1024:2048, :] = matmul(deep(n2)[...], deep(slope)[...], 0, 0).astype(BF)
    up_out = pltpu.make_async_copy(deep(send).at[1024:2048], gfc1, in_sems.at[1])
    up_out.start()
    for s in range(SEQS):
        ring.step_u(*ends(2, s), s)
        mix_copy(s).wait()
        kv_out(s).wait()
    last.wait()
    down_out.wait()
    up_out.wait()
    for copy in kept:
        copy.wait()


def front_call(nf, *args):
    anys = pl.BlockSpec(memory_space=pl.ANY)
    vmem = pl.BlockSpec(memory_space=pltpu.VMEM)
    dma = pltpu.SemaphoreType.DMA
    big = lambda *lead: pltpu.VMEM((*lead, GROUP, 1024), BF)
    shape = jax.ShapeDtypeStruct
    return pl.pallas_call(
        functools.partial(front_kernel, nf),
        out_shape=(
            shape((SEQS, GROUP, 1024), BF),
            shape((SEQS, GROUP, 1024), BF),
            shape((SEQS, QUARTER, 1024), F32),
            shape((1024, 1024), BF),
            shape((1024, 1024), BF),
            shape((8, 1024), F32),
            shape((SEQS, GROUP, LOCAL), BF),
            shape((SEQS, GROUP, LOCAL), BF),
            shape((SEQS, 3, GROUP, 2 * LOCAL), BF),
            shape((SEQS, GROUP, 128), F32),
            shape((SEQS, GROUP, 1024), BF),
            shape((3, 1024, LOCAL), BF),
            shape((LOCAL, 1024), BF),
        ),
        in_specs=[anys] * 7 + [vmem] * 3,
        out_specs=(anys, anys, anys, anys, anys, vmem, vmem, vmem, anys, vmem, anys, anys, anys),
        scratch_shapes=[
            pltpu.VMEM((3, 1024, LOCAL), BF),
            pltpu.VMEM((LOCAL, 1024), BF),
            pltpu.VMEM((1024, 1024), BF),
            pltpu.VMEM((1024, 1024), BF),
            big(SEQS),
            big(SEQS),
            big(SEQS),
            big(SEQS),
            big(SEQS),
            pltpu.VMEM((SEQS, HALF, 1024), BF),
            pltpu.VMEM((SEQS, QUARTER, 1024), BF),
            pltpu.VMEM((SEQS, QUARTER, 1024), BF),
            pltpu.VMEM((SEQS, QUARTER, 1024), F32),
            pltpu.VMEM((SEQS, QUARTER, 1024), F32),
            pltpu.VMEM((SEQS, QUARTER, 1024), BF),
            pltpu.VMEM((SEQS, QUARTER, 1024), BF),
            pltpu.VMEM((SEQS, QUARTER, 1024), BF),
            big(2),
            pltpu.VMEM((8, 3072), F32),
            pltpu.VMEM((HALF, SPAN), F32),
            pltpu.VMEM((SEQS, 3, GROUP, 2 * LOCAL), BF),
            pltpu.VMEM((4 + nf, 8, 128), F32),
            dma((4, nf - 1)),
            dma((4, nf - 1)),
            dma((4,)),
            dma((5, 2, SEQS)),
            dma((3,)),
            dma((2,)),
            dma((SEQS,)),
            dma,
            dma((SEQS,)),
            dma((2, SEQS)),
            dma((2, SEQS)),
            dma((2, 3)),
            dma((2, nf - 1)),
            dma((SEQS,)),
            dma((2,)),
        ],
        compiler_params=pltpu.CompilerParams(
            collective_id=1, has_side_effects=True, vmem_limit_bytes=63 * 2**20
        ),
        cost_estimate=pl.CostEstimate(
            flops=2 * 2048 * 1024 * 1024 * 9, bytes_accessed=30 * 2**20, transcendentals=0
        ),
        name="front",
    )(*args)


class Reduce:
    def __init__(self, at, cut, size, rows, full, arrived, shard, half, quarter, sems):
        self.at, self.cut, self.size, self.rows = at, cut, size, rows
        self.full, self.arrived, self.shard = full, arrived, shard
        self.half, self.quarter = half, quarter
        self.x_sems, self.z_sems = sems
        self.a, self.b = lax.rem(at.z, 2), at.z // 2
        self.side = (at.f, at.z + 1 - 2 * self.a, at.t)
        self.across = (at.f, lax.rem(at.z + 2, 4), at.t)

    def own(self, f):
        return self.cut(self.full, aligned(f * self.size, self.size, math.gcd(self.size, 128)))

    def part(self, ref, start, size):
        where = aligned(start, size, 16)
        return ref.at[:, where, :] if len(ref.shape) == 3 else ref.at[where, :]

    def x_copy(self, j):
        there = lax.rem(self.at.f + 1 + j, self.at.nf)
        pair = (self.x_sems.at[0, j], self.x_sems.at[1, j])
        return remote(self.own(there), self.arrived.at[j], pair, self.at.peers_f[j])

    def z_copy(self, stage):
        h, q = self.rows // 2, self.rows // 4
        pair = (self.z_sems.at[0, stage], self.z_sems.at[1, stage])
        own = self.own(self.at.f)
        if stage == 0:
            return remote(self.part(own, (1 - self.a) * h, h), self.half, pair, self.side)
        if stage == 1:
            src = self.part(own, self.a * h + (1 - self.b) * q, q)
            return remote(src, self.quarter, pair, self.across)
        if stage == 2:
            kept = self.part(self.shard, self.a * h + self.b * q, q)
            return remote(kept, kept, pair, self.across)
        kept = self.part(self.shard, self.a * h, h)
        return remote(kept, kept, pair, self.side)

    def add(self, target, first, others):
        total = first[...].astype(F32)
        for other in others:
            total = total + other[...].astype(F32)
        target[...] = total.astype(BF)

    def run(self, stage):
        h, q = self.rows // 2, self.rows // 4
        peers = range(self.at.nf - 1)
        own = self.own(self.at.f)
        if stage == 0:
            for j in peers:
                self.x_copy(j).start()
            return
        if stage == 1:
            for j in peers:
                self.x_copy(j).wait()
            self.add(own, own, [self.arrived.at[j] for j in peers])
        else:
            self.z_copy(stage - 2).wait()
        if stage == 2:
            kept = self.part(own, self.a * h, h)
            self.add(kept, kept, [self.half])
        elif stage == 3:
            start = self.a * h + self.b * q
            self.add(self.part(self.shard, start, q), self.part(own, start, q), [self.quarter])
        if stage < 5:
            self.z_copy(stage - 1).start()


def back_kernel(
    nf,
    gmix_h,
    gmid_h,
    gfc1_h,
    gfc2_h,
    att,
    q,
    kv_h,
    lse,
    n1_h,
    tokens,
    wqkv,
    wout,
    vec,
    segs,
    ig_h,
    small,
    s_qkv,
    s_out,
    s_fc1,
    s_fc2,
    gm,
    kvs,
    n1s,
    ga,
    dots,
    bias,
    segk,
    dkvt,
    dfar,
    dnear,
    down,
    m1,
    m2,
    gq,
    send,
    recv_c,
    send_y,
    recv_y,
    gmid,
    tok_q,
    a_qkv,
    a_out,
    f_qkv,
    f_fc1,
    f_fc2,
    x_qkv,
    x_out,
    x_fc1,
    x_fc2,
    h_qkv,
    h_out,
    h_fc1,
    h_fc2,
    k_qkv,
    k_out,
    k_fc1,
    k_fc2,
    ring_sems,
    load_sems,
    first_sems,
    m1_sems,
    m2_sems,
    red_x,
    red_z,
):
    at = Place(nf)
    at.barrier()
    ring = Ring(at, send, recv_c, send_y, recv_y, ring_sems)
    mine = aligned(at.mine, QUARTER)
    rows_cut = lambda ref, where: ref.at[where, :]
    cols_cut = lambda ref, where: ref.at[:, where]
    deep_cut = lambda ref, where: ref.at[:, where, :]
    fs = 1024 // nf
    f_out = gm.at[0:LOCAL]

    def reducer(i, cut, rows, full, arrived, shard, half, quarter):
        sems = (red_x.at[i], red_z.at[i])
        return Reduce(at, cut, fs, rows, full, arrived, shard, half, quarter, sems)

    red_qkv = reducer(0, deep_cut, fs, f_qkv, x_qkv, s_qkv, h_qkv, k_qkv)
    red_out = reducer(1, cols_cut, LOCAL, f_out, x_out, s_out, h_out, k_out)
    red_fc1 = reducer(2, rows_cut, fs, f_fc1, x_fc1, s_fc1, h_fc1, k_fc1)
    red_fc2 = reducer(3, cols_cut, 1024, f_fc2, x_fc2, s_fc2, h_fc2, k_fc2)

    firsts = (
        (gfc1_h, f_fc1),
        (gfc2_h, f_fc2),
        (gmid_h.at[0], gmid),
        (tokens.at[:, mine, :], tok_q),
    )

    def first_copy(i):
        return pltpu.make_async_copy(firsts[i][0], firsts[i][1], first_sems.at[i])

    def load_copies(s):
        return (
            pltpu.make_async_copy(gmix_h.at[s], gm, load_sems.at[0, 0]),
            pltpu.make_async_copy(kv_h.at[s], kvs, load_sems.at[1, 0]),
        )

    def norm_load(s):
        return pltpu.make_async_copy(n1_h.at[s], n1s, load_sems.at[2, 0])

    def mid_load(s):
        return pltpu.make_async_copy(gmid_h.at[s], gmid, load_sems.at[2, 1])

    for copy in load_copies(0):
        copy.start()
    for i in range(4):
        first_copy(i).start()
    norm_load(0).start()

    segk[...] = jnp.full(segk.shape, -1.0, F32)
    segk[0:4, 1024:3072] = segs[...].astype(F32)
    small[...] = jnp.zeros_like(small)
    a_qkv[...] = jnp.zeros_like(a_qkv)
    a_out[...] = jnp.zeros_like(a_out)
    def m1_copy(s):
        return remote(dfar.at[s], m1.at[s], (m1_sems.at[0, s], m1_sems.at[1, s]), at.down)

    def m2_copy(s):
        return remote(dnear.at[s], m2.at[s], (m2_sems.at[0, s], m2_sems.at[1, s]), at.down)

    def step_e(s):
        for copy in load_copies(s):
            copy.wait()

        ga[...] = matmul(gm[...], wout[...], 1, 1).astype(BF)
        a_out[...] += matmul(att[s], gm[...], 0, 0)

        lane = lax.broadcasted_iota(jnp.int32, (1, LOCAL), 1) // HD
        keys = kvs.reshape(3 * GROUP, 2 * LOCAL)
        here_segs = segk.at[:, aligned(at.z * GROUP, 3 * GROUP)]
        which = lax.broadcasted_iota(jnp.int32, (8, SPAN), 0) == s
        dkvt[...] = jnp.zeros_like(dkvt)

        def block(b, carry):
            start = pl.multiple_of(b * HALF, HALF)
            here = pl.ds(start, HALF)
            span = pl.ds(start, SPAN)
            seg_row = jnp.sum(
                jnp.where(which, here_segs[:, span], 0.0), axis=0, keepdims=True
            )
            logs = lse[s, here]
            bias[...] = allowed_bias(logs[:, 5:6], seg_row)
            query = q[s, here]
            grad = ga[here]
            k_block = keys[span, 0:LOCAL]
            v_block = keys[span, LOCAL:]
            dots[0] = jnp.transpose(query)
            dots[1] = jnp.transpose(grad)
            product = grad.astype(F32) * att[s, here].astype(F32)
            grad_query = jnp.zeros((HALF, LOCAL), F32)
            for h in range(LOCAL // HD):
                mine_h = lane == h
                one = jnp.where(mine_h, query, jnp.zeros_like(query))
                grad_one = jnp.where(mine_h, grad, jnp.zeros_like(grad))
                delta = jnp.sum(jnp.where(mine_h, product, 0.0), axis=-1, keepdims=True)
                scores = matmul(one, k_block, 1, 1) + bias[...]
                probs = jnp.exp(scores - logs[:, h : h + 1])
                dprobs = matmul(grad_one, v_block, 1, 1)
                grad_scores = (probs * (dprobs - delta)).astype(BF)
                grad_query = jnp.where(mine_h, matmul(grad_scores, k_block, 1, 0), grad_query)
                k_rows = pl.ds(h * HD, HD)
                v_rows = pl.ds(LOCAL + h * HD, HD)
                dkvt[k_rows, span] += matmul(dots[0, k_rows], grad_scores, 1, 0)
                dkvt[v_rows, span] += matmul(dots[1, k_rows], probs.astype(BF), 1, 0)
            gq[s, here] = (grad_query * 0.125).astype(BF)
            return carry

        lax.fori_loop(0, 2, block, 0)

        @pl.when(s < 3)
        def _():
            for copy in load_copies(s + 1):
                copy.start()

        for i, target in enumerate((dfar, dnear, down)):
            target[s] = jnp.transpose(dkvt[:, i * GROUP : (i + 1) * GROUP].astype(BF))

        @pl.when(at.z > 1)
        def _():
            m1_copy(s).start()

    def step_i(s):
        @pl.when((at.z > 0) & (at.z < 3))
        def _():
            m1_copy(s).wait_recv()
            dnear[s] = (dnear[s].astype(F32) + m1[s].astype(F32)).astype(BF)

        @pl.when(at.z > 0)
        def _():
            m2_copy(s).start()

    def step_f(s):
        @pl.when(at.z < 3)
        def _():
            m2_copy(s).wait_recv()
            down[s] = (down[s].astype(F32) + m2[s].astype(F32)).astype(BF)

        norm_load(s).wait()
        grads = (gq[s], down[s, :, 0:LOCAL], down[s, :, LOCAL:])
        send[s] = (
            matmul(grads[0], wqkv[0], 1, 1)
            + matmul(grads[1], wqkv[1], 1, 1)
            + matmul(grads[2], wqkv[2], 1, 1)
        ).astype(BF)
        ring.rs_core(s).start()
        normed = n1s[...]
        for i in range(3):
            a_qkv[i] += matmul(normed, grads[i], 0, 0)

        @pl.when(s < 3)
        def _():
            norm_load(s + 1).start()

        small[2:3, 0:LOCAL] += column_sum(grads[0].astype(F32))
        small[2:3, LOCAL : 2 * LOCAL] += column_sum(grads[2].astype(F32))

    def ends(s):
        return tok_q.at[s], ig_h

    def ig_copy(s):
        return pltpu.make_async_copy(tok_q.at[s], ig_h.at[s, mine], first_sems.at[s])

    def step_r(s):
        summed = ring.total(s)
        xhat, inverse = norm_parts(tok_q[s].astype(F32))
        small[0:1, :] += column_sum(summed * xhat)
        small[1:2, :] += column_sum(summed)
        @pl.when(s > 0)
        def _():
            mid_load(s).wait()

        grad = gmid[...] + norm_back(summed, xhat, inverse, vec[5:6, :])
        tok_q[s] = grad.astype(BF)

        @pl.when(s < 3)
        def _():
            mid_load(s + 1).start()

        ig_copy(s).start()
        ring.spread(*ends(s), s)

    def inside(s, action):
        @pl.when((s >= 0) & (s < SEQS))
        def _():
            action(s)

    for i in range(4):
        first_copy(i).wait()
    red_fc1.run(0)
    red_fc2.run(0)

    def wave(m, carry):
        inside(m, step_e)
        inside(m - 1, step_i)
        inside(m - 4, lambda s: ring.step_t(*ends(s), s))
        inside(m - 3, step_r)
        inside(m - 2, step_f)
        inside(m - 2, ring.step_q)
        return carry

    lax.fori_loop(0, 6, wave, 0)
    f_out[...] = a_out[...].astype(BF)
    f_qkv[...] = a_qkv[...].astype(BF)
    red_out.run(0)
    red_qkv.run(0)
    for reduce in (red_fc1, red_fc2):
        reduce.run(1)
    ring.step_t(*ends(2), 2)
    step_r(3)
    for reduce in (red_out, red_qkv):
        reduce.run(1)
    ring.step_t(*ends(3), 3)
    for stage in (2, 3, 4, 5):
        for reduce in (red_fc1, red_fc2, red_out, red_qkv):
            reduce.run(stage)
    for s in range(SEQS):
        ring.step_u(*ends(s), s)
        ig_copy(s).wait()

        @pl.when(at.z > 1)
        def _():
            m1_copy(s).wait_send()

        @pl.when(at.z > 0)
        def _():
            m2_copy(s).wait_send()


def back_call(nf, *args):
    anys = pl.BlockSpec(memory_space=pl.ANY)
    vmem = pl.BlockSpec(memory_space=pltpu.VMEM)
    dma = pltpu.SemaphoreType.DMA
    big = lambda *lead: pltpu.VMEM((*lead, GROUP, 1024), BF)
    shape = jax.ShapeDtypeStruct
    fs = 1024 // nf
    low = lambda *dims: pltpu.VMEM(dims, BF)
    return pl.pallas_call(
        functools.partial(back_kernel, nf),
        out_shape=(
            shape((SEQS, GROUP, 1024), BF),
            shape((8, 1024), F32),
            shape((3, fs, LOCAL), BF),
            shape((LOCAL, fs), BF),
            shape((fs, 1024), BF),
            shape((1024, fs), BF),
        ),
        in_specs=[anys] * 4 + [vmem, vmem, anys, vmem, anys, anys, vmem, vmem, vmem, vmem],
        out_specs=(anys, vmem, vmem, vmem, vmem, vmem),
        scratch_shapes=[
            low(GROUP, 1024),
            low(3, GROUP, 2 * LOCAL),
            low(GROUP, 1024),
            low(GROUP, LOCAL),
            low(2, LOCAL, HALF),
            pltpu.VMEM((HALF, SPAN), F32),
            pltpu.VMEM((8, 3072), F32),
            pltpu.VMEM((2 * LOCAL, 3 * GROUP), F32),
            low(SEQS, GROUP, 2 * LOCAL),
            low(SEQS, GROUP, 2 * LOCAL),
            low(SEQS, GROUP, 2 * LOCAL),
            low(SEQS, GROUP, 2 * LOCAL),
            low(SEQS, GROUP, 2 * LOCAL),
            low(SEQS, GROUP, LOCAL),
            big(SEQS),
            low(SEQS, HALF, 1024),
            low(SEQS, QUARTER, 1024),
            low(SEQS, QUARTER, 1024),
            pltpu.VMEM((QUARTER, 1024), F32),
            low(SEQS, QUARTER, 1024),
            pltpu.VMEM((3, 1024, LOCAL), F32),
            pltpu.VMEM((LOCAL, 1024), F32),
            low(3, 1024, LOCAL),
            low(1024, 1024),
            low(1024, 1024),
            low(nf - 1, 3, fs, LOCAL),
            low(nf - 1, LOCAL, fs),
            low(nf - 1, fs, 1024),
            low(nf - 1, 1024, fs),
            low(3, fs // 2, LOCAL),
            low(LOCAL // 2, fs),
            low(fs // 2, 1024),
            low(512, fs),
            low(3, fs // 4, LOCAL),
            low(LOCAL // 4, fs),
            low(fs // 4, 1024),
            low(256, fs),
            dma((5, 2, SEQS)),
            dma((3, 2)),
            dma((4,)),
            dma((2, SEQS)),
            dma((2, SEQS)),
            dma((4, 2, nf - 1)),
            dma((4, 2, 4)),
        ],
        compiler_params=pltpu.CompilerParams(
            collective_id=2, has_side_effects=True, vmem_limit_bytes=63 * 2**20
        ),
        cost_estimate=pl.CostEstimate(
            flops=2 * 2048 * 1024 * 1024 * 6, bytes_accessed=30 * 2**20, transcendentals=0
        ),
        name="back",
    )(*args)


def local(
    tokens,
    cotangent,
    teacher,
    valid_mask,
    segment_ids,
    ln1_gain,
    ln1_bias,
    w_qkv,
    b_qv,
    w_out,
    b_out,
    ln2_gain,
    ln2_bias,
    w_fc1,
    b_fc1,
    w_fc2,
    b_fc2,
):
    nf = lax.axis_size("fsdp")
    pieces = (b_out, ln2_gain, ln2_bias, b_fc2, ln1_gain, ln1_bias, b_qv, b_fc1)
    flat = lax.all_gather(jnp.concatenate([piece.reshape(-1) for piece in pieces]), "fsdp", axis=0)
    flat = flat.astype(F32)
    wide = b_out.shape[0]
    rows = [flat[:, i * wide : (i + 1) * wide].reshape(1, D) for i in range(6)]
    small_qv = flat[:, 6 * wide : 6 * wide + b_qv.size].reshape(nf, *b_qv.shape)
    small_up = flat[:, 6 * wide + b_qv.size :].reshape(nf, *b_fc1.shape)
    bias_qv = jnp.moveaxis(small_qv, 0, 2).reshape(1, 2 * LOCAL)
    bias_up = jnp.moveaxis(small_up, 0, 1).reshape(1, D)
    vec = jnp.concatenate(
        rows[:3]
        + [bias_up]
        + rows[3:]
        + [jnp.concatenate([bias_qv, jnp.zeros((1, D - 2 * LOCAL), F32)], axis=1)],
        axis=0,
    )
    mask_f = jnp.concatenate([valid_mask, jnp.zeros_like(valid_mask)], axis=0).astype(F32)
    front = front_call(
        nf, w_qkv, w_out, w_fc1, w_fc2, tokens, teacher, cotangent, vec, mask_f, segment_ids
    )
    (output, grad_mix, grad_middle, gfc1, gfc2, sums_one, att, q, kv, lse, n1, wqkv, wout) = front
    input_grad, sums_two, s_qkv, s_out, s_fc1, s_fc2 = back_call(
        nf, grad_mix, grad_middle, gfc1, gfc2, att, q, kv, lse, n1, tokens, wqkv, wout, vec, segment_ids
    )
    place_f = lax.axis_index("fsdp")
    place_t = lax.axis_index("tensor")
    by_tensor = jnp.stack([sums_one[4], sums_two[2]])
    slots = jnp.where(jnp.arange(4)[:, None, None] == place_t, by_tensor[None], 0.0)
    everything = jnp.concatenate([sums_one[0:4], sums_one[5:6], sums_two[0:2], slots.reshape(8, D)])
    everything = lax.psum(everything, ("fsdp", "context", "tensor"))
    loss = jnp.sum(everything[4]) / (2.0 * D * sums_one[6, 0])
    ours = lax.dynamic_index_in_dim(everything[7:].reshape(4, 2, D), place_t, 0, keepdims=False)
    part = lax.dynamic_slice_in_dim(everything[0:7], place_f * wide, wide, 1)
    grad_up = ours[0].reshape(b_fc1.shape[0], -1)
    grad_up = lax.dynamic_slice_in_dim(grad_up, place_f * b_fc1.shape[1], b_fc1.shape[1], 1)
    grad_qv = ours[1, : 2 * LOCAL].reshape(2, LOCAL // HD, HD)
    grad_qv = lax.dynamic_slice_in_dim(grad_qv, place_f * b_qv.shape[2], b_qv.shape[2], 2)
    return (
        output,
        loss,
        input_grad,
        part[5],
        part[6],
        s_qkv.astype(F32),
        grad_qv,
        s_out.astype(F32),
        part[3],
        part[1],
        part[2],
        s_fc1.astype(F32),
        grad_up,
        s_fc2.astype(F32),
        part[0],
    )


def solution(mesh):
    return jax.shard_map(
        local,
        mesh=mesh,
        in_specs=(
            P("fsdp", "context", None),
            P("fsdp", "context", None),
            P("fsdp", "context", None),
            P("fsdp", "context"),
            P("fsdp", None),
            P("fsdp"),
            P("fsdp"),
            P(None, "fsdp", "tensor"),
            P(None, "tensor", "fsdp"),
            P("tensor", "fsdp"),
            P("fsdp"),
            P("fsdp"),
            P("fsdp"),
            P("fsdp", "tensor"),
            P("tensor", "fsdp"),
            P("tensor", "fsdp"),
            P("fsdp"),
        ),
        out_specs=(
            P("fsdp", "context", None),
            P(),
            P("fsdp", "context", None),
            P("fsdp"),
            P("fsdp"),
            P(None, "fsdp", "tensor"),
            P(None, "tensor", "fsdp"),
            P("tensor", "fsdp"),
            P("fsdp"),
            P("fsdp"),
            P("fsdp"),
            P("fsdp", "tensor"),
            P("tensor", "fsdp"),
            P("tensor", "fsdp"),
            P("fsdp"),
        ),
        check_vma=False,
    )
```

```python
import functools
import math

import jax
import jax.numpy as jnp
from jax import lax
from jax.experimental import pallas as pl
from jax.experimental.pallas import tpu as pltpu
from jax.sharding import PartitionSpec as P

MESH = pl.DeviceIdType.MESH
BF = jnp.bfloat16
F32 = jnp.float32
D = 1024
HD = 64
WINDOW = 1024
EPSILON = 1e-05
MASKED = -1e30
SEQS = 4
GROUP = 512
QUARTER = 128
HALF = 256
SPAN = 1280
LOCAL = 256


def matmul(left, right, over_left, over_right):
    dims = (((over_left,), (over_right,)), ((), ()))
    return lax.dot_general(left, right, dims, preferred_element_type=F32)


def norm_parts(values):
    mean = jnp.mean(values, axis=-1, keepdims=True)
    center = values - mean
    spread = jnp.mean(center * center, axis=-1, keepdims=True)
    inverse = lax.rsqrt(spread + EPSILON)
    return center * inverse, inverse


def norm_back(grad_normed, xhat, inverse, gain):
    e = grad_normed * gain
    return inverse * (
        e
        - jnp.mean(e, axis=-1, keepdims=True)
        - xhat * jnp.mean(e * xhat, axis=-1, keepdims=True)
    )


def column_sum(values):
    return jnp.sum(values, axis=0, keepdims=True)


def aligned(start, size, unit=128):
    return pl.ds(pl.multiple_of(start, unit), size)


def allowed_bias(query_seg, key_seg):
    ahead = lax.broadcasted_iota(jnp.int32, (HALF, SPAN), 1) - lax.broadcasted_iota(
        jnp.int32, (HALF, SPAN), 0
    )
    allowed = (ahead > 0) & (ahead <= WINDOW) & (query_seg == key_seg)
    return jnp.where(allowed, 0.0, MASKED)


class Place:
    def __init__(self, nf):
        self.nf = nf
        self.f = lax.axis_index("fsdp")
        self.z = lax.axis_index("context")
        self.t = lax.axis_index("tensor")
        self.y, self.c = self.t // 2, lax.rem(self.t, 2)
        self.mate_c = (self.f, self.z, self.t + 1 - 2 * self.c)
        self.mate_y = (self.f, self.z, lax.rem(self.t + 2, 4))
        self.mine = (2 * self.c + self.y) * QUARTER
        self.over_y = (2 * self.c + 1 - self.y) * QUARTER
        self.peers_f = [(lax.rem(self.f + j, nf), self.z, self.t) for j in range(1, nf)]
        self.peers_z = [(self.f, lax.rem(self.z + j, 4), self.t) for j in range(1, 4)]
        self.up = (self.f, lax.rem(self.z + 1, 4), self.t)
        self.down = (self.f, lax.rem(self.z + 3, 4), self.t)

    def barrier(self):
        semaphore = pltpu.get_barrier_semaphore()
        everyone = [self.mate_c, self.mate_y] + self.peers_f + self.peers_z
        for peer in everyone:
            pl.semaphore_signal(semaphore, inc=1, device_id=peer, device_id_type=MESH)
        pl.semaphore_wait(semaphore, len(everyone))


def remote(src, dst, pair, mate):
    return pltpu.make_async_remote_copy(
        src, dst, pair[0], pair[1], device_id=mate, device_id_type=MESH
    )


def run_order(actions, order):
    names = list(actions)
    codes = [names.index(name) * 8 + s for name, s in order]

    def step(i, carry):
        code = jnp.int32(codes[0])
        for j, other in enumerate(codes[1:]):
            code = jnp.where(i == j + 1, other, code)
        kind, s = code // 8, lax.rem(code, 8)
        for j, name in enumerate(names):

            @pl.when(kind == j)
            def _(action=actions[name]):
                action(s)

        return carry

    lax.fori_loop(0, len(order), step, 0)


class Ring:
    def __init__(self, at, send, recv_c, send_y, recv_y, sems):
        self.at, self.send, self.recv_c = at, send, recv_c
        self.send_y, self.recv_y, self.sems = send_y, recv_y, sems

    def pair(self, which, s):
        return self.sems.at[which, 0, s], self.sems.at[which, 1, s]

    def rs_core(self, s):
        half = aligned((1 - self.at.c) * HALF, HALF)
        return remote(self.send.at[s, half], self.recv_c.at[s], self.pair(0, s), self.at.mate_c)

    def rs_y(self, s):
        return remote(self.send_y.at[s], self.recv_y.at[s], self.pair(1, s), self.at.mate_y)

    def back_y(self, src, dst, s):
        return remote(
            src, dst.at[s, aligned(self.at.mine, QUARTER)], self.pair(2, s), self.at.mate_y
        )

    def back_own(self, src, dst, s):
        return remote(
            src, dst.at[s, aligned(self.at.mine, QUARTER)], self.pair(3, s), self.at.mate_c
        )

    def back_over(self, dst, s):
        there = dst.at[s, aligned(self.at.over_y, QUARTER)]
        return remote(there, there, self.pair(4, s), self.at.mate_c)

    def step_q(self, s):
        self.rs_core(s).wait()
        self.send_y[s] = (
            self.send[s, aligned(self.at.over_y, QUARTER)].astype(F32)
            + self.recv_c[s, aligned((1 - self.at.y) * QUARTER, QUARTER)].astype(F32)
        ).astype(BF)
        self.rs_y(s).start()

    def total(self, s):
        self.rs_y(s).wait()
        return (
            self.send[s, aligned(self.at.mine, QUARTER)].astype(F32)
            + self.recv_c[s, aligned(self.at.y * QUARTER, QUARTER)].astype(F32)
            + self.recv_y[s].astype(F32)
        )

    def spread(self, src, dst, s):
        self.back_y(src, dst, s).start()
        self.back_own(src, dst, s).start()

    def step_t(self, src, dst, s):
        self.back_y(src, dst, s).wait()
        self.back_over(dst, s).start()

    def step_u(self, src, dst, s):
        self.back_own(src, dst, s).wait()
        self.back_over(dst, s).wait()


FRONT_ORDER = (
    ("A", 0),
    ("A", 1),
    ("A", 2),
    ("A", 3),
    ("C", 0),
    ("H", 0),
    ("V", 0),
    ("P0", 0),
    ("Q", 0),
    ("H", 1),
    ("R0", 0),
    ("P0", 1),
    ("T0", 0),
    ("Q", 1),
    ("D", 0),
    ("W", 0),
    ("P1", 0),
    ("H", 2),
    ("Q", 0),
    ("R0", 1),
    ("R1", 0),
    ("P0", 2),
    ("T0", 1),
    ("T1", 0),
    ("Q", 2),
    ("P1", 1),
    ("H", 3),
    ("P2", 0),
    ("Q", 1),
    ("R0", 2),
    ("Q", 0),
    ("P0", 3),
    ("R1", 1),
    ("T0", 2),
    ("Q", 3),
    ("P1", 2),
    ("R2", 0),
    ("T1", 1),
    ("Q", 2),
    ("P2", 1),
    ("R0", 3),
    ("Q", 1),
    ("T2", 0),
    ("R1", 2),
    ("T0", 3),
    ("P1", 3),
    ("R2", 1),
    ("Q", 3),
    ("T1", 2),
    ("P2", 2),
    ("T2", 1),
    ("Q", 2),
    ("R1", 3),
    ("R2", 2),
    ("T1", 3),
    ("P2", 3),
    ("T2", 2),
    ("Q", 3),
    ("gdown", 0),
    ("R2", 3),
    ("gup", 0),
    ("T2", 3),
)


def front_kernel(
    nf,
    wqkv_s,
    wout_s,
    wfc1_s,
    wfc2_s,
    tokens,
    teacher,
    cot,
    vec,
    mask,
    segs,
    out_h,
    gmix_h,
    gmid_h,
    gfc1,
    gfc2,
    small,
    att,
    q,
    kv_h,
    lse,
    n1_h,
    wqkv_h,
    wout_h,
    wqkv,
    wout,
    wfc1,
    wfc2,
    n2,
    blk,
    act,
    slope,
    send,
    recv_c,
    send_y,
    recv_y,
    mid,
    gblk,
    tok_q,
    tea_q,
    cot_q,
    stage,
    segk,
    bias,
    kv,
    cnt,
    w_send,
    w_recv,
    w_loc,
    ring_sems,
    q_sems,
    in_sems,
    n1_sem,
    out_sem,
    mix_sem,
    near_sems,
    far_sems,
    cz_sems,
    cf_sems,
    res_sem,
    keep_sem,
):
    at = Place(nf)
    at.barrier()
    ring = Ring(at, send, recv_c, send_y, recv_y, ring_sems)
    mine = aligned(at.mine, QUARTER)

    fs = wout_s.shape[1]
    own = aligned(at.f * fs, fs)
    places = (
        (wqkv_s, wqkv.at[:, own, :]),
        (wout_s, wout.at[:, own]),
        (wfc1_s, wfc1.at[own, :]),
        (wfc2_s, wfc2.at[:, own]),
    )

    def weight_copy(i, j):
        pair = (w_send.at[i, j], w_recv.at[i, j])
        return remote(places[i][0], places[i][1], pair, at.peers_f[j])

    def weight_start(i):
        for j in range(nf - 1):
            weight_copy(i, j).start()
        pltpu.make_async_copy(places[i][0], places[i][1], w_loc.at[i]).start()

    def weight_wait(i):
        pltpu.make_async_copy(places[i][0], places[i][1], w_loc.at[i]).wait()
        for j in range(nf - 1):
            weight_copy(i, j).wait()

    weight_start(0)

    def token_copy(s):
        slot = lax.rem(s, 2)
        return pltpu.make_async_copy(tokens.at[s], stage.at[slot], in_sems.at[slot])

    token_copy(0).start()
    quarters = ((tokens, tok_q), (teacher, tea_q), (cot, cot_q))
    for i, (source, target) in enumerate(quarters):
        pltpu.make_async_copy(source.at[:, mine, :], target, q_sems.at[i]).start()

    masks = mask[...]
    cnt[0] = jnp.broadcast_to(jnp.sum(masks, keepdims=True), (8, 128))

    def count_z(j):
        pair = (cz_sems.at[0, j], cz_sems.at[1, j])
        return remote(cnt.at[0], cnt.at[1 + j], pair, at.peers_z[j])

    def count_f(j):
        pair = (cf_sems.at[0, j], cf_sems.at[1, j])
        return remote(cnt.at[4], cnt.at[5 + j], pair, at.peers_f[j])

    for j in range(3):
        count_z(j).start()

    turned = jnp.transpose(masks)
    segk[...] = jnp.full(segk.shape, -1.0, F32)
    segk[0:4, 1024:3072] = segs[...].astype(F32)
    seg_turned = jnp.transpose(segk[:, aligned(1024 + at.z * GROUP, GROUP)])
    column = lax.broadcasted_iota(jnp.int32, (1, 128), 1)
    for s in range(SEQS):
        lse[s] = jnp.where(column == 4, turned[:, s : s + 1], seg_turned[:, s : s + 1])
    small[...] = jnp.zeros_like(small)
    @pl.when(at.z < 2)
    def _():
        def clear(s, carry):
            kv[s, 0] = jnp.zeros((GROUP, 2 * LOCAL), BF)
            return carry

        lax.fori_loop(0, SEQS, clear, 0)

    @pl.when(at.z < 1)
    def _():
        def clear(s, carry):
            kv[s, 1] = jnp.zeros((GROUP, 2 * LOCAL), BF)
            return carry

        lax.fori_loop(0, SEQS, clear, 0)

    def near_copy(s):
        return remote(
            kv.at[s, 2], kv.at[s, 1], (near_sems.at[0, s], near_sems.at[1, s]), at.up
        )

    def far_copy(s):
        return remote(kv.at[s, 1], kv.at[s, 0], (far_sems.at[0, s], far_sems.at[1, s]), at.up)

    def norm_copy(s):
        return pltpu.make_async_copy(act.at[s], n1_h.at[s], n1_sem.at[s])

    def step_norm(s, carry):
        token_copy(s).wait()

        @pl.when(s < 3)
        def _():
            token_copy(s + 1).start()

        for part in range(2):
            here = pl.ds(part * 256, 256)
            xhat, _ = norm_parts(stage[lax.rem(s, 2), here].astype(F32))
            act[s, here] = (xhat * vec[5:6, :] + vec[6:7, :]).astype(BF)
        norm_copy(s).start()
        return carry

    def step_a(s):
        normed = act[s]
        q[s] = ((matmul(normed, wqkv[0], 1, 0) + vec[7:8, 0:256]) * 0.125).astype(BF)
        kv[s, 2, :, 0:LOCAL] = matmul(normed, wqkv[1], 1, 0).astype(BF)
        kv[s, 2, :, LOCAL:] = (matmul(normed, wqkv[2], 1, 0) + vec[7:8, 256:512]).astype(BF)

        @pl.when((at.z < 3) & ((at.z == 0) | (s == 0)))
        def _():
            near_copy(s).start()

    lax.fori_loop(0, SEQS, step_norm, 0)
    weight_wait(0)
    for i in range(1, 4):
        weight_start(i)
    for i, (source, target) in enumerate(quarters):
        pltpu.make_async_copy(source.at[:, mine, :], target, q_sems.at[i]).wait()

    def step_count(s):
        for j in range(3):
            count_z(j).wait()
        cnt[4] = cnt[0] + cnt[1] + cnt[2] + cnt[3]
        for j in range(nf - 1):
            count_f(j).start()

    def step_counted(s):
        for j in range(nf - 1):
            count_f(j).wait()
        total_count = cnt[4]
        for j in range(nf - 1):
            total_count = total_count + cnt[5 + j]
        small[6:7, 0:128] = total_count[0:1, :]
        cnt[0] = (SEQS * GROUP * nf * 4) / total_count
        for i in range(SEQS):
            norm_copy(i).wait()
        for copy in block_copies(0):
            copy.start()

    def factor():
        return cnt[0, 0:1, 0:1]

    def block_copies(s):
        return (
            pltpu.make_async_copy(teacher.at[s], stage.at[0], in_sems.at[0]),
            pltpu.make_async_copy(cot.at[s], stage.at[1], in_sems.at[1]),
        )

    def kv_out(s):
        return pltpu.make_async_copy(kv.at[s], kv_h.at[s], res_sem.at[s])

    def mix_copy(s):
        return pltpu.make_async_copy(tok_q.at[s], gmix_h.at[s, mine], mix_sem.at[s])

    def ends(k, s):
        if k == 2:
            return tok_q.at[s], gmix_h
        target = (n2, blk)[k]
        return target.at[s, mine], target

    def step_r(k, s):
        summed = ring.total(s)
        if k == 0:
            middle = tok_q[s].astype(F32) + summed + vec[0:1, :]
            mid[s] = middle
            xhat, _ = norm_parts(middle)
            n2[s, mine] = (xhat * vec[1:2, :] + vec[2:3, :]).astype(BF)
        elif k == 1:
            block = mid[s] + summed + vec[4:5, :]
            blk[s, mine] = block.astype(BF)
            difference = block - tea_q[s].astype(F32)
            masked = lse[s, mine, 4:5] * difference
            small[5:6, :] += column_sum(masked * difference)
            grad = cot_q[s].astype(F32) + masked * factor()
            gblk[s] = grad
            small[0:1, :] += column_sum(grad)
        else:
            xhat, inverse = norm_parts(mid[s])
            small[1:2, :] += column_sum(summed * xhat)
            small[2:3, :] += column_sum(summed)
            grad = gblk[s] + norm_back(summed, xhat, inverse, vec[1:2, :])
            gblk[s] = grad
            small[3:4, :] += column_sum(grad)
            tok_q[s] = grad.astype(BF)
            mix_copy(s).start()
        ring.spread(*ends(k, s), s)

    def halo(s):
        @pl.when(at.z > 0)
        def _():
            near_copy(s).wait_recv()

        @pl.when((at.z > 0) & (at.z < 3))
        def _():
            far_copy(s).start()

            @pl.when(s < 3)
            def _():
                near_copy(s + 1).start()

    def step_p0(s):
        @pl.when(at.z < 3)
        def _():
            near_copy(s).wait_send()

        @pl.when((at.z > 0) & (at.z < 3))
        def _():
            far_copy(s).wait_send()

        @pl.when(at.z > 1)
        def _():
            far_copy(s).wait_recv()

        kv_out(s).start()
        lane = lax.broadcasted_iota(jnp.int32, (1, LOCAL), 1) // HD
        slot = lax.broadcasted_iota(jnp.int32, (1, 128), 1)
        keys = kv.at[s].reshape(3 * GROUP, 2 * LOCAL)
        here_segs = segk.at[:, aligned(at.z * GROUP, 3 * GROUP)]
        which = lax.broadcasted_iota(jnp.int32, (8, SPAN), 0) == s

        def block(b, carry):
            start = pl.multiple_of(b * HALF, HALF)
            here = pl.ds(start, HALF)
            span = pl.ds(start, SPAN)
            seg_row = jnp.sum(
                jnp.where(which, here_segs[:, span], 0.0), axis=0, keepdims=True
            )
            columns = lse[s, here]
            bias[...] = allowed_bias(columns[:, 5:6], seg_row)
            query = q[s, here]
            k_block = keys[span, 0:LOCAL]
            v_block = keys[span, LOCAL:]
            mixed = jnp.zeros((HALF, LOCAL), F32)
            logs = columns
            for h in range(LOCAL // HD):
                one = jnp.where(lane == h, query, jnp.zeros_like(query))
                scores = matmul(one, k_block, 1, 1) + bias[...]
                top = jnp.max(scores, axis=-1, keepdims=True)
                weights = jnp.exp(scores - top)
                whole = jnp.sum(weights, axis=-1, keepdims=True)
                part = matmul(weights.astype(BF), v_block, 1, 0) / whole
                mixed = jnp.where(lane == h, part, mixed)
                logs = jnp.where(slot == h, top + jnp.log(whole), logs)
            att[s, here] = mixed.astype(BF)
            lse[s, here] = logs
            return carry

        lax.fori_loop(0, 2, block, 0)
        send[s] = matmul(att[s], wout[...], 1, 0).astype(BF)
        ring.rs_core(s).start()

    def step_p1(s):
        ring.step_u(*ends(0, s), s)
        for part in range(2):
            here = pl.ds(part * 256, 256)
            h = matmul(n2[s, here], wfc1[...], 1, 0) + vec[3:4, :]
            t = jnp.tanh(0.7978845608028654 * (h + 0.044715 * h * h * h))
            act[s, here] = (0.5 * h * (1.0 + t)).astype(BF)
            slope[s, here] = (
                0.5 * (1.0 + t)
                + 0.5 * h * (1.0 - t * t) * (0.7978845608028654 * (1.0 + 0.134145 * h * h))
            ).astype(BF)
        send[s] = matmul(act[s], wfc2[...], 1, 0).astype(BF)
        ring.rs_core(s).start()

    def step_p2(s):
        ring.step_u(*ends(1, s), s)
        out = pltpu.make_async_copy(blk.at[s], out_h.at[s], out_sem)
        out.start()
        for copy in block_copies(s):
            copy.wait()
        out.wait()
        for part in range(2):
            here = pl.ds(part * 256, 256)
            difference = blk[s, here].astype(F32) - stage[0, here].astype(F32)
            scaled = lse[s, here, 4:5] * factor()
            down = (stage[1, here].astype(F32) + scaled * difference).astype(BF)
            blk[s, here] = down
            up = matmul(down, wfc2[...], 1, 1) * slope[s, here].astype(F32)
            rounded = up.astype(BF)
            slope[s, here] = rounded
            small[4:5, :] += column_sum(rounded.astype(F32))

        @pl.when(s < 3)
        def _():
            for copy in block_copies(s + 1):
                copy.start()

        send[s] = matmul(slope[s], wfc1[...], 1, 1).astype(BF)
        ring.rs_core(s).start()

    deep = lambda ref: ref.reshape(SEQS * GROUP, 1024)

    def down_out():
        return pltpu.make_async_copy(deep(send).at[0:1024], gfc2, in_sems.at[0])

    def up_out():
        return pltpu.make_async_copy(deep(act).at[0:1024], gfc1, in_sems.at[1])

    def step_gdown(s):
        deep(send)[0:1024, :] = matmul(deep(act)[...], deep(blk)[...], 0, 0).astype(BF)
        down_out().start()

    def step_gup(s):
        deep(act)[0:1024, :] = matmul(deep(n2)[...], deep(slope)[...], 0, 0).astype(BF)
        up_out().start()

    actions = {
        "A": step_a,
        "H": halo,
        "C": step_count,
        "D": step_counted,
        "W": lambda s: weight_wait(s),
        "P0": step_p0,
        "P1": step_p1,
        "P2": step_p2,
        "Q": ring.step_q,
        "gdown": step_gdown,
        "gup": step_gup,
    }
    for k in range(3):
        actions[f"R{k}"] = functools.partial(step_r, k)
        actions[f"T{k}"] = lambda s, k=k: ring.step_t(*ends(k, s), s)
    actions["W"] = lambda s: [weight_wait(i) for i in (2, 3)]
    actions["V"] = lambda s: weight_wait(1)
    run_order(actions, FRONT_ORDER)
    last = pltpu.make_async_copy(gblk, gmid_h, out_sem)
    last.start()
    kept = (
        pltpu.make_async_copy(wqkv, wqkv_h, keep_sem.at[0]),
        pltpu.make_async_copy(wout, wout_h, keep_sem.at[1]),
    )
    for copy in kept:
        copy.start()
    for s in range(SEQS):
        ring.step_u(*ends(2, s), s)
        mix_copy(s).wait()
        kv_out(s).wait()
    last.wait()
    down_out().wait()
    up_out().wait()
    for copy in kept:
        copy.wait()


def front_call(nf, *args):
    anys = pl.BlockSpec(memory_space=pl.ANY)
    vmem = pl.BlockSpec(memory_space=pltpu.VMEM)
    dma = pltpu.SemaphoreType.DMA
    big = lambda *lead: pltpu.VMEM((*lead, GROUP, 1024), BF)
    shape = jax.ShapeDtypeStruct
    return pl.pallas_call(
        functools.partial(front_kernel, nf),
        out_shape=(
            shape((SEQS, GROUP, 1024), BF),
            shape((SEQS, GROUP, 1024), BF),
            shape((SEQS, QUARTER, 1024), F32),
            shape((1024, 1024), BF),
            shape((1024, 1024), BF),
            shape((8, 1024), F32),
            shape((SEQS, GROUP, LOCAL), BF),
            shape((SEQS, GROUP, LOCAL), BF),
            shape((SEQS, 3, GROUP, 2 * LOCAL), BF),
            shape((SEQS, GROUP, 128), F32),
            shape((SEQS, GROUP, 1024), BF),
            shape((3, 1024, LOCAL), BF),
            shape((LOCAL, 1024), BF),
        ),
        in_specs=[anys] * 7 + [vmem] * 3,
        out_specs=(anys, anys, anys, anys, anys, vmem, vmem, vmem, anys, vmem, anys, anys, anys),
        scratch_shapes=[
            pltpu.VMEM((3, 1024, LOCAL), BF),
            pltpu.VMEM((LOCAL, 1024), BF),
            pltpu.VMEM((1024, 1024), BF),
            pltpu.VMEM((1024, 1024), BF),
            big(SEQS),
            big(SEQS),
            big(SEQS),
            big(SEQS),
            big(SEQS),
            pltpu.VMEM((SEQS, HALF, 1024), BF),
            pltpu.VMEM((SEQS, QUARTER, 1024), BF),
            pltpu.VMEM((SEQS, QUARTER, 1024), BF),
            pltpu.VMEM((SEQS, QUARTER, 1024), F32),
            pltpu.VMEM((SEQS, QUARTER, 1024), F32),
            pltpu.VMEM((SEQS, QUARTER, 1024), BF),
            pltpu.VMEM((SEQS, QUARTER, 1024), BF),
            pltpu.VMEM((SEQS, QUARTER, 1024), BF),
            big(2),
            pltpu.VMEM((8, 3072), F32),
            pltpu.VMEM((HALF, SPAN), F32),
            pltpu.VMEM((SEQS, 3, GROUP, 2 * LOCAL), BF),
            pltpu.VMEM((4 + nf, 8, 128), F32),
            dma((4, nf - 1)),
            dma((4, nf - 1)),
            dma((4,)),
            dma((5, 2, SEQS)),
            dma((3,)),
            dma((2,)),
            dma((SEQS,)),
            dma,
            dma((SEQS,)),
            dma((2, SEQS)),
            dma((2, SEQS)),
            dma((2, 3)),
            dma((2, nf - 1)),
            dma((SEQS,)),
            dma((2,)),
        ],
        compiler_params=pltpu.CompilerParams(
            collective_id=1, has_side_effects=True, vmem_limit_bytes=63 * 2**20
        ),
        cost_estimate=pl.CostEstimate(
            flops=2 * 2048 * 1024 * 1024 * 9, bytes_accessed=30 * 2**20, transcendentals=0
        ),
        name="front",
    )(*args)


class Reduce:
    def __init__(self, at, cut, size, rows, full, arrived, shard, half, quarter, sems):
        self.at, self.cut, self.size, self.rows = at, cut, size, rows
        self.full, self.arrived, self.shard = full, arrived, shard
        self.half, self.quarter = half, quarter
        self.x_sems, self.z_sems = sems
        self.a, self.b = lax.rem(at.z, 2), at.z // 2
        self.side = (at.f, at.z + 1 - 2 * self.a, at.t)
        self.across = (at.f, lax.rem(at.z + 2, 4), at.t)

    def own(self, f):
        return self.cut(self.full, aligned(f * self.size, self.size, math.gcd(self.size, 128)))

    def part(self, ref, start, size):
        where = aligned(start, size, 16)
        return ref.at[:, where, :] if len(ref.shape) == 3 else ref.at[where, :]

    def x_copy(self, j):
        there = lax.rem(self.at.f + 1 + j, self.at.nf)
        pair = (self.x_sems.at[0, j], self.x_sems.at[1, j])
        return remote(self.own(there), self.arrived.at[j], pair, self.at.peers_f[j])

    def z_copy(self, stage):
        h, q = self.rows // 2, self.rows // 4
        pair = (self.z_sems.at[0, stage], self.z_sems.at[1, stage])
        own = self.own(self.at.f)
        if stage == 0:
            return remote(self.part(own, (1 - self.a) * h, h), self.half, pair, self.side)
        if stage == 1:
            src = self.part(own, self.a * h + (1 - self.b) * q, q)
            return remote(src, self.quarter, pair, self.across)
        if stage == 2:
            kept = self.part(self.shard, self.a * h + self.b * q, q)
            return remote(kept, kept, pair, self.across)
        kept = self.part(self.shard, self.a * h, h)
        return remote(kept, kept, pair, self.side)

    def add(self, target, first, others):
        total = first[...].astype(F32)
        for other in others:
            total = total + other[...].astype(F32)
        target[...] = total.astype(BF)

    def run(self, stage):
        h, q = self.rows // 2, self.rows // 4
        peers = range(self.at.nf - 1)
        own = self.own(self.at.f)
        if stage == 0:
            for j in peers:
                self.x_copy(j).start()
            return
        if stage == 1:
            for j in peers:
                self.x_copy(j).wait()
            self.add(own, own, [self.arrived.at[j] for j in peers])
        else:
            self.z_copy(stage - 2).wait()
        if stage == 2:
            kept = self.part(own, self.a * h, h)
            self.add(kept, kept, [self.half])
        elif stage == 3:
            start = self.a * h + self.b * q
            self.add(self.part(self.shard, start, q), self.part(own, start, q), [self.quarter])
        if stage < 5:
            self.z_copy(stage - 1).start()


BACK_ORDER = (
    ("A0", 0),
    ("G0", 0),
    ("E", 0),
    ("E", 1),
    ("E", 2),
    ("I", 0),
    ("A1", 0),
    ("E", 3),
    ("I", 1),
    ("B0", 0),
    ("I", 2),
    ("G1", 0),
    ("F", 0),
    ("B1", 0),
    ("Q", 0),
    ("A2", 0),
    ("R", 0),
    ("I", 3),
    ("T", 0),
    ("F", 1),
    ("Q", 1),
    ("F", 2),
    ("R", 1),
    ("Q", 2),
    ("G2", 0),
    ("T", 1),
    ("B2", 0),
    ("R", 2),
    ("A3", 0),
    ("T", 2),
    ("F", 3),
    ("C0", 0),
    ("Q", 3),
    ("G3", 0),
    ("B3", 0),
    ("R", 3),
    ("S0", 0),
    ("C1", 0),
    ("A4", 0),
    ("S1", 0),
    ("S2", 0),
    ("T", 3),
    ("G4", 0),
    ("S3", 0),
    ("B4", 0),
    ("S4", 0),
    ("S5", 0),
    ("C2", 0),
    ("A5", 0),
    ("G5", 0),
    ("B5", 0),
    ("C3", 0),
    ("C4", 0),
    ("C5", 0),
)


def back_kernel(
    nf,
    gmix_h,
    gmid_h,
    gfc1_h,
    gfc2_h,
    att,
    q,
    kv_h,
    lse,
    n1_h,
    tokens,
    wqkv,
    wout,
    vec,
    segs,
    sums_one,
    ig_h,
    small,
    s_qkv,
    s_out,
    s_fc1,
    s_fc2,
    gm,
    kvs,
    n1s,
    ga,
    dots,
    bias,
    segk,
    dkvt,
    dfar,
    dnear,
    down,
    m1,
    m2,
    gq,
    send,
    recv_c,
    send_y,
    recv_y,
    gmid,
    tok_q,
    a_qkv,
    a_out,
    f_qkv,
    f_fc1,
    f_fc2,
    x_qkv,
    x_out,
    x_fc1,
    x_fc2,
    h_qkv,
    h_out,
    h_fc1,
    h_fc2,
    k_qkv,
    k_out,
    k_fc1,
    k_fc2,
    ring_sems,
    load_sems,
    first_sems,
    m1_sems,
    m2_sems,
    red_x,
    red_z,
    got_core,
    got_y,
    got_f,
    got_z,
    sum_sems,
    sum_f_sems,
    n1e,
):
    at = Place(nf)
    at.barrier()
    ring = Ring(at, send, recv_c, send_y, recv_y, ring_sems)
    mine = aligned(at.mine, QUARTER)
    rows_cut = lambda ref, where: ref.at[where, :]
    cols_cut = lambda ref, where: ref.at[:, where]
    deep_cut = lambda ref, where: ref.at[:, where, :]
    fs = 1024 // nf
    f_out = gm.at[0:LOCAL]

    def reducer(i, cut, rows, full, arrived, shard, half, quarter):
        sems = (red_x.at[i], red_z.at[i])
        return Reduce(at, cut, fs, rows, full, arrived, shard, half, quarter, sems)

    first, rest = pl.ds(0, 1), pl.ds(1, 2)
    red_q = reducer(
        0, deep_cut, fs, f_qkv.at[first], x_qkv.at[:, first], s_qkv.at[first], h_qkv.at[first], k_qkv.at[first]
    )
    red_kv = reducer(
        4, deep_cut, fs, f_qkv.at[rest], x_qkv.at[:, rest], s_qkv.at[rest], h_qkv.at[rest], k_qkv.at[rest]
    )
    red_out = reducer(1, cols_cut, LOCAL, f_out, x_out, s_out, h_out, k_out)
    red_fc1 = reducer(2, rows_cut, fs, f_fc1, x_fc1, s_fc1, h_fc1, k_fc1)
    red_fc2 = reducer(3, cols_cut, 1024, f_fc2, x_fc2, s_fc2, h_fc2, k_fc2)

    firsts = (
        (gfc1_h, f_fc1),
        (gfc2_h, f_fc2),
        (gmid_h.at[0], gmid),
        (tokens.at[:, mine, :], tok_q),
    )

    def first_copy(i):
        return pltpu.make_async_copy(firsts[i][0], firsts[i][1], first_sems.at[i])

    def load_copies(s):
        return (
            pltpu.make_async_copy(gmix_h.at[s], gm, load_sems.at[0, 0]),
            pltpu.make_async_copy(kv_h.at[s], kvs, load_sems.at[1, 0]),
        )

    def norm_load(s):
        return pltpu.make_async_copy(n1_h.at[s], n1s, load_sems.at[2, 0])

    def norm_early(s):
        return pltpu.make_async_copy(n1_h.at[s], n1e, load_sems.at[0, 1])

    def mid_load(s):
        return pltpu.make_async_copy(gmid_h.at[s], gmid, load_sems.at[2, 1])

    for copy in load_copies(0):
        copy.start()
    for i in range(4):
        first_copy(i).start()
    norm_load(0).start()
    norm_early(0).start()

    segk[...] = jnp.full(segk.shape, -1.0, F32)
    segk[0:4, 1024:3072] = segs[...].astype(F32)
    small[...] = jnp.zeros_like(small)
    a_qkv[...] = jnp.zeros_like(a_qkv)
    a_out[...] = jnp.zeros_like(a_out)
    def m1_copy(s):
        return remote(dfar.at[s], m1.at[s], (m1_sems.at[0, s], m1_sems.at[1, s]), at.down)

    def m2_copy(s):
        return remote(dnear.at[s], m2.at[s], (m2_sems.at[0, s], m2_sems.at[1, s]), at.down)

    def step_e(s):
        for copy in load_copies(s):
            copy.wait()

        ga[...] = matmul(gm[...], wout[...], 1, 1).astype(BF)
        a_out[...] += matmul(att[s], gm[...], 0, 0)

        lane = lax.broadcasted_iota(jnp.int32, (1, LOCAL), 1) // HD
        keys = kvs.reshape(3 * GROUP, 2 * LOCAL)
        here_segs = segk.at[:, aligned(at.z * GROUP, 3 * GROUP)]
        which = lax.broadcasted_iota(jnp.int32, (8, SPAN), 0) == s
        dkvt[...] = jnp.zeros_like(dkvt)

        def block(b, carry):
            start = pl.multiple_of(b * HALF, HALF)
            here = pl.ds(start, HALF)
            span = pl.ds(start, SPAN)
            seg_row = jnp.sum(
                jnp.where(which, here_segs[:, span], 0.0), axis=0, keepdims=True
            )
            logs = lse[s, here]
            bias[...] = allowed_bias(logs[:, 5:6], seg_row)
            query = q[s, here]
            grad = ga[here]
            k_block = keys[span, 0:LOCAL]
            v_block = keys[span, LOCAL:]
            dots[0] = jnp.transpose(query)
            dots[1] = jnp.transpose(grad)
            product = grad.astype(F32) * att[s, here].astype(F32)
            grad_query = jnp.zeros((HALF, LOCAL), F32)
            for h in range(LOCAL // HD):
                mine_h = lane == h
                one = jnp.where(mine_h, query, jnp.zeros_like(query))
                grad_one = jnp.where(mine_h, grad, jnp.zeros_like(grad))
                delta = jnp.sum(jnp.where(mine_h, product, 0.0), axis=-1, keepdims=True)
                scores = matmul(one, k_block, 1, 1) + bias[...]
                probs = jnp.exp(scores - logs[:, h : h + 1])
                dprobs = matmul(grad_one, v_block, 1, 1)
                grad_scores = (probs * (dprobs - delta)).astype(BF)
                grad_query = jnp.where(mine_h, matmul(grad_scores, k_block, 1, 0), grad_query)
                k_rows = pl.ds(h * HD, HD)
                v_rows = pl.ds(LOCAL + h * HD, HD)
                dkvt[k_rows, span] += matmul(dots[0, k_rows], grad_scores, 1, 0)
                dkvt[v_rows, span] += matmul(dots[1, k_rows], probs.astype(BF), 1, 0)
            gq[s, here] = (grad_query * 0.125).astype(BF)
            return carry

        lax.fori_loop(0, 2, block, 0)

        @pl.when(s < 3)
        def _():
            for copy in load_copies(s + 1):
                copy.start()

        for i, target in enumerate((dfar, dnear, down)):
            target[s] = jnp.transpose(dkvt[:, i * GROUP : (i + 1) * GROUP].astype(BF))

        @pl.when(at.z > 1)
        def _():
            m1_copy(s).start()

        norm_early(s).wait()
        a_qkv[0] += matmul(n1e[...], gq[s], 0, 0)

        @pl.when(s < 3)
        def _():
            norm_early(s + 1).start()

    def step_i(s):
        @pl.when((at.z > 0) & (at.z < 3))
        def _():
            m1_copy(s).wait_recv()
            dnear[s] = (dnear[s].astype(F32) + m1[s].astype(F32)).astype(BF)

        @pl.when(at.z > 0)
        def _():
            m2_copy(s).start()

    def step_f(s):
        @pl.when(at.z < 3)
        def _():
            m2_copy(s).wait_recv()
            down[s] = (down[s].astype(F32) + m2[s].astype(F32)).astype(BF)

        norm_load(s).wait()
        grads = (gq[s], down[s, :, 0:LOCAL], down[s, :, LOCAL:])
        send[s] = (
            matmul(grads[0], wqkv[0], 1, 1)
            + matmul(grads[1], wqkv[1], 1, 1)
            + matmul(grads[2], wqkv[2], 1, 1)
        ).astype(BF)
        ring.rs_core(s).start()
        normed = n1s[...]
        for i in (1, 2):
            a_qkv[i] += matmul(normed, grads[i], 0, 0)

        @pl.when(s < 3)
        def _():
            norm_load(s + 1).start()

        small[9:10, 0:LOCAL] += column_sum(grads[0].astype(F32))
        small[9:10, LOCAL : 2 * LOCAL] += column_sum(grads[2].astype(F32))

    def ends(s):
        return tok_q.at[s], ig_h

    def ig_copy(s):
        return pltpu.make_async_copy(tok_q.at[s], ig_h.at[s, mine], first_sems.at[s])

    def step_r(s):
        summed = ring.total(s)
        xhat, inverse = norm_parts(tok_q[s].astype(F32))
        small[0:1, :] += column_sum(summed * xhat)
        small[1:2, :] += column_sum(summed)
        @pl.when(s > 0)
        def _():
            mid_load(s).wait()

        grad = gmid[...] + norm_back(summed, xhat, inverse, vec[5:6, :])
        tok_q[s] = grad.astype(BF)

        @pl.when(s < 3)
        def _():
            mid_load(s + 1).start()

        ig_copy(s).start()
        ring.spread(*ends(s), s)

    def sum_copy(stage, j=0):
        pair = (sum_sems.at[0, stage], sum_sems.at[1, stage])
        top = small.at[0:8]
        if stage == 0:
            return remote(top, got_core, pair, at.mate_c)
        if stage == 1:
            return remote(top, got_y, pair, at.mate_y)
        if stage == 2:
            pair = (sum_f_sems.at[0, j], sum_f_sems.at[1, j])
            return remote(small, got_f.at[j], pair, at.peers_f[j])
        mate = red_q.side if stage == 3 else red_q.across
        return remote(small, got_z.at[stage - 3], pair, mate)

    def step_sum(stage, s):
        if stage == 0:
            small[2:6, :] = sums_one[0:4, :]
            small[6:7, :] = sums_one[5:6, :]
            small[8:9, :] = sums_one[4:5, :]
        elif stage == 3:
            for j in range(nf - 1):
                sum_copy(2, j).wait()
            for j in range(nf - 1):
                small[...] += got_f[j]
        else:
            sum_copy(stage - 1).wait()
            if stage == 1:
                small[0:8, :] += got_core[...]
            elif stage == 2:
                small[0:8, :] += got_y[...]
            else:
                small[...] += got_z[stage - 4]
        if stage == 2:
            for j in range(nf - 1):
                sum_copy(2, j).start()
        elif stage < 5:
            sum_copy(stage).start()

    def step_group(group, stage, s):
        if stage == 0:
            if group == "B":
                f_out[...] = a_out[...].astype(BF)
                f_qkv[0] = a_qkv[0].astype(BF)
            elif group == "C":
                for i in (1, 2):
                    f_qkv[i] = a_qkv[i].astype(BF)
        for reduce in groups[group]:
            reduce.run(stage)

    groups = {"A": (red_fc2,), "G": (red_fc1,), "B": (red_out, red_q), "C": (red_kv,)}
    for i in range(4):
        first_copy(i).wait()
    actions = {
        "E": step_e,
        "I": step_i,
        "F": step_f,
        "Q": ring.step_q,
        "R": step_r,
        "T": lambda s: ring.step_t(*ends(s), s),
    }
    for stage in range(6):
        actions[f"S{stage}"] = functools.partial(step_sum, stage)
        for group in groups:
            actions[f"{group}{stage}"] = functools.partial(step_group, group, stage)
    run_order(actions, BACK_ORDER)
    for s in range(SEQS):
        ring.step_u(*ends(s), s)
        ig_copy(s).wait()

        @pl.when(at.z > 1)
        def _():
            m1_copy(s).wait_send()

        @pl.when(at.z > 0)
        def _():
            m2_copy(s).wait_send()


def back_call(nf, *args):
    anys = pl.BlockSpec(memory_space=pl.ANY)
    vmem = pl.BlockSpec(memory_space=pltpu.VMEM)
    dma = pltpu.SemaphoreType.DMA
    big = lambda *lead: pltpu.VMEM((*lead, GROUP, 1024), BF)
    shape = jax.ShapeDtypeStruct
    fs = 1024 // nf
    low = lambda *dims: pltpu.VMEM(dims, BF)
    return pl.pallas_call(
        functools.partial(back_kernel, nf),
        out_shape=(
            shape((SEQS, GROUP, 1024), BF),
            shape((16, 1024), F32),
            shape((3, fs, LOCAL), BF),
            shape((LOCAL, fs), BF),
            shape((fs, 1024), BF),
            shape((1024, fs), BF),
        ),
        in_specs=[anys] * 4 + [vmem, vmem, anys, vmem, anys, anys, vmem, vmem, vmem, vmem, vmem],
        out_specs=(anys, vmem, vmem, vmem, vmem, vmem),
        scratch_shapes=[
            low(GROUP, 1024),
            low(3, GROUP, 2 * LOCAL),
            low(GROUP, 1024),
            low(GROUP, LOCAL),
            low(2, LOCAL, HALF),
            pltpu.VMEM((HALF, SPAN), F32),
            pltpu.VMEM((8, 3072), F32),
            pltpu.VMEM((2 * LOCAL, 3 * GROUP), F32),
            low(SEQS, GROUP, 2 * LOCAL),
            low(SEQS, GROUP, 2 * LOCAL),
            low(SEQS, GROUP, 2 * LOCAL),
            low(SEQS, GROUP, 2 * LOCAL),
            low(SEQS, GROUP, 2 * LOCAL),
            low(SEQS, GROUP, LOCAL),
            big(SEQS),
            low(SEQS, HALF, 1024),
            low(SEQS, QUARTER, 1024),
            low(SEQS, QUARTER, 1024),
            pltpu.VMEM((QUARTER, 1024), F32),
            low(SEQS, QUARTER, 1024),
            pltpu.VMEM((3, 1024, LOCAL), F32),
            pltpu.VMEM((LOCAL, 1024), F32),
            low(3, 1024, LOCAL),
            low(1024, 1024),
            low(1024, 1024),
            low(nf - 1, 3, fs, LOCAL),
            low(nf - 1, LOCAL, fs),
            low(nf - 1, fs, 1024),
            low(nf - 1, 1024, fs),
            low(3, fs // 2, LOCAL),
            low(LOCAL // 2, fs),
            low(fs // 2, 1024),
            low(512, fs),
            low(3, fs // 4, LOCAL),
            low(LOCAL // 4, fs),
            low(fs // 4, 1024),
            low(256, fs),
            dma((5, 2, SEQS)),
            dma((3, 2)),
            dma((4,)),
            dma((2, SEQS)),
            dma((2, SEQS)),
            dma((5, 2, nf - 1)),
            dma((5, 2, 4)),
            pltpu.VMEM((8, 1024), F32),
            pltpu.VMEM((8, 1024), F32),
            pltpu.VMEM((nf - 1, 16, 1024), F32),
            pltpu.VMEM((2, 16, 1024), F32),
            dma((2, 5)),
            dma((2, nf - 1)),
            low(GROUP, 1024),
        ],
        compiler_params=pltpu.CompilerParams(
            collective_id=2, has_side_effects=True, vmem_limit_bytes=63 * 2**20
        ),
        cost_estimate=pl.CostEstimate(
            flops=2 * 2048 * 1024 * 1024 * 6, bytes_accessed=30 * 2**20, transcendentals=0
        ),
        name="back",
    )(*args)


def local(
    tokens,
    cotangent,
    teacher,
    valid_mask,
    segment_ids,
    ln1_gain,
    ln1_bias,
    w_qkv,
    b_qv,
    w_out,
    b_out,
    ln2_gain,
    ln2_bias,
    w_fc1,
    b_fc1,
    w_fc2,
    b_fc2,
):
    nf = lax.axis_size("fsdp")
    pieces = (b_out, ln2_gain, ln2_bias, b_fc2, ln1_gain, ln1_bias, b_qv, b_fc1)
    flat = lax.all_gather(jnp.concatenate([piece.reshape(-1) for piece in pieces]), "fsdp", axis=0)
    flat = flat.astype(F32)
    wide = b_out.shape[0]
    rows = [flat[:, i * wide : (i + 1) * wide].reshape(1, D) for i in range(6)]
    small_qv = flat[:, 6 * wide : 6 * wide + b_qv.size].reshape(nf, *b_qv.shape)
    small_up = flat[:, 6 * wide + b_qv.size :].reshape(nf, *b_fc1.shape)
    bias_qv = jnp.moveaxis(small_qv, 0, 2).reshape(1, 2 * LOCAL)
    bias_up = jnp.moveaxis(small_up, 0, 1).reshape(1, D)
    vec = jnp.concatenate(
        rows[:3]
        + [bias_up]
        + rows[3:]
        + [jnp.concatenate([bias_qv, jnp.zeros((1, D - 2 * LOCAL), F32)], axis=1)],
        axis=0,
    )
    mask_f = jnp.concatenate([valid_mask, jnp.zeros_like(valid_mask)], axis=0).astype(F32)
    front = front_call(
        nf, w_qkv, w_out, w_fc1, w_fc2, tokens, teacher, cotangent, vec, mask_f, segment_ids
    )
    (output, grad_mix, grad_middle, gfc1, gfc2, sums_one, att, q, kv, lse, n1, wqkv, wout) = front
    input_grad, everything, s_qkv, s_out, s_fc1, s_fc2 = back_call(
        nf, grad_mix, grad_middle, gfc1, gfc2, att, q, kv, lse, n1, tokens, wqkv, wout, vec, segment_ids, sums_one
    )
    place_f = lax.axis_index("fsdp")
    loss = jnp.sum(everything[6]) / (2.0 * D * sums_one[6, 0])
    ours = everything[8:10]
    part = lax.dynamic_slice_in_dim(everything[0:7], place_f * wide, wide, 1)
    grad_up = ours[0].reshape(b_fc1.shape[0], -1)
    grad_up = lax.dynamic_slice_in_dim(grad_up, place_f * b_fc1.shape[1], b_fc1.shape[1], 1)
    grad_qv = ours[1, : 2 * LOCAL].reshape(2, LOCAL // HD, HD)
    grad_qv = lax.dynamic_slice_in_dim(grad_qv, place_f * b_qv.shape[2], b_qv.shape[2], 2)
    return (
        output,
        loss,
        input_grad,
        part[0],
        part[1],
        s_qkv.astype(F32),
        grad_qv,
        s_out.astype(F32),
        part[5],
        part[3],
        part[4],
        s_fc1.astype(F32),
        grad_up,
        s_fc2.astype(F32),
        part[2],
    )


def solution(mesh):
    return jax.shard_map(
        local,
        mesh=mesh,
        in_specs=(
            P("fsdp", "context", None),
            P("fsdp", "context", None),
            P("fsdp", "context", None),
            P("fsdp", "context"),
            P("fsdp", None),
            P("fsdp"),
            P("fsdp"),
            P(None, "fsdp", "tensor"),
            P(None, "tensor", "fsdp"),
            P("tensor", "fsdp"),
            P("fsdp"),
            P("fsdp"),
            P("fsdp"),
            P("fsdp", "tensor"),
            P("tensor", "fsdp"),
            P("tensor", "fsdp"),
            P("fsdp"),
        ),
        out_specs=(
            P("fsdp", "context", None),
            P(),
            P("fsdp", "context", None),
            P("fsdp"),
            P("fsdp"),
            P(None, "fsdp", "tensor"),
            P(None, "tensor", "fsdp"),
            P("tensor", "fsdp"),
            P("fsdp"),
            P("fsdp"),
            P("fsdp"),
            P("fsdp", "tensor"),
            P("tensor", "fsdp"),
            P("tensor", "fsdp"),
            P("fsdp"),
        ),
        check_vma=False,
    )
```

```python
import functools
import math

import jax
import jax.numpy as jnp
from jax import lax
from jax.experimental import pallas as pl
from jax.experimental.pallas import tpu as pltpu
from jax.sharding import PartitionSpec as P

MESH = pl.DeviceIdType.MESH
BF = jnp.bfloat16
F32 = jnp.float32
D = 1024
HD = 64
WINDOW = 1024
EPSILON = 1e-05
MASKED = -1e30
SEQS = 4
GROUP = 512
QUARTER = 128
HALF = 256
SPAN = 1280
LOCAL = 256


def matmul(left, right, over_left, over_right):
    dims = (((over_left,), (over_right,)), ((), ()))
    return lax.dot_general(left, right, dims, preferred_element_type=F32)


def norm_parts(values):
    mean = jnp.mean(values, axis=-1, keepdims=True)
    center = values - mean
    spread = jnp.mean(center * center, axis=-1, keepdims=True)
    inverse = lax.rsqrt(spread + EPSILON)
    return center * inverse, inverse


def norm_back(grad_normed, xhat, inverse, gain):
    e = grad_normed * gain
    return inverse * (
        e
        - jnp.mean(e, axis=-1, keepdims=True)
        - xhat * jnp.mean(e * xhat, axis=-1, keepdims=True)
    )


def column_sum(values):
    return jnp.sum(values, axis=0, keepdims=True)


def aligned(start, size, unit=128):
    return pl.ds(pl.multiple_of(start, unit), size)


def allowed_bias(query_seg, key_seg):
    ahead = lax.broadcasted_iota(jnp.int32, (HALF, SPAN), 1) - lax.broadcasted_iota(
        jnp.int32, (HALF, SPAN), 0
    )
    allowed = (ahead > 0) & (ahead <= WINDOW) & (query_seg == key_seg)
    return jnp.where(allowed, 0.0, MASKED)


class Place:
    def __init__(self, nf):
        self.nf = nf
        self.f = lax.axis_index("fsdp")
        self.z = lax.axis_index("context")
        self.t = lax.axis_index("tensor")
        self.y, self.c = self.t // 2, lax.rem(self.t, 2)
        self.mate_c = (self.f, self.z, self.t + 1 - 2 * self.c)
        self.mate_y = (self.f, self.z, lax.rem(self.t + 2, 4))
        self.mine = (2 * self.c + self.y) * QUARTER
        self.over_y = (2 * self.c + 1 - self.y) * QUARTER
        self.peers_f = [(lax.rem(self.f + j, nf), self.z, self.t) for j in range(1, nf)]
        self.peers_z = [(self.f, lax.rem(self.z + j, 4), self.t) for j in range(1, 4)]
        self.up = (self.f, lax.rem(self.z + 1, 4), self.t)
        self.down = (self.f, lax.rem(self.z + 3, 4), self.t)

    def barrier(self):
        semaphore = pltpu.get_barrier_semaphore()
        everyone = [self.mate_c, self.mate_y] + self.peers_f + self.peers_z
        for peer in everyone:
            pl.semaphore_signal(semaphore, inc=1, device_id=peer, device_id_type=MESH)
        pl.semaphore_wait(semaphore, len(everyone))


def remote(src, dst, pair, mate):
    return pltpu.make_async_remote_copy(
        src, dst, pair[0], pair[1], device_id=mate, device_id_type=MESH
    )


def run_order(actions, order):
    names = list(actions)
    codes = [names.index(name) * 8 + s for name, s in order]

    def step(i, carry):
        code = jnp.int32(codes[0])
        for j, other in enumerate(codes[1:]):
            code = jnp.where(i == j + 1, other, code)
        kind, s = code // 8, lax.rem(code, 8)
        for j, name in enumerate(names):

            @pl.when(kind == j)
            def _(action=actions[name]):
                action(s)

        return carry

    lax.fori_loop(0, len(order), step, 0)


class Ring:
    def __init__(self, at, send, recv_c, send_y, recv_y, sems):
        self.at, self.send, self.recv_c = at, send, recv_c
        self.send_y, self.recv_y, self.sems = send_y, recv_y, sems

    def pair(self, which, s):
        return self.sems.at[which, 0, s], self.sems.at[which, 1, s]

    def rs_core(self, s):
        half = aligned((1 - self.at.c) * HALF, HALF)
        return remote(self.send.at[s, half], self.recv_c.at[s], self.pair(0, s), self.at.mate_c)

    def rs_y(self, s):
        return remote(self.send_y.at[s], self.recv_y.at[s], self.pair(1, s), self.at.mate_y)

    def back_y(self, src, dst, s):
        return remote(
            src, dst.at[s, aligned(self.at.mine, QUARTER)], self.pair(2, s), self.at.mate_y
        )

    def back_own(self, src, dst, s):
        return remote(
            src, dst.at[s, aligned(self.at.mine, QUARTER)], self.pair(3, s), self.at.mate_c
        )

    def back_over(self, dst, s):
        there = dst.at[s, aligned(self.at.over_y, QUARTER)]
        return remote(there, there, self.pair(4, s), self.at.mate_c)

    def step_q(self, s):
        self.rs_core(s).wait()
        self.send_y[s] = (
            self.send[s, aligned(self.at.over_y, QUARTER)].astype(F32)
            + self.recv_c[s, aligned((1 - self.at.y) * QUARTER, QUARTER)].astype(F32)
        ).astype(BF)
        self.rs_y(s).start()

    def total(self, s):
        self.rs_y(s).wait()
        return (
            self.send[s, aligned(self.at.mine, QUARTER)].astype(F32)
            + self.recv_c[s, aligned(self.at.y * QUARTER, QUARTER)].astype(F32)
            + self.recv_y[s].astype(F32)
        )

    def spread(self, src, dst, s):
        self.back_y(src, dst, s).start()
        self.back_own(src, dst, s).start()

    def step_t(self, src, dst, s):
        self.back_y(src, dst, s).wait()
        self.back_over(dst, s).start()

    def step_u(self, src, dst, s):
        self.back_own(src, dst, s).wait()
        self.back_over(dst, s).wait()


FRONT_ORDER = (
    ("A", 0),
    ("A", 1),
    ("H", 0),
    ("A", 2),
    ("V", 0),
    ("P0", 0),
    ("A", 3),
    ("C", 0),
    ("Q", 0),
    ("H", 1),
    ("R0", 0),
    ("P0", 1),
    ("T0", 0),
    ("H", 2),
    ("Q", 1),
    ("D", 0),
    ("W", 0),
    ("P1", 0),
    ("Q", 0),
    ("R0", 1),
    ("P0", 2),
    ("R1", 0),
    ("T0", 1),
    ("Q", 2),
    ("H", 3),
    ("P1", 1),
    ("Q", 1),
    ("R0", 2),
    ("P0", 3),
    ("R1", 1),
    ("Q", 3),
    ("T0", 2),
    ("P1", 2),
    ("T1", 0),
    ("T1", 1),
    ("Q", 2),
    ("P2", 0),
    ("R0", 3),
    ("P2", 1),
    ("Q", 0),
    ("T0", 3),
    ("R1", 2),
    ("P1", 3),
    ("Q", 3),
    ("T1", 2),
    ("Q", 1),
    ("P2", 2),
    ("R1", 3),
    ("R2", 1),
    ("Q", 2),
    ("T1", 3),
    ("P2", 3),
    ("R2", 0),
    ("Q", 3),
    ("gdown", 0),
    ("T2", 0),
    ("R2", 2),
    ("T2", 1),
    ("gup", 0),
    ("R2", 3),
    ("T2", 2),
    ("T2", 3),
)


def front_kernel(
    nf,
    wqkv_s,
    wout_s,
    wfc1_s,
    wfc2_s,
    tokens,
    teacher,
    cot,
    part_bo,
    part_g2,
    part_b2,
    part_bd,
    part_g1,
    part_b1,
    part_qv,
    part_up,
    mask,
    segs,
    out_h,
    gmix_h,
    gmid_h,
    gfc1,
    gfc2,
    small,
    att,
    q,
    kv_h,
    lse,
    n1_h,
    wqkv_h,
    wout_h,
    wqkv,
    wout,
    wfc1,
    wfc2,
    n2,
    blk,
    act,
    slope,
    send,
    recv_c,
    send_y,
    recv_y,
    mid,
    gblk,
    tok_q,
    tea_q,
    cot_q,
    stage,
    segk,
    bias,
    kv,
    cnt,
    w_send,
    w_recv,
    w_loc,
    ring_sems,
    q_sems,
    in_sems,
    n1_sem,
    out_sem,
    mix_sem,
    near_sems,
    far_sems,
    cz_sems,
    cf_sems,
    res_sem,
    keep_sem,
    vec,
    vec_own,
    vec_got,
    v_sems,
):
    at = Place(nf)
    at.barrier()
    ring = Ring(at, send, recv_c, send_y, recv_y, ring_sems)
    mine = aligned(at.mine, QUARTER)

    fs = wout_s.shape[1]
    own = aligned(at.f * fs, fs)
    places = (
        (wqkv_s, wqkv.at[:, own, :]),
        (wout_s, wout.at[:, own]),
        (wfc1_s, wfc1.at[own, :]),
        (wfc2_s, wfc2.at[:, own]),
    )

    def weight_copy(i, j):
        pair = (w_send.at[i, j], w_recv.at[i, j])
        return remote(places[i][0], places[i][1], pair, at.peers_f[j])

    def weight_start(i):
        for j in range(nf - 1):
            weight_copy(i, j).start()
        pltpu.make_async_copy(places[i][0], places[i][1], w_loc.at[i]).start()

    def weight_wait(i):
        pltpu.make_async_copy(places[i][0], places[i][1], w_loc.at[i]).wait()
        for j in range(nf - 1):
            weight_copy(i, j).wait()

    weight_start(0)

    def token_copy(s):
        slot = lax.rem(s, 2)
        return pltpu.make_async_copy(tokens.at[s], stage.at[slot], in_sems.at[slot])

    token_copy(0).start()
    quarters = ((tokens, tok_q), (teacher, tea_q), (cot, cot_q))
    for i, (source, target) in enumerate(quarters):
        pltpu.make_async_copy(source.at[:, mine, :], target, q_sems.at[i]).start()

    vec_own[...] = jnp.zeros_like(vec_own)
    rows = ((0, part_bo), (1, part_g2), (2, part_b2), (4, part_bd), (5, part_g1), (6, part_b1))
    for i, part in rows:
        vec_own[i : i + 1, own] = part[...].astype(F32).reshape(1, fs)

    def scatter(part, count):
        wide = part.shape[1]
        unit = wide * nf
        column = lax.broadcasted_iota(jnp.int32, (wide, count * unit), 1)
        inside = lax.broadcasted_iota(jnp.int32, (wide, count * unit), 0) + at.f * wide
        spread = (lax.rem(column, unit) == inside).astype(BF)
        full = matmul(part, spread, 1, 0)
        group = lax.broadcasted_iota(jnp.int32, full.shape, 1) // unit
        owner = lax.broadcasted_iota(jnp.int32, full.shape, 0)
        return jnp.sum(jnp.where(group == owner, full, 0.0), axis=0, keepdims=True)

    vec_own[3:4, :] = scatter(part_up[...], part_up.shape[0])
    for i in range(2):
        columns = pl.ds(i * LOCAL, LOCAL)
        vec_own[7:8, columns] = scatter(part_qv[i], part_qv.shape[1])

    def vec_copy(j):
        pair = (v_sems.at[0, j], v_sems.at[1, j])
        return remote(vec_own, vec_got.at[j], pair, at.peers_f[j])

    for j in range(nf - 1):
        vec_copy(j).start()

    valid = mask[...].astype(F32)
    masks = jnp.concatenate([valid, jnp.zeros_like(valid)], axis=0)
    cnt[0] = jnp.broadcast_to(jnp.sum(masks, keepdims=True), (8, 128))

    def count_z(j):
        pair = (cz_sems.at[0, j], cz_sems.at[1, j])
        return remote(cnt.at[0], cnt.at[1 + j], pair, at.peers_z[j])

    def count_f(j):
        pair = (cf_sems.at[0, j], cf_sems.at[1, j])
        return remote(cnt.at[4], cnt.at[5 + j], pair, at.peers_f[j])

    for j in range(3):
        count_z(j).start()

    turned = jnp.transpose(masks)
    segk[...] = jnp.full(segk.shape, -1.0, F32)
    segk[0:4, 1024:3072] = segs[...].astype(F32)
    seg_turned = jnp.transpose(segk[:, aligned(1024 + at.z * GROUP, GROUP)])
    column = lax.broadcasted_iota(jnp.int32, (1, 128), 1)
    for s in range(SEQS):
        lse[s] = jnp.where(column == 4, turned[:, s : s + 1], seg_turned[:, s : s + 1])
    small[...] = jnp.zeros_like(small)
    @pl.when(at.z < 2)
    def _():
        def clear(s, carry):
            kv[s, 0] = jnp.zeros((GROUP, 2 * LOCAL), BF)
            return carry

        lax.fori_loop(0, SEQS, clear, 0)

    @pl.when(at.z < 1)
    def _():
        def clear(s, carry):
            kv[s, 1] = jnp.zeros((GROUP, 2 * LOCAL), BF)
            return carry

        lax.fori_loop(0, SEQS, clear, 0)

    def near_copy(s):
        return remote(
            kv.at[s, 2], kv.at[s, 1], (near_sems.at[0, s], near_sems.at[1, s]), at.up
        )

    def far_copy(s):
        return remote(kv.at[s, 1], kv.at[s, 0], (far_sems.at[0, s], far_sems.at[1, s]), at.up)

    def norm_copy(s):
        return pltpu.make_async_copy(act.at[s], n1_h.at[s], n1_sem.at[s])

    def step_norm(s, carry):
        token_copy(s).wait()

        @pl.when(s < 3)
        def _():
            token_copy(s + 1).start()

        for part in range(2):
            here = pl.ds(part * 256, 256)
            xhat, _ = norm_parts(stage[lax.rem(s, 2), here].astype(F32))
            act[s, here] = (xhat * vec[5:6, :] + vec[6:7, :]).astype(BF)
        norm_copy(s).start()
        return carry

    def step_a(s):
        normed = act[s]
        q[s] = ((matmul(normed, wqkv[0], 1, 0) + vec[7:8, 0:256]) * 0.125).astype(BF)
        kv[s, 2, :, 0:LOCAL] = matmul(normed, wqkv[1], 1, 0).astype(BF)
        kv[s, 2, :, LOCAL:] = (matmul(normed, wqkv[2], 1, 0) + vec[7:8, 256:512]).astype(BF)

        @pl.when((at.z < 3) & ((at.z == 0) | (s == 0)))
        def _():
            near_copy(s).start()

    for j in range(nf - 1):
        vec_copy(j).wait()
    whole = vec_own[...]
    for j in range(nf - 1):
        whole = whole + vec_got[j]
    vec[...] = whole
    small[7:8, :] = vec[5:6, :]
    lax.fori_loop(0, SEQS, step_norm, 0)
    weight_wait(0)
    for i in range(1, 4):
        weight_start(i)
    for i, (source, target) in enumerate(quarters):
        pltpu.make_async_copy(source.at[:, mine, :], target, q_sems.at[i]).wait()

    def step_count(s):
        for j in range(3):
            count_z(j).wait()
        cnt[4] = cnt[0] + cnt[1] + cnt[2] + cnt[3]
        for j in range(nf - 1):
            count_f(j).start()

    def step_counted(s):
        for j in range(nf - 1):
            count_f(j).wait()
        total_count = cnt[4]
        for j in range(nf - 1):
            total_count = total_count + cnt[5 + j]
        small[6:7, 0:128] = total_count[0:1, :]
        cnt[0] = (SEQS * GROUP * nf * 4) / total_count
        for i in range(SEQS):
            norm_copy(i).wait()
        for copy in block_copies(0):
            copy.start()

    def factor():
        return cnt[0, 0:1, 0:1]

    def block_copies(s):
        return (
            pltpu.make_async_copy(teacher.at[s], stage.at[0], in_sems.at[0]),
            pltpu.make_async_copy(cot.at[s], stage.at[1], in_sems.at[1]),
        )

    def kv_out(s):
        return pltpu.make_async_copy(kv.at[s], kv_h.at[s], res_sem.at[s])

    def mix_copy(s):
        return pltpu.make_async_copy(tok_q.at[s], gmix_h.at[s, mine], mix_sem.at[s])

    def ends(k, s):
        if k == 2:
            return tok_q.at[s], gmix_h
        target = (n2, blk)[k]
        return target.at[s, mine], target

    def step_r(k, s):
        summed = ring.total(s)
        if k == 0:
            middle = tok_q[s].astype(F32) + summed + vec[0:1, :]
            mid[s] = middle
            xhat, _ = norm_parts(middle)
            n2[s, mine] = (xhat * vec[1:2, :] + vec[2:3, :]).astype(BF)
        elif k == 1:
            block = mid[s] + summed + vec[4:5, :]
            blk[s, mine] = block.astype(BF)
            difference = block - tea_q[s].astype(F32)
            masked = lse[s, mine, 4:5] * difference
            small[5:6, :] += column_sum(masked * difference)
            grad = cot_q[s].astype(F32) + masked * factor()
            gblk[s] = grad
            small[0:1, :] += column_sum(grad)
        else:
            xhat, inverse = norm_parts(mid[s])
            small[1:2, :] += column_sum(summed * xhat)
            small[2:3, :] += column_sum(summed)
            grad = gblk[s] + norm_back(summed, xhat, inverse, vec[1:2, :])
            gblk[s] = grad
            small[3:4, :] += column_sum(grad)
            tok_q[s] = grad.astype(BF)
            mix_copy(s).start()
        ring.spread(*ends(k, s), s)

    def halo(s):
        @pl.when(at.z > 0)
        def _():
            near_copy(s).wait_recv()

        @pl.when((at.z > 0) & (at.z < 3))
        def _():
            far_copy(s).start()

            @pl.when(s < 3)
            def _():
                near_copy(s + 1).start()

    def step_p0(s):
        @pl.when(at.z < 3)
        def _():
            near_copy(s).wait_send()

        @pl.when((at.z > 0) & (at.z < 3))
        def _():
            far_copy(s).wait_send()

        @pl.when(at.z > 1)
        def _():
            far_copy(s).wait_recv()

        kv_out(s).start()
        lane = lax.broadcasted_iota(jnp.int32, (1, LOCAL), 1) // HD
        slot = lax.broadcasted_iota(jnp.int32, (1, 128), 1)
        keys = kv.at[s].reshape(3 * GROUP, 2 * LOCAL)
        here_segs = segk.at[:, aligned(at.z * GROUP, 3 * GROUP)]
        which = lax.broadcasted_iota(jnp.int32, (8, SPAN), 0) == s

        def block(b, carry):
            start = pl.multiple_of(b * HALF, HALF)
            here = pl.ds(start, HALF)
            span = pl.ds(start, SPAN)
            seg_row = jnp.sum(
                jnp.where(which, here_segs[:, span], 0.0), axis=0, keepdims=True
            )
            columns = lse[s, here]
            bias[...] = allowed_bias(columns[:, 5:6], seg_row)
            query = q[s, here]
            k_block = keys[span, 0:LOCAL]
            v_block = keys[span, LOCAL:]
            mixed = jnp.zeros((HALF, LOCAL), F32)
            logs = columns
            for h in range(LOCAL // HD):
                one = jnp.where(lane == h, query, jnp.zeros_like(query))
                scores = matmul(one, k_block, 1, 1) + bias[...]
                top = jnp.max(scores, axis=-1, keepdims=True)
                weights = jnp.exp(scores - top)
                whole = jnp.sum(weights, axis=-1, keepdims=True)
                part = matmul(weights.astype(BF), v_block, 1, 0) / whole
                mixed = jnp.where(lane == h, part, mixed)
                logs = jnp.where(slot == h, top + jnp.log(whole), logs)
            att[s, here] = mixed.astype(BF)
            lse[s, here] = logs
            return carry

        lax.fori_loop(0, 2, block, 0)
        send[s] = matmul(att[s], wout[...], 1, 0).astype(BF)
        ring.rs_core(s).start()

    def step_p1(s):
        ring.step_u(*ends(0, s), s)
        for part in range(2):
            here = pl.ds(part * 256, 256)
            h = matmul(n2[s, here], wfc1[...], 1, 0) + vec[3:4, :]
            t = jnp.tanh(0.7978845608028654 * (h + 0.044715 * h * h * h))
            act[s, here] = (0.5 * h * (1.0 + t)).astype(BF)
            slope[s, here] = (
                0.5 * (1.0 + t)
                + 0.5 * h * (1.0 - t * t) * (0.7978845608028654 * (1.0 + 0.134145 * h * h))
            ).astype(BF)
        send[s] = matmul(act[s], wfc2[...], 1, 0).astype(BF)
        ring.rs_core(s).start()

    def step_p2(s):
        ring.step_u(*ends(1, s), s)
        out = pltpu.make_async_copy(blk.at[s], out_h.at[s], out_sem)
        out.start()
        for copy in block_copies(s):
            copy.wait()
        out.wait()
        for part in range(2):
            here = pl.ds(part * 256, 256)
            difference = blk[s, here].astype(F32) - stage[0, here].astype(F32)
            scaled = lse[s, here, 4:5] * factor()
            down = (stage[1, here].astype(F32) + scaled * difference).astype(BF)
            blk[s, here] = down
            up = matmul(down, wfc2[...], 1, 1) * slope[s, here].astype(F32)
            rounded = up.astype(BF)
            slope[s, here] = rounded
            small[4:5, :] += column_sum(rounded.astype(F32))

        @pl.when(s < 3)
        def _():
            for copy in block_copies(s + 1):
                copy.start()

        send[s] = matmul(slope[s], wfc1[...], 1, 1).astype(BF)
        ring.rs_core(s).start()

    deep = lambda ref: ref.reshape(SEQS * GROUP, 1024)

    def down_out():
        return pltpu.make_async_copy(deep(send).at[0:1024], gfc2, in_sems.at[0])

    def up_out():
        return pltpu.make_async_copy(deep(act).at[0:1024], gfc1, in_sems.at[1])

    def step_gdown(s):
        deep(send)[0:1024, :] = matmul(deep(act)[...], deep(blk)[...], 0, 0).astype(BF)
        down_out().start()

    def step_gup(s):
        deep(act)[0:1024, :] = matmul(deep(n2)[...], deep(slope)[...], 0, 0).astype(BF)
        up_out().start()

    actions = {
        "A": step_a,
        "H": halo,
        "C": step_count,
        "D": step_counted,
        "W": lambda s: weight_wait(s),
        "P0": step_p0,
        "P1": step_p1,
        "P2": step_p2,
        "Q": ring.step_q,
        "gdown": step_gdown,
        "gup": step_gup,
    }
    for k in range(3):
        actions[f"R{k}"] = functools.partial(step_r, k)
        actions[f"T{k}"] = lambda s, k=k: ring.step_t(*ends(k, s), s)
    actions["W"] = lambda s: [weight_wait(i) for i in (2, 3)]
    actions["V"] = lambda s: weight_wait(1)
    run_order(actions, FRONT_ORDER)
    last = pltpu.make_async_copy(gblk, gmid_h, out_sem)
    last.start()
    kept = (
        pltpu.make_async_copy(wqkv, wqkv_h, keep_sem.at[0]),
        pltpu.make_async_copy(wout, wout_h, keep_sem.at[1]),
    )
    for copy in kept:
        copy.start()
    for s in range(SEQS):
        ring.step_u(*ends(2, s), s)
        mix_copy(s).wait()
        kv_out(s).wait()
    last.wait()
    down_out().wait()
    up_out().wait()
    for copy in kept:
        copy.wait()


def front_call(nf, *args):
    anys = pl.BlockSpec(memory_space=pl.ANY)
    vmem = pl.BlockSpec(memory_space=pltpu.VMEM)
    dma = pltpu.SemaphoreType.DMA
    big = lambda *lead: pltpu.VMEM((*lead, GROUP, 1024), BF)
    shape = jax.ShapeDtypeStruct
    return pl.pallas_call(
        functools.partial(front_kernel, nf),
        out_shape=(
            shape((SEQS, GROUP, 1024), BF),
            shape((SEQS, GROUP, 1024), BF),
            shape((SEQS, QUARTER, 1024), F32),
            shape((1024, 1024), BF),
            shape((1024, 1024), BF),
            shape((8, 1024), F32),
            shape((SEQS, GROUP, LOCAL), BF),
            shape((SEQS, GROUP, LOCAL), BF),
            shape((SEQS, 3, GROUP, 2 * LOCAL), BF),
            shape((SEQS, GROUP, 128), F32),
            shape((SEQS, GROUP, 1024), BF),
            shape((3, 1024, LOCAL), BF),
            shape((LOCAL, 1024), BF),
        ),
        in_specs=[anys] * 7 + [vmem] * 10,
        out_specs=(anys, anys, anys, anys, anys, vmem, vmem, vmem, anys, vmem, anys, anys, anys),
        scratch_shapes=[
            pltpu.VMEM((3, 1024, LOCAL), BF),
            pltpu.VMEM((LOCAL, 1024), BF),
            pltpu.VMEM((1024, 1024), BF),
            pltpu.VMEM((1024, 1024), BF),
            big(SEQS),
            big(SEQS),
            big(SEQS),
            big(SEQS),
            big(SEQS),
            pltpu.VMEM((SEQS, HALF, 1024), BF),
            pltpu.VMEM((SEQS, QUARTER, 1024), BF),
            pltpu.VMEM((SEQS, QUARTER, 1024), BF),
            pltpu.VMEM((SEQS, QUARTER, 1024), F32),
            pltpu.VMEM((SEQS, QUARTER, 1024), F32),
            pltpu.VMEM((SEQS, QUARTER, 1024), BF),
            pltpu.VMEM((SEQS, QUARTER, 1024), BF),
            pltpu.VMEM((SEQS, QUARTER, 1024), BF),
            big(2),
            pltpu.VMEM((8, 3072), F32),
            pltpu.VMEM((HALF, SPAN), F32),
            pltpu.VMEM((SEQS, 3, GROUP, 2 * LOCAL), BF),
            pltpu.VMEM((4 + nf, 8, 128), F32),
            dma((4, nf - 1)),
            dma((4, nf - 1)),
            dma((4,)),
            dma((5, 2, SEQS)),
            dma((3,)),
            dma((2,)),
            dma((SEQS,)),
            dma,
            dma((SEQS,)),
            dma((2, SEQS)),
            dma((2, SEQS)),
            dma((2, 3)),
            dma((2, nf - 1)),
            dma((SEQS,)),
            dma((2,)),
            pltpu.VMEM((8, 1024), F32),
            pltpu.VMEM((8, 1024), F32),
            pltpu.VMEM((nf - 1, 8, 1024), F32),
            dma((2, nf - 1)),
        ],
        compiler_params=pltpu.CompilerParams(
            collective_id=1, has_side_effects=True, vmem_limit_bytes=63 * 2**20
        ),
        cost_estimate=pl.CostEstimate(
            flops=2 * 2048 * 1024 * 1024 * 9, bytes_accessed=30 * 2**20, transcendentals=0
        ),
        name="front",
    )(*args)


class Reduce:
    def __init__(self, at, cut, size, rows, full, arrived, shard, half, quarter, sems):
        self.at, self.cut, self.size, self.rows = at, cut, size, rows
        self.full, self.arrived, self.shard = full, arrived, shard
        self.half, self.quarter = half, quarter
        self.x_sems, self.z_sems = sems
        self.a, self.b = lax.rem(at.z, 2), at.z // 2
        self.side = (at.f, at.z + 1 - 2 * self.a, at.t)
        self.across = (at.f, lax.rem(at.z + 2, 4), at.t)

    def own(self, f):
        return self.cut(self.full, aligned(f * self.size, self.size, math.gcd(self.size, 128)))

    def part(self, ref, start, size):
        where = aligned(start, size, 16)
        return ref.at[:, where, :] if len(ref.shape) == 3 else ref.at[where, :]

    def x_copy(self, j):
        there = lax.rem(self.at.f + 1 + j, self.at.nf)
        pair = (self.x_sems.at[0, j], self.x_sems.at[1, j])
        return remote(self.own(there), self.arrived.at[j], pair, self.at.peers_f[j])

    def z_copy(self, stage):
        h, q = self.rows // 2, self.rows // 4
        pair = (self.z_sems.at[0, stage], self.z_sems.at[1, stage])
        own = self.own(self.at.f)
        if stage == 0:
            return remote(self.part(own, (1 - self.a) * h, h), self.half, pair, self.side)
        if stage == 1:
            src = self.part(own, self.a * h + (1 - self.b) * q, q)
            return remote(src, self.quarter, pair, self.across)
        if stage == 2:
            kept = self.part(self.shard, self.a * h + self.b * q, q)
            return remote(kept, kept, pair, self.across)
        kept = self.part(self.shard, self.a * h, h)
        return remote(kept, kept, pair, self.side)

    def add(self, target, first, others):
        total = first[...].astype(F32)
        for other in others:
            total = total + other[...].astype(F32)
        target[...] = total.astype(BF)

    def run(self, stage):
        h, q = self.rows // 2, self.rows // 4
        peers = range(self.at.nf - 1)
        own = self.own(self.at.f)
        if stage == 0:
            for j in peers:
                self.x_copy(j).start()
            return
        if stage == 1:
            for j in peers:
                self.x_copy(j).wait()
            self.add(own, own, [self.arrived.at[j] for j in peers])
        else:
            self.z_copy(stage - 2).wait()
        if stage == 2:
            kept = self.part(own, self.a * h, h)
            self.add(kept, kept, [self.half])
        elif stage == 3:
            start = self.a * h + self.b * q
            self.add(self.part(self.shard, start, q), self.part(own, start, q), [self.quarter])
        if stage < 5:
            self.z_copy(stage - 1).start()


BACK_ORDER = (
    ("E", 0),
    ("K0", 0),
    ("E", 1),
    ("K1", 0),
    ("K0", 1),
    ("K0", 2),
    ("I", 0),
    ("E", 2),
    ("K2", 0),
    ("K1", 1),
    ("E", 3),
    ("K0", 3),
    ("K3", 0),
    ("K1", 2),
    ("K2", 1),
    ("K3", 1),
    ("I", 1),
    ("B0", 0),
    ("K2", 2),
    ("K4", 0),
    ("F", 0),
    ("I", 2),
    ("K4", 1),
    ("D1", 0),
    ("I", 3),
    ("F", 1),
    ("D2", 0),
    ("Q", 1),
    ("K1", 3),
    ("Q", 0),
    ("K3", 2),
    ("D1", 1),
    ("B1", 0),
    ("F", 2),
    ("D1", 3),
    ("D1", 2),
    ("K2", 3),
    ("K3", 3),
    ("F", 3),
    ("Q", 2),
    ("D2", 1),
    ("C0", 0),
    ("B2", 0),
    ("R", 0),
    ("D2", 3),
    ("R", 1),
    ("D2", 2),
    ("B3", 0),
    ("Q", 3),
    ("K4", 2),
    ("D1", 4),
    ("K4", 3),
    ("D1", 5),
    ("D3", 0),
    ("D1", 6),
    ("C1", 0),
    ("B4", 0),
    ("T", 1),
    ("D2", 4),
    ("R", 2),
    ("D1", 7),
    ("T", 0),
    ("D3", 3),
    ("D2", 5),
    ("R", 3),
    ("S0", 0),
    ("S1", 0),
    ("D2", 6),
    ("S2", 0),
    ("D3", 2),
    ("C2", 0),
    ("C3", 0),
    ("D3", 6),
    ("T", 3),
    ("D2", 7),
    ("S3", 0),
    ("D3", 5),
    ("C4", 0),
    ("D3", 7),
    ("T", 2),
    ("S4", 0),
    ("D3", 1),
    ("B5", 0),
    ("D3", 4),
    ("S5", 0),
    ("C5", 0),
)


class Chain(Reduce):
    def piece(self, ref, half):
        return self.part(ref, half * (self.rows // 2), self.rows // 2)

    def x_half(self, j, half):
        there = lax.rem(self.at.f + 1 + j, self.at.nf)
        pair = (self.x_sems.at[0, j, half], self.x_sems.at[1, j, half])
        src = self.piece(self.own(there), half)
        return remote(src, self.piece(self.arrived.at[j], half), pair, self.at.peers_f[j])

    def up_copy(self, half):
        pair = (self.z_sems.at[0, half], self.z_sems.at[1, half])
        src = self.piece(self.own(self.at.f), half)
        return remote(src, self.piece(self.shard, half), pair, self.at.up)

    def down_copy(self, half, j):
        q = self.rows // 4
        part = self.part(self.shard, half * (self.rows // 2) + j * q, q)
        which = 2 + half * 2 + j
        pair = (self.z_sems.at[0, which], self.z_sems.at[1, which])
        return remote(part, part, pair, self.at.down)

    def climb(self, stage, half):
        own = self.piece(self.own(self.at.f), half)
        peers = range(self.at.nf - 1)
        if stage == 0:
            for j in peers:
                self.x_half(j, half).start()
            return
        if stage == 1:
            for j in peers:
                self.x_half(j, half).wait()
            self.add(own, own, [self.piece(self.arrived.at[j], half) for j in peers])

        @pl.when(self.at.z == stage - 1)
        def _():
            shard = self.piece(self.shard, half)
            if stage > 1:
                self.up_copy(half).wait_recv()
                self.add(own if stage < 4 else shard, own, [shard])
            if stage < 4:
                self.up_copy(half).start()
            else:
                for j in range(2):
                    self.down_copy(half, j).start()

    def hand_down(self, hop, half, j):
        @pl.when(self.at.z == 3 - hop)
        def _():
            self.down_copy(half, j).wait_recv()
            if hop < 3:
                self.down_copy(half, j).start()

    def finish(self):
        for half in range(2):

            @pl.when(self.at.z < 3)
            def _():
                self.up_copy(half).wait_send()

            @pl.when(self.at.z > 0)
            def _():
                for j in range(2):
                    self.down_copy(half, j).wait_send()


def back_kernel(
    nf,
    gmix_h,
    gmid_h,
    gfc1_h,
    gfc2_h,
    att,
    q,
    kv_h,
    lse,
    n1_h,
    tokens,
    wqkv,
    wout,
    segs,
    sums_one,
    ig_h,
    small,
    s_qkv,
    s_out,
    s_fc1,
    s_fc2,
    gm,
    kvs,
    n1s,
    ga,
    dots,
    bias,
    segk,
    dkvt,
    dfar,
    dnear,
    down,
    m1,
    m2,
    gq,
    send,
    recv_c,
    send_y,
    recv_y,
    gmid,
    tok_q,
    a_qkv,
    a_out,
    f_qkv,
    f_fc1,
    f_fc2,
    x_qkv,
    x_out,
    x_fc1,
    x_fc2,
    h_qkv,
    h_out,
    k_qkv,
    k_out,
    ring_sems,
    load_sems,
    first_sems,
    m1_sems,
    m2_sems,
    red_x,
    red_z,
    chain_x,
    chain_z,
    got_core,
    got_y,
    got_f,
    got_z,
    sum_sems,
    sum_f_sems,
    n1e,
):
    at = Place(nf)
    at.barrier()
    ring = Ring(at, send, recv_c, send_y, recv_y, ring_sems)
    mine = aligned(at.mine, QUARTER)
    rows_cut = lambda ref, where: ref.at[where, :]
    cols_cut = lambda ref, where: ref.at[:, where]
    deep_cut = lambda ref, where: ref.at[:, where, :]
    fs = 1024 // nf
    f_out = gm.at[0:LOCAL]

    def reducer(i, cut, rows, full, arrived, shard, half, quarter, kind=Reduce):
        sems = (chain_x.at[i - 2], chain_z.at[i - 2]) if kind is Chain else (red_x.at[i], red_z.at[i])
        return kind(at, cut, fs, rows, full, arrived, shard, half, quarter, sems)

    first, rest = pl.ds(0, 1), pl.ds(1, 2)
    red_q = reducer(
        0, deep_cut, fs, f_qkv.at[first], x_qkv.at[:, first], s_qkv.at[first], h_qkv.at[first], k_qkv.at[first]
    )
    red_kv = reducer(
        4, deep_cut, fs, f_qkv.at[rest], x_qkv.at[:, rest], s_qkv.at[rest], h_qkv.at[rest], k_qkv.at[rest]
    )
    red_out = reducer(1, cols_cut, LOCAL, f_out, x_out, s_out, h_out, k_out)
    red_fc1 = reducer(2, rows_cut, fs, f_fc1, x_fc1, s_fc1, None, None, Chain)
    red_fc2 = reducer(3, cols_cut, 1024, f_fc2, x_fc2, s_fc2, None, None, Chain)

    firsts = (
        (gfc1_h, f_fc1),
        (gfc2_h, f_fc2),
        (gmid_h.at[0], gmid),
        (tokens.at[:, mine, :], tok_q),
    )

    def first_copy_of(i):
        return pltpu.make_async_copy(gfc1_h, f_fc1, first_sems.at[i])

    def first_copy(i):
        return pltpu.make_async_copy(firsts[i][0], firsts[i][1], first_sems.at[i])

    def load_copies(s):
        return (
            pltpu.make_async_copy(gmix_h.at[s], gm, load_sems.at[0, 0]),
            pltpu.make_async_copy(kv_h.at[s], kvs, load_sems.at[1, 0]),
        )

    def norm_load(s):
        return pltpu.make_async_copy(n1_h.at[s], n1s, load_sems.at[2, 0])

    def norm_early(s):
        return pltpu.make_async_copy(n1_h.at[s], n1e, load_sems.at[0, 1])

    def mid_load(s):
        return pltpu.make_async_copy(gmid_h.at[s], gmid, load_sems.at[2, 1])

    for copy in load_copies(0):
        copy.start()
    for i in range(4):
        first_copy(i).start()
    norm_load(0).start()
    norm_early(0).start()

    segk[...] = jnp.full(segk.shape, -1.0, F32)
    segk[0:4, 1024:3072] = segs[...].astype(F32)
    small[...] = jnp.zeros_like(small)
    a_qkv[...] = jnp.zeros_like(a_qkv)
    a_out[...] = jnp.zeros_like(a_out)
    def m1_copy(s):
        return remote(dfar.at[s], m1.at[s], (m1_sems.at[0, s], m1_sems.at[1, s]), at.down)

    def m2_copy(s):
        return remote(dnear.at[s], m2.at[s], (m2_sems.at[0, s], m2_sems.at[1, s]), at.down)

    def step_e(s):
        for copy in load_copies(s):
            copy.wait()

        ga[...] = matmul(gm[...], wout[...], 1, 1).astype(BF)
        a_out[...] += matmul(att[s], gm[...], 0, 0)

        lane = lax.broadcasted_iota(jnp.int32, (1, LOCAL), 1) // HD
        keys = kvs.reshape(3 * GROUP, 2 * LOCAL)
        here_segs = segk.at[:, aligned(at.z * GROUP, 3 * GROUP)]
        which = lax.broadcasted_iota(jnp.int32, (8, SPAN), 0) == s
        dkvt[...] = jnp.zeros_like(dkvt)

        def block(b, carry):
            start = pl.multiple_of(b * HALF, HALF)
            here = pl.ds(start, HALF)
            span = pl.ds(start, SPAN)
            seg_row = jnp.sum(
                jnp.where(which, here_segs[:, span], 0.0), axis=0, keepdims=True
            )
            logs = lse[s, here]
            bias[...] = allowed_bias(logs[:, 5:6], seg_row)
            query = q[s, here]
            grad = ga[here]
            k_block = keys[span, 0:LOCAL]
            v_block = keys[span, LOCAL:]
            dots[0] = jnp.transpose(query)
            dots[1] = jnp.transpose(grad)
            product = grad.astype(F32) * att[s, here].astype(F32)
            grad_query = jnp.zeros((HALF, LOCAL), F32)
            for h in range(LOCAL // HD):
                mine_h = lane == h
                one = jnp.where(mine_h, query, jnp.zeros_like(query))
                grad_one = jnp.where(mine_h, grad, jnp.zeros_like(grad))
                delta = jnp.sum(jnp.where(mine_h, product, 0.0), axis=-1, keepdims=True)
                scores = matmul(one, k_block, 1, 1) + bias[...]
                probs = jnp.exp(scores - logs[:, h : h + 1])
                dprobs = matmul(grad_one, v_block, 1, 1)
                grad_scores = (probs * (dprobs - delta)).astype(BF)
                grad_query = jnp.where(mine_h, matmul(grad_scores, k_block, 1, 0), grad_query)
                k_rows = pl.ds(h * HD, HD)
                v_rows = pl.ds(LOCAL + h * HD, HD)
                dkvt[k_rows, span] += matmul(dots[0, k_rows], grad_scores, 1, 0)
                dkvt[v_rows, span] += matmul(dots[1, k_rows], probs.astype(BF), 1, 0)
            gq[s, here] = (grad_query * 0.125).astype(BF)
            return carry

        lax.fori_loop(0, 2, block, 0)

        @pl.when(s < 3)
        def _():
            for copy in load_copies(s + 1):
                copy.start()

        for i, target in enumerate((dfar, dnear, down)):
            target[s] = jnp.transpose(dkvt[:, i * GROUP : (i + 1) * GROUP].astype(BF))

        @pl.when(at.z > 1)
        def _():
            m1_copy(s).start()

        norm_early(s).wait()
        a_qkv[0] += matmul(n1e[...], gq[s], 0, 0)

        @pl.when(s < 3)
        def _():
            norm_early(s + 1).start()

    def step_i(s):
        @pl.when((at.z > 0) & (at.z < 3))
        def _():
            m1_copy(s).wait_recv()
            dnear[s] = (dnear[s].astype(F32) + m1[s].astype(F32)).astype(BF)

        @pl.when(at.z > 0)
        def _():
            m2_copy(s).start()

    def step_f(s):
        @pl.when(at.z < 3)
        def _():
            m2_copy(s).wait_recv()
            down[s] = (down[s].astype(F32) + m2[s].astype(F32)).astype(BF)

        norm_load(s).wait()
        grads = (gq[s], down[s, :, 0:LOCAL], down[s, :, LOCAL:])
        send[s] = (
            matmul(grads[0], wqkv[0], 1, 1)
            + matmul(grads[1], wqkv[1], 1, 1)
            + matmul(grads[2], wqkv[2], 1, 1)
        ).astype(BF)
        ring.rs_core(s).start()
        normed = n1s[...]
        for i in (1, 2):
            a_qkv[i] += matmul(normed, grads[i], 0, 0)

        @pl.when(s < 3)
        def _():
            norm_load(s + 1).start()

        small[9:10, 0:LOCAL] += column_sum(grads[0].astype(F32))
        small[9:10, LOCAL : 2 * LOCAL] += column_sum(grads[2].astype(F32))

    def ends(s):
        return tok_q.at[s], ig_h

    def ig_copy(s):
        return pltpu.make_async_copy(tok_q.at[s], ig_h.at[s, mine], first_sems.at[s])

    def step_r(s):
        @pl.when(s == 0)
        def _():
            first_copy(2).wait()
            first_copy(3).wait()

        summed = ring.total(s)
        xhat, inverse = norm_parts(tok_q[s].astype(F32))
        small[0:1, :] += column_sum(summed * xhat)
        small[1:2, :] += column_sum(summed)
        @pl.when(s > 0)
        def _():
            mid_load(s).wait()

        grad = gmid[...] + norm_back(summed, xhat, inverse, sums_one[7:8, :])
        tok_q[s] = grad.astype(BF)

        @pl.when(s < 3)
        def _():
            mid_load(s + 1).start()

        ig_copy(s).start()
        ring.spread(*ends(s), s)

    def sum_copy(stage, j=0):
        pair = (sum_sems.at[0, stage], sum_sems.at[1, stage])
        top = small.at[0:8]
        if stage == 0:
            return remote(top, got_core, pair, at.mate_c)
        if stage == 1:
            return remote(top, got_y, pair, at.mate_y)
        if stage == 2:
            pair = (sum_f_sems.at[0, j], sum_f_sems.at[1, j])
            return remote(small, got_f.at[j], pair, at.peers_f[j])
        mate = red_q.side if stage == 3 else red_q.across
        return remote(small, got_z.at[stage - 3], pair, mate)

    def step_sum(stage, s):
        if stage == 0:
            small[2:6, :] = sums_one[0:4, :]
            small[6:7, :] = sums_one[5:6, :]
            small[8:9, :] = sums_one[4:5, :]
        elif stage == 3:
            for j in range(nf - 1):
                sum_copy(2, j).wait()
            for j in range(nf - 1):
                small[...] += got_f[j]
        else:
            sum_copy(stage - 1).wait()
            if stage == 1:
                small[0:8, :] += got_core[...]
            elif stage == 2:
                small[0:8, :] += got_y[...]
            else:
                small[...] += got_z[stage - 4]
        if stage == 2:
            for j in range(nf - 1):
                sum_copy(2, j).start()
        elif stage < 5:
            sum_copy(stage).start()

    def step_group(group, stage, s):
        if stage == 0:
            if group == "B":
                f_out[...] = a_out[...].astype(BF)
                f_qkv[0] = a_qkv[0].astype(BF)
            elif group == "C":
                for i in (1, 2):
                    f_qkv[i] = a_qkv[i].astype(BF)
        for reduce in groups[group]:
            reduce.run(stage)

    groups = {"B": (red_out, red_q), "C": (red_kv,)}
    chains = (red_fc2, red_fc1)
    actions = {
        "E": step_e,
        "I": step_i,
        "F": step_f,
        "Q": ring.step_q,
        "R": step_r,
        "T": lambda s: ring.step_t(*ends(s), s),
    }
    for stage in range(6):
        actions[f"S{stage}"] = functools.partial(step_sum, stage)
        for group in groups:
            actions[f"{group}{stage}"] = functools.partial(step_group, group, stage)

    def step_climb(stage, s):
        if stage == 0:

            @pl.when(lax.rem(s, 2) == 0)
            def _():
                first_copy_of(1 - s // 2).wait()

        for i, chain in enumerate(chains):

            @pl.when(s // 2 == i)
            def _(chain=chain):
                chain.climb(stage, lax.rem(s, 2))

    def step_down(hop, s):
        for i, chain in enumerate(chains):

            @pl.when(s // 4 == i)
            def _(chain=chain):
                chain.hand_down(hop, lax.rem(s // 2, 2), lax.rem(s, 2))

    for stage in range(5):
        actions[f"K{stage}"] = functools.partial(step_climb, stage)
    for hop in (1, 2, 3):
        actions[f"D{hop}"] = functools.partial(step_down, hop)
    run_order(actions, BACK_ORDER)
    for chain in chains:
        chain.finish()
    for s in range(SEQS):
        ring.step_u(*ends(s), s)
        ig_copy(s).wait()

        @pl.when(at.z > 1)
        def _():
            m1_copy(s).wait_send()

        @pl.when(at.z > 0)
        def _():
            m2_copy(s).wait_send()


def back_call(nf, *args):
    anys = pl.BlockSpec(memory_space=pl.ANY)
    vmem = pl.BlockSpec(memory_space=pltpu.VMEM)
    dma = pltpu.SemaphoreType.DMA
    big = lambda *lead: pltpu.VMEM((*lead, GROUP, 1024), BF)
    shape = jax.ShapeDtypeStruct
    fs = 1024 // nf
    low = lambda *dims: pltpu.VMEM(dims, BF)
    return pl.pallas_call(
        functools.partial(back_kernel, nf),
        out_shape=(
            shape((SEQS, GROUP, 1024), BF),
            shape((16, 1024), F32),
            shape((3, fs, LOCAL), BF),
            shape((LOCAL, fs), BF),
            shape((fs, 1024), BF),
            shape((1024, fs), BF),
        ),
        in_specs=[anys] * 4 + [vmem, vmem, anys, vmem, anys, anys, vmem, vmem, vmem, vmem],
        out_specs=(anys, vmem, vmem, vmem, vmem, vmem),
        scratch_shapes=[
            low(GROUP, 1024),
            low(3, GROUP, 2 * LOCAL),
            low(GROUP, 1024),
            low(GROUP, LOCAL),
            low(2, LOCAL, HALF),
            pltpu.VMEM((HALF, SPAN), F32),
            pltpu.VMEM((8, 3072), F32),
            pltpu.VMEM((2 * LOCAL, 3 * GROUP), F32),
            low(SEQS, GROUP, 2 * LOCAL),
            low(SEQS, GROUP, 2 * LOCAL),
            low(SEQS, GROUP, 2 * LOCAL),
            low(SEQS, GROUP, 2 * LOCAL),
            low(SEQS, GROUP, 2 * LOCAL),
            low(SEQS, GROUP, LOCAL),
            big(SEQS),
            low(SEQS, HALF, 1024),
            low(SEQS, QUARTER, 1024),
            low(SEQS, QUARTER, 1024),
            pltpu.VMEM((QUARTER, 1024), F32),
            low(SEQS, QUARTER, 1024),
            pltpu.VMEM((3, 1024, LOCAL), F32),
            pltpu.VMEM((LOCAL, 1024), F32),
            low(3, 1024, LOCAL),
            low(1024, 1024),
            low(1024, 1024),
            low(nf - 1, 3, fs, LOCAL),
            low(nf - 1, LOCAL, fs),
            low(nf - 1, fs, 1024),
            low(nf - 1, 1024, fs),
            low(3, fs // 2, LOCAL),
            low(LOCAL // 2, fs),
            low(3, fs // 4, LOCAL),
            low(LOCAL // 4, fs),
            dma((5, 2, SEQS)),
            dma((3, 2)),
            dma((4,)),
            dma((2, SEQS)),
            dma((2, SEQS)),
            dma((5, 2, nf - 1)),
            dma((5, 2, 4)),
            dma((2, 2, nf - 1, 2)),
            dma((2, 2, 6)),
            pltpu.VMEM((8, 1024), F32),
            pltpu.VMEM((8, 1024), F32),
            pltpu.VMEM((nf - 1, 16, 1024), F32),
            pltpu.VMEM((2, 16, 1024), F32),
            dma((2, 5)),
            dma((2, nf - 1)),
            low(GROUP, 1024),
        ],
        compiler_params=pltpu.CompilerParams(
            collective_id=2, has_side_effects=True, vmem_limit_bytes=63 * 2**20
        ),
        cost_estimate=pl.CostEstimate(
            flops=2 * 2048 * 1024 * 1024 * 6, bytes_accessed=30 * 2**20, transcendentals=0
        ),
        name="back",
    )(*args)


def local(
    tokens,
    cotangent,
    teacher,
    valid_mask,
    segment_ids,
    ln1_gain,
    ln1_bias,
    w_qkv,
    b_qv,
    w_out,
    b_out,
    ln2_gain,
    ln2_bias,
    w_fc1,
    b_fc1,
    w_fc2,
    b_fc2,
):
    nf = lax.axis_size("fsdp")
    wide = b_out.shape[0]
    front = front_call(
        nf,
        w_qkv,
        w_out,
        w_fc1,
        w_fc2,
        tokens,
        teacher,
        cotangent,
        b_out,
        ln2_gain,
        ln2_bias,
        b_fc2,
        ln1_gain,
        ln1_bias,
        b_qv,
        b_fc1,
        valid_mask,
        segment_ids,
    )
    (output, grad_mix, grad_middle, gfc1, gfc2, sums_one, att, q, kv, lse, n1, wqkv, wout) = front
    input_grad, everything, s_qkv, s_out, s_fc1, s_fc2 = back_call(
        nf, grad_mix, grad_middle, gfc1, gfc2, att, q, kv, lse, n1, tokens, wqkv, wout, segment_ids, sums_one
    )
    place_f = lax.axis_index("fsdp")
    loss = jnp.sum(everything[6]) / (2.0 * D * sums_one[6, 0])
    ours = everything[8:10]
    part = lax.dynamic_slice_in_dim(everything[0:7], place_f * wide, wide, 1)
    grad_up = ours[0].reshape(b_fc1.shape[0], -1)
    grad_up = lax.dynamic_slice_in_dim(grad_up, place_f * b_fc1.shape[1], b_fc1.shape[1], 1)
    grad_qv = ours[1, : 2 * LOCAL].reshape(2, LOCAL // HD, HD)
    grad_qv = lax.dynamic_slice_in_dim(grad_qv, place_f * b_qv.shape[2], b_qv.shape[2], 2)
    return (
        output,
        loss,
        input_grad,
        part[0],
        part[1],
        s_qkv.astype(F32),
        grad_qv,
        s_out.astype(F32),
        part[5],
        part[3],
        part[4],
        s_fc1.astype(F32),
        grad_up,
        s_fc2.astype(F32),
        part[2],
    )


def solution(mesh):
    return jax.shard_map(
        local,
        mesh=mesh,
        in_specs=(
            P("fsdp", "context", None),
            P("fsdp", "context", None),
            P("fsdp", "context", None),
            P("fsdp", "context"),
            P("fsdp", None),
            P("fsdp"),
            P("fsdp"),
            P(None, "fsdp", "tensor"),
            P(None, "tensor", "fsdp"),
            P("tensor", "fsdp"),
            P("fsdp"),
            P("fsdp"),
            P("fsdp"),
            P("fsdp", "tensor"),
            P("tensor", "fsdp"),
            P("tensor", "fsdp"),
            P("fsdp"),
        ),
        out_specs=(
            P("fsdp", "context", None),
            P(),
            P("fsdp", "context", None),
            P("fsdp"),
            P("fsdp"),
            P(None, "fsdp", "tensor"),
            P(None, "tensor", "fsdp"),
            P("tensor", "fsdp"),
            P("fsdp"),
            P("fsdp"),
            P("fsdp"),
            P("fsdp", "tensor"),
            P("tensor", "fsdp"),
            P("tensor", "fsdp"),
            P("fsdp"),
        ),
        check_vma=False,
    )
```

```python
import functools
import math

import jax
import jax.numpy as jnp
from jax import lax
from jax.experimental import pallas as pl
from jax.experimental.pallas import tpu as pltpu
from jax.sharding import PartitionSpec as P

MESH = pl.DeviceIdType.MESH
BF = jnp.bfloat16
F32 = jnp.float32
D = 1024
HD = 64
WINDOW = 1024
EPSILON = 1e-05
MASKED = -1e30
SEQS = 4
GROUP = 512
QUARTER = 128
HALF = 256
SPAN = 1280
LOCAL = 256


def matmul(left, right, over_left, over_right):
    dims = (((over_left,), (over_right,)), ((), ()))
    return lax.dot_general(left, right, dims, preferred_element_type=F32)


def norm_parts(values):
    mean = jnp.mean(values, axis=-1, keepdims=True)
    center = values - mean
    spread = jnp.mean(center * center, axis=-1, keepdims=True)
    inverse = lax.rsqrt(spread + EPSILON)
    return center * inverse, inverse


def norm_back(grad_normed, xhat, inverse, gain):
    e = grad_normed * gain
    return inverse * (
        e
        - jnp.mean(e, axis=-1, keepdims=True)
        - xhat * jnp.mean(e * xhat, axis=-1, keepdims=True)
    )


def column_sum(values):
    return jnp.sum(values, axis=0, keepdims=True)


def aligned(start, size, unit=128):
    return pl.ds(pl.multiple_of(start, unit), size)


def allowed_bias(query_seg, key_seg, skipped=0, size=SPAN):
    column = lax.broadcasted_iota(jnp.int32, (HALF, size), 1) + skipped
    ahead = column - lax.broadcasted_iota(jnp.int32, (HALF, size), 0)
    allowed = (ahead > 0) & (ahead <= WINDOW) & (query_seg == key_seg)
    return jnp.where(allowed, 0.0, MASKED)


class Place:
    def __init__(self, nf):
        self.nf = nf
        self.f = lax.axis_index("fsdp")
        self.z = lax.axis_index("context")
        self.t = lax.axis_index("tensor")
        self.y, self.c = self.t // 2, lax.rem(self.t, 2)
        self.mate_c = (self.f, self.z, self.t + 1 - 2 * self.c)
        self.mate_y = (self.f, self.z, lax.rem(self.t + 2, 4))
        self.mine = (2 * self.c + self.y) * QUARTER
        self.over_y = (2 * self.c + 1 - self.y) * QUARTER
        self.peers_f = [(lax.rem(self.f + j, nf), self.z, self.t) for j in range(1, nf)]
        self.peers_z = [(self.f, lax.rem(self.z + j, 4), self.t) for j in range(1, 4)]
        self.up = (self.f, lax.rem(self.z + 1, 4), self.t)
        self.down = (self.f, lax.rem(self.z + 3, 4), self.t)

    def barrier(self):
        semaphore = pltpu.get_barrier_semaphore()
        everyone = [self.mate_c, self.mate_y] + self.peers_f + self.peers_z
        for peer in everyone:
            pl.semaphore_signal(semaphore, inc=1, device_id=peer, device_id_type=MESH)
        pl.semaphore_wait(semaphore, len(everyone))


def remote(src, dst, pair, mate):
    return pltpu.make_async_remote_copy(
        src, dst, pair[0], pair[1], device_id=mate, device_id_type=MESH
    )


def run_order(actions, order):
    names = list(actions)
    codes = [names.index(name) * 8 + s for name, s in order]

    def step(i, carry):
        code = jnp.int32(codes[0])
        for j, other in enumerate(codes[1:]):
            code = jnp.where(i == j + 1, other, code)
        kind, s = code // 8, lax.rem(code, 8)
        for j, name in enumerate(names):

            @pl.when(kind == j)
            def _(action=actions[name]):
                action(s)

        return carry

    lax.fori_loop(0, len(order), step, 0)


class Ring:
    def __init__(self, at, send, recv_c, send_y, recv_y, sems):
        self.at, self.send, self.recv_c = at, send, recv_c
        self.send_y, self.recv_y, self.sems = send_y, recv_y, sems

    def pair(self, which, s):
        return self.sems.at[which, 0, s], self.sems.at[which, 1, s]

    def rs_core(self, s):
        half = aligned((1 - self.at.c) * HALF, HALF)
        return remote(self.send.at[s, half], self.recv_c.at[s], self.pair(0, s), self.at.mate_c)

    def rs_y(self, s):
        return remote(self.send_y.at[s], self.recv_y.at[s], self.pair(1, s), self.at.mate_y)

    def back_y(self, src, dst, s):
        return remote(
            src, dst.at[s, aligned(self.at.mine, QUARTER)], self.pair(2, s), self.at.mate_y
        )

    def back_own(self, src, dst, s):
        return remote(
            src, dst.at[s, aligned(self.at.mine, QUARTER)], self.pair(3, s), self.at.mate_c
        )

    def back_over(self, dst, s):
        there = dst.at[s, aligned(self.at.over_y, QUARTER)]
        return remote(there, there, self.pair(4, s), self.at.mate_c)

    def step_q(self, s):
        self.rs_core(s).wait()
        self.send_y[s] = (
            self.send[s, aligned(self.at.over_y, QUARTER)].astype(F32)
            + self.recv_c[s, aligned((1 - self.at.y) * QUARTER, QUARTER)].astype(F32)
        ).astype(BF)
        self.rs_y(s).start()

    def total(self, s):
        self.rs_y(s).wait()
        return (
            self.send[s, aligned(self.at.mine, QUARTER)].astype(F32)
            + self.recv_c[s, aligned(self.at.y * QUARTER, QUARTER)].astype(F32)
            + self.recv_y[s].astype(F32)
        )

    def spread(self, src, dst, s):
        self.back_y(src, dst, s).start()
        self.back_own(src, dst, s).start()

    def step_t(self, src, dst, s):
        self.back_y(src, dst, s).wait()
        self.back_over(dst, s).start()

    def step_u(self, src, dst, s):
        self.back_own(src, dst, s).wait()
        self.back_over(dst, s).wait()


FRONT_ORDER = (
    ("A", 0),
    ("A", 1),
    ("H", 0),
    ("A", 2),
    ("V", 0),
    ("P0", 0),
    ("A", 3),
    ("C", 0),
    ("Q", 0),
    ("H", 1),
    ("R0", 0),
    ("P0", 1),
    ("T0", 0),
    ("H", 2),
    ("Q", 1),
    ("D", 0),
    ("W", 0),
    ("P1", 0),
    ("Q", 0),
    ("R0", 1),
    ("P0", 2),
    ("R1", 0),
    ("T0", 1),
    ("Q", 2),
    ("H", 3),
    ("P1", 1),
    ("Q", 1),
    ("R0", 2),
    ("P0", 3),
    ("R1", 1),
    ("Q", 3),
    ("T0", 2),
    ("P1", 2),
    ("T1", 0),
    ("T1", 1),
    ("Q", 2),
    ("P2", 0),
    ("R0", 3),
    ("P2", 1),
    ("Q", 0),
    ("T0", 3),
    ("R1", 2),
    ("P1", 3),
    ("Q", 3),
    ("T1", 2),
    ("Q", 1),
    ("P2", 2),
    ("R1", 3),
    ("R2", 1),
    ("Q", 2),
    ("T1", 3),
    ("P2", 3),
    ("R2", 0),
    ("Q", 3),
    ("gdown", 0),
    ("T2", 0),
    ("R2", 2),
    ("T2", 1),
    ("gup", 0),
    ("R2", 3),
    ("T2", 2),
    ("T2", 3),
)


def front_kernel(
    nf,
    wqkv_s,
    wout_s,
    wfc1_s,
    wfc2_s,
    tokens,
    teacher,
    cot,
    part_bo,
    part_g2,
    part_b2,
    part_bd,
    part_g1,
    part_b1,
    part_qv,
    part_up,
    mask,
    segs,
    out_h,
    gmix_h,
    gmid_h,
    gfc1,
    gfc2,
    small,
    att,
    q,
    kv_h,
    lse,
    n1_h,
    wqkv_h,
    wout_h,
    wqkv,
    wout,
    wfc1,
    wfc2,
    n2,
    blk,
    act,
    slope,
    send,
    recv_c,
    send_y,
    recv_y,
    mid,
    gblk,
    tok_q,
    tea_q,
    cot_q,
    stage,
    segk,
    bias,
    kv,
    cnt,
    w_send,
    w_recv,
    w_loc,
    ring_sems,
    q_sems,
    in_sems,
    n1_sem,
    out_sem,
    mix_sem,
    near_sems,
    far_sems,
    cz_sems,
    cf_sems,
    res_sem,
    keep_sem,
    vec,
    vec_own,
    vec_got,
    v_sems,
):
    at = Place(nf)
    at.barrier()
    ring = Ring(at, send, recv_c, send_y, recv_y, ring_sems)
    mine = aligned(at.mine, QUARTER)

    fs = wout_s.shape[1]
    own = aligned(at.f * fs, fs)
    query, pair_kv = pl.ds(0, 1), pl.ds(1, 2)
    places = (
        (wqkv_s.at[pair_kv], wqkv.at[pair_kv, own, :]),
        (wout_s, wout.at[:, own]),
        (wfc1_s, wfc1.at[own, :]),
        (wfc2_s, wfc2.at[:, own]),
        (wqkv_s.at[query], wqkv.at[query, own, :]),
    )

    def weight_copy(i, j):
        pair = (w_send.at[i, j], w_recv.at[i, j])
        return remote(places[i][0], places[i][1], pair, at.peers_f[j])

    def weight_start(i):
        for j in range(nf - 1):
            weight_copy(i, j).start()
        pltpu.make_async_copy(places[i][0], places[i][1], w_loc.at[i]).start()

    def weight_wait(i):
        pltpu.make_async_copy(places[i][0], places[i][1], w_loc.at[i]).wait()
        for j in range(nf - 1):
            weight_copy(i, j).wait()

    weight_start(0)

    def token_copy(s):
        slot = lax.rem(s, 2)
        return pltpu.make_async_copy(tokens.at[s], stage.at[slot], in_sems.at[slot])

    token_copy(0).start()
    quarters = ((tokens, tok_q), (teacher, tea_q), (cot, cot_q))
    for i, (source, target) in enumerate(quarters):
        pltpu.make_async_copy(source.at[:, mine, :], target, q_sems.at[i]).start()

    vec_own[...] = jnp.zeros_like(vec_own)
    rows = ((0, part_bo), (1, part_g2), (2, part_b2), (4, part_bd), (5, part_g1), (6, part_b1))
    for i, part in rows:
        vec_own[i : i + 1, own] = part[...].astype(F32).reshape(1, fs)

    def scatter(part, count):
        wide = part.shape[1]
        unit = wide * nf
        column = lax.broadcasted_iota(jnp.int32, (wide, count * unit), 1)
        inside = lax.broadcasted_iota(jnp.int32, (wide, count * unit), 0) + at.f * wide
        spread = (lax.rem(column, unit) == inside).astype(BF)
        full = matmul(part, spread, 1, 0)
        group = lax.broadcasted_iota(jnp.int32, full.shape, 1) // unit
        owner = lax.broadcasted_iota(jnp.int32, full.shape, 0)
        return jnp.sum(jnp.where(group == owner, full, 0.0), axis=0, keepdims=True)

    vec_own[3:4, :] = scatter(part_up[...], part_up.shape[0])
    for i in range(2):
        columns = pl.ds(i * LOCAL, LOCAL)
        vec_own[7:8, columns] = scatter(part_qv[i], part_qv.shape[1])

    def vec_copy(j):
        pair = (v_sems.at[0, j], v_sems.at[1, j])
        return remote(vec_own, vec_got.at[j], pair, at.peers_f[j])

    for j in range(nf - 1):
        vec_copy(j).start()

    valid = mask[...].astype(F32)
    masks = jnp.concatenate([valid, jnp.zeros_like(valid)], axis=0)
    cnt[0] = jnp.broadcast_to(jnp.sum(masks, keepdims=True), (8, 128))

    def count_z(j):
        pair = (cz_sems.at[0, j], cz_sems.at[1, j])
        return remote(cnt.at[0], cnt.at[1 + j], pair, at.peers_z[j])

    def count_f(j):
        pair = (cf_sems.at[0, j], cf_sems.at[1, j])
        return remote(cnt.at[4], cnt.at[5 + j], pair, at.peers_f[j])

    for j in range(3):
        count_z(j).start()

    turned = jnp.transpose(masks)
    segk[...] = jnp.full(segk.shape, -1.0, F32)
    segk[0:4, 1024:3072] = segs[...].astype(F32)
    seg_turned = jnp.transpose(segk[:, aligned(1024 + at.z * GROUP, GROUP)])
    column = lax.broadcasted_iota(jnp.int32, (1, 128), 1)
    for s in range(SEQS):
        lse[s] = jnp.where(column == 4, turned[:, s : s + 1], seg_turned[:, s : s + 1])
    small[...] = jnp.zeros_like(small)
    @pl.when(at.z < 2)
    def _():
        def clear(s, carry):
            kv[s, 0] = jnp.zeros((GROUP, 2 * LOCAL), BF)
            return carry

        lax.fori_loop(0, SEQS, clear, 0)

    @pl.when(at.z < 1)
    def _():
        def clear(s, carry):
            kv[s, 1] = jnp.zeros((GROUP, 2 * LOCAL), BF)
            return carry

        lax.fori_loop(0, SEQS, clear, 0)

    def near_copy(s, half):
        part = pl.ds(half * HALF, HALF)
        pair = (near_sems.at[0, s, half], near_sems.at[1, s, half])
        return remote(kv.at[s, 2, part], kv.at[s, 1, part], pair, at.up)

    def far_copy(s, half):
        part = pl.ds(half * HALF, HALF)
        pair = (far_sems.at[0, s, half], far_sems.at[1, s, half])
        return remote(kv.at[s, 1, part], kv.at[s, 0, part], pair, at.up)

    def near_start(s):
        for half in range(2):
            near_copy(s, half).start()

    def norm_copy(s):
        return pltpu.make_async_copy(act.at[s], n1_h.at[s], n1_sem.at[s])

    def step_norm(s, carry):
        token_copy(s).wait()

        @pl.when(s < 3)
        def _():
            token_copy(s + 1).start()

        for part in range(2):
            here = pl.ds(part * 256, 256)
            xhat, _ = norm_parts(stage[lax.rem(s, 2), here].astype(F32))
            act[s, here] = (xhat * vec[5:6, :] + vec[6:7, :]).astype(BF)
        norm_copy(s).start()
        return carry

    def step_a(s):
        normed = act[s]
        kv[s, 2, :, 0:LOCAL] = matmul(normed, wqkv[1], 1, 0).astype(BF)
        kv[s, 2, :, LOCAL:] = (matmul(normed, wqkv[2], 1, 0) + vec[7:8, 256:512]).astype(BF)

        @pl.when((at.z < 3) & ((at.z == 0) | (s == 0)))
        def _():
            near_start(s)

    for j in range(nf - 1):
        vec_copy(j).wait()
    whole = vec_own[...]
    for j in range(nf - 1):
        whole = whole + vec_got[j]
    vec[...] = whole
    small[7:8, :] = vec[5:6, :]
    lax.fori_loop(0, SEQS, step_norm, 0)
    weight_wait(0)
    for i in (4, 1, 2, 3):
        weight_start(i)
    for i, (source, target) in enumerate(quarters):
        pltpu.make_async_copy(source.at[:, mine, :], target, q_sems.at[i]).wait()

    def step_count(s):
        for j in range(3):
            count_z(j).wait()
        cnt[4] = cnt[0] + cnt[1] + cnt[2] + cnt[3]
        for j in range(nf - 1):
            count_f(j).start()

    def step_counted(s):
        for j in range(nf - 1):
            count_f(j).wait()
        total_count = cnt[4]
        for j in range(nf - 1):
            total_count = total_count + cnt[5 + j]
        small[6:7, 0:128] = total_count[0:1, :]
        cnt[0] = (SEQS * GROUP * nf * 4) / total_count
        for i in range(SEQS):
            norm_copy(i).wait()
        for copy in block_copies(0):
            copy.start()

    def factor():
        return cnt[0, 0:1, 0:1]

    def block_copies(s):
        return (
            pltpu.make_async_copy(teacher.at[s], stage.at[0], in_sems.at[0]),
            pltpu.make_async_copy(cot.at[s], stage.at[1], in_sems.at[1]),
        )

    def kv_out(s):
        return pltpu.make_async_copy(kv.at[s], kv_h.at[s], res_sem.at[s])

    def mix_copy(s):
        return pltpu.make_async_copy(tok_q.at[s], gmix_h.at[s, mine], mix_sem.at[s])

    def ends(k, s):
        if k == 2:
            return tok_q.at[s], gmix_h
        target = (n2, blk)[k]
        return target.at[s, mine], target

    def step_r(k, s):
        summed = ring.total(s)
        if k == 0:
            middle = tok_q[s].astype(F32) + summed + vec[0:1, :]
            mid[s] = middle
            xhat, _ = norm_parts(middle)
            n2[s, mine] = (xhat * vec[1:2, :] + vec[2:3, :]).astype(BF)
        elif k == 1:
            block = mid[s] + summed + vec[4:5, :]
            blk[s, mine] = block.astype(BF)
            difference = block - tea_q[s].astype(F32)
            masked = lse[s, mine, 4:5] * difference
            small[5:6, :] += column_sum(masked * difference)
            grad = cot_q[s].astype(F32) + masked * factor()
            gblk[s] = grad
            small[0:1, :] += column_sum(grad)
        else:
            xhat, inverse = norm_parts(mid[s])
            small[1:2, :] += column_sum(summed * xhat)
            small[2:3, :] += column_sum(summed)
            grad = gblk[s] + norm_back(summed, xhat, inverse, vec[1:2, :])
            gblk[s] = grad
            small[3:4, :] += column_sum(grad)
            tok_q[s] = grad.astype(BF)
            mix_copy(s).start()
        ring.spread(*ends(k, s), s)

    def halo(s):
        for half in range(2):

            @pl.when(at.z > 0)
            def _():
                near_copy(s, half).wait_recv()

            @pl.when((at.z > 0) & (at.z < 3))
            def _():
                far_copy(s, half).start()

        @pl.when((at.z > 0) & (at.z < 3) & (s < 3))
        def _():
            near_start(s + 1)

    def step_p0(s):
        for half in range(2):

            @pl.when(at.z < 3)
            def _():
                near_copy(s, half).wait_send()

            @pl.when((at.z > 0) & (at.z < 3))
            def _():
                far_copy(s, half).wait_send()

            @pl.when(at.z > 1)
            def _():
                far_copy(s, half).wait_recv()

        kv_out(s).start()
        q[s] = ((matmul(act[s], wqkv[0], 1, 0) + vec[7:8, 0:256]) * 0.125).astype(BF)
        lane = lax.broadcasted_iota(jnp.int32, (1, LOCAL), 1) // HD
        slot = lax.broadcasted_iota(jnp.int32, (1, 128), 1)
        keys = kv.at[s].reshape(3 * GROUP, 2 * LOCAL)
        here_segs = segk.at[:, aligned(at.z * GROUP, 3 * GROUP)]
        which = lax.broadcasted_iota(jnp.int32, (8, SPAN), 0) == s

        def block(b, carry):
            start = pl.multiple_of(b * HALF, HALF)
            here = pl.ds(start, HALF)
            span = pl.ds(start, SPAN)
            seg_row = jnp.sum(
                jnp.where(which, here_segs[:, span], 0.0), axis=0, keepdims=True
            )
            columns = lse[s, here]
            bias[...] = allowed_bias(columns[:, 5:6], seg_row)
            query = q[s, here]
            k_block = keys[span, 0:LOCAL]
            v_block = keys[span, LOCAL:]
            mixed = jnp.zeros((HALF, LOCAL), F32)
            logs = columns
            for h in range(LOCAL // HD):
                one = jnp.where(lane == h, query, jnp.zeros_like(query))
                scores = matmul(one, k_block, 1, 1) + bias[...]
                top = jnp.max(scores, axis=-1, keepdims=True)
                weights = jnp.exp(scores - top)
                whole = jnp.sum(weights, axis=-1, keepdims=True)
                part = matmul(weights.astype(BF), v_block, 1, 0) / whole
                mixed = jnp.where(lane == h, part, mixed)
                logs = jnp.where(slot == h, top + jnp.log(whole), logs)
            att[s, here] = mixed.astype(BF)
            lse[s, here] = logs
            return carry

        lax.fori_loop(0, 2, block, 0)
        send[s] = matmul(att[s], wout[...], 1, 0).astype(BF)
        ring.rs_core(s).start()

    def step_p1(s):
        ring.step_u(*ends(0, s), s)

        @pl.when(s == 0)
        def _():
            weight_wait(2)

        for part in range(2):
            here = pl.ds(part * 256, 256)
            h = matmul(n2[s, here], wfc1[...], 1, 0) + vec[3:4, :]
            t = jnp.tanh(0.7978845608028654 * (h + 0.044715 * h * h * h))
            act[s, here] = (0.5 * h * (1.0 + t)).astype(BF)
            slope[s, here] = (
                0.5 * (1.0 + t)
                + 0.5 * h * (1.0 - t * t) * (0.7978845608028654 * (1.0 + 0.134145 * h * h))
            ).astype(BF)

        @pl.when(s == 0)
        def _():
            weight_wait(3)

        send[s] = matmul(act[s], wfc2[...], 1, 0).astype(BF)
        ring.rs_core(s).start()

    def step_p2(s):
        ring.step_u(*ends(1, s), s)
        out = pltpu.make_async_copy(blk.at[s], out_h.at[s], out_sem)
        out.start()
        for copy in block_copies(s):
            copy.wait()
        out.wait()
        for part in range(2):
            here = pl.ds(part * 256, 256)
            difference = blk[s, here].astype(F32) - stage[0, here].astype(F32)
            scaled = lse[s, here, 4:5] * factor()
            down = (stage[1, here].astype(F32) + scaled * difference).astype(BF)
            blk[s, here] = down
            up = matmul(down, wfc2[...], 1, 1) * slope[s, here].astype(F32)
            rounded = up.astype(BF)
            slope[s, here] = rounded
            small[4:5, :] += column_sum(rounded.astype(F32))

        @pl.when(s < 3)
        def _():
            for copy in block_copies(s + 1):
                copy.start()

        send[s] = matmul(slope[s], wfc1[...], 1, 1).astype(BF)
        ring.rs_core(s).start()

    deep = lambda ref: ref.reshape(SEQS * GROUP, 1024)

    def down_out():
        return pltpu.make_async_copy(deep(send).at[0:1024], gfc2, in_sems.at[0])

    def up_out():
        return pltpu.make_async_copy(deep(act).at[0:1024], gfc1, in_sems.at[1])

    def step_gdown(s):
        deep(send)[0:1024, :] = matmul(deep(act)[...], deep(blk)[...], 0, 0).astype(BF)
        down_out().start()

    def step_gup(s):
        deep(act)[0:1024, :] = matmul(deep(n2)[...], deep(slope)[...], 0, 0).astype(BF)
        up_out().start()

    actions = {
        "A": step_a,
        "H": halo,
        "C": step_count,
        "D": step_counted,
        "W": lambda s: weight_wait(s),
        "P0": step_p0,
        "P1": step_p1,
        "P2": step_p2,
        "Q": ring.step_q,
        "gdown": step_gdown,
        "gup": step_gup,
    }
    for k in range(3):
        actions[f"R{k}"] = functools.partial(step_r, k)
        actions[f"T{k}"] = lambda s, k=k: ring.step_t(*ends(k, s), s)
    actions["W"] = lambda s: None
    actions["V"] = lambda s: [weight_wait(i) for i in (4, 1)]
    run_order(actions, FRONT_ORDER)
    last = pltpu.make_async_copy(gblk, gmid_h, out_sem)
    last.start()
    kept = (
        pltpu.make_async_copy(wqkv, wqkv_h, keep_sem.at[0]),
        pltpu.make_async_copy(wout, wout_h, keep_sem.at[1]),
    )
    for copy in kept:
        copy.start()
    for s in range(SEQS):
        ring.step_u(*ends(2, s), s)
        mix_copy(s).wait()
        kv_out(s).wait()
    last.wait()
    down_out().wait()
    up_out().wait()
    for copy in kept:
        copy.wait()


def front_call(nf, *args):
    anys = pl.BlockSpec(memory_space=pl.ANY)
    vmem = pl.BlockSpec(memory_space=pltpu.VMEM)
    dma = pltpu.SemaphoreType.DMA
    big = lambda *lead: pltpu.VMEM((*lead, GROUP, 1024), BF)
    shape = jax.ShapeDtypeStruct
    return pl.pallas_call(
        functools.partial(front_kernel, nf),
        out_shape=(
            shape((SEQS, GROUP, 1024), BF),
            shape((SEQS, GROUP, 1024), BF),
            shape((SEQS, QUARTER, 1024), F32),
            shape((1024, 1024), BF),
            shape((1024, 1024), BF),
            shape((8, 1024), F32),
            shape((SEQS, GROUP, LOCAL), BF),
            shape((SEQS, GROUP, LOCAL), BF),
            shape((SEQS, 3, GROUP, 2 * LOCAL), BF),
            shape((SEQS, GROUP, 128), F32),
            shape((SEQS, GROUP, 1024), BF),
            shape((3, 1024, LOCAL), BF),
            shape((LOCAL, 1024), BF),
        ),
        in_specs=[anys] * 7 + [vmem] * 10,
        out_specs=(anys, anys, anys, anys, anys, vmem, vmem, vmem, anys, vmem, anys, anys, anys),
        scratch_shapes=[
            pltpu.VMEM((3, 1024, LOCAL), BF),
            pltpu.VMEM((LOCAL, 1024), BF),
            pltpu.VMEM((1024, 1024), BF),
            pltpu.VMEM((1024, 1024), BF),
            big(SEQS),
            big(SEQS),
            big(SEQS),
            big(SEQS),
            big(SEQS),
            pltpu.VMEM((SEQS, HALF, 1024), BF),
            pltpu.VMEM((SEQS, QUARTER, 1024), BF),
            pltpu.VMEM((SEQS, QUARTER, 1024), BF),
            pltpu.VMEM((SEQS, QUARTER, 1024), F32),
            pltpu.VMEM((SEQS, QUARTER, 1024), F32),
            pltpu.VMEM((SEQS, QUARTER, 1024), BF),
            pltpu.VMEM((SEQS, QUARTER, 1024), BF),
            pltpu.VMEM((SEQS, QUARTER, 1024), BF),
            big(2),
            pltpu.VMEM((8, 3072), F32),
            pltpu.VMEM((HALF, SPAN), F32),
            pltpu.VMEM((SEQS, 3, GROUP, 2 * LOCAL), BF),
            pltpu.VMEM((4 + nf, 8, 128), F32),
            dma((5, nf - 1)),
            dma((5, nf - 1)),
            dma((5,)),
            dma((5, 2, SEQS)),
            dma((3,)),
            dma((2,)),
            dma((SEQS,)),
            dma,
            dma((SEQS,)),
            dma((2, SEQS, 2)),
            dma((2, SEQS, 2)),
            dma((2, 3)),
            dma((2, nf - 1)),
            dma((SEQS,)),
            dma((2,)),
            pltpu.VMEM((8, 1024), F32),
            pltpu.VMEM((8, 1024), F32),
            pltpu.VMEM((nf - 1, 8, 1024), F32),
            dma((2, nf - 1)),
        ],
        compiler_params=pltpu.CompilerParams(
            collective_id=1, has_side_effects=True, vmem_limit_bytes=63 * 2**20
        ),
        cost_estimate=pl.CostEstimate(
            flops=2 * 2048 * 1024 * 1024 * 9, bytes_accessed=30 * 2**20, transcendentals=0
        ),
        name="front",
    )(*args)


class Reduce:
    def __init__(self, at, cut, size, rows, full, arrived, shard, half, quarter, sems):
        self.at, self.cut, self.size, self.rows = at, cut, size, rows
        self.full, self.arrived, self.shard = full, arrived, shard
        self.half, self.quarter = half, quarter
        self.x_sems, self.z_sems = sems
        self.a, self.b = lax.rem(at.z, 2), at.z // 2
        self.side = (at.f, at.z + 1 - 2 * self.a, at.t)
        self.across = (at.f, lax.rem(at.z + 2, 4), at.t)

    def own(self, f):
        return self.cut(self.full, aligned(f * self.size, self.size, math.gcd(self.size, 128)))

    def part(self, ref, start, size):
        where = aligned(start, size, 16)
        return ref.at[:, where, :] if len(ref.shape) == 3 else ref.at[where, :]

    def x_copy(self, j):
        there = lax.rem(self.at.f + 1 + j, self.at.nf)
        pair = (self.x_sems.at[0, j], self.x_sems.at[1, j])
        return remote(self.own(there), self.arrived.at[j], pair, self.at.peers_f[j])

    def z_copy(self, stage):
        h, q = self.rows // 2, self.rows // 4
        pair = (self.z_sems.at[0, stage], self.z_sems.at[1, stage])
        own = self.own(self.at.f)
        if stage == 0:
            return remote(self.part(own, (1 - self.a) * h, h), self.half, pair, self.side)
        if stage == 1:
            src = self.part(own, self.a * h + (1 - self.b) * q, q)
            return remote(src, self.quarter, pair, self.across)
        if stage == 2:
            kept = self.part(self.shard, self.a * h + self.b * q, q)
            return remote(kept, kept, pair, self.across)
        kept = self.part(self.shard, self.a * h, h)
        return remote(kept, kept, pair, self.side)

    def add(self, target, first, others):
        total = first[...].astype(F32)
        for other in others:
            total = total + other[...].astype(F32)
        target[...] = total.astype(BF)

    def run(self, stage):
        h, q = self.rows // 2, self.rows // 4
        peers = range(self.at.nf - 1)
        own = self.own(self.at.f)
        if stage == 0:
            for j in peers:
                self.x_copy(j).start()
            return
        if stage == 1:
            for j in peers:
                self.x_copy(j).wait()
            self.add(own, own, [self.arrived.at[j] for j in peers])
        else:
            self.z_copy(stage - 2).wait()
        if stage == 2:
            kept = self.part(own, self.a * h, h)
            self.add(kept, kept, [self.half])
        elif stage == 3:
            start = self.a * h + self.b * q
            self.add(self.part(self.shard, start, q), self.part(own, start, q), [self.quarter])
        if stage < 5:
            self.z_copy(stage - 1).start()


BACK_ORDER = (
    ("K0", 0),
    ("E", 0),
    ("E", 1),
    ("K1", 0),
    ("K0", 1),
    ("K0", 2),
    ("I", 0),
    ("E", 2),
    ("K2", 0),
    ("K1", 1),
    ("E", 3),
    ("K0", 3),
    ("K3", 0),
    ("K1", 2),
    ("K2", 1),
    ("I", 1),
    ("B0", 0),
    ("K2", 2),
    ("K3", 1),
    ("K4", 0),
    ("F", 0),
    ("I", 2),
    ("K4", 1),
    ("D1", 0),
    ("I", 3),
    ("F", 1),
    ("D2", 0),
    ("Q", 1),
    ("K1", 3),
    ("Q", 0),
    ("K3", 2),
    ("D1", 1),
    ("B1", 0),
    ("F", 2),
    ("D1", 3),
    ("D1", 2),
    ("K2", 3),
    ("K3", 3),
    ("F", 3),
    ("Q", 2),
    ("D2", 1),
    ("C0", 0),
    ("B2", 0),
    ("R", 0),
    ("D2", 3),
    ("R", 1),
    ("D2", 2),
    ("B3", 0),
    ("Q", 3),
    ("K4", 2),
    ("D1", 4),
    ("K4", 3),
    ("D1", 5),
    ("D3", 0),
    ("D1", 6),
    ("C1", 0),
    ("B4", 0),
    ("D2", 4),
    ("R", 2),
    ("D1", 7),
    ("T", 0),
    ("T", 1),
    ("D3", 3),
    ("D2", 5),
    ("R", 3),
    ("S0", 0),
    ("S1", 0),
    ("D2", 6),
    ("S2", 0),
    ("D3", 2),
    ("C2", 0),
    ("C3", 0),
    ("D3", 6),
    ("T", 3),
    ("D2", 7),
    ("S3", 0),
    ("D3", 5),
    ("C4", 0),
    ("D3", 7),
    ("T", 2),
    ("S4", 0),
    ("D3", 1),
    ("B5", 0),
    ("D3", 4),
    ("S5", 0),
    ("C5", 0),
)


class Chain(Reduce):
    def piece(self, ref, half):
        return self.part(ref, half * (self.rows // 2), self.rows // 2)

    def x_half(self, j, half):
        there = lax.rem(self.at.f + 1 + j, self.at.nf)
        pair = (self.x_sems.at[0, j, half], self.x_sems.at[1, j, half])
        src = self.piece(self.own(there), half)
        return remote(src, self.piece(self.arrived.at[j], half), pair, self.at.peers_f[j])

    def up_copy(self, half):
        pair = (self.z_sems.at[0, half], self.z_sems.at[1, half])
        src = self.piece(self.own(self.at.f), half)
        return remote(src, self.piece(self.shard, half), pair, self.at.up)

    def down_copy(self, half, j):
        q = self.rows // 4
        part = self.part(self.shard, half * (self.rows // 2) + j * q, q)
        which = 2 + half * 2 + j
        pair = (self.z_sems.at[0, which], self.z_sems.at[1, which])
        return remote(part, part, pair, self.at.down)

    def climb(self, stage, half):
        own = self.piece(self.own(self.at.f), half)
        peers = range(self.at.nf - 1)
        if stage == 0:
            for j in peers:
                self.x_half(j, half).start()
            return
        if stage == 1:
            for j in peers:
                self.x_half(j, half).wait()
            self.add(own, own, [self.piece(self.arrived.at[j], half) for j in peers])

        @pl.when(self.at.z == stage - 1)
        def _():
            shard = self.piece(self.shard, half)
            if stage > 1:
                self.up_copy(half).wait_recv()
                self.add(own if stage < 4 else shard, own, [shard])
            if stage < 4:
                self.up_copy(half).start()
            else:
                for j in range(2):
                    self.down_copy(half, j).start()

    def hand_down(self, hop, half, j):
        @pl.when(self.at.z == 3 - hop)
        def _():
            self.down_copy(half, j).wait_recv()
            if hop < 3:
                self.down_copy(half, j).start()

    def finish(self):
        for half in range(2):

            @pl.when(self.at.z < 3)
            def _():
                self.up_copy(half).wait_send()

            @pl.when(self.at.z > 0)
            def _():
                for j in range(2):
                    self.down_copy(half, j).wait_send()


def back_kernel(
    nf,
    gmix_h,
    gmid_h,
    gfc1_h,
    gfc2_h,
    att,
    q,
    kv_h,
    lse,
    n1_h,
    tokens,
    wqkv,
    wout,
    segs,
    sums_one,
    ig_h,
    small,
    s_qkv,
    s_out,
    s_fc1,
    s_fc2,
    gm,
    kvs,
    n1s,
    ga,
    dq,
    dots,
    bias,
    segk,
    dkvt,
    dfar,
    dnear,
    down,
    m1,
    m2,
    gq,
    send,
    recv_c,
    send_y,
    recv_y,
    gmid,
    tok_q,
    a_qkv,
    a_out,
    f_qkv,
    f_fc1,
    f_fc2,
    x_qkv,
    x_out,
    x_fc1,
    x_fc2,
    h_qkv,
    h_out,
    k_qkv,
    k_out,
    ring_sems,
    load_sems,
    first_sems,
    m1_sems,
    m2_sems,
    red_x,
    red_z,
    chain_x,
    chain_z,
    got_core,
    got_y,
    got_f,
    got_z,
    sum_sems,
    sum_f_sems,
    n1e,
):
    at = Place(nf)
    at.barrier()
    ring = Ring(at, send, recv_c, send_y, recv_y, ring_sems)
    mine = aligned(at.mine, QUARTER)
    rows_cut = lambda ref, where: ref.at[where, :]
    cols_cut = lambda ref, where: ref.at[:, where]
    deep_cut = lambda ref, where: ref.at[:, where, :]
    fs = 1024 // nf
    f_out = gm.at[0:LOCAL]

    def reducer(i, cut, rows, full, arrived, shard, half, quarter, kind=Reduce):
        sems = (chain_x.at[i - 2], chain_z.at[i - 2]) if kind is Chain else (red_x.at[i], red_z.at[i])
        return kind(at, cut, fs, rows, full, arrived, shard, half, quarter, sems)

    first, rest = pl.ds(0, 1), pl.ds(1, 2)
    red_q = reducer(
        0, deep_cut, fs, f_qkv.at[first], x_qkv.at[:, first], s_qkv.at[first], h_qkv.at[first], k_qkv.at[first]
    )
    red_kv = reducer(
        4, deep_cut, fs, f_qkv.at[rest], x_qkv.at[:, rest], s_qkv.at[rest], h_qkv.at[rest], k_qkv.at[rest]
    )
    red_out = reducer(1, cols_cut, LOCAL, f_out, x_out, s_out, h_out, k_out)
    red_fc1 = reducer(2, rows_cut, fs, f_fc1, x_fc1, s_fc1, None, None, Chain)
    red_fc2 = reducer(3, cols_cut, 1024, f_fc2, x_fc2, s_fc2, None, None, Chain)

    firsts = (
        (gfc1_h, f_fc1),
        (gfc2_h, f_fc2),
        (gmid_h.at[0], gmid),
        (tokens.at[:, mine, :], tok_q),
    )

    def first_copy_of(i):
        return pltpu.make_async_copy(gfc1_h, f_fc1, first_sems.at[i])

    def first_copy(i):
        return pltpu.make_async_copy(firsts[i][0], firsts[i][1], first_sems.at[i])

    def load_copies(s):
        return (
            pltpu.make_async_copy(gmix_h.at[s], gm, load_sems.at[0, 0]),
            pltpu.make_async_copy(kv_h.at[s], kvs, load_sems.at[1, 0]),
        )

    def norm_load(s):
        return pltpu.make_async_copy(n1_h.at[s], n1s, load_sems.at[2, 0])

    def norm_early(s):
        return pltpu.make_async_copy(n1_h.at[s], n1e, load_sems.at[0, 1])

    def mid_load(s):
        return pltpu.make_async_copy(gmid_h.at[s], gmid, load_sems.at[2, 1])

    for copy in load_copies(0):
        copy.start()
    for i in range(4):
        first_copy(i).start()
    norm_load(0).start()
    norm_early(0).start()

    segk[...] = jnp.full(segk.shape, -1.0, F32)
    segk[0:4, 1024:3072] = segs[...].astype(F32)
    small[...] = jnp.zeros_like(small)
    a_qkv[...] = jnp.zeros_like(a_qkv)
    a_out[...] = jnp.zeros_like(a_out)
    def m1_copy(s):
        return remote(dfar.at[s], m1.at[s], (m1_sems.at[0, s], m1_sems.at[1, s]), at.down)

    def m2_copy(s):
        return remote(dnear.at[s], m2.at[s], (m2_sems.at[0, s], m2_sems.at[1, s]), at.down)

    def step_e(s):
        for copy in load_copies(s):
            copy.wait()

        ga[...] = matmul(gm[...], wout[...], 1, 1).astype(BF)
        lane = lax.broadcasted_iota(jnp.int32, (1, LOCAL), 1) // HD
        keys = kvs.reshape(3 * GROUP, 2 * LOCAL)
        here_segs = segk.at[:, aligned(at.z * GROUP, 3 * GROUP)]
        dkvt[...] = jnp.zeros_like(dkvt)

        def pairs(b, low, size, first):
            here, span = pl.ds(b * HALF, HALF), pl.ds(low, size)
            which = lax.broadcasted_iota(jnp.int32, (8, size), 0) == s
            seg_row = jnp.sum(
                jnp.where(which, here_segs[:, span], 0.0), axis=0, keepdims=True
            )
            logs = lse[s, here]
            bias[:, 0:size] = allowed_bias(logs[:, 5:6], seg_row, low - b * HALF, size)
            query = q[s, here]
            grad = ga[here]
            k_block = keys[span, 0:LOCAL]
            v_block = keys[span, LOCAL:]
            dots[0] = jnp.transpose(query)
            dots[1] = jnp.transpose(grad)
            product = grad.astype(F32) * att[s, here].astype(F32)
            grad_query = jnp.zeros((HALF, LOCAL), F32) if first else dq[here]
            for h in range(LOCAL // HD):
                mine_h = lane == h
                one = jnp.where(mine_h, query, jnp.zeros_like(query))
                grad_one = jnp.where(mine_h, grad, jnp.zeros_like(grad))
                delta = jnp.sum(jnp.where(mine_h, product, 0.0), axis=-1, keepdims=True)
                scores = matmul(one, k_block, 1, 1) + bias[:, 0:size]
                probs = jnp.exp(scores - logs[:, h : h + 1])
                dprobs = matmul(grad_one, v_block, 1, 1)
                grad_scores = (probs * (dprobs - delta)).astype(BF)
                part = matmul(grad_scores, k_block, 1, 0)
                grad_query = jnp.where(mine_h, grad_query + part, grad_query)
                k_rows = pl.ds(h * HD, HD)
                v_rows = pl.ds(LOCAL + h * HD, HD)
                dkvt[k_rows, span] += matmul(dots[0, k_rows], grad_scores, 1, 0)
                dkvt[v_rows, span] += matmul(dots[1, k_rows], probs.astype(BF), 1, 0)
            if first:
                dq[here] = grad_query
            else:
                gq[s, here] = (grad_query * 0.125).astype(BF)

        def turned(i):
            return jnp.transpose(dkvt[:, i * GROUP : (i + 1) * GROUP].astype(BF))

        pairs(0, 0, GROUP, True)
        pairs(1, HALF, HALF, True)
        dfar[s] = turned(0)

        @pl.when(at.z > 1)
        def _():
            m1_copy(s).start()

        pairs(0, GROUP, SPAN - GROUP, False)
        pairs(1, GROUP, SPAN - HALF, False)
        dnear[s] = turned(1)
        down[s] = turned(2)
        a_out[...] += matmul(att[s], gm[...], 0, 0)

        @pl.when(s < 3)
        def _():
            for copy in load_copies(s + 1):
                copy.start()

        norm_early(s).wait()
        a_qkv[0] += matmul(n1e[...], gq[s], 0, 0)

        @pl.when(s < 3)
        def _():
            norm_early(s + 1).start()

    def step_i(s):
        @pl.when((at.z > 0) & (at.z < 3))
        def _():
            m1_copy(s).wait_recv()
            dnear[s] = (dnear[s].astype(F32) + m1[s].astype(F32)).astype(BF)

        @pl.when(at.z > 0)
        def _():
            m2_copy(s).start()

    def step_f(s):
        @pl.when(at.z < 3)
        def _():
            m2_copy(s).wait_recv()
            down[s] = (down[s].astype(F32) + m2[s].astype(F32)).astype(BF)

        norm_load(s).wait()
        grads = (gq[s], down[s, :, 0:LOCAL], down[s, :, LOCAL:])
        send[s] = (
            matmul(grads[0], wqkv[0], 1, 1)
            + matmul(grads[1], wqkv[1], 1, 1)
            + matmul(grads[2], wqkv[2], 1, 1)
        ).astype(BF)
        ring.rs_core(s).start()
        normed = n1s[...]
        for i in (1, 2):
            a_qkv[i] += matmul(normed, grads[i], 0, 0)

        @pl.when(s < 3)
        def _():
            norm_load(s + 1).start()

        small[9:10, 0:LOCAL] += column_sum(grads[0].astype(F32))
        small[9:10, LOCAL : 2 * LOCAL] += column_sum(grads[2].astype(F32))

    def ends(s):
        return tok_q.at[s], ig_h

    def ig_copy(s):
        return pltpu.make_async_copy(tok_q.at[s], ig_h.at[s, mine], first_sems.at[s])

    def step_r(s):
        @pl.when(s == 0)
        def _():
            first_copy(2).wait()
            first_copy(3).wait()

        summed = ring.total(s)
        xhat, inverse = norm_parts(tok_q[s].astype(F32))
        small[0:1, :] += column_sum(summed * xhat)
        small[1:2, :] += column_sum(summed)
        @pl.when(s > 0)
        def _():
            mid_load(s).wait()

        grad = gmid[...] + norm_back(summed, xhat, inverse, sums_one[7:8, :])
        tok_q[s] = grad.astype(BF)

        @pl.when(s < 3)
        def _():
            mid_load(s + 1).start()

        ig_copy(s).start()
        ring.spread(*ends(s), s)

    def sum_copy(stage, j=0):
        pair = (sum_sems.at[0, stage], sum_sems.at[1, stage])
        top = small.at[0:8]
        if stage == 0:
            return remote(top, got_core, pair, at.mate_c)
        if stage == 1:
            return remote(top, got_y, pair, at.mate_y)
        if stage == 2:
            pair = (sum_f_sems.at[0, j], sum_f_sems.at[1, j])
            return remote(small, got_f.at[j], pair, at.peers_f[j])
        mate = red_q.side if stage == 3 else red_q.across
        return remote(small, got_z.at[stage - 3], pair, mate)

    def step_sum(stage, s):
        if stage == 0:
            small[2:6, :] = sums_one[0:4, :]
            small[6:7, :] = sums_one[5:6, :]
            small[8:9, :] = sums_one[4:5, :]
        elif stage == 3:
            for j in range(nf - 1):
                sum_copy(2, j).wait()
            for j in range(nf - 1):
                small[...] += got_f[j]
        else:
            sum_copy(stage - 1).wait()
            if stage == 1:
                small[0:8, :] += got_core[...]
            elif stage == 2:
                small[0:8, :] += got_y[...]
            else:
                small[...] += got_z[stage - 4]
        if stage == 2:
            for j in range(nf - 1):
                sum_copy(2, j).start()
        elif stage < 5:
            sum_copy(stage).start()

    def step_group(group, stage, s):
        if stage == 0:
            if group == "B":
                f_out[...] = a_out[...].astype(BF)
                f_qkv[0] = a_qkv[0].astype(BF)
            elif group == "C":
                for i in (1, 2):
                    f_qkv[i] = a_qkv[i].astype(BF)
        for reduce in groups[group]:
            reduce.run(stage)

    groups = {"B": (red_out, red_q), "C": (red_kv,)}
    chains = (red_fc2, red_fc1)
    actions = {
        "E": step_e,
        "I": step_i,
        "F": step_f,
        "Q": ring.step_q,
        "R": step_r,
        "T": lambda s: ring.step_t(*ends(s), s),
    }
    for stage in range(6):
        actions[f"S{stage}"] = functools.partial(step_sum, stage)
        for group in groups:
            actions[f"{group}{stage}"] = functools.partial(step_group, group, stage)

    def step_climb(stage, s):
        if stage == 0:

            @pl.when(lax.rem(s, 2) == 0)
            def _():
                first_copy_of(1 - s // 2).wait()

        for i, chain in enumerate(chains):

            @pl.when(s // 2 == i)
            def _(chain=chain):
                chain.climb(stage, lax.rem(s, 2))

    def step_down(hop, s):
        for i, chain in enumerate(chains):

            @pl.when(s // 4 == i)
            def _(chain=chain):
                chain.hand_down(hop, lax.rem(s // 2, 2), lax.rem(s, 2))

    for stage in range(5):
        actions[f"K{stage}"] = functools.partial(step_climb, stage)
    for hop in (1, 2, 3):
        actions[f"D{hop}"] = functools.partial(step_down, hop)
    run_order(actions, BACK_ORDER)
    for chain in chains:
        chain.finish()
    for s in range(SEQS):
        ring.step_u(*ends(s), s)
        ig_copy(s).wait()

        @pl.when(at.z > 1)
        def _():
            m1_copy(s).wait_send()

        @pl.when(at.z > 0)
        def _():
            m2_copy(s).wait_send()


def back_call(nf, *args):
    anys = pl.BlockSpec(memory_space=pl.ANY)
    vmem = pl.BlockSpec(memory_space=pltpu.VMEM)
    dma = pltpu.SemaphoreType.DMA
    big = lambda *lead: pltpu.VMEM((*lead, GROUP, 1024), BF)
    shape = jax.ShapeDtypeStruct
    fs = 1024 // nf
    low = lambda *dims: pltpu.VMEM(dims, BF)
    return pl.pallas_call(
        functools.partial(back_kernel, nf),
        out_shape=(
            shape((SEQS, GROUP, 1024), BF),
            shape((16, 1024), F32),
            shape((3, fs, LOCAL), BF),
            shape((LOCAL, fs), BF),
            shape((fs, 1024), BF),
            shape((1024, fs), BF),
        ),
        in_specs=[anys] * 4 + [vmem, vmem, anys, vmem, anys, anys, vmem, vmem, vmem, vmem],
        out_specs=(anys, vmem, vmem, vmem, vmem, vmem),
        scratch_shapes=[
            low(GROUP, 1024),
            low(3, GROUP, 2 * LOCAL),
            low(GROUP, 1024),
            low(GROUP, LOCAL),
            pltpu.VMEM((GROUP, LOCAL), F32),
            low(2, LOCAL, HALF),
            pltpu.VMEM((HALF, SPAN), F32),
            pltpu.VMEM((8, 3072), F32),
            pltpu.VMEM((2 * LOCAL, 3 * GROUP), F32),
            low(SEQS, GROUP, 2 * LOCAL),
            low(SEQS, GROUP, 2 * LOCAL),
            low(SEQS, GROUP, 2 * LOCAL),
            low(SEQS, GROUP, 2 * LOCAL),
            low(SEQS, GROUP, 2 * LOCAL),
            low(SEQS, GROUP, LOCAL),
            big(SEQS),
            low(SEQS, HALF, 1024),
            low(SEQS, QUARTER, 1024),
            low(SEQS, QUARTER, 1024),
            pltpu.VMEM((QUARTER, 1024), F32),
            low(SEQS, QUARTER, 1024),
            pltpu.VMEM((3, 1024, LOCAL), F32),
            pltpu.VMEM((LOCAL, 1024), F32),
            low(3, 1024, LOCAL),
            low(1024, 1024),
            low(1024, 1024),
            low(nf - 1, 3, fs, LOCAL),
            low(nf - 1, LOCAL, fs),
            low(nf - 1, fs, 1024),
            low(nf - 1, 1024, fs),
            low(3, fs // 2, LOCAL),
            low(LOCAL // 2, fs),
            low(3, fs // 4, LOCAL),
            low(LOCAL // 4, fs),
            dma((5, 2, SEQS)),
            dma((3, 2)),
            dma((4,)),
            dma((2, SEQS)),
            dma((2, SEQS)),
            dma((5, 2, nf - 1)),
            dma((5, 2, 4)),
            dma((2, 2, nf - 1, 2)),
            dma((2, 2, 6)),
            pltpu.VMEM((8, 1024), F32),
            pltpu.VMEM((8, 1024), F32),
            pltpu.VMEM((nf - 1, 16, 1024), F32),
            pltpu.VMEM((2, 16, 1024), F32),
            dma((2, 5)),
            dma((2, nf - 1)),
            low(GROUP, 1024),
        ],
        compiler_params=pltpu.CompilerParams(
            collective_id=2, has_side_effects=True, vmem_limit_bytes=63 * 2**20
        ),
        cost_estimate=pl.CostEstimate(
            flops=2 * 2048 * 1024 * 1024 * 6, bytes_accessed=30 * 2**20, transcendentals=0
        ),
        name="back",
    )(*args)


def finish_kernel(
    nf,
    out_in,
    ig_in,
    sums,
    sums_one,
    s_qkv,
    s_out,
    s_fc1,
    s_fc2,
    out,
    loss,
    ig,
    g_g1,
    g_b1,
    g_qkv,
    g_qv,
    g_out,
    g_bo,
    g_g2,
    g_b2,
    g_fc1,
    g_up,
    g_fc2,
    g_bd,
    low,
    wide_qkv,
    wide_out,
    wide_fc1,
    wide_fc2,
    low_qkv,
    low_out,
    low_fc1,
    low_fc2,
    in_sems,
    out_sems,
):
    shards = (
        (s_fc1, low_fc1, wide_fc1, g_fc1),
        (s_fc2, low_fc2, wide_fc2, g_fc2),
        (s_qkv, low_qkv, wide_qkv, g_qkv),
        (s_out, low_out, wide_out, g_out),
    )
    inward, outward = [], []
    for i, (source, kept, widened, target) in enumerate(shards):
        inward.append(pltpu.make_async_copy(source, kept, in_sems.at[i]))
        outward.append(pltpu.make_async_copy(widened, target, out_sems.at[i]))
    for i, (source, target) in enumerate(((out_in, out), (ig_in, ig))):
        for s in range(SEQS):
            which = 4 + i * SEQS + s
            inward.append(
                pltpu.make_async_copy(source.at[s], low.at[i, s], in_sems.at[which])
            )
            outward.append(
                pltpu.make_async_copy(low.at[i, s], target.at[s], out_sems.at[which])
            )
    for copy in inward:
        copy.start()
    for i, (_, kept, widened, _) in enumerate(shards):
        inward[i].wait()
        widened[...] = kept[...].astype(F32)
        outward[i].start()
    for i in range(4, len(inward)):
        inward[i].wait()
        outward[i].start()
    place = lax.axis_index("fsdp")
    fs = g_g1.shape[0]
    here = aligned(place * fs, fs)
    for i, target in enumerate((g_g1, g_b1, g_bd, g_g2, g_b2, g_bo)):
        target[...] = sums[i : i + 1, here].reshape(fs)
    scale = 1.0 / (2.0 * D * sums_one[6:7, 0:1])
    loss[...] = jnp.sum(sums[6:7, :], axis=1, keepdims=True) * scale
    own = sums[8:16, :]
    wide = g_up.shape[1]
    up = pltpu.roll(own, lax.rem(1024 - place * wide, 1024), 1)
    for i in range(g_up.shape[0]):
        g_up[i : i + 1, :] = up[0:1, i * nf * wide : i * nf * wide + wide]
    wide = g_qv.shape[2]
    qv = pltpu.roll(own, lax.rem(1024 - place * wide, 1024), 1)
    for i in range(2):
        for h in range(LOCAL // HD):
            start = i * LOCAL + h * HD
            g_qv[i, h : h + 1, :] = qv[1:2, start : start + wide]
    for copy in outward:
        copy.wait()


def finish_call(nf, *args):
    anys = pl.BlockSpec(memory_space=pl.ANY)
    vmem = pl.BlockSpec(memory_space=pltpu.VMEM)
    shape = jax.ShapeDtypeStruct
    fs = 1024 // nf
    block = shape((SEQS, GROUP, 1024), BF)
    row = shape((fs,), F32)
    return pl.pallas_call(
        functools.partial(finish_kernel, nf),
        out_shape=(
            block,
            shape((1, 1), F32),
            block,
            row,
            row,
            shape((3, fs, LOCAL), F32),
            shape((2, LOCAL // HD, HD // nf), F32),
            shape((LOCAL, fs), F32),
            row,
            row,
            row,
            shape((fs, 1024), F32),
            shape((4, 256 // nf), F32),
            shape((1024, fs), F32),
            row,
        ),
        in_specs=[anys, anys, vmem, vmem] + [anys] * 4,
        out_specs=(anys, vmem, anys, vmem, vmem, anys, vmem, anys)
        + (vmem, vmem, vmem, anys, vmem, anys, vmem),
        scratch_shapes=[
            pltpu.VMEM((2, SEQS, GROUP, 1024), BF),
            pltpu.VMEM((3, fs, LOCAL), F32),
            pltpu.VMEM((LOCAL, fs), F32),
            pltpu.VMEM((fs, 1024), F32),
            pltpu.VMEM((1024, fs), F32),
            pltpu.VMEM((3, fs, LOCAL), BF),
            pltpu.VMEM((LOCAL, fs), BF),
            pltpu.VMEM((fs, 1024), BF),
            pltpu.VMEM((1024, fs), BF),
            pltpu.SemaphoreType.DMA((4 + 2 * SEQS,)),
            pltpu.SemaphoreType.DMA((4 + 2 * SEQS,)),
        ],
        compiler_params=pltpu.CompilerParams(vmem_limit_bytes=63 * 2**20),
        name="finish",
    )(*args)


def local(
    tokens,
    cotangent,
    teacher,
    valid_mask,
    segment_ids,
    ln1_gain,
    ln1_bias,
    w_qkv,
    b_qv,
    w_out,
    b_out,
    ln2_gain,
    ln2_bias,
    w_fc1,
    b_fc1,
    w_fc2,
    b_fc2,
):
    nf = lax.axis_size("fsdp")
    front = front_call(
        nf,
        w_qkv,
        w_out,
        w_fc1,
        w_fc2,
        tokens,
        teacher,
        cotangent,
        b_out,
        ln2_gain,
        ln2_bias,
        b_fc2,
        ln1_gain,
        ln1_bias,
        b_qv,
        b_fc1,
        valid_mask,
        segment_ids,
    )
    (output, grad_mix, grad_middle, gfc1, gfc2, sums_one, att, q, kv, lse, n1, wqkv, wout) = front
    input_grad, everything, s_qkv, s_out, s_fc1, s_fc2 = back_call(
        nf, grad_mix, grad_middle, gfc1, gfc2, att, q, kv, lse, n1, tokens, wqkv, wout, segment_ids, sums_one
    )
    results = finish_call(
        nf, output, input_grad, everything, sums_one, s_qkv, s_out, s_fc1, s_fc2
    )
    return (results[0], results[1].reshape(()), *results[2:])


def solution(mesh):
    return jax.shard_map(
        local,
        mesh=mesh,
        in_specs=(
            P("fsdp", "context", None),
            P("fsdp", "context", None),
            P("fsdp", "context", None),
            P("fsdp", "context"),
            P("fsdp", None),
            P("fsdp"),
            P("fsdp"),
            P(None, "fsdp", "tensor"),
            P(None, "tensor", "fsdp"),
            P("tensor", "fsdp"),
            P("fsdp"),
            P("fsdp"),
            P("fsdp"),
            P("fsdp", "tensor"),
            P("tensor", "fsdp"),
            P("tensor", "fsdp"),
            P("fsdp"),
        ),
        out_specs=(
            P("fsdp", "context", None),
            P(),
            P("fsdp", "context", None),
            P("fsdp"),
            P("fsdp"),
            P(None, "fsdp", "tensor"),
            P(None, "tensor", "fsdp"),
            P("tensor", "fsdp"),
            P("fsdp"),
            P("fsdp"),
            P("fsdp"),
            P("fsdp", "tensor"),
            P("tensor", "fsdp"),
            P("tensor", "fsdp"),
            P("fsdp"),
        ),
        check_vma=False,
    )
```

```python
import functools
import math

import jax
import jax.numpy as jnp
from jax import lax
from jax.experimental import pallas as pl
from jax.experimental.pallas import tpu as pltpu
from jax.sharding import PartitionSpec as P

MESH = pl.DeviceIdType.MESH
BF = jnp.bfloat16
F32 = jnp.float32
D = 1024
HD = 64
WINDOW = 1024
EPSILON = 1e-05
MASKED = -1e30
SEQS = 4
GROUP = 512
QUARTER = 128
HALF = 256
SPAN = 1280
LOCAL = 256


def matmul(left, right, over_left, over_right):
    dims = (((over_left,), (over_right,)), ((), ()))
    return lax.dot_general(left, right, dims, preferred_element_type=F32)


def norm_parts(values):
    mean = jnp.mean(values, axis=-1, keepdims=True)
    center = values - mean
    spread = jnp.mean(center * center, axis=-1, keepdims=True)
    inverse = lax.rsqrt(spread + EPSILON)
    return center * inverse, inverse


def norm_back(grad_normed, xhat, inverse, gain):
    e = grad_normed * gain
    return inverse * (
        e
        - jnp.mean(e, axis=-1, keepdims=True)
        - xhat * jnp.mean(e * xhat, axis=-1, keepdims=True)
    )


def column_sum(values):
    return jnp.sum(values, axis=0, keepdims=True)


def aligned(start, size, unit=128):
    return pl.ds(pl.multiple_of(start, unit), size)


def allowed_bias(query_seg, key_seg, skipped=0, size=SPAN):
    column = lax.broadcasted_iota(jnp.int32, (HALF, size), 1) + skipped
    ahead = column - lax.broadcasted_iota(jnp.int32, (HALF, size), 0)
    allowed = (ahead > 0) & (ahead <= WINDOW) & (query_seg == key_seg)
    return jnp.where(allowed, 0.0, MASKED)


class Place:
    def __init__(self, nf):
        self.nf = nf
        self.f = lax.axis_index("fsdp")
        self.z = lax.axis_index("context")
        self.t = lax.axis_index("tensor")
        self.y, self.c = self.t // 2, lax.rem(self.t, 2)
        self.mate_c = (self.f, self.z, self.t + 1 - 2 * self.c)
        self.mate_y = (self.f, self.z, lax.rem(self.t + 2, 4))
        self.mine = (2 * self.c + self.y) * QUARTER
        self.over_y = (2 * self.c + 1 - self.y) * QUARTER
        self.peers_f = [(lax.rem(self.f + j, nf), self.z, self.t) for j in range(1, nf)]
        self.peers_z = [(self.f, lax.rem(self.z + j, 4), self.t) for j in range(1, 4)]
        self.up = (self.f, lax.rem(self.z + 1, 4), self.t)
        self.down = (self.f, lax.rem(self.z + 3, 4), self.t)

    def barrier(self):
        semaphore = pltpu.get_barrier_semaphore()
        everyone = [self.mate_c, self.mate_y] + self.peers_f + self.peers_z
        for peer in everyone:
            pl.semaphore_signal(semaphore, inc=1, device_id=peer, device_id_type=MESH)
        pl.semaphore_wait(semaphore, len(everyone))


def remote(src, dst, pair, mate):
    return pltpu.make_async_remote_copy(
        src, dst, pair[0], pair[1], device_id=mate, device_id_type=MESH
    )


def run_order(actions, order):
    names = list(actions)
    codes = [names.index(name) * 8 + s for name, s in order]

    def step(i, carry):
        code = jnp.int32(codes[0])
        for j, other in enumerate(codes[1:]):
            code = jnp.where(i == j + 1, other, code)
        kind, s = code // 8, lax.rem(code, 8)
        for j, name in enumerate(names):

            @pl.when(kind == j)
            def _(action=actions[name]):
                action(s)

        return carry

    lax.fori_loop(0, len(order), step, 0)


class Ring:
    def __init__(self, at, send, recv_c, send_y, recv_y, sems):
        self.at, self.send, self.recv_c = at, send, recv_c
        self.send_y, self.recv_y, self.sems = send_y, recv_y, sems

    def pair(self, which, s):
        return self.sems.at[which, 0, s], self.sems.at[which, 1, s]

    def rs_core(self, s):
        half = aligned((1 - self.at.c) * HALF, HALF)
        return remote(self.send.at[s, half], self.recv_c.at[s], self.pair(0, s), self.at.mate_c)

    def rs_y(self, s):
        return remote(self.send_y.at[s], self.recv_y.at[s], self.pair(1, s), self.at.mate_y)

    def back_y(self, src, dst, s):
        return remote(
            src, dst.at[s, aligned(self.at.mine, QUARTER)], self.pair(2, s), self.at.mate_y
        )

    def back_own(self, src, dst, s):
        return remote(
            src, dst.at[s, aligned(self.at.mine, QUARTER)], self.pair(3, s), self.at.mate_c
        )

    def back_over(self, dst, s):
        there = dst.at[s, aligned(self.at.over_y, QUARTER)]
        return remote(there, there, self.pair(4, s), self.at.mate_c)

    def step_q(self, s):
        self.rs_core(s).wait()
        self.send_y[s] = (
            self.send[s, aligned(self.at.over_y, QUARTER)].astype(F32)
            + self.recv_c[s, aligned((1 - self.at.y) * QUARTER, QUARTER)].astype(F32)
        ).astype(BF)
        self.rs_y(s).start()

    def total(self, s):
        self.rs_y(s).wait()
        return (
            self.send[s, aligned(self.at.mine, QUARTER)].astype(F32)
            + self.recv_c[s, aligned(self.at.y * QUARTER, QUARTER)].astype(F32)
            + self.recv_y[s].astype(F32)
        )

    def spread(self, src, dst, s):
        self.back_y(src, dst, s).start()
        self.back_own(src, dst, s).start()

    def step_t(self, src, dst, s):
        self.back_y(src, dst, s).wait()
        self.back_over(dst, s).start()

    def step_u(self, src, dst, s):
        self.back_own(src, dst, s).wait()
        self.back_over(dst, s).wait()


FRONT_ORDER = (
    ("A", 0),
    ("A", 1),
    ("H", 0),
    ("A", 2),
    ("V", 0),
    ("P0", 0),
    ("A", 3),
    ("C", 0),
    ("Q", 0),
    ("H", 1),
    ("R0", 0),
    ("P0", 1),
    ("T0", 0),
    ("H", 2),
    ("Q", 1),
    ("D", 0),
    ("W", 0),
    ("P1", 0),
    ("Q", 0),
    ("R0", 1),
    ("P0", 2),
    ("R1", 0),
    ("T0", 1),
    ("Q", 2),
    ("H", 3),
    ("P1", 1),
    ("Q", 1),
    ("R0", 2),
    ("P0", 3),
    ("R1", 1),
    ("Q", 3),
    ("T0", 2),
    ("P1", 2),
    ("T1", 0),
    ("T1", 1),
    ("Q", 2),
    ("P2", 0),
    ("R0", 3),
    ("P2", 1),
    ("Q", 0),
    ("T0", 3),
    ("R1", 2),
    ("P1", 3),
    ("Q", 3),
    ("T1", 2),
    ("Q", 1),
    ("P2", 2),
    ("R1", 3),
    ("R2", 1),
    ("Q", 2),
    ("T1", 3),
    ("P2", 3),
    ("R2", 0),
    ("Q", 3),
    ("gdown", 0),
    ("T2", 0),
    ("R2", 2),
    ("T2", 1),
    ("gup", 0),
    ("R2", 3),
    ("T2", 2),
)


def front_kernel(
    nf,
    wqkv_s,
    wout_s,
    wfc1_s,
    wfc2_s,
    tokens,
    teacher,
    cot,
    part_bo,
    part_g2,
    part_b2,
    part_bd,
    part_g1,
    part_b1,
    part_qv,
    part_up,
    mask,
    segs,
    out_h,
    gmix_h,
    gmid_h,
    gfc1,
    gfc2,
    small,
    att,
    q,
    kv_h,
    lse,
    n1_h,
    wqkv_h,
    wout_h,
    wqkv,
    wout,
    wfc1,
    wfc2,
    n2,
    blk,
    act,
    slope,
    send,
    recv_c,
    send_y,
    recv_y,
    mid,
    gblk,
    tok_q,
    tea_q,
    cot_q,
    stage,
    segk,
    bias,
    kv,
    cnt,
    w_send,
    w_recv,
    w_loc,
    ring_sems,
    q_sems,
    in_sems,
    n1_sem,
    out_sem,
    mix_sem,
    near_sems,
    far_sems,
    cz_sems,
    cf_sems,
    res_sem,
    keep_sem,
    vec,
    vec_own,
    vec_got,
    v_sems,
):
    at = Place(nf)
    at.barrier()
    ring = Ring(at, send, recv_c, send_y, recv_y, ring_sems)
    mine = aligned(at.mine, QUARTER)

    fs = wout_s.shape[1]
    own = aligned(at.f * fs, fs)
    query, pair_kv = pl.ds(0, 1), pl.ds(1, 2)
    places = (
        (wqkv_s.at[pair_kv], wqkv.at[pair_kv, own, :]),
        (wout_s, wout.at[:, own]),
        (wfc1_s, wfc1.at[own, :]),
        (wfc2_s, wfc2.at[:, own]),
        (wqkv_s.at[query], wqkv.at[query, own, :]),
    )

    def weight_copy(i, j):
        pair = (w_send.at[i, j], w_recv.at[i, j])
        return remote(places[i][0], places[i][1], pair, at.peers_f[j])

    def weight_start(i):
        for j in range(nf - 1):
            weight_copy(i, j).start()
        pltpu.make_async_copy(places[i][0], places[i][1], w_loc.at[i]).start()

    def weight_wait(i):
        pltpu.make_async_copy(places[i][0], places[i][1], w_loc.at[i]).wait()
        for j in range(nf - 1):
            weight_copy(i, j).wait()

    weight_start(0)

    def token_copy(s):
        slot = lax.rem(s, 2)
        return pltpu.make_async_copy(tokens.at[s], stage.at[slot], in_sems.at[slot])

    token_copy(0).start()
    quarters = ((tokens, tok_q), (teacher, tea_q), (cot, cot_q))
    for i, (source, target) in enumerate(quarters):
        pltpu.make_async_copy(source.at[:, mine, :], target, q_sems.at[i]).start()

    vec_own[...] = jnp.zeros_like(vec_own)
    rows = ((0, part_bo), (1, part_g2), (2, part_b2), (4, part_bd), (5, part_g1), (6, part_b1))
    for i, part in rows:
        vec_own[i : i + 1, own] = part[...].astype(F32).reshape(1, fs)

    def scatter(part, count):
        wide = part.shape[1]
        unit = wide * nf
        column = lax.broadcasted_iota(jnp.int32, (wide, count * unit), 1)
        inside = lax.broadcasted_iota(jnp.int32, (wide, count * unit), 0) + at.f * wide
        spread = (lax.rem(column, unit) == inside).astype(BF)
        full = matmul(part, spread, 1, 0)
        group = lax.broadcasted_iota(jnp.int32, full.shape, 1) // unit
        owner = lax.broadcasted_iota(jnp.int32, full.shape, 0)
        return jnp.sum(jnp.where(group == owner, full, 0.0), axis=0, keepdims=True)

    vec_own[3:4, :] = scatter(part_up[...], part_up.shape[0])
    for i in range(2):
        columns = pl.ds(i * LOCAL, LOCAL)
        vec_own[7:8, columns] = scatter(part_qv[i], part_qv.shape[1])

    def vec_copy(j):
        pair = (v_sems.at[0, j], v_sems.at[1, j])
        return remote(vec_own, vec_got.at[j], pair, at.peers_f[j])

    for j in range(nf - 1):
        vec_copy(j).start()

    valid = mask[...].astype(F32)
    masks = jnp.concatenate([valid, jnp.zeros_like(valid)], axis=0)
    cnt[0] = jnp.broadcast_to(jnp.sum(masks, keepdims=True), (8, 128))

    def count_z(j):
        pair = (cz_sems.at[0, j], cz_sems.at[1, j])
        return remote(cnt.at[0], cnt.at[1 + j], pair, at.peers_z[j])

    def count_f(j):
        pair = (cf_sems.at[0, j], cf_sems.at[1, j])
        return remote(cnt.at[4], cnt.at[5 + j], pair, at.peers_f[j])

    for j in range(3):
        count_z(j).start()

    turned = jnp.transpose(masks)
    segk[...] = jnp.full(segk.shape, -1.0, F32)
    segk[0:4, 1024:3072] = segs[...].astype(F32)
    seg_turned = jnp.transpose(segk[:, aligned(1024 + at.z * GROUP, GROUP)])
    column = lax.broadcasted_iota(jnp.int32, (1, 128), 1)
    for s in range(SEQS):
        lse[s] = jnp.where(column == 4, turned[:, s : s + 1], seg_turned[:, s : s + 1])
    small[...] = jnp.zeros_like(small)
    @pl.when(at.z < 2)
    def _():
        def clear(s, carry):
            kv[s, 0] = jnp.zeros((GROUP, 2 * LOCAL), BF)
            return carry

        lax.fori_loop(0, SEQS, clear, 0)

    @pl.when(at.z < 1)
    def _():
        def clear(s, carry):
            kv[s, 1] = jnp.zeros((GROUP, 2 * LOCAL), BF)
            return carry

        lax.fori_loop(0, SEQS, clear, 0)

    def near_copy(s, half):
        part = pl.ds(half * HALF, HALF)
        pair = (near_sems.at[0, s, half], near_sems.at[1, s, half])
        return remote(kv.at[s, 2, part], kv.at[s, 1, part], pair, at.up)

    def far_copy(s, half):
        part = pl.ds(half * HALF, HALF)
        pair = (far_sems.at[0, s, half], far_sems.at[1, s, half])
        return remote(kv.at[s, 1, part], kv.at[s, 0, part], pair, at.up)

    def near_start(s):
        for half in range(2):
            near_copy(s, half).start()

    def norm_copy(s):
        return pltpu.make_async_copy(act.at[s], n1_h.at[s], n1_sem.at[s])

    def step_norm(s, carry):
        token_copy(s).wait()

        @pl.when(s < 3)
        def _():
            token_copy(s + 1).start()

        for part in range(2):
            here = pl.ds(part * 256, 256)
            xhat, _ = norm_parts(stage[lax.rem(s, 2), here].astype(F32))
            act[s, here] = (xhat * vec[5:6, :] + vec[6:7, :]).astype(BF)
        norm_copy(s).start()
        return carry

    def step_a(s):
        normed = act[s]
        kv[s, 2, :, 0:LOCAL] = matmul(normed, wqkv[1], 1, 0).astype(BF)
        kv[s, 2, :, LOCAL:] = (matmul(normed, wqkv[2], 1, 0) + vec[7:8, 256:512]).astype(BF)

        @pl.when((at.z < 3) & ((at.z == 0) | (s == 0)))
        def _():
            near_start(s)

    for j in range(nf - 1):
        vec_copy(j).wait()
    whole = vec_own[...]
    for j in range(nf - 1):
        whole = whole + vec_got[j]
    vec[...] = whole
    small[7:8, :] = vec[5:6, :]
    lax.fori_loop(0, SEQS, step_norm, 0)
    weight_wait(0)
    for i in (4, 1, 2, 3):
        weight_start(i)
    for i, (source, target) in enumerate(quarters):
        pltpu.make_async_copy(source.at[:, mine, :], target, q_sems.at[i]).wait()

    def step_count(s):
        for j in range(3):
            count_z(j).wait()
        cnt[4] = cnt[0] + cnt[1] + cnt[2] + cnt[3]
        for j in range(nf - 1):
            count_f(j).start()

    def step_counted(s):
        for j in range(nf - 1):
            count_f(j).wait()
        total_count = cnt[4]
        for j in range(nf - 1):
            total_count = total_count + cnt[5 + j]
        small[6:7, 0:128] = total_count[0:1, :]
        cnt[0] = (SEQS * GROUP * nf * 4) / total_count
        for i in range(SEQS):
            norm_copy(i).wait()
        for copy in block_copies(0):
            copy.start()

    def factor():
        return cnt[0, 0:1, 0:1]

    def block_copies(s):
        return (
            pltpu.make_async_copy(teacher.at[s], stage.at[0], in_sems.at[0]),
            pltpu.make_async_copy(cot.at[s], stage.at[1], in_sems.at[1]),
        )

    def kv_out(s):
        return pltpu.make_async_copy(kv.at[s], kv_h.at[s], res_sem.at[s])

    def mix_copy(s):
        return pltpu.make_async_copy(tok_q.at[s], gmix_h.at[s, mine], mix_sem.at[s])

    def ends(k, s):
        if k == 2:
            return tok_q.at[s], gmix_h
        target = (n2, blk)[k]
        return target.at[s, mine], target

    def step_r(k, s):
        summed = ring.total(s)
        if k == 0:
            middle = tok_q[s].astype(F32) + summed + vec[0:1, :]
            mid[s] = middle
            xhat, _ = norm_parts(middle)
            n2[s, mine] = (xhat * vec[1:2, :] + vec[2:3, :]).astype(BF)
        elif k == 1:
            block = mid[s] + summed + vec[4:5, :]
            blk[s, mine] = block.astype(BF)
            difference = block - tea_q[s].astype(F32)
            masked = lse[s, mine, 4:5] * difference
            small[5:6, :] += column_sum(masked * difference)
            grad = cot_q[s].astype(F32) + masked * factor()
            gblk[s] = grad
            small[0:1, :] += column_sum(grad)
        else:
            xhat, inverse = norm_parts(mid[s])
            small[1:2, :] += column_sum(summed * xhat)
            small[2:3, :] += column_sum(summed)
            grad = gblk[s] + norm_back(summed, xhat, inverse, vec[1:2, :])
            gblk[s] = grad
            small[3:4, :] += column_sum(grad)
            tok_q[s] = grad.astype(BF)
            mix_copy(s).start()
        if k < 2:
            ring.spread(*ends(k, s), s)
        else:

            @pl.when(s < SEQS - 1)
            def _():
                ring.spread(*ends(k, s), s)


    def halo(s):
        for half in range(2):

            @pl.when(at.z > 0)
            def _():
                near_copy(s, half).wait_recv()

            @pl.when((at.z > 0) & (at.z < 3))
            def _():
                far_copy(s, half).start()

        @pl.when((at.z > 0) & (at.z < 3) & (s < 3))
        def _():
            near_start(s + 1)

    def step_p0(s):
        for half in range(2):

            @pl.when(at.z < 3)
            def _():
                near_copy(s, half).wait_send()

            @pl.when((at.z > 0) & (at.z < 3))
            def _():
                far_copy(s, half).wait_send()

            @pl.when(at.z > 1)
            def _():
                far_copy(s, half).wait_recv()

        kv_out(s).start()
        q[s] = ((matmul(act[s], wqkv[0], 1, 0) + vec[7:8, 0:256]) * 0.125).astype(BF)
        lane = lax.broadcasted_iota(jnp.int32, (1, LOCAL), 1) // HD
        slot = lax.broadcasted_iota(jnp.int32, (1, 128), 1)
        keys = kv.at[s].reshape(3 * GROUP, 2 * LOCAL)
        here_segs = segk.at[:, aligned(at.z * GROUP, 3 * GROUP)]
        which = lax.broadcasted_iota(jnp.int32, (8, SPAN), 0) == s

        def block(b, carry):
            start = pl.multiple_of(b * HALF, HALF)
            here = pl.ds(start, HALF)
            span = pl.ds(start, SPAN)
            seg_row = jnp.sum(
                jnp.where(which, here_segs[:, span], 0.0), axis=0, keepdims=True
            )
            columns = lse[s, here]
            bias[...] = allowed_bias(columns[:, 5:6], seg_row)
            query = q[s, here]
            k_block = keys[span, 0:LOCAL]
            v_block = keys[span, LOCAL:]
            mixed = jnp.zeros((HALF, LOCAL), F32)
            logs = columns
            for h in range(LOCAL // HD):
                one = jnp.where(lane == h, query, jnp.zeros_like(query))
                scores = matmul(one, k_block, 1, 1) + bias[...]
                top = jnp.max(scores, axis=-1, keepdims=True)
                weights = jnp.exp(scores - top)
                whole = jnp.sum(weights, axis=-1, keepdims=True)
                part = matmul(weights.astype(BF), v_block, 1, 0) / whole
                mixed = jnp.where(lane == h, part, mixed)
                logs = jnp.where(slot == h, top + jnp.log(whole), logs)
            att[s, here] = mixed.astype(BF)
            lse[s, here] = logs
            return carry

        lax.fori_loop(0, 2, block, 0)
        send[s] = matmul(att[s], wout[...], 1, 0).astype(BF)
        ring.rs_core(s).start()

    def step_p1(s):
        ring.step_u(*ends(0, s), s)

        @pl.when(s == 0)
        def _():
            weight_wait(2)

        for part in range(2):
            here = pl.ds(part * 256, 256)
            h = matmul(n2[s, here], wfc1[...], 1, 0) + vec[3:4, :]
            t = jnp.tanh(0.7978845608028654 * (h + 0.044715 * h * h * h))
            act[s, here] = (0.5 * h * (1.0 + t)).astype(BF)
            slope[s, here] = (
                0.5 * (1.0 + t)
                + 0.5 * h * (1.0 - t * t) * (0.7978845608028654 * (1.0 + 0.134145 * h * h))
            ).astype(BF)

        @pl.when(s == 0)
        def _():
            weight_wait(3)

        send[s] = matmul(act[s], wfc2[...], 1, 0).astype(BF)
        ring.rs_core(s).start()

    def step_p2(s):
        ring.step_u(*ends(1, s), s)
        out = pltpu.make_async_copy(blk.at[s], out_h.at[s], out_sem)
        out.start()
        for copy in block_copies(s):
            copy.wait()
        out.wait()
        for part in range(2):
            here = pl.ds(part * 256, 256)
            difference = blk[s, here].astype(F32) - stage[0, here].astype(F32)
            scaled = lse[s, here, 4:5] * factor()
            down = (stage[1, here].astype(F32) + scaled * difference).astype(BF)
            blk[s, here] = down
            up = matmul(down, wfc2[...], 1, 1) * slope[s, here].astype(F32)
            rounded = up.astype(BF)
            slope[s, here] = rounded
            small[4:5, :] += column_sum(rounded.astype(F32))

        @pl.when(s < 3)
        def _():
            for copy in block_copies(s + 1):
                copy.start()

        send[s] = matmul(slope[s], wfc1[...], 1, 1).astype(BF)
        ring.rs_core(s).start()

    deep = lambda ref: ref.reshape(SEQS * GROUP, 1024)

    def down_out():
        return pltpu.make_async_copy(deep(send).at[0:1024], gfc2, in_sems.at[0])

    def up_out():
        return pltpu.make_async_copy(deep(act).at[0:1024], gfc1, in_sems.at[1])

    def step_gdown(s):
        deep(send)[0:1024, :] = matmul(deep(act)[...], deep(blk)[...], 0, 0).astype(BF)
        down_out().start()

    def step_gup(s):
        deep(act)[0:1024, :] = matmul(deep(n2)[...], deep(slope)[...], 0, 0).astype(BF)
        up_out().start()

    actions = {
        "A": step_a,
        "H": halo,
        "C": step_count,
        "D": step_counted,
        "W": lambda s: weight_wait(s),
        "P0": step_p0,
        "P1": step_p1,
        "P2": step_p2,
        "Q": ring.step_q,
        "gdown": step_gdown,
        "gup": step_gup,
    }
    for k in range(3):
        actions[f"R{k}"] = functools.partial(step_r, k)
        actions[f"T{k}"] = lambda s, k=k: ring.step_t(*ends(k, s), s)
    actions["W"] = lambda s: None
    actions["V"] = lambda s: [weight_wait(i) for i in (4, 1)]
    run_order(actions, FRONT_ORDER)
    last = pltpu.make_async_copy(gblk, gmid_h, out_sem)
    last.start()
    kept = (
        pltpu.make_async_copy(wqkv, wqkv_h, keep_sem.at[0]),
        pltpu.make_async_copy(wout, wout_h, keep_sem.at[1]),
    )
    for copy in kept:
        copy.start()
    for s in range(SEQS):
        if s < SEQS - 1:
            ring.step_u(*ends(2, s), s)
        mix_copy(s).wait()
        kv_out(s).wait()
    last.wait()
    down_out().wait()
    up_out().wait()
    for copy in kept:
        copy.wait()


def front_call(nf, *args):
    anys = pl.BlockSpec(memory_space=pl.ANY)
    vmem = pl.BlockSpec(memory_space=pltpu.VMEM)
    dma = pltpu.SemaphoreType.DMA
    big = lambda *lead: pltpu.VMEM((*lead, GROUP, 1024), BF)
    shape = jax.ShapeDtypeStruct
    return pl.pallas_call(
        functools.partial(front_kernel, nf),
        out_shape=(
            shape((SEQS, GROUP, 1024), BF),
            shape((SEQS, GROUP, 1024), BF),
            shape((SEQS, QUARTER, 1024), F32),
            shape((1024, 1024), BF),
            shape((1024, 1024), BF),
            shape((8, 1024), F32),
            shape((SEQS, GROUP, LOCAL), BF),
            shape((SEQS, GROUP, LOCAL), BF),
            shape((SEQS, 3, GROUP, 2 * LOCAL), BF),
            shape((SEQS, GROUP, 128), F32),
            shape((SEQS, GROUP, 1024), BF),
            shape((3, 1024, LOCAL), BF),
            shape((LOCAL, 1024), BF),
        ),
        in_specs=[anys] * 7 + [vmem] * 10,
        out_specs=(anys, anys, anys, anys, anys, vmem, vmem, vmem, anys, vmem, anys, anys, anys),
        scratch_shapes=[
            pltpu.VMEM((3, 1024, LOCAL), BF),
            pltpu.VMEM((LOCAL, 1024), BF),
            pltpu.VMEM((1024, 1024), BF),
            pltpu.VMEM((1024, 1024), BF),
            big(SEQS),
            big(SEQS),
            big(SEQS),
            big(SEQS),
            big(SEQS),
            pltpu.VMEM((SEQS, HALF, 1024), BF),
            pltpu.VMEM((SEQS, QUARTER, 1024), BF),
            pltpu.VMEM((SEQS, QUARTER, 1024), BF),
            pltpu.VMEM((SEQS, QUARTER, 1024), F32),
            pltpu.VMEM((SEQS, QUARTER, 1024), F32),
            pltpu.VMEM((SEQS, QUARTER, 1024), BF),
            pltpu.VMEM((SEQS, QUARTER, 1024), BF),
            pltpu.VMEM((SEQS, QUARTER, 1024), BF),
            big(2),
            pltpu.VMEM((8, 3072), F32),
            pltpu.VMEM((HALF, SPAN), F32),
            pltpu.VMEM((SEQS, 3, GROUP, 2 * LOCAL), BF),
            pltpu.VMEM((4 + nf, 8, 128), F32),
            dma((5, nf - 1)),
            dma((5, nf - 1)),
            dma((5,)),
            dma((5, 2, SEQS)),
            dma((3,)),
            dma((2,)),
            dma((SEQS,)),
            dma,
            dma((SEQS,)),
            dma((2, SEQS, 2)),
            dma((2, SEQS, 2)),
            dma((2, 3)),
            dma((2, nf - 1)),
            dma((SEQS,)),
            dma((2,)),
            pltpu.VMEM((8, 1024), F32),
            pltpu.VMEM((8, 1024), F32),
            pltpu.VMEM((nf - 1, 8, 1024), F32),
            dma((2, nf - 1)),
        ],
        compiler_params=pltpu.CompilerParams(
            collective_id=1, has_side_effects=True, vmem_limit_bytes=63 * 2**20
        ),
        cost_estimate=pl.CostEstimate(
            flops=2 * 2048 * 1024 * 1024 * 9, bytes_accessed=30 * 2**20, transcendentals=0
        ),
        name="front",
    )(*args)


class Reduce:
    def __init__(self, at, cut, size, rows, full, arrived, shard, half, quarter, sems):
        self.at, self.cut, self.size, self.rows = at, cut, size, rows
        self.full, self.arrived, self.shard = full, arrived, shard
        self.half, self.quarter = half, quarter
        self.x_sems, self.z_sems = sems
        self.a, self.b = lax.rem(at.z, 2), at.z // 2
        self.side = (at.f, at.z + 1 - 2 * self.a, at.t)
        self.across = (at.f, lax.rem(at.z + 2, 4), at.t)

    def own(self, f):
        return self.cut(self.full, aligned(f * self.size, self.size, math.gcd(self.size, 128)))

    def part(self, ref, start, size):
        where = aligned(start, size, 16)
        return ref.at[:, where, :] if len(ref.shape) == 3 else ref.at[where, :]

    def x_copy(self, j):
        there = lax.rem(self.at.f + 1 + j, self.at.nf)
        pair = (self.x_sems.at[0, j], self.x_sems.at[1, j])
        return remote(self.own(there), self.arrived.at[j], pair, self.at.peers_f[j])

    def z_copy(self, stage):
        h, q = self.rows // 2, self.rows // 4
        pair = (self.z_sems.at[0, stage], self.z_sems.at[1, stage])
        own = self.own(self.at.f)
        if stage == 0:
            return remote(self.part(own, (1 - self.a) * h, h), self.half, pair, self.side)
        if stage == 1:
            src = self.part(own, self.a * h + (1 - self.b) * q, q)
            return remote(src, self.quarter, pair, self.across)
        if stage == 2:
            kept = self.part(self.shard, self.a * h + self.b * q, q)
            return remote(kept, kept, pair, self.across)
        kept = self.part(self.shard, self.a * h, h)
        return remote(kept, kept, pair, self.side)

    def add(self, target, first, others):
        total = first[...].astype(F32)
        for other in others:
            total = total + other[...].astype(F32)
        target[...] = total.astype(BF)

    def run(self, stage):
        h, q = self.rows // 2, self.rows // 4
        peers = range(self.at.nf - 1)
        own = self.own(self.at.f)
        if stage == 0:
            for j in peers:
                self.x_copy(j).start()
            return
        if stage == 1:
            for j in peers:
                self.x_copy(j).wait()
            self.add(own, own, [self.arrived.at[j] for j in peers])
        else:
            self.z_copy(stage - 2).wait()
        if stage == 2:
            kept = self.part(own, self.a * h, h)
            self.add(kept, kept, [self.half])
        elif stage == 3:
            start = self.a * h + self.b * q
            self.add(self.part(self.shard, start, q), self.part(own, start, q), [self.quarter])
        if stage < 5:
            self.z_copy(stage - 1).start()


BACK_ORDER = (
    ("K0", 0),
    ("E", 0),
    ("E", 1),
    ("L", 0),
    ("K1", 0),
    ("K0", 1),
    ("K0", 2),
    ("I", 0),
    ("E", 2),
    ("K2", 0),
    ("K1", 1),
    ("E", 3),
    ("K0", 3),
    ("K3", 0),
    ("K1", 2),
    ("K2", 1),
    ("I", 1),
    ("B0", 0),
    ("K2", 2),
    ("K3", 1),
    ("K4", 0),
    ("F", 0),
    ("I", 2),
    ("K4", 1),
    ("D1", 0),
    ("I", 3),
    ("F", 1),
    ("D2", 0),
    ("Q", 1),
    ("K1", 3),
    ("Q", 0),
    ("K3", 2),
    ("D1", 1),
    ("B1", 0),
    ("F", 2),
    ("D1", 3),
    ("D1", 2),
    ("K2", 3),
    ("K3", 3),
    ("F", 3),
    ("Q", 2),
    ("D2", 1),
    ("C0", 0),
    ("B2", 0),
    ("R", 0),
    ("D2", 3),
    ("R", 1),
    ("D2", 2),
    ("B3", 0),
    ("Q", 3),
    ("K4", 2),
    ("D1", 4),
    ("K4", 3),
    ("D1", 5),
    ("D3", 0),
    ("D1", 6),
    ("C1", 0),
    ("B4", 0),
    ("D2", 4),
    ("R", 2),
    ("D1", 7),
    ("T", 0),
    ("T", 1),
    ("D3", 3),
    ("D2", 5),
    ("R", 3),
    ("S0", 0),
    ("S1", 0),
    ("D2", 6),
    ("S2", 0),
    ("D3", 2),
    ("C2", 0),
    ("C3", 0),
    ("D3", 6),
    ("T", 3),
    ("D2", 7),
    ("S3", 0),
    ("D3", 5),
    ("C4", 0),
    ("D3", 7),
    ("T", 2),
    ("S4", 0),
    ("D3", 1),
    ("B5", 0),
    ("D3", 4),
    ("S5", 0),
    ("C5", 0),
)


class Chain(Reduce):
    def piece(self, ref, half):
        return self.part(ref, half * (self.rows // 2), self.rows // 2)

    def x_half(self, j, half):
        there = lax.rem(self.at.f + 1 + j, self.at.nf)
        pair = (self.x_sems.at[0, j, half], self.x_sems.at[1, j, half])
        src = self.piece(self.own(there), half)
        return remote(src, self.piece(self.arrived.at[j], half), pair, self.at.peers_f[j])

    def up_copy(self, half):
        pair = (self.z_sems.at[0, half], self.z_sems.at[1, half])
        src = self.piece(self.own(self.at.f), half)
        return remote(src, self.piece(self.shard, half), pair, self.at.up)

    def down_copy(self, half, j):
        q = self.rows // 4
        part = self.part(self.shard, half * (self.rows // 2) + j * q, q)
        which = 2 + half * 2 + j
        pair = (self.z_sems.at[0, which], self.z_sems.at[1, which])
        return remote(part, part, pair, self.at.down)

    def climb(self, stage, half):
        own = self.piece(self.own(self.at.f), half)
        peers = range(self.at.nf - 1)
        if stage == 0:
            for j in peers:
                self.x_half(j, half).start()
            return
        if stage == 1:
            for j in peers:
                self.x_half(j, half).wait()
            self.add(own, own, [self.piece(self.arrived.at[j], half) for j in peers])

        @pl.when(self.at.z == stage - 1)
        def _():
            shard = self.piece(self.shard, half)
            if stage > 1:
                self.up_copy(half).wait_recv()
                self.add(own if stage < 4 else shard, own, [shard])
            if stage < 4:
                self.up_copy(half).start()
            else:
                for j in range(2):
                    self.down_copy(half, j).start()

    def hand_down(self, hop, half, j):
        @pl.when(self.at.z == 3 - hop)
        def _():
            self.down_copy(half, j).wait_recv()
            if hop < 3:
                self.down_copy(half, j).start()

    def finish(self):
        for half in range(2):

            @pl.when(self.at.z < 3)
            def _():
                self.up_copy(half).wait_send()

            @pl.when(self.at.z > 0)
            def _():
                for j in range(2):
                    self.down_copy(half, j).wait_send()


def back_kernel(
    nf,
    gmix_h,
    gmid_h,
    gfc1_h,
    gfc2_h,
    att,
    q,
    kv_h,
    lse,
    n1_h,
    tokens,
    wqkv,
    wout,
    segs,
    sums_one,
    ig_h,
    small,
    s_qkv,
    s_out,
    s_fc1,
    s_fc2,
    gm,
    gm_last,
    kvs,
    n1s,
    ga,
    dq,
    dots,
    bias,
    segk,
    dkvt,
    dfar,
    dnear,
    down,
    m1,
    m2,
    gq,
    send,
    recv_c,
    send_y,
    recv_y,
    gmid,
    tok_q,
    a_qkv,
    a_out,
    f_qkv,
    f_fc1,
    f_fc2,
    x_qkv,
    x_out,
    x_fc1,
    x_fc2,
    h_qkv,
    h_out,
    k_qkv,
    k_out,
    ring_sems,
    load_sems,
    last_sem,
    first_sems,
    m1_sems,
    m2_sems,
    red_x,
    red_z,
    chain_x,
    chain_z,
    got_core,
    got_y,
    got_f,
    got_z,
    sum_sems,
    sum_f_sems,
    n1e,
):
    at = Place(nf)
    at.barrier()
    ring = Ring(at, send, recv_c, send_y, recv_y, ring_sems)
    mine = aligned(at.mine, QUARTER)
    rows_cut = lambda ref, where: ref.at[where, :]
    cols_cut = lambda ref, where: ref.at[:, where]
    deep_cut = lambda ref, where: ref.at[:, where, :]
    fs = 1024 // nf
    f_out = gm.at[0:LOCAL]

    def reducer(i, cut, rows, full, arrived, shard, half, quarter, kind=Reduce):
        sems = (chain_x.at[i - 2], chain_z.at[i - 2]) if kind is Chain else (red_x.at[i], red_z.at[i])
        return kind(at, cut, fs, rows, full, arrived, shard, half, quarter, sems)

    first, rest = pl.ds(0, 1), pl.ds(1, 2)
    red_q = reducer(
        0, deep_cut, fs, f_qkv.at[first], x_qkv.at[:, first], s_qkv.at[first], h_qkv.at[first], k_qkv.at[first]
    )
    red_kv = reducer(
        4, deep_cut, fs, f_qkv.at[rest], x_qkv.at[:, rest], s_qkv.at[rest], h_qkv.at[rest], k_qkv.at[rest]
    )
    red_out = reducer(1, cols_cut, LOCAL, f_out, x_out, s_out, h_out, k_out)
    red_fc1 = reducer(2, rows_cut, fs, f_fc1, x_fc1, s_fc1, None, None, Chain)
    red_fc2 = reducer(3, cols_cut, 1024, f_fc2, x_fc2, s_fc2, None, None, Chain)

    firsts = (
        (gfc1_h, f_fc1),
        (gfc2_h, f_fc2),
        (gmid_h.at[0], gmid),
        (tokens.at[:, mine, :], tok_q),
    )

    def first_copy_of(i):
        return pltpu.make_async_copy(gfc1_h, f_fc1, first_sems.at[i])

    def first_copy(i):
        return pltpu.make_async_copy(firsts[i][0], firsts[i][1], first_sems.at[i])

    def mix_load(s):
        return pltpu.make_async_copy(gmix_h.at[s], gm, load_sems.at[0, 0])

    def kv_load(s):
        return pltpu.make_async_copy(kv_h.at[s], kvs, load_sems.at[1, 0])

    last = SEQS - 1
    over = aligned(at.over_y, QUARTER)
    last_own = pltpu.make_async_copy(gmix_h.at[last, mine], gm_last.at[mine], last_sem)
    last_y = remote(gmix_h.at[last, mine], gm_last.at[mine], ring.pair(2, last), at.mate_y)
    last_c = remote(gmix_h.at[last, mine], gm_last.at[mine], ring.pair(3, last), at.mate_c)
    last_over = remote(gm_last.at[over], gm_last.at[over], ring.pair(4, last), at.mate_c)

    def step_last(s):
        last_y.wait()
        last_over.start()

    def norm_load(s):
        return pltpu.make_async_copy(n1_h.at[s], n1s, load_sems.at[2, 0])

    def norm_early(s):
        return pltpu.make_async_copy(n1_h.at[s], n1e, load_sems.at[0, 1])

    def mid_load(s):
        return pltpu.make_async_copy(gmid_h.at[s], gmid, load_sems.at[2, 1])

    mix_load(0).start()
    kv_load(0).start()
    for copy in (last_own, last_y, last_c):
        copy.start()
    for i in range(4):
        first_copy(i).start()
    norm_load(0).start()
    norm_early(0).start()

    segk[...] = jnp.full(segk.shape, -1.0, F32)
    segk[0:4, 1024:3072] = segs[...].astype(F32)
    small[...] = jnp.zeros_like(small)
    a_qkv[...] = jnp.zeros_like(a_qkv)
    a_out[...] = jnp.zeros_like(a_out)
    def m1_copy(s):
        return remote(dfar.at[lax.rem(s, 2)], m1.at[s], (m1_sems.at[0, s], m1_sems.at[1, s]), at.down)

    def m2_copy(s):
        return remote(dnear.at[s], m2.at[s], (m2_sems.at[0, s], m2_sems.at[1, s]), at.down)

    def step_e(s):
        kv_load(s).wait()

        @pl.when(s < last)
        def _():
            mix_load(s).wait()

        @pl.when(s == last)
        def _():
            for copy in (last_own, last_c, last_over):
                copy.wait()
            gm[...] = gm_last[...]

        ga[...] = matmul(gm[...], wout[...], 1, 1).astype(BF)
        lane = lax.broadcasted_iota(jnp.int32, (1, LOCAL), 1) // HD
        keys = kvs.reshape(3 * GROUP, 2 * LOCAL)
        here_segs = segk.at[:, aligned(at.z * GROUP, 3 * GROUP)]
        dkvt[...] = jnp.zeros_like(dkvt)

        def pairs(b, low, size, first):
            here, span = pl.ds(b * HALF, HALF), pl.ds(low, size)
            which = lax.broadcasted_iota(jnp.int32, (8, size), 0) == s
            seg_row = jnp.sum(
                jnp.where(which, here_segs[:, span], 0.0), axis=0, keepdims=True
            )
            logs = lse[s, here]
            bias[:, 0:size] = allowed_bias(logs[:, 5:6], seg_row, low - b * HALF, size)
            query = q[s, here]
            grad = ga[here]
            k_block = keys[span, 0:LOCAL]
            v_block = keys[span, LOCAL:]
            dots[0] = jnp.transpose(query)
            dots[1] = jnp.transpose(grad)
            product = grad.astype(F32) * att[s, here].astype(F32)
            grad_query = jnp.zeros((HALF, LOCAL), F32) if first else dq[here]
            for h in range(LOCAL // HD):
                mine_h = lane == h
                one = jnp.where(mine_h, query, jnp.zeros_like(query))
                grad_one = jnp.where(mine_h, grad, jnp.zeros_like(grad))
                delta = jnp.sum(jnp.where(mine_h, product, 0.0), axis=-1, keepdims=True)
                scores = matmul(one, k_block, 1, 1) + bias[:, 0:size]
                probs = jnp.exp(scores - logs[:, h : h + 1])
                dprobs = matmul(grad_one, v_block, 1, 1)
                grad_scores = (probs * (dprobs - delta)).astype(BF)
                part = matmul(grad_scores, k_block, 1, 0)
                grad_query = jnp.where(mine_h, grad_query + part, grad_query)
                k_rows = pl.ds(h * HD, HD)
                v_rows = pl.ds(LOCAL + h * HD, HD)
                dkvt[k_rows, span] += matmul(dots[0, k_rows], grad_scores, 1, 0)
                dkvt[v_rows, span] += matmul(dots[1, k_rows], probs.astype(BF), 1, 0)
            if first:
                dq[here] = grad_query
            else:
                gq[s, here] = (grad_query * 0.125).astype(BF)

        def turned(i):
            return jnp.transpose(dkvt[:, i * GROUP : (i + 1) * GROUP].astype(BF))

        pairs(0, 0, GROUP, True)
        pairs(1, HALF, HALF, True)

        @pl.when((at.z > 1) & (s > 1))
        def _():
            m1_copy(s - 2).wait_send()

        dfar[lax.rem(s, 2)] = turned(0)

        @pl.when(at.z > 1)
        def _():
            m1_copy(s).start()

        pairs(0, GROUP, SPAN - GROUP, False)
        pairs(1, GROUP, SPAN - HALF, False)
        dnear[s] = turned(1)
        down[s] = turned(2)
        a_out[...] += matmul(att[s], gm[...], 0, 0)

        @pl.when(s < last)
        def _():
            kv_load(s + 1).start()

        @pl.when(s < last - 1)
        def _():
            mix_load(s + 1).start()

        norm_early(s).wait()
        a_qkv[0] += matmul(n1e[...], gq[s], 0, 0)

        @pl.when(s < 3)
        def _():
            norm_early(s + 1).start()

    def step_i(s):
        @pl.when((at.z > 0) & (at.z < 3))
        def _():
            m1_copy(s).wait_recv()
            dnear[s] = (dnear[s].astype(F32) + m1[s].astype(F32)).astype(BF)

        @pl.when(at.z > 0)
        def _():
            m2_copy(s).start()

    def step_f(s):
        @pl.when(at.z < 3)
        def _():
            m2_copy(s).wait_recv()
            down[s] = (down[s].astype(F32) + m2[s].astype(F32)).astype(BF)

        norm_load(s).wait()
        grads = (gq[s], down[s, :, 0:LOCAL], down[s, :, LOCAL:])
        send[s] = (
            matmul(grads[0], wqkv[0], 1, 1)
            + matmul(grads[1], wqkv[1], 1, 1)
            + matmul(grads[2], wqkv[2], 1, 1)
        ).astype(BF)
        ring.rs_core(s).start()
        normed = n1s[...]
        for i in (1, 2):
            a_qkv[i] += matmul(normed, grads[i], 0, 0)

        @pl.when(s < 3)
        def _():
            norm_load(s + 1).start()

        small[9:10, 0:LOCAL] += column_sum(grads[0].astype(F32))
        small[9:10, LOCAL : 2 * LOCAL] += column_sum(grads[2].astype(F32))

    def ends(s):
        return tok_q.at[s], ig_h

    def ig_copy(s):
        return pltpu.make_async_copy(tok_q.at[s], ig_h.at[s, mine], first_sems.at[s])

    def step_r(s):
        @pl.when(s == 0)
        def _():
            first_copy(2).wait()
            first_copy(3).wait()

        summed = ring.total(s)
        xhat, inverse = norm_parts(tok_q[s].astype(F32))
        small[0:1, :] += column_sum(summed * xhat)
        small[1:2, :] += column_sum(summed)
        @pl.when(s > 0)
        def _():
            mid_load(s).wait()

        grad = gmid[...] + norm_back(summed, xhat, inverse, sums_one[7:8, :])
        tok_q[s] = grad.astype(BF)

        @pl.when(s < 3)
        def _():
            mid_load(s + 1).start()

        ig_copy(s).start()
        ring.spread(*ends(s), s)

    def sum_copy(stage, j=0):
        pair = (sum_sems.at[0, stage], sum_sems.at[1, stage])
        top = small.at[0:8]
        if stage == 0:
            return remote(top, got_core, pair, at.mate_c)
        if stage == 1:
            return remote(top, got_y, pair, at.mate_y)
        if stage == 2:
            pair = (sum_f_sems.at[0, j], sum_f_sems.at[1, j])
            return remote(small, got_f.at[j], pair, at.peers_f[j])
        mate = red_q.side if stage == 3 else red_q.across
        return remote(small, got_z.at[stage - 3], pair, mate)

    def step_sum(stage, s):
        if stage == 0:
            small[2:6, :] = sums_one[0:4, :]
            small[6:7, :] = sums_one[5:6, :]
            small[8:9, :] = sums_one[4:5, :]
        elif stage == 3:
            for j in range(nf - 1):
                sum_copy(2, j).wait()
            for j in range(nf - 1):
                small[...] += got_f[j]
        else:
            sum_copy(stage - 1).wait()
            if stage == 1:
                small[0:8, :] += got_core[...]
            elif stage == 2:
                small[0:8, :] += got_y[...]
            else:
                small[...] += got_z[stage - 4]
        if stage == 2:
            for j in range(nf - 1):
                sum_copy(2, j).start()
        elif stage < 5:
            sum_copy(stage).start()

    def step_group(group, stage, s):
        if stage == 0:
            if group == "B":
                f_out[...] = a_out[...].astype(BF)
                f_qkv[0] = a_qkv[0].astype(BF)
            elif group == "C":
                for i in (1, 2):
                    f_qkv[i] = a_qkv[i].astype(BF)
        for reduce in groups[group]:
            reduce.run(stage)

    groups = {"B": (red_out, red_q), "C": (red_kv,)}
    chains = (red_fc2, red_fc1)
    actions = {
        "E": step_e,
        "L": step_last,
        "I": step_i,
        "F": step_f,
        "Q": ring.step_q,
        "R": step_r,
        "T": lambda s: ring.step_t(*ends(s), s),
    }
    for stage in range(6):
        actions[f"S{stage}"] = functools.partial(step_sum, stage)
        for group in groups:
            actions[f"{group}{stage}"] = functools.partial(step_group, group, stage)

    def step_climb(stage, s):
        if stage == 0:

            @pl.when(lax.rem(s, 2) == 0)
            def _():
                first_copy_of(1 - s // 2).wait()

        for i, chain in enumerate(chains):

            @pl.when(s // 2 == i)
            def _(chain=chain):
                chain.climb(stage, lax.rem(s, 2))

    def step_down(hop, s):
        for i, chain in enumerate(chains):

            @pl.when(s // 4 == i)
            def _(chain=chain):
                chain.hand_down(hop, lax.rem(s // 2, 2), lax.rem(s, 2))

    for stage in range(5):
        actions[f"K{stage}"] = functools.partial(step_climb, stage)
    for hop in (1, 2, 3):
        actions[f"D{hop}"] = functools.partial(step_down, hop)
    run_order(actions, BACK_ORDER)
    for chain in chains:
        chain.finish()
    for s in range(SEQS):
        ring.step_u(*ends(s), s)
        ig_copy(s).wait()

        if s > 1:

            @pl.when(at.z > 1)
            def _():
                m1_copy(s).wait_send()

        @pl.when(at.z > 0)
        def _():
            m2_copy(s).wait_send()


def back_call(nf, *args):
    anys = pl.BlockSpec(memory_space=pl.ANY)
    vmem = pl.BlockSpec(memory_space=pltpu.VMEM)
    dma = pltpu.SemaphoreType.DMA
    big = lambda *lead: pltpu.VMEM((*lead, GROUP, 1024), BF)
    shape = jax.ShapeDtypeStruct
    fs = 1024 // nf
    low = lambda *dims: pltpu.VMEM(dims, BF)
    return pl.pallas_call(
        functools.partial(back_kernel, nf),
        out_shape=(
            shape((SEQS, GROUP, 1024), BF),
            shape((16, 1024), F32),
            shape((3, fs, LOCAL), BF),
            shape((LOCAL, fs), BF),
            shape((fs, 1024), BF),
            shape((1024, fs), BF),
        ),
        in_specs=[anys] * 4 + [vmem, vmem, anys, vmem, anys, anys, vmem, vmem, vmem, vmem],
        out_specs=(anys, vmem, vmem, vmem, vmem, vmem),
        scratch_shapes=[
            low(GROUP, 1024),
            low(GROUP, 1024),
            low(3, GROUP, 2 * LOCAL),
            low(GROUP, 1024),
            low(GROUP, LOCAL),
            pltpu.VMEM((GROUP, LOCAL), F32),
            low(2, LOCAL, HALF),
            pltpu.VMEM((HALF, SPAN), F32),
            pltpu.VMEM((8, 3072), F32),
            pltpu.VMEM((2 * LOCAL, 3 * GROUP), F32),
            low(2, GROUP, 2 * LOCAL),
            low(SEQS, GROUP, 2 * LOCAL),
            low(SEQS, GROUP, 2 * LOCAL),
            low(SEQS, GROUP, 2 * LOCAL),
            low(SEQS, GROUP, 2 * LOCAL),
            low(SEQS, GROUP, LOCAL),
            big(SEQS),
            low(SEQS, HALF, 1024),
            low(SEQS, QUARTER, 1024),
            low(SEQS, QUARTER, 1024),
            pltpu.VMEM((QUARTER, 1024), F32),
            low(SEQS, QUARTER, 1024),
            pltpu.VMEM((3, 1024, LOCAL), F32),
            pltpu.VMEM((LOCAL, 1024), F32),
            low(3, 1024, LOCAL),
            low(1024, 1024),
            low(1024, 1024),
            low(nf - 1, 3, fs, LOCAL),
            low(nf - 1, LOCAL, fs),
            low(nf - 1, fs, 1024),
            low(nf - 1, 1024, fs),
            low(3, fs // 2, LOCAL),
            low(LOCAL // 2, fs),
            low(3, fs // 4, LOCAL),
            low(LOCAL // 4, fs),
            dma((5, 2, SEQS)),
            dma((3, 2)),
            dma,
            dma((4,)),
            dma((2, SEQS)),
            dma((2, SEQS)),
            dma((5, 2, nf - 1)),
            dma((5, 2, 4)),
            dma((2, 2, nf - 1, 2)),
            dma((2, 2, 6)),
            pltpu.VMEM((8, 1024), F32),
            pltpu.VMEM((8, 1024), F32),
            pltpu.VMEM((nf - 1, 16, 1024), F32),
            pltpu.VMEM((2, 16, 1024), F32),
            dma((2, 5)),
            dma((2, nf - 1)),
            low(GROUP, 1024),
        ],
        compiler_params=pltpu.CompilerParams(
            collective_id=2, has_side_effects=True, vmem_limit_bytes=63 * 2**20
        ),
        cost_estimate=pl.CostEstimate(
            flops=2 * 2048 * 1024 * 1024 * 6, bytes_accessed=30 * 2**20, transcendentals=0
        ),
        name="back",
    )(*args)


def finish_kernel(
    nf,
    out_in,
    ig_in,
    sums,
    sums_one,
    s_qkv,
    s_out,
    s_fc1,
    s_fc2,
    out,
    loss,
    ig,
    g_g1,
    g_b1,
    g_qkv,
    g_qv,
    g_out,
    g_bo,
    g_g2,
    g_b2,
    g_fc1,
    g_up,
    g_fc2,
    g_bd,
    low,
    wide_qkv,
    wide_out,
    wide_fc1,
    wide_fc2,
    low_qkv,
    low_out,
    low_fc1,
    low_fc2,
    in_sems,
    out_sems,
):
    shards = (
        (s_fc1, low_fc1, wide_fc1, g_fc1),
        (s_fc2, low_fc2, wide_fc2, g_fc2),
        (s_qkv, low_qkv, wide_qkv, g_qkv),
        (s_out, low_out, wide_out, g_out),
    )
    inward, outward = [], []
    for i, (source, kept, widened, target) in enumerate(shards):
        inward.append(pltpu.make_async_copy(source, kept, in_sems.at[i]))
        outward.append(pltpu.make_async_copy(widened, target, out_sems.at[i]))
    for i, (source, target) in enumerate(((out_in, out), (ig_in, ig))):
        for s in range(SEQS):
            which = 4 + i * SEQS + s
            inward.append(
                pltpu.make_async_copy(source.at[s], low.at[i, s], in_sems.at[which])
            )
            outward.append(
                pltpu.make_async_copy(low.at[i, s], target.at[s], out_sems.at[which])
            )
    for copy in inward:
        copy.start()
    for i, (_, kept, widened, _) in enumerate(shards):
        inward[i].wait()
        widened[...] = kept[...].astype(F32)
        outward[i].start()
    for i in range(4, len(inward)):
        inward[i].wait()
        outward[i].start()
    place = lax.axis_index("fsdp")
    fs = g_g1.shape[0]
    here = aligned(place * fs, fs)
    for i, target in enumerate((g_g1, g_b1, g_bd, g_g2, g_b2, g_bo)):
        target[...] = sums[i : i + 1, here].reshape(fs)
    scale = 1.0 / (2.0 * D * sums_one[6:7, 0:1])
    loss[...] = jnp.sum(sums[6:7, :], axis=1, keepdims=True) * scale
    own = sums[8:16, :]
    wide = g_up.shape[1]
    up = pltpu.roll(own, lax.rem(1024 - place * wide, 1024), 1)
    for i in range(g_up.shape[0]):
        g_up[i : i + 1, :] = up[0:1, i * nf * wide : i * nf * wide + wide]
    wide = g_qv.shape[2]
    qv = pltpu.roll(own, lax.rem(1024 - place * wide, 1024), 1)
    for i in range(2):
        for h in range(LOCAL // HD):
            start = i * LOCAL + h * HD
            g_qv[i, h : h + 1, :] = qv[1:2, start : start + wide]
    for copy in outward:
        copy.wait()


def finish_call(nf, *args):
    anys = pl.BlockSpec(memory_space=pl.ANY)
    vmem = pl.BlockSpec(memory_space=pltpu.VMEM)
    shape = jax.ShapeDtypeStruct
    fs = 1024 // nf
    block = shape((SEQS, GROUP, 1024), BF)
    row = shape((fs,), F32)
    return pl.pallas_call(
        functools.partial(finish_kernel, nf),
        out_shape=(
            block,
            shape((1, 1), F32),
            block,
            row,
            row,
            shape((3, fs, LOCAL), F32),
            shape((2, LOCAL // HD, HD // nf), F32),
            shape((LOCAL, fs), F32),
            row,
            row,
            row,
            shape((fs, 1024), F32),
            shape((4, 256 // nf), F32),
            shape((1024, fs), F32),
            row,
        ),
        in_specs=[anys, anys, vmem, vmem] + [anys] * 4,
        out_specs=(anys, vmem, anys, vmem, vmem, anys, vmem, anys)
        + (vmem, vmem, vmem, anys, vmem, anys, vmem),
        scratch_shapes=[
            pltpu.VMEM((2, SEQS, GROUP, 1024), BF),
            pltpu.VMEM((3, fs, LOCAL), F32),
            pltpu.VMEM((LOCAL, fs), F32),
            pltpu.VMEM((fs, 1024), F32),
            pltpu.VMEM((1024, fs), F32),
            pltpu.VMEM((3, fs, LOCAL), BF),
            pltpu.VMEM((LOCAL, fs), BF),
            pltpu.VMEM((fs, 1024), BF),
            pltpu.VMEM((1024, fs), BF),
            pltpu.SemaphoreType.DMA((4 + 2 * SEQS,)),
            pltpu.SemaphoreType.DMA((4 + 2 * SEQS,)),
        ],
        compiler_params=pltpu.CompilerParams(vmem_limit_bytes=63 * 2**20),
        name="finish",
    )(*args)


def local(
    tokens,
    cotangent,
    teacher,
    valid_mask,
    segment_ids,
    ln1_gain,
    ln1_bias,
    w_qkv,
    b_qv,
    w_out,
    b_out,
    ln2_gain,
    ln2_bias,
    w_fc1,
    b_fc1,
    w_fc2,
    b_fc2,
):
    nf = lax.axis_size("fsdp")
    front = front_call(
        nf,
        w_qkv,
        w_out,
        w_fc1,
        w_fc2,
        tokens,
        teacher,
        cotangent,
        b_out,
        ln2_gain,
        ln2_bias,
        b_fc2,
        ln1_gain,
        ln1_bias,
        b_qv,
        b_fc1,
        valid_mask,
        segment_ids,
    )
    (output, grad_mix, grad_middle, gfc1, gfc2, sums_one, att, q, kv, lse, n1, wqkv, wout) = front
    input_grad, everything, s_qkv, s_out, s_fc1, s_fc2 = back_call(
        nf, grad_mix, grad_middle, gfc1, gfc2, att, q, kv, lse, n1, tokens, wqkv, wout, segment_ids, sums_one
    )
    results = finish_call(
        nf, output, input_grad, everything, sums_one, s_qkv, s_out, s_fc1, s_fc2
    )
    return (results[0], results[1].reshape(()), *results[2:])


def solution(mesh):
    return jax.shard_map(
        local,
        mesh=mesh,
        in_specs=(
            P("fsdp", "context", None),
            P("fsdp", "context", None),
            P("fsdp", "context", None),
            P("fsdp", "context"),
            P("fsdp", None),
            P("fsdp"),
            P("fsdp"),
            P(None, "fsdp", "tensor"),
            P(None, "tensor", "fsdp"),
            P("tensor", "fsdp"),
            P("fsdp"),
            P("fsdp"),
            P("fsdp"),
            P("fsdp", "tensor"),
            P("tensor", "fsdp"),
            P("tensor", "fsdp"),
            P("fsdp"),
        ),
        out_specs=(
            P("fsdp", "context", None),
            P(),
            P("fsdp", "context", None),
            P("fsdp"),
            P("fsdp"),
            P(None, "fsdp", "tensor"),
            P(None, "tensor", "fsdp"),
            P("tensor", "fsdp"),
            P("fsdp"),
            P("fsdp"),
            P("fsdp"),
            P("fsdp", "tensor"),
            P("tensor", "fsdp"),
            P("tensor", "fsdp"),
            P("fsdp"),
        ),
        check_vma=False,
    )
```

```python
import functools
import math

import jax
import jax.numpy as jnp
from jax import lax
from jax.experimental import pallas as pl
from jax.experimental.pallas import tpu as pltpu
from jax.sharding import PartitionSpec as P

MESH = pl.DeviceIdType.MESH
BF = jnp.bfloat16
F32 = jnp.float32
D = 1024
HD = 64
WINDOW = 1024
EPSILON = 1e-05
MASKED = -1e30
SEQS = 4
GROUP = 512
QUARTER = 128
HALF = 256
SPAN = 1280
LOCAL = 256


def matmul(left, right, over_left, over_right):
    dims = (((over_left,), (over_right,)), ((), ()))
    return lax.dot_general(left, right, dims, preferred_element_type=F32)


def norm_parts(values):
    mean = jnp.mean(values, axis=-1, keepdims=True)
    center = values - mean
    spread = jnp.mean(center * center, axis=-1, keepdims=True)
    inverse = lax.rsqrt(spread + EPSILON)
    return center * inverse, inverse


def norm_back(grad_normed, xhat, inverse, gain):
    e = grad_normed * gain
    return inverse * (
        e
        - jnp.mean(e, axis=-1, keepdims=True)
        - xhat * jnp.mean(e * xhat, axis=-1, keepdims=True)
    )


def column_sum(values):
    return jnp.sum(values, axis=0, keepdims=True)


def aligned(start, size, unit=128):
    return pl.ds(pl.multiple_of(start, unit), size)


def allowed_bias(query_seg, key_seg, skipped=0, size=SPAN):
    column = lax.broadcasted_iota(jnp.int32, (HALF, size), 1) + skipped
    ahead = column - lax.broadcasted_iota(jnp.int32, (HALF, size), 0)
    allowed = (ahead > 0) & (ahead <= WINDOW) & (query_seg == key_seg)
    return jnp.where(allowed, 0.0, MASKED)


class Place:
    def __init__(self, nf):
        self.nf = nf
        self.f = lax.axis_index("fsdp")
        self.z = lax.axis_index("context")
        self.t = lax.axis_index("tensor")
        self.y, self.c = self.t // 2, lax.rem(self.t, 2)
        self.mate_c = (self.f, self.z, self.t + 1 - 2 * self.c)
        self.mate_y = (self.f, self.z, lax.rem(self.t + 2, 4))
        self.mine = (2 * self.c + self.y) * QUARTER
        self.over_y = (2 * self.c + 1 - self.y) * QUARTER
        self.peers_f = [(lax.rem(self.f + j, nf), self.z, self.t) for j in range(1, nf)]
        self.peers_z = [(self.f, lax.rem(self.z + j, 4), self.t) for j in range(1, 4)]
        self.up = (self.f, lax.rem(self.z + 1, 4), self.t)
        self.down = (self.f, lax.rem(self.z + 3, 4), self.t)

    def barrier(self):
        semaphore = pltpu.get_barrier_semaphore()
        everyone = [self.mate_c, self.mate_y] + self.peers_f + self.peers_z
        for peer in everyone:
            pl.semaphore_signal(semaphore, inc=1, device_id=peer, device_id_type=MESH)
        pl.semaphore_wait(semaphore, len(everyone))


def remote(src, dst, pair, mate):
    return pltpu.make_async_remote_copy(
        src, dst, pair[0], pair[1], device_id=mate, device_id_type=MESH
    )


def run_order(actions, order):
    names = list(actions)
    codes = [names.index(name) * 8 + s for name, s in order]

    def step(i, carry):
        code = jnp.int32(codes[0])
        for j, other in enumerate(codes[1:]):
            code = jnp.where(i == j + 1, other, code)
        kind, s = code // 8, lax.rem(code, 8)
        for j, name in enumerate(names):

            @pl.when(kind == j)
            def _(action=actions[name]):
                action(s)

        return carry

    lax.fori_loop(0, len(order), step, 0)


class Ring:
    def __init__(self, at, send, recv_c, send_y, recv_y, sems):
        self.at, self.send, self.recv_c = at, send, recv_c
        self.send_y, self.recv_y, self.sems = send_y, recv_y, sems

    def pair(self, which, s):
        return self.sems.at[which, 0, s], self.sems.at[which, 1, s]

    def rs_core(self, s):
        half = aligned((1 - self.at.c) * HALF, HALF)
        return remote(self.send.at[s, half], self.recv_c.at[s], self.pair(0, s), self.at.mate_c)

    def rs_y(self, s):
        return remote(self.send_y.at[s], self.recv_y.at[s], self.pair(1, s), self.at.mate_y)

    def back_y(self, src, dst, s):
        return remote(
            src, dst.at[s, aligned(self.at.mine, QUARTER)], self.pair(2, s), self.at.mate_y
        )

    def back_own(self, src, dst, s):
        return remote(
            src, dst.at[s, aligned(self.at.mine, QUARTER)], self.pair(3, s), self.at.mate_c
        )

    def back_over(self, dst, s):
        there = dst.at[s, aligned(self.at.over_y, QUARTER)]
        return remote(there, there, self.pair(4, s), self.at.mate_c)

    def step_q(self, s):
        self.rs_core(s).wait()
        self.send_y[s] = (
            self.send[s, aligned(self.at.over_y, QUARTER)].astype(F32)
            + self.recv_c[s, aligned((1 - self.at.y) * QUARTER, QUARTER)].astype(F32)
        ).astype(BF)
        self.rs_y(s).start()

    def total(self, s):
        self.rs_y(s).wait()
        return (
            self.send[s, aligned(self.at.mine, QUARTER)].astype(F32)
            + self.recv_c[s, aligned(self.at.y * QUARTER, QUARTER)].astype(F32)
            + self.recv_y[s].astype(F32)
        )

    def spread(self, src, dst, s):
        self.back_y(src, dst, s).start()
        self.back_own(src, dst, s).start()

    def step_t(self, src, dst, s):
        self.back_y(src, dst, s).wait()
        self.back_over(dst, s).start()

    def step_u(self, src, dst, s):
        self.back_own(src, dst, s).wait()
        self.back_over(dst, s).wait()


FRONT_ORDER = (
    ("A", 0),
    ("A", 1),
    ("H", 0),
    ("A", 2),
    ("V", 0),
    ("P0", 0),
    ("A", 3),
    ("C", 0),
    ("Q", 0),
    ("H", 1),
    ("R0", 0),
    ("P0", 1),
    ("T0", 0),
    ("H", 2),
    ("Q", 1),
    ("D", 0),
    ("W", 0),
    ("P1", 0),
    ("Q", 0),
    ("R0", 1),
    ("P0", 2),
    ("R1", 0),
    ("T0", 1),
    ("Q", 2),
    ("H", 3),
    ("P1", 1),
    ("Q", 1),
    ("R0", 2),
    ("P0", 3),
    ("R1", 1),
    ("Q", 3),
    ("T0", 2),
    ("P1", 2),
    ("T1", 0),
    ("T1", 1),
    ("Q", 2),
    ("P2", 0),
    ("R0", 3),
    ("P2", 1),
    ("Q", 0),
    ("T0", 3),
    ("R1", 2),
    ("P1", 3),
    ("Q", 3),
    ("T1", 2),
    ("Q", 1),
    ("P2", 2),
    ("R1", 3),
    ("R2", 1),
    ("Q", 2),
    ("T1", 3),
    ("P2", 3),
    ("R2", 0),
    ("Q", 3),
    ("gdown", 0),
    ("T2", 0),
    ("R2", 2),
    ("T2", 1),
    ("gup", 0),
    ("R2", 3),
    ("T2", 2),
)


def front_kernel(
    nf,
    wqkv_s,
    wout_s,
    wfc1_s,
    wfc2_s,
    tokens,
    teacher,
    cot,
    part_bo,
    part_g2,
    part_b2,
    part_bd,
    part_g1,
    part_b1,
    part_qv,
    part_up,
    mask,
    segs,
    out_h,
    gmix_h,
    gmid_h,
    gfc1,
    gfc2,
    small,
    att_h,
    q_h,
    kv_h,
    lse_h,
    n1_h,
    wqkv_h,
    wout_h,
    wqkv,
    wout,
    wfc1,
    wfc2,
    n2,
    blk,
    act,
    slope,
    send,
    recv_c,
    send_y,
    recv_y,
    mid,
    gblk,
    tok_q,
    tea_q,
    cot_q,
    stage,
    segk,
    bias,
    kv,
    cnt,
    w_send,
    w_recv,
    w_loc,
    ring_sems,
    q_sems,
    in_sems,
    n1_sem,
    out_sem,
    mix_sem,
    near_sems,
    far_sems,
    cz_sems,
    cf_sems,
    res_sem,
    keep_sem,
    vec,
    vec_own,
    vec_got,
    v_sems,
    att,
    q,
    lse,
    head_sems,
    mid_sems,
):
    at = Place(nf)
    at.barrier()
    ring = Ring(at, send, recv_c, send_y, recv_y, ring_sems)
    mine = aligned(at.mine, QUARTER)

    fs = wout_s.shape[1]
    own = aligned(at.f * fs, fs)
    query, pair_kv = pl.ds(0, 1), pl.ds(1, 2)
    places = (
        (wqkv_s.at[pair_kv], wqkv.at[pair_kv, own, :]),
        (wout_s, wout.at[:, own]),
        (wfc1_s, wfc1.at[own, :]),
        (wfc2_s, wfc2.at[:, own]),
        (wqkv_s.at[query], wqkv.at[query, own, :]),
    )

    def weight_copy(i, j):
        pair = (w_send.at[i, j], w_recv.at[i, j])
        return remote(places[i][0], places[i][1], pair, at.peers_f[j])

    def weight_start(i):
        for j in range(nf - 1):
            weight_copy(i, j).start()
        pltpu.make_async_copy(places[i][0], places[i][1], w_loc.at[i]).start()

    def weight_wait(i):
        pltpu.make_async_copy(places[i][0], places[i][1], w_loc.at[i]).wait()
        for j in range(nf - 1):
            weight_copy(i, j).wait()

    weight_start(0)

    def token_copy(s):
        slot = lax.rem(s, 2)
        return pltpu.make_async_copy(tokens.at[s], stage.at[slot], in_sems.at[slot])

    token_copy(0).start()
    quarters = ((tokens, tok_q), (teacher, tea_q), (cot, cot_q))
    for i, (source, target) in enumerate(quarters):
        pltpu.make_async_copy(source.at[:, mine, :], target, q_sems.at[i]).start()

    vec_own[...] = jnp.zeros_like(vec_own)
    rows = ((0, part_bo), (1, part_g2), (2, part_b2), (4, part_bd), (5, part_g1), (6, part_b1))
    for i, part in rows:
        vec_own[i : i + 1, own] = part[...].astype(F32).reshape(1, fs)

    def scatter(part, count):
        wide = part.shape[1]
        unit = wide * nf
        column = lax.broadcasted_iota(jnp.int32, (wide, count * unit), 1)
        inside = lax.broadcasted_iota(jnp.int32, (wide, count * unit), 0) + at.f * wide
        spread = (lax.rem(column, unit) == inside).astype(BF)
        full = matmul(part, spread, 1, 0)
        group = lax.broadcasted_iota(jnp.int32, full.shape, 1) // unit
        owner = lax.broadcasted_iota(jnp.int32, full.shape, 0)
        return jnp.sum(jnp.where(group == owner, full, 0.0), axis=0, keepdims=True)

    vec_own[3:4, :] = scatter(part_up[...], part_up.shape[0])
    for i in range(2):
        columns = pl.ds(i * LOCAL, LOCAL)
        vec_own[7:8, columns] = scatter(part_qv[i], part_qv.shape[1])

    def vec_copy(j):
        pair = (v_sems.at[0, j], v_sems.at[1, j])
        return remote(vec_own, vec_got.at[j], pair, at.peers_f[j])

    for j in range(nf - 1):
        vec_copy(j).start()

    valid = mask[...].astype(F32)
    masks = jnp.concatenate([valid, jnp.zeros_like(valid)], axis=0)
    cnt[0] = jnp.broadcast_to(jnp.sum(masks, keepdims=True), (8, 128))

    def count_z(j):
        pair = (cz_sems.at[0, j], cz_sems.at[1, j])
        return remote(cnt.at[0], cnt.at[1 + j], pair, at.peers_z[j])

    def count_f(j):
        pair = (cf_sems.at[0, j], cf_sems.at[1, j])
        return remote(cnt.at[4], cnt.at[5 + j], pair, at.peers_f[j])

    for j in range(3):
        count_z(j).start()

    turned = jnp.transpose(masks)
    segk[...] = jnp.full(segk.shape, -1.0, F32)
    segk[0:4, 1024:3072] = segs[...].astype(F32)
    seg_turned = jnp.transpose(segk[:, aligned(1024 + at.z * GROUP, GROUP)])
    column = lax.broadcasted_iota(jnp.int32, (1, 128), 1)
    for s in range(SEQS):
        lse[s] = jnp.where(column == 4, turned[:, s : s + 1], seg_turned[:, s : s + 1])
    small[...] = jnp.zeros_like(small)
    @pl.when(at.z < 2)
    def _():
        def clear(s, carry):
            kv[s, 0] = jnp.zeros((GROUP, 2 * LOCAL), BF)
            return carry

        lax.fori_loop(0, SEQS, clear, 0)

    @pl.when(at.z < 1)
    def _():
        def clear(s, carry):
            kv[s, 1] = jnp.zeros((GROUP, 2 * LOCAL), BF)
            return carry

        lax.fori_loop(0, SEQS, clear, 0)

    def near_copy(s, half):
        part = pl.ds(half * HALF, HALF)
        pair = (near_sems.at[0, s, half], near_sems.at[1, s, half])
        return remote(kv.at[s, 2, part], kv.at[s, 1, part], pair, at.up)

    def far_copy(s, half):
        part = pl.ds(half * HALF, HALF)
        pair = (far_sems.at[0, s, half], far_sems.at[1, s, half])
        return remote(kv.at[s, 1, part], kv.at[s, 0, part], pair, at.up)

    def near_start(s):
        for half in range(2):
            near_copy(s, half).start()

    def norm_copy(s):
        return pltpu.make_async_copy(act.at[s], n1_h.at[s], n1_sem.at[s])

    def step_norm(s, carry):
        token_copy(s).wait()

        @pl.when(s < 3)
        def _():
            token_copy(s + 1).start()

        for part in range(2):
            here = pl.ds(part * 256, 256)
            xhat, _ = norm_parts(stage[lax.rem(s, 2), here].astype(F32))
            act[s, here] = (xhat * vec[5:6, :] + vec[6:7, :]).astype(BF)
        norm_copy(s).start()
        return carry

    def step_a(s):
        normed = act[s]
        kv[s, 2, :, 0:LOCAL] = matmul(normed, wqkv[1], 1, 0).astype(BF)
        kv[s, 2, :, LOCAL:] = (matmul(normed, wqkv[2], 1, 0) + vec[7:8, 256:512]).astype(BF)

        @pl.when((at.z < 3) & ((at.z == 0) | (s == 0)))
        def _():
            near_start(s)

    for j in range(nf - 1):
        vec_copy(j).wait()
    whole = vec_own[...]
    for j in range(nf - 1):
        whole = whole + vec_got[j]
    vec[...] = whole
    small[7:8, :] = vec[5:6, :]
    lax.fori_loop(0, SEQS, step_norm, 0)
    weight_wait(0)
    for i in (4, 1, 2, 3):
        weight_start(i)
    for i, (source, target) in enumerate(quarters):
        pltpu.make_async_copy(source.at[:, mine, :], target, q_sems.at[i]).wait()

    def step_count(s):
        for j in range(3):
            count_z(j).wait()
        cnt[4] = cnt[0] + cnt[1] + cnt[2] + cnt[3]
        for j in range(nf - 1):
            count_f(j).start()

    def step_counted(s):
        for j in range(nf - 1):
            count_f(j).wait()
        total_count = cnt[4]
        for j in range(nf - 1):
            total_count = total_count + cnt[5 + j]
        small[6:7, 0:128] = total_count[0:1, :]
        cnt[0] = (SEQS * GROUP * nf * 4) / total_count
        for i in range(SEQS):
            norm_copy(i).wait()
        for copy in block_copies(0):
            copy.start()

    def factor():
        return cnt[0, 0:1, 0:1]

    def block_copies(s):
        return (
            pltpu.make_async_copy(teacher.at[s], stage.at[0], in_sems.at[0]),
            pltpu.make_async_copy(cot.at[s], stage.at[1], in_sems.at[1]),
        )

    def kv_out(s):
        return pltpu.make_async_copy(kv.at[s], kv_h.at[s], res_sem.at[s])

    def head_copies(s):
        pairs = ((att, att_h), (q, q_h), (lse, lse_h))
        return [
            pltpu.make_async_copy(source.at[s], target.at[s], head_sems.at[i, s])
            for i, (source, target) in enumerate(pairs)
        ]

    def mid_copy(s):
        return pltpu.make_async_copy(gblk.at[s], gmid_h.at[s], mid_sems.at[s])

    def mix_copy(s):
        return pltpu.make_async_copy(tok_q.at[s], gmix_h.at[s, mine], mix_sem.at[s])

    def ends(k, s):
        if k == 2:
            return tok_q.at[s], gmix_h
        target = (n2, blk)[k]
        return target.at[s, mine], target

    def step_r(k, s):
        summed = ring.total(s)
        if k == 0:
            middle = tok_q[s].astype(F32) + summed + vec[0:1, :]
            mid[s] = middle
            xhat, _ = norm_parts(middle)
            n2[s, mine] = (xhat * vec[1:2, :] + vec[2:3, :]).astype(BF)
        elif k == 1:
            block = mid[s] + summed + vec[4:5, :]
            blk[s, mine] = block.astype(BF)
            difference = block - tea_q[s].astype(F32)
            masked = lse[s, mine, 4:5] * difference
            small[5:6, :] += column_sum(masked * difference)
            grad = cot_q[s].astype(F32) + masked * factor()
            gblk[s] = grad
            small[0:1, :] += column_sum(grad)
        else:
            xhat, inverse = norm_parts(mid[s])
            small[1:2, :] += column_sum(summed * xhat)
            small[2:3, :] += column_sum(summed)
            grad = gblk[s] + norm_back(summed, xhat, inverse, vec[1:2, :])
            gblk[s] = grad
            mid_copy(s).start()
            small[3:4, :] += column_sum(grad)
            tok_q[s] = grad.astype(BF)
            mix_copy(s).start()
        if k < 2:
            ring.spread(*ends(k, s), s)
        else:

            @pl.when(s < SEQS - 1)
            def _():
                ring.spread(*ends(k, s), s)


    def halo(s):
        for half in range(2):

            @pl.when(at.z > 0)
            def _():
                near_copy(s, half).wait_recv()

            @pl.when((at.z > 0) & (at.z < 3))
            def _():
                far_copy(s, half).start()

        @pl.when((at.z > 0) & (at.z < 3) & (s < 3))
        def _():
            near_start(s + 1)

    def step_p0(s):
        for half in range(2):

            @pl.when(at.z < 3)
            def _():
                near_copy(s, half).wait_send()

            @pl.when((at.z > 0) & (at.z < 3))
            def _():
                far_copy(s, half).wait_send()

            @pl.when(at.z > 1)
            def _():
                far_copy(s, half).wait_recv()

        kv_out(s).start()
        q[s] = ((matmul(act[s], wqkv[0], 1, 0) + vec[7:8, 0:256]) * 0.125).astype(BF)
        lane = lax.broadcasted_iota(jnp.int32, (1, LOCAL), 1) // HD
        slot = lax.broadcasted_iota(jnp.int32, (1, 128), 1)
        keys = kv.at[s].reshape(3 * GROUP, 2 * LOCAL)
        here_segs = segk.at[:, aligned(at.z * GROUP, 3 * GROUP)]
        which = lax.broadcasted_iota(jnp.int32, (8, SPAN), 0) == s

        def block(b, carry):
            start = pl.multiple_of(b * HALF, HALF)
            here = pl.ds(start, HALF)
            span = pl.ds(start, SPAN)
            seg_row = jnp.sum(
                jnp.where(which, here_segs[:, span], 0.0), axis=0, keepdims=True
            )
            columns = lse[s, here]
            bias[...] = allowed_bias(columns[:, 5:6], seg_row)
            query = q[s, here]
            k_block = keys[span, 0:LOCAL]
            v_block = keys[span, LOCAL:]
            mixed = jnp.zeros((HALF, LOCAL), F32)
            logs = columns
            for h in range(LOCAL // HD):
                one = jnp.where(lane == h, query, jnp.zeros_like(query))
                scores = matmul(one, k_block, 1, 1) + bias[...]
                top = jnp.max(scores, axis=-1, keepdims=True)
                weights = jnp.exp(scores - top)
                whole = jnp.sum(weights, axis=-1, keepdims=True)
                part = matmul(weights.astype(BF), v_block, 1, 0) / whole
                mixed = jnp.where(lane == h, part, mixed)
                logs = jnp.where(slot == h, top + jnp.log(whole), logs)
            att[s, here] = mixed.astype(BF)
            lse[s, here] = logs
            return carry

        lax.fori_loop(0, 2, block, 0)
        for copy in head_copies(s):
            copy.start()
        send[s] = matmul(att[s], wout[...], 1, 0).astype(BF)
        ring.rs_core(s).start()

    def step_p1(s):
        ring.step_u(*ends(0, s), s)

        @pl.when(s == 0)
        def _():
            weight_wait(2)

        for part in range(2):
            here = pl.ds(part * 256, 256)
            h = matmul(n2[s, here], wfc1[...], 1, 0) + vec[3:4, :]
            t = jnp.tanh(0.7978845608028654 * (h + 0.044715 * h * h * h))
            act[s, here] = (0.5 * h * (1.0 + t)).astype(BF)
            slope[s, here] = (
                0.5 * (1.0 + t)
                + 0.5 * h * (1.0 - t * t) * (0.7978845608028654 * (1.0 + 0.134145 * h * h))
            ).astype(BF)

        @pl.when(s == 0)
        def _():
            weight_wait(3)

        send[s] = matmul(act[s], wfc2[...], 1, 0).astype(BF)
        ring.rs_core(s).start()

    def step_p2(s):
        ring.step_u(*ends(1, s), s)
        out = pltpu.make_async_copy(blk.at[s], out_h.at[s], out_sem)
        out.start()
        for copy in block_copies(s):
            copy.wait()
        out.wait()
        for part in range(2):
            here = pl.ds(part * 256, 256)
            difference = blk[s, here].astype(F32) - stage[0, here].astype(F32)
            scaled = lse[s, here, 4:5] * factor()
            down = (stage[1, here].astype(F32) + scaled * difference).astype(BF)
            blk[s, here] = down
            up = matmul(down, wfc2[...], 1, 1) * slope[s, here].astype(F32)
            rounded = up.astype(BF)
            slope[s, here] = rounded
            small[4:5, :] += column_sum(rounded.astype(F32))

        @pl.when(s < 3)
        def _():
            for copy in block_copies(s + 1):
                copy.start()

        send[s] = matmul(slope[s], wfc1[...], 1, 1).astype(BF)
        ring.rs_core(s).start()

    deep = lambda ref: ref.reshape(SEQS * GROUP, 1024)

    def down_out():
        return pltpu.make_async_copy(deep(send).at[0:1024], gfc2, in_sems.at[0])

    def up_out():
        return pltpu.make_async_copy(deep(act).at[0:1024], gfc1, in_sems.at[1])

    def step_gdown(s):
        deep(send)[0:1024, :] = matmul(deep(act)[...], deep(blk)[...], 0, 0).astype(BF)
        down_out().start()

    def step_gup(s):
        deep(act)[0:1024, :] = matmul(deep(n2)[...], deep(slope)[...], 0, 0).astype(BF)
        up_out().start()

    actions = {
        "A": step_a,
        "H": halo,
        "C": step_count,
        "D": step_counted,
        "W": lambda s: weight_wait(s),
        "P0": step_p0,
        "P1": step_p1,
        "P2": step_p2,
        "Q": ring.step_q,
        "gdown": step_gdown,
        "gup": step_gup,
    }
    for k in range(3):
        actions[f"R{k}"] = functools.partial(step_r, k)
        actions[f"T{k}"] = lambda s, k=k: ring.step_t(*ends(k, s), s)
    kept = (
        pltpu.make_async_copy(wqkv, wqkv_h, keep_sem.at[0]),
        pltpu.make_async_copy(wout, wout_h, keep_sem.at[1]),
    )

    def step_weights(s):
        for i in (4, 1):
            weight_wait(i)
        for copy in kept:
            copy.start()

    actions["W"] = lambda s: None
    actions["V"] = step_weights
    run_order(actions, FRONT_ORDER)
    for s in range(SEQS):
        if s < SEQS - 1:
            ring.step_u(*ends(2, s), s)
        mix_copy(s).wait()
        kv_out(s).wait()
        mid_copy(s).wait()
        for copy in head_copies(s):
            copy.wait()
    down_out().wait()
    up_out().wait()
    for copy in kept:
        copy.wait()


def front_call(nf, *args):
    anys = pl.BlockSpec(memory_space=pl.ANY)
    vmem = pl.BlockSpec(memory_space=pltpu.VMEM)
    dma = pltpu.SemaphoreType.DMA
    big = lambda *lead: pltpu.VMEM((*lead, GROUP, 1024), BF)
    shape = jax.ShapeDtypeStruct
    return pl.pallas_call(
        functools.partial(front_kernel, nf),
        out_shape=(
            shape((SEQS, GROUP, 1024), BF),
            shape((SEQS, GROUP, 1024), BF),
            shape((SEQS, QUARTER, 1024), F32),
            shape((1024, 1024), BF),
            shape((1024, 1024), BF),
            shape((8, 1024), F32),
            shape((SEQS, GROUP, LOCAL), BF),
            shape((SEQS, GROUP, LOCAL), BF),
            shape((SEQS, 3, GROUP, 2 * LOCAL), BF),
            shape((SEQS, GROUP, 128), F32),
            shape((SEQS, GROUP, 1024), BF),
            shape((3, 1024, LOCAL), BF),
            shape((LOCAL, 1024), BF),
        ),
        in_specs=[anys] * 7 + [vmem] * 10,
        out_specs=(anys, anys, anys, anys, anys, vmem, anys, anys, anys, anys, anys, anys, anys),
        scratch_shapes=[
            pltpu.VMEM((3, 1024, LOCAL), BF),
            pltpu.VMEM((LOCAL, 1024), BF),
            pltpu.VMEM((1024, 1024), BF),
            pltpu.VMEM((1024, 1024), BF),
            big(SEQS),
            big(SEQS),
            big(SEQS),
            big(SEQS),
            big(SEQS),
            pltpu.VMEM((SEQS, HALF, 1024), BF),
            pltpu.VMEM((SEQS, QUARTER, 1024), BF),
            pltpu.VMEM((SEQS, QUARTER, 1024), BF),
            pltpu.VMEM((SEQS, QUARTER, 1024), F32),
            pltpu.VMEM((SEQS, QUARTER, 1024), F32),
            pltpu.VMEM((SEQS, QUARTER, 1024), BF),
            pltpu.VMEM((SEQS, QUARTER, 1024), BF),
            pltpu.VMEM((SEQS, QUARTER, 1024), BF),
            big(2),
            pltpu.VMEM((8, 3072), F32),
            pltpu.VMEM((HALF, SPAN), F32),
            pltpu.VMEM((SEQS, 3, GROUP, 2 * LOCAL), BF),
            pltpu.VMEM((4 + nf, 8, 128), F32),
            dma((5, nf - 1)),
            dma((5, nf - 1)),
            dma((5,)),
            dma((5, 2, SEQS)),
            dma((3,)),
            dma((2,)),
            dma((SEQS,)),
            dma,
            dma((SEQS,)),
            dma((2, SEQS, 2)),
            dma((2, SEQS, 2)),
            dma((2, 3)),
            dma((2, nf - 1)),
            dma((SEQS,)),
            dma((2,)),
            pltpu.VMEM((8, 1024), F32),
            pltpu.VMEM((8, 1024), F32),
            pltpu.VMEM((nf - 1, 8, 1024), F32),
            dma((2, nf - 1)),
            pltpu.VMEM((SEQS, GROUP, LOCAL), BF),
            pltpu.VMEM((SEQS, GROUP, LOCAL), BF),
            pltpu.VMEM((SEQS, GROUP, 128), F32),
            dma((3, SEQS)),
            dma((SEQS,)),
        ],
        compiler_params=pltpu.CompilerParams(
            collective_id=1, has_side_effects=True, vmem_limit_bytes=63 * 2**20
        ),
        cost_estimate=pl.CostEstimate(
            flops=2 * 2048 * 1024 * 1024 * 9, bytes_accessed=30 * 2**20, transcendentals=0
        ),
        name="front",
    )(*args)


class Reduce:
    def __init__(self, at, cut, size, rows, full, arrived, shard, half, quarter, sems):
        self.at, self.cut, self.size, self.rows = at, cut, size, rows
        self.full, self.arrived, self.shard = full, arrived, shard
        self.half, self.quarter = half, quarter
        self.x_sems, self.z_sems = sems
        self.a, self.b = lax.rem(at.z, 2), at.z // 2
        self.side = (at.f, at.z + 1 - 2 * self.a, at.t)
        self.across = (at.f, lax.rem(at.z + 2, 4), at.t)

    def own(self, f):
        return self.cut(self.full, aligned(f * self.size, self.size, math.gcd(self.size, 128)))

    def part(self, ref, start, size):
        where = aligned(start, size, 16)
        return ref.at[:, where, :] if len(ref.shape) == 3 else ref.at[where, :]

    def x_copy(self, j):
        there = lax.rem(self.at.f + 1 + j, self.at.nf)
        pair = (self.x_sems.at[0, j], self.x_sems.at[1, j])
        return remote(self.own(there), self.arrived.at[j], pair, self.at.peers_f[j])

    def z_copy(self, stage):
        h, q = self.rows // 2, self.rows // 4
        pair = (self.z_sems.at[0, stage], self.z_sems.at[1, stage])
        own = self.own(self.at.f)
        if stage == 0:
            return remote(self.part(own, (1 - self.a) * h, h), self.half, pair, self.side)
        if stage == 1:
            src = self.part(own, self.a * h + (1 - self.b) * q, q)
            return remote(src, self.quarter, pair, self.across)
        if stage == 2:
            kept = self.part(self.shard, self.a * h + self.b * q, q)
            return remote(kept, kept, pair, self.across)
        kept = self.part(self.shard, self.a * h, h)
        return remote(kept, kept, pair, self.side)

    def add(self, target, first, others):
        total = first[...].astype(F32)
        for other in others:
            total = total + other[...].astype(F32)
        target[...] = total.astype(BF)

    def run(self, stage):
        h, q = self.rows // 2, self.rows // 4
        peers = range(self.at.nf - 1)
        own = self.own(self.at.f)
        if stage == 0:
            for j in peers:
                self.x_copy(j).start()
            return
        if stage == 1:
            for j in peers:
                self.x_copy(j).wait()
            self.add(own, own, [self.arrived.at[j] for j in peers])
        else:
            self.z_copy(stage - 2).wait()
        if stage == 2:
            kept = self.part(own, self.a * h, h)
            self.add(kept, kept, [self.half])
        elif stage == 3:
            start = self.a * h + self.b * q
            self.add(self.part(self.shard, start, q), self.part(own, start, q), [self.quarter])
        if stage < 5:
            self.z_copy(stage - 1).start()


BACK_ORDER = (
    ("K0", 0),
    ("E", 0),
    ("E", 1),
    ("L", 0),
    ("K1", 0),
    ("K0", 1),
    ("K0", 2),
    ("I", 0),
    ("E", 2),
    ("K2", 0),
    ("K1", 1),
    ("E", 3),
    ("K0", 3),
    ("K3", 0),
    ("K1", 2),
    ("K2", 1),
    ("I", 1),
    ("B0", 0),
    ("K2", 2),
    ("K3", 1),
    ("K4", 0),
    ("F", 0),
    ("I", 2),
    ("K4", 1),
    ("D1", 0),
    ("I", 3),
    ("F", 1),
    ("D2", 0),
    ("Q", 1),
    ("K1", 3),
    ("Q", 0),
    ("K3", 2),
    ("D1", 1),
    ("B1", 0),
    ("F", 2),
    ("D1", 3),
    ("D1", 2),
    ("K2", 3),
    ("K3", 3),
    ("F", 3),
    ("Q", 2),
    ("D2", 1),
    ("C0", 0),
    ("B2", 0),
    ("R", 0),
    ("D2", 3),
    ("R", 1),
    ("D2", 2),
    ("B3", 0),
    ("Q", 3),
    ("K4", 2),
    ("D1", 4),
    ("K4", 3),
    ("D1", 5),
    ("D3", 0),
    ("D1", 6),
    ("C1", 0),
    ("B4", 0),
    ("D2", 4),
    ("R", 2),
    ("D1", 7),
    ("T", 0),
    ("T", 1),
    ("D3", 3),
    ("D2", 5),
    ("R", 3),
    ("S0", 0),
    ("S1", 0),
    ("D2", 6),
    ("S2", 0),
    ("D3", 2),
    ("C2", 0),
    ("C3", 0),
    ("D3", 6),
    ("T", 3),
    ("D2", 7),
    ("S3", 0),
    ("D3", 5),
    ("C4", 0),
    ("D3", 7),
    ("T", 2),
    ("S4", 0),
    ("D3", 1),
    ("B5", 0),
    ("D3", 4),
    ("S5", 0),
    ("C5", 0),
)


class Chain(Reduce):
    def piece(self, ref, half):
        return self.part(ref, half * (self.rows // 2), self.rows // 2)

    def x_half(self, j, half):
        there = lax.rem(self.at.f + 1 + j, self.at.nf)
        pair = (self.x_sems.at[0, j, half], self.x_sems.at[1, j, half])
        src = self.piece(self.own(there), half)
        return remote(src, self.piece(self.arrived.at[j], half), pair, self.at.peers_f[j])

    def up_copy(self, half):
        pair = (self.z_sems.at[0, half], self.z_sems.at[1, half])
        src = self.piece(self.own(self.at.f), half)
        return remote(src, self.piece(self.shard, half), pair, self.at.up)

    def down_copy(self, half, j):
        q = self.rows // 4
        part = self.part(self.shard, half * (self.rows // 2) + j * q, q)
        which = 2 + half * 2 + j
        pair = (self.z_sems.at[0, which], self.z_sems.at[1, which])
        return remote(part, part, pair, self.at.down)

    def climb(self, stage, half):
        own = self.piece(self.own(self.at.f), half)
        peers = range(self.at.nf - 1)
        if stage == 0:
            for j in peers:
                self.x_half(j, half).start()
            return
        if stage == 1:
            for j in peers:
                self.x_half(j, half).wait()
            self.add(own, own, [self.piece(self.arrived.at[j], half) for j in peers])

        @pl.when(self.at.z == stage - 1)
        def _():
            shard = self.piece(self.shard, half)
            if stage > 1:
                self.up_copy(half).wait_recv()
                self.add(own if stage < 4 else shard, own, [shard])
            if stage < 4:
                self.up_copy(half).start()
            else:
                for j in range(2):
                    self.down_copy(half, j).start()

    def hand_down(self, hop, half, j):
        @pl.when(self.at.z == 3 - hop)
        def _():
            self.down_copy(half, j).wait_recv()
            if hop < 3:
                self.down_copy(half, j).start()

    def finish(self):
        for half in range(2):

            @pl.when(self.at.z < 3)
            def _():
                self.up_copy(half).wait_send()

            @pl.when(self.at.z > 0)
            def _():
                for j in range(2):
                    self.down_copy(half, j).wait_send()


def back_kernel(
    nf,
    gmix_h,
    gmid_h,
    gfc1_h,
    gfc2_h,
    att_h,
    q_h,
    kv_h,
    lse_h,
    n1_h,
    tokens,
    wqkv_h,
    wout,
    segs,
    sums_one,
    ig_h,
    small,
    s_qkv,
    s_out,
    s_fc1,
    s_fc2,
    gm,
    gm_last,
    kvs,
    n1s,
    ga,
    dq,
    dots,
    bias,
    segk,
    dkvt,
    dfar,
    dnear,
    down,
    m1,
    m2,
    gq,
    send,
    recv_c,
    send_y,
    recv_y,
    gmid,
    tok_q,
    a_qkv,
    a_out,
    f_qkv,
    f_fc1,
    f_fc2,
    x_qkv,
    x_out,
    x_fc1,
    x_fc2,
    h_qkv,
    h_out,
    k_qkv,
    k_out,
    ring_sems,
    load_sems,
    last_sem,
    first_sems,
    m1_sems,
    m2_sems,
    red_x,
    red_z,
    chain_x,
    chain_z,
    got_core,
    got_y,
    got_f,
    got_z,
    sum_sems,
    sum_f_sems,
    n1e,
    att,
    q,
    lse,
    wqkv,
    head_sems,
    w_sem,
):
    at = Place(nf)
    ring = Ring(at, send, recv_c, send_y, recv_y, ring_sems)
    mine = aligned(at.mine, QUARTER)
    rows_cut = lambda ref, where: ref.at[where, :]
    cols_cut = lambda ref, where: ref.at[:, where]
    deep_cut = lambda ref, where: ref.at[:, where, :]
    fs = 1024 // nf
    f_out = gm.at[0:LOCAL]

    def reducer(i, cut, rows, full, arrived, shard, half, quarter, kind=Reduce):
        sems = (chain_x.at[i - 2], chain_z.at[i - 2]) if kind is Chain else (red_x.at[i], red_z.at[i])
        return kind(at, cut, fs, rows, full, arrived, shard, half, quarter, sems)

    first, rest = pl.ds(0, 1), pl.ds(1, 2)
    red_q = reducer(
        0, deep_cut, fs, f_qkv.at[first], x_qkv.at[:, first], s_qkv.at[first], h_qkv.at[first], k_qkv.at[first]
    )
    red_kv = reducer(
        4, deep_cut, fs, f_qkv.at[rest], x_qkv.at[:, rest], s_qkv.at[rest], h_qkv.at[rest], k_qkv.at[rest]
    )
    red_out = reducer(1, cols_cut, LOCAL, f_out, x_out, s_out, h_out, k_out)
    red_fc1 = reducer(2, rows_cut, fs, f_fc1, x_fc1, s_fc1, None, None, Chain)
    red_fc2 = reducer(3, cols_cut, 1024, f_fc2, x_fc2, s_fc2, None, None, Chain)

    firsts = (
        (gfc1_h, f_fc1),
        (gfc2_h, f_fc2),
        (gmid_h.at[0], gmid),
        (tokens.at[:, mine, :], tok_q),
    )

    def first_copy_of(i):
        return pltpu.make_async_copy(gfc1_h, f_fc1, first_sems.at[i])

    def first_copy(i):
        return pltpu.make_async_copy(firsts[i][0], firsts[i][1], first_sems.at[i])

    def mix_load(s):
        return pltpu.make_async_copy(gmix_h.at[s], gm, load_sems.at[0, 0])

    def kv_load(s):
        return pltpu.make_async_copy(kv_h.at[s], kvs, load_sems.at[1, 0])

    last = SEQS - 1
    over = aligned(at.over_y, QUARTER)
    last_own = pltpu.make_async_copy(gmix_h.at[last, mine], gm_last.at[mine], last_sem)
    last_y = remote(gmix_h.at[last, mine], gm_last.at[mine], ring.pair(2, last), at.mate_y)
    last_c = remote(gmix_h.at[last, mine], gm_last.at[mine], ring.pair(3, last), at.mate_c)
    last_over = remote(gm_last.at[over], gm_last.at[over], ring.pair(4, last), at.mate_c)

    def step_last(s):
        last_y.wait()
        last_over.start()

    def norm_load(s):
        return pltpu.make_async_copy(n1_h.at[s], n1s, load_sems.at[2, 0])

    def norm_early(s):
        return pltpu.make_async_copy(n1_h.at[s], n1e, load_sems.at[0, 1])

    def mid_load(s):
        return pltpu.make_async_copy(gmid_h.at[s], gmid, load_sems.at[2, 1])

    def head_loads(s):
        pairs = ((att_h, att), (q_h, q), (lse_h, lse))
        return [
            pltpu.make_async_copy(source.at[s], target.at[s], head_sems.at[i, s])
            for i, (source, target) in enumerate(pairs)
        ]

    w_load = pltpu.make_async_copy(wqkv_h, wqkv, w_sem)
    mix_load(0).start()
    kv_load(0).start()
    for copy in head_loads(0):
        copy.start()
    at.barrier()
    for copy in (last_own, last_y, last_c):
        copy.start()
    for s in range(1, SEQS):
        for copy in head_loads(s):
            copy.start()
    w_load.start()
    for i in range(4):
        first_copy(i).start()
    norm_load(0).start()
    norm_early(0).start()

    segk[...] = jnp.full(segk.shape, -1.0, F32)
    segk[0:4, 1024:3072] = segs[...].astype(F32)
    small[...] = jnp.zeros_like(small)
    def m1_copy(s):
        return remote(dfar.at[lax.rem(s, 2)], m1.at[s], (m1_sems.at[0, s], m1_sems.at[1, s]), at.down)

    def m2_copy(s):
        return remote(dnear.at[s], m2.at[s], (m2_sems.at[0, s], m2_sems.at[1, s]), at.down)

    def step_e(s):
        kv_load(s).wait()
        for copy in head_loads(s):
            copy.wait()

        @pl.when(s < last)
        def _():
            mix_load(s).wait()

        @pl.when(s == last)
        def _():
            for copy in (last_own, last_c, last_over):
                copy.wait()
            gm[...] = gm_last[...]

        ga[...] = matmul(gm[...], wout[...], 1, 1).astype(BF)
        lane = lax.broadcasted_iota(jnp.int32, (1, LOCAL), 1) // HD
        keys = kvs.reshape(3 * GROUP, 2 * LOCAL)
        here_segs = segk.at[:, aligned(at.z * GROUP, 3 * GROUP)]
        dkvt[...] = jnp.zeros_like(dkvt)

        def pairs(b, low, size, first):
            here, span = pl.ds(b * HALF, HALF), pl.ds(low, size)
            which = lax.broadcasted_iota(jnp.int32, (8, size), 0) == s
            seg_row = jnp.sum(
                jnp.where(which, here_segs[:, span], 0.0), axis=0, keepdims=True
            )
            logs = lse[s, here]
            bias[:, 0:size] = allowed_bias(logs[:, 5:6], seg_row, low - b * HALF, size)
            query = q[s, here]
            grad = ga[here]
            k_block = keys[span, 0:LOCAL]
            v_block = keys[span, LOCAL:]
            dots[0] = jnp.transpose(query)
            dots[1] = jnp.transpose(grad)
            product = grad.astype(F32) * att[s, here].astype(F32)
            grad_query = jnp.zeros((HALF, LOCAL), F32) if first else dq[here]
            for h in range(LOCAL // HD):
                mine_h = lane == h
                one = jnp.where(mine_h, query, jnp.zeros_like(query))
                grad_one = jnp.where(mine_h, grad, jnp.zeros_like(grad))
                delta = jnp.sum(jnp.where(mine_h, product, 0.0), axis=-1, keepdims=True)
                scores = matmul(one, k_block, 1, 1) + bias[:, 0:size]
                probs = jnp.exp(scores - logs[:, h : h + 1])
                dprobs = matmul(grad_one, v_block, 1, 1)
                grad_scores = (probs * (dprobs - delta)).astype(BF)
                part = matmul(grad_scores, k_block, 1, 0)
                grad_query = jnp.where(mine_h, grad_query + part, grad_query)
                k_rows = pl.ds(h * HD, HD)
                v_rows = pl.ds(LOCAL + h * HD, HD)
                dkvt[k_rows, span] += matmul(dots[0, k_rows], grad_scores, 1, 0)
                dkvt[v_rows, span] += matmul(dots[1, k_rows], probs.astype(BF), 1, 0)
            if first:
                dq[here] = grad_query
            else:
                gq[s, here] = (grad_query * 0.125).astype(BF)

        def turned(i):
            return jnp.transpose(dkvt[:, i * GROUP : (i + 1) * GROUP].astype(BF))

        pairs(0, 0, GROUP, True)
        pairs(1, HALF, HALF, True)

        @pl.when((at.z > 1) & (s > 1))
        def _():
            m1_copy(s - 2).wait_send()

        dfar[lax.rem(s, 2)] = turned(0)

        @pl.when(at.z > 1)
        def _():
            m1_copy(s).start()

        @pl.when(s == 0)
        def _():
            a_qkv[...] = jnp.zeros_like(a_qkv)
            a_out[...] = jnp.zeros_like(a_out)

        pairs(0, GROUP, SPAN - GROUP, False)
        pairs(1, GROUP, SPAN - HALF, False)
        dnear[s] = turned(1)
        down[s] = turned(2)
        a_out[...] += matmul(att[s], gm[...], 0, 0)

        @pl.when(s < last)
        def _():
            kv_load(s + 1).start()

        @pl.when(s < last - 1)
        def _():
            mix_load(s + 1).start()

        norm_early(s).wait()
        a_qkv[0] += matmul(n1e[...], gq[s], 0, 0)

        @pl.when(s < 3)
        def _():
            norm_early(s + 1).start()

    def step_i(s):
        @pl.when((at.z > 0) & (at.z < 3))
        def _():
            m1_copy(s).wait_recv()
            dnear[s] = (dnear[s].astype(F32) + m1[s].astype(F32)).astype(BF)

        @pl.when(at.z > 0)
        def _():
            m2_copy(s).start()

    def step_f(s):
        @pl.when(at.z < 3)
        def _():
            m2_copy(s).wait_recv()
            down[s] = (down[s].astype(F32) + m2[s].astype(F32)).astype(BF)

        norm_load(s).wait()
        @pl.when(s == 0)
        def _():
            w_load.wait()

        grads = (gq[s], down[s, :, 0:LOCAL], down[s, :, LOCAL:])
        send[s] = (
            matmul(grads[0], wqkv[0], 1, 1)
            + matmul(grads[1], wqkv[1], 1, 1)
            + matmul(grads[2], wqkv[2], 1, 1)
        ).astype(BF)
        ring.rs_core(s).start()
        normed = n1s[...]
        for i in (1, 2):
            a_qkv[i] += matmul(normed, grads[i], 0, 0)

        @pl.when(s < 3)
        def _():
            norm_load(s + 1).start()

        small[9:10, 0:LOCAL] += column_sum(grads[0].astype(F32))
        small[9:10, LOCAL : 2 * LOCAL] += column_sum(grads[2].astype(F32))

    def ends(s):
        return tok_q.at[s], ig_h

    def ig_copy(s):
        return pltpu.make_async_copy(tok_q.at[s], ig_h.at[s, mine], first_sems.at[s])

    def step_r(s):
        @pl.when(s == 0)
        def _():
            first_copy(2).wait()
            first_copy(3).wait()

        summed = ring.total(s)
        xhat, inverse = norm_parts(tok_q[s].astype(F32))
        small[0:1, :] += column_sum(summed * xhat)
        small[1:2, :] += column_sum(summed)
        @pl.when(s > 0)
        def _():
            mid_load(s).wait()

        grad = gmid[...] + norm_back(summed, xhat, inverse, sums_one[7:8, :])
        tok_q[s] = grad.astype(BF)

        @pl.when(s < 3)
        def _():
            mid_load(s + 1).start()

        ig_copy(s).start()
        ring.spread(*ends(s), s)

    def sum_copy(stage, j=0):
        pair = (sum_sems.at[0, stage], sum_sems.at[1, stage])
        top = small.at[0:8]
        if stage == 0:
            return remote(top, got_core, pair, at.mate_c)
        if stage == 1:
            return remote(top, got_y, pair, at.mate_y)
        if stage == 2:
            pair = (sum_f_sems.at[0, j], sum_f_sems.at[1, j])
            return remote(small, got_f.at[j], pair, at.peers_f[j])
        mate = red_q.side if stage == 3 else red_q.across
        return remote(small, got_z.at[stage - 3], pair, mate)

    def step_sum(stage, s):
        if stage == 0:
            small[2:6, :] = sums_one[0:4, :]
            small[6:7, :] = sums_one[5:6, :]
            small[8:9, :] = sums_one[4:5, :]
        elif stage == 3:
            for j in range(nf - 1):
                sum_copy(2, j).wait()
            for j in range(nf - 1):
                small[...] += got_f[j]
        else:
            sum_copy(stage - 1).wait()
            if stage == 1:
                small[0:8, :] += got_core[...]
            elif stage == 2:
                small[0:8, :] += got_y[...]
            else:
                small[...] += got_z[stage - 4]
        if stage == 2:
            for j in range(nf - 1):
                sum_copy(2, j).start()
        elif stage < 5:
            sum_copy(stage).start()

    def step_group(group, stage, s):
        if stage == 0:
            if group == "B":
                f_out[...] = a_out[...].astype(BF)
                f_qkv[0] = a_qkv[0].astype(BF)
            elif group == "C":
                for i in (1, 2):
                    f_qkv[i] = a_qkv[i].astype(BF)
        for reduce in groups[group]:
            reduce.run(stage)

    groups = {"B": (red_out, red_q), "C": (red_kv,)}
    chains = (red_fc2, red_fc1)
    actions = {
        "E": step_e,
        "L": step_last,
        "I": step_i,
        "F": step_f,
        "Q": ring.step_q,
        "R": step_r,
        "T": lambda s: ring.step_t(*ends(s), s),
    }
    for stage in range(6):
        actions[f"S{stage}"] = functools.partial(step_sum, stage)
        for group in groups:
            actions[f"{group}{stage}"] = functools.partial(step_group, group, stage)

    def step_climb(stage, s):
        if stage == 0:

            @pl.when(lax.rem(s, 2) == 0)
            def _():
                first_copy_of(1 - s // 2).wait()

        for i, chain in enumerate(chains):

            @pl.when(s // 2 == i)
            def _(chain=chain):
                chain.climb(stage, lax.rem(s, 2))

    def step_down(hop, s):
        for i, chain in enumerate(chains):

            @pl.when(s // 4 == i)
            def _(chain=chain):
                chain.hand_down(hop, lax.rem(s // 2, 2), lax.rem(s, 2))

    for stage in range(5):
        actions[f"K{stage}"] = functools.partial(step_climb, stage)
    for hop in (1, 2, 3):
        actions[f"D{hop}"] = functools.partial(step_down, hop)
    run_order(actions, BACK_ORDER)
    for chain in chains:
        chain.finish()
    for s in range(SEQS):
        ring.step_u(*ends(s), s)
        ig_copy(s).wait()

        if s > 1:

            @pl.when(at.z > 1)
            def _():
                m1_copy(s).wait_send()

        @pl.when(at.z > 0)
        def _():
            m2_copy(s).wait_send()


def back_call(nf, *args):
    anys = pl.BlockSpec(memory_space=pl.ANY)
    vmem = pl.BlockSpec(memory_space=pltpu.VMEM)
    dma = pltpu.SemaphoreType.DMA
    big = lambda *lead: pltpu.VMEM((*lead, GROUP, 1024), BF)
    shape = jax.ShapeDtypeStruct
    fs = 1024 // nf
    low = lambda *dims: pltpu.VMEM(dims, BF)
    return pl.pallas_call(
        functools.partial(back_kernel, nf),
        out_shape=(
            shape((SEQS, GROUP, 1024), BF),
            shape((16, 1024), F32),
            shape((3, fs, LOCAL), BF),
            shape((LOCAL, fs), BF),
            shape((fs, 1024), BF),
            shape((1024, fs), BF),
        ),
        in_specs=[anys] * 11 + [vmem, vmem, vmem],
        out_specs=(anys, vmem, vmem, vmem, vmem, vmem),
        scratch_shapes=[
            low(GROUP, 1024),
            low(GROUP, 1024),
            low(3, GROUP, 2 * LOCAL),
            low(GROUP, 1024),
            low(GROUP, LOCAL),
            pltpu.VMEM((GROUP, LOCAL), F32),
            low(2, LOCAL, HALF),
            pltpu.VMEM((HALF, SPAN), F32),
            pltpu.VMEM((8, 3072), F32),
            pltpu.VMEM((2 * LOCAL, 3 * GROUP), F32),
            low(2, GROUP, 2 * LOCAL),
            low(SEQS, GROUP, 2 * LOCAL),
            low(SEQS, GROUP, 2 * LOCAL),
            low(SEQS, GROUP, 2 * LOCAL),
            low(SEQS, GROUP, 2 * LOCAL),
            low(SEQS, GROUP, LOCAL),
            big(SEQS),
            low(SEQS, HALF, 1024),
            low(SEQS, QUARTER, 1024),
            low(SEQS, QUARTER, 1024),
            pltpu.VMEM((QUARTER, 1024), F32),
            low(SEQS, QUARTER, 1024),
            pltpu.VMEM((3, 1024, LOCAL), F32),
            pltpu.VMEM((LOCAL, 1024), F32),
            low(3, 1024, LOCAL),
            low(1024, 1024),
            low(1024, 1024),
            low(nf - 1, 3, fs, LOCAL),
            low(nf - 1, LOCAL, fs),
            low(nf - 1, fs, 1024),
            low(nf - 1, 1024, fs),
            low(3, fs // 2, LOCAL),
            low(LOCAL // 2, fs),
            low(3, fs // 4, LOCAL),
            low(LOCAL // 4, fs),
            dma((5, 2, SEQS)),
            dma((3, 2)),
            dma,
            dma((4,)),
            dma((2, SEQS)),
            dma((2, SEQS)),
            dma((5, 2, nf - 1)),
            dma((5, 2, 4)),
            dma((2, 2, nf - 1, 2)),
            dma((2, 2, 6)),
            pltpu.VMEM((8, 1024), F32),
            pltpu.VMEM((8, 1024), F32),
            pltpu.VMEM((nf - 1, 16, 1024), F32),
            pltpu.VMEM((2, 16, 1024), F32),
            dma((2, 5)),
            dma((2, nf - 1)),
            low(GROUP, 1024),
            low(SEQS, GROUP, LOCAL),
            low(SEQS, GROUP, LOCAL),
            pltpu.VMEM((SEQS, GROUP, 128), F32),
            low(3, 1024, LOCAL),
            dma((3, SEQS)),
            dma,
        ],
        compiler_params=pltpu.CompilerParams(
            collective_id=2, has_side_effects=True, vmem_limit_bytes=63 * 2**20
        ),
        cost_estimate=pl.CostEstimate(
            flops=2 * 2048 * 1024 * 1024 * 6, bytes_accessed=30 * 2**20, transcendentals=0
        ),
        name="back",
    )(*args)


def finish_kernel(
    nf,
    out_in,
    ig_in,
    sums,
    sums_one,
    s_qkv,
    s_out,
    s_fc1,
    s_fc2,
    out,
    loss,
    ig,
    g_g1,
    g_b1,
    g_qkv,
    g_qv,
    g_out,
    g_bo,
    g_g2,
    g_b2,
    g_fc1,
    g_up,
    g_fc2,
    g_bd,
    low,
    wide_qkv,
    wide_out,
    wide_fc1,
    wide_fc2,
    low_qkv,
    low_out,
    low_fc1,
    low_fc2,
    in_sems,
    out_sems,
):
    shards = (
        (s_fc1, low_fc1, wide_fc1, g_fc1),
        (s_fc2, low_fc2, wide_fc2, g_fc2),
        (s_qkv, low_qkv, wide_qkv, g_qkv),
        (s_out, low_out, wide_out, g_out),
    )
    inward, outward = [], []
    for i, (source, kept, widened, target) in enumerate(shards):
        inward.append(pltpu.make_async_copy(source, kept, in_sems.at[i]))
        outward.append(pltpu.make_async_copy(widened, target, out_sems.at[i]))
    for i, (source, target) in enumerate(((out_in, out), (ig_in, ig))):
        for s in range(SEQS):
            which = 4 + i * SEQS + s
            inward.append(
                pltpu.make_async_copy(source.at[s], low.at[i, s], in_sems.at[which])
            )
            outward.append(
                pltpu.make_async_copy(low.at[i, s], target.at[s], out_sems.at[which])
            )
    for copy in inward:
        copy.start()
    for i, (_, kept, widened, _) in enumerate(shards):
        inward[i].wait()
        widened[...] = kept[...].astype(F32)
        outward[i].start()
    for i in range(4, len(inward)):
        inward[i].wait()
        outward[i].start()
    place = lax.axis_index("fsdp")
    fs = g_g1.shape[0]
    here = aligned(place * fs, fs)
    for i, target in enumerate((g_g1, g_b1, g_bd, g_g2, g_b2, g_bo)):
        target[...] = sums[i : i + 1, here].reshape(fs)
    scale = 1.0 / (2.0 * D * sums_one[6:7, 0:1])
    loss[...] = jnp.sum(sums[6:7, :], axis=1, keepdims=True) * scale
    own = sums[8:16, :]
    wide = g_up.shape[1]
    up = pltpu.roll(own, lax.rem(1024 - place * wide, 1024), 1)
    for i in range(g_up.shape[0]):
        g_up[i : i + 1, :] = up[0:1, i * nf * wide : i * nf * wide + wide]
    wide = g_qv.shape[2]
    qv = pltpu.roll(own, lax.rem(1024 - place * wide, 1024), 1)
    for i in range(2):
        for h in range(LOCAL // HD):
            start = i * LOCAL + h * HD
            g_qv[i, h : h + 1, :] = qv[1:2, start : start + wide]
    for copy in outward:
        copy.wait()


def finish_call(nf, *args):
    anys = pl.BlockSpec(memory_space=pl.ANY)
    vmem = pl.BlockSpec(memory_space=pltpu.VMEM)
    shape = jax.ShapeDtypeStruct
    fs = 1024 // nf
    block = shape((SEQS, GROUP, 1024), BF)
    row = shape((fs,), F32)
    return pl.pallas_call(
        functools.partial(finish_kernel, nf),
        out_shape=(
            block,
            shape((1, 1), F32),
            block,
            row,
            row,
            shape((3, fs, LOCAL), F32),
            shape((2, LOCAL // HD, HD // nf), F32),
            shape((LOCAL, fs), F32),
            row,
            row,
            row,
            shape((fs, 1024), F32),
            shape((4, 256 // nf), F32),
            shape((1024, fs), F32),
            row,
        ),
        in_specs=[anys, anys, vmem, vmem] + [anys] * 4,
        out_specs=(anys, vmem, anys, vmem, vmem, anys, vmem, anys)
        + (vmem, vmem, vmem, anys, vmem, anys, vmem),
        scratch_shapes=[
            pltpu.VMEM((2, SEQS, GROUP, 1024), BF),
            pltpu.VMEM((3, fs, LOCAL), F32),
            pltpu.VMEM((LOCAL, fs), F32),
            pltpu.VMEM((fs, 1024), F32),
            pltpu.VMEM((1024, fs), F32),
            pltpu.VMEM((3, fs, LOCAL), BF),
            pltpu.VMEM((LOCAL, fs), BF),
            pltpu.VMEM((fs, 1024), BF),
            pltpu.VMEM((1024, fs), BF),
            pltpu.SemaphoreType.DMA((4 + 2 * SEQS,)),
            pltpu.SemaphoreType.DMA((4 + 2 * SEQS,)),
        ],
        compiler_params=pltpu.CompilerParams(vmem_limit_bytes=63 * 2**20),
        name="finish",
    )(*args)


def local(
    tokens,
    cotangent,
    teacher,
    valid_mask,
    segment_ids,
    ln1_gain,
    ln1_bias,
    w_qkv,
    b_qv,
    w_out,
    b_out,
    ln2_gain,
    ln2_bias,
    w_fc1,
    b_fc1,
    w_fc2,
    b_fc2,
):
    nf = lax.axis_size("fsdp")
    front = front_call(
        nf,
        w_qkv,
        w_out,
        w_fc1,
        w_fc2,
        tokens,
        teacher,
        cotangent,
        b_out,
        ln2_gain,
        ln2_bias,
        b_fc2,
        ln1_gain,
        ln1_bias,
        b_qv,
        b_fc1,
        valid_mask,
        segment_ids,
    )
    (output, grad_mix, grad_middle, gfc1, gfc2, sums_one, att, q, kv, lse, n1, wqkv, wout) = front
    input_grad, everything, s_qkv, s_out, s_fc1, s_fc2 = back_call(
        nf, grad_mix, grad_middle, gfc1, gfc2, att, q, kv, lse, n1, tokens, wqkv, wout, segment_ids, sums_one
    )
    results = finish_call(
        nf, output, input_grad, everything, sums_one, s_qkv, s_out, s_fc1, s_fc2
    )
    return (results[0], results[1].reshape(()), *results[2:])


def solution(mesh):
    return jax.shard_map(
        local,
        mesh=mesh,
        in_specs=(
            P("fsdp", "context", None),
            P("fsdp", "context", None),
            P("fsdp", "context", None),
            P("fsdp", "context"),
            P("fsdp", None),
            P("fsdp"),
            P("fsdp"),
            P(None, "fsdp", "tensor"),
            P(None, "tensor", "fsdp"),
            P("tensor", "fsdp"),
            P("fsdp"),
            P("fsdp"),
            P("fsdp"),
            P("fsdp", "tensor"),
            P("tensor", "fsdp"),
            P("tensor", "fsdp"),
            P("fsdp"),
        ),
        out_specs=(
            P("fsdp", "context", None),
            P(),
            P("fsdp", "context", None),
            P("fsdp"),
            P("fsdp"),
            P(None, "fsdp", "tensor"),
            P(None, "tensor", "fsdp"),
            P("tensor", "fsdp"),
            P("fsdp"),
            P("fsdp"),
            P("fsdp"),
            P("fsdp", "tensor"),
            P("tensor", "fsdp"),
            P("tensor", "fsdp"),
            P("fsdp"),
        ),
        check_vma=False,
    )
```

```python
import functools
import math

import jax
import jax.numpy as jnp
from jax import lax
from jax.experimental import pallas as pl
from jax.experimental.pallas import tpu as pltpu
from jax.sharding import PartitionSpec as P

MESH = pl.DeviceIdType.MESH
BF = jnp.bfloat16
F32 = jnp.float32
D = 1024
HD = 64
WINDOW = 1024
EPSILON = 1e-05
MASKED = -1e30
SEQS = 4
GROUP = 512
QUARTER = 128
HALF = 256
SPAN = 1280
LOCAL = 256


def matmul(left, right, over_left, over_right):
    dims = (((over_left,), (over_right,)), ((), ()))
    return lax.dot_general(left, right, dims, preferred_element_type=F32)


def norm_parts(values):
    mean = jnp.mean(values, axis=-1, keepdims=True)
    center = values - mean
    spread = jnp.mean(center * center, axis=-1, keepdims=True)
    inverse = lax.rsqrt(spread + EPSILON)
    return center * inverse, inverse


def norm_back(grad_normed, xhat, inverse, gain):
    e = grad_normed * gain
    return inverse * (
        e
        - jnp.mean(e, axis=-1, keepdims=True)
        - xhat * jnp.mean(e * xhat, axis=-1, keepdims=True)
    )


def column_sum(values):
    return jnp.sum(values, axis=0, keepdims=True)


def aligned(start, size, unit=128):
    return pl.ds(pl.multiple_of(start, unit), size)


def allowed_bias(query_seg, key_seg, skipped=0, size=SPAN):
    column = lax.broadcasted_iota(jnp.int32, (HALF, size), 1) + skipped
    ahead = column - lax.broadcasted_iota(jnp.int32, (HALF, size), 0)
    allowed = (ahead > 0) & (ahead <= WINDOW) & (query_seg == key_seg)
    return jnp.where(allowed, 0.0, MASKED)


class Place:
    def __init__(self, nf):
        self.nf = nf
        self.f = lax.axis_index("fsdp")
        self.z = lax.axis_index("context")
        self.t = lax.axis_index("tensor")
        self.y, self.c = self.t // 2, lax.rem(self.t, 2)
        self.mate_c = (self.f, self.z, self.t + 1 - 2 * self.c)
        self.mate_y = (self.f, self.z, lax.rem(self.t + 2, 4))
        self.mine = (2 * self.c + self.y) * QUARTER
        self.over_y = (2 * self.c + 1 - self.y) * QUARTER
        self.peers_f = [(lax.rem(self.f + j, nf), self.z, self.t) for j in range(1, nf)]
        self.peers_z = [(self.f, lax.rem(self.z + j, 4), self.t) for j in range(1, 4)]
        self.up = (self.f, lax.rem(self.z + 1, 4), self.t)
        self.down = (self.f, lax.rem(self.z + 3, 4), self.t)

    def barrier(self):
        semaphore = pltpu.get_barrier_semaphore()
        everyone = [self.mate_c, self.mate_y] + self.peers_f + self.peers_z
        for peer in everyone:
            pl.semaphore_signal(semaphore, inc=1, device_id=peer, device_id_type=MESH)
        pl.semaphore_wait(semaphore, len(everyone))


def remote(src, dst, pair, mate):
    return pltpu.make_async_remote_copy(
        src, dst, pair[0], pair[1], device_id=mate, device_id_type=MESH
    )


def run_order(actions, order):
    names = list(actions)
    codes = [names.index(name) * 8 + s for name, s in order]

    def step(i, carry):
        code = jnp.int32(codes[0])
        for j, other in enumerate(codes[1:]):
            code = jnp.where(i == j + 1, other, code)
        kind, s = code // 8, lax.rem(code, 8)
        for j, name in enumerate(names):

            @pl.when(kind == j)
            def _(action=actions[name]):
                action(s)

        return carry

    lax.fori_loop(0, len(order), step, 0)


class Ring:
    def __init__(self, at, send, recv_c, send_y, recv_y, sems):
        self.at, self.send, self.recv_c = at, send, recv_c
        self.send_y, self.recv_y, self.sems = send_y, recv_y, sems

    def pair(self, which, s):
        return self.sems.at[which, 0, s], self.sems.at[which, 1, s]

    def rs_core(self, s):
        half = aligned((1 - self.at.c) * HALF, HALF)
        return remote(self.send.at[s, half], self.recv_c.at[s], self.pair(0, s), self.at.mate_c)

    def rs_y(self, s):
        return remote(self.send_y.at[s], self.recv_y.at[s], self.pair(1, s), self.at.mate_y)

    def back_y(self, src, dst, s):
        return remote(
            src, dst.at[s, aligned(self.at.mine, QUARTER)], self.pair(2, s), self.at.mate_y
        )

    def back_own(self, src, dst, s):
        return remote(
            src, dst.at[s, aligned(self.at.mine, QUARTER)], self.pair(3, s), self.at.mate_c
        )

    def back_over(self, dst, s):
        there = dst.at[s, aligned(self.at.over_y, QUARTER)]
        return remote(there, there, self.pair(4, s), self.at.mate_c)

    def step_q(self, s):
        self.rs_core(s).wait()
        self.send_y[s] = (
            self.send[s, aligned(self.at.over_y, QUARTER)].astype(F32)
            + self.recv_c[s, aligned((1 - self.at.y) * QUARTER, QUARTER)].astype(F32)
        ).astype(BF)
        self.rs_y(s).start()

    def total(self, s):
        self.rs_y(s).wait()
        return (
            self.send[s, aligned(self.at.mine, QUARTER)].astype(F32)
            + self.recv_c[s, aligned(self.at.y * QUARTER, QUARTER)].astype(F32)
            + self.recv_y[s].astype(F32)
        )

    def spread(self, src, dst, s):
        self.back_y(src, dst, s).start()
        self.back_own(src, dst, s).start()

    def step_t(self, src, dst, s):
        self.back_y(src, dst, s).wait()
        self.back_over(dst, s).start()

    def step_u(self, src, dst, s):
        self.back_own(src, dst, s).wait()
        self.back_over(dst, s).wait()


FRONT_ORDER = (
    ("A", 0),
    ("A", 1),
    ("H", 0),
    ("A", 2),
    ("V", 0),
    ("P0", 0),
    ("A", 3),
    ("C", 0),
    ("Q", 0),
    ("H", 1),
    ("R0", 0),
    ("P0", 1),
    ("T0", 0),
    ("H", 2),
    ("Q", 1),
    ("D", 0),
    ("W", 0),
    ("P1", 0),
    ("Q", 0),
    ("R0", 1),
    ("P0", 2),
    ("R1", 0),
    ("T0", 1),
    ("Q", 2),
    ("H", 3),
    ("P1", 1),
    ("Q", 1),
    ("R0", 2),
    ("P0", 3),
    ("R1", 1),
    ("Q", 3),
    ("T0", 2),
    ("P1", 2),
    ("T1", 0),
    ("T1", 1),
    ("Q", 2),
    ("P2", 0),
    ("R0", 3),
    ("P2", 1),
    ("Q", 0),
    ("T0", 3),
    ("R1", 2),
    ("P1", 3),
    ("Q", 3),
    ("T1", 2),
    ("Q", 1),
    ("P2", 2),
    ("R1", 3),
    ("R2", 1),
    ("Q", 2),
    ("T1", 3),
    ("P2", 3),
    ("R2", 0),
    ("Q", 3),
    ("gdown", 0),
    ("T2", 0),
    ("R2", 2),
    ("T2", 1),
    ("gup", 0),
    ("R2", 3),
    ("T2", 2),
)


def front_kernel(
    nf,
    wqkv_s,
    wout_s,
    wfc1_s,
    wfc2_s,
    tokens,
    teacher,
    cot,
    part_bo,
    part_g2,
    part_b2,
    part_bd,
    part_g1,
    part_b1,
    part_qv,
    part_up,
    mask,
    segs,
    out_h,
    gmix_h,
    gmid_h,
    gfc1,
    gfc2,
    small,
    att_h,
    q_h,
    kv_h,
    lse_h,
    n1_h,
    wqkv_h,
    wout_h,
    wqkv,
    wout,
    wfc1,
    wfc2,
    n2,
    blk,
    act,
    slope,
    send,
    recv_c,
    send_y,
    recv_y,
    mid,
    gblk,
    tok_q,
    tea_q,
    cot_q,
    stage,
    segk,
    bias,
    kv,
    cnt,
    w_send,
    w_recv,
    w_loc,
    ring_sems,
    q_sems,
    in_sems,
    n1_sem,
    out_sem,
    mix_sem,
    near_sems,
    far_sems,
    cz_sems,
    cf_sems,
    res_sem,
    keep_sem,
    vec,
    vec_own,
    vec_got,
    v_sems,
    att,
    q,
    lse,
    head_sems,
    mid_sems,
):
    at = Place(nf)
    at.barrier()
    ring = Ring(at, send, recv_c, send_y, recv_y, ring_sems)
    mine = aligned(at.mine, QUARTER)

    fs = wout_s.shape[1]
    own = aligned(at.f * fs, fs)
    query, pair_kv = pl.ds(0, 1), pl.ds(1, 2)
    places = (
        (wqkv_s.at[pair_kv], wqkv.at[pair_kv, own, :]),
        (wout_s, wout.at[:, own]),
        (wfc1_s, wfc1.at[own, :]),
        (wfc2_s, wfc2.at[:, own]),
        (wqkv_s.at[query], wqkv.at[query, own, :]),
    )

    def weight_copy(i, j):
        pair = (w_send.at[i, j], w_recv.at[i, j])
        return remote(places[i][0], places[i][1], pair, at.peers_f[j])

    def weight_start(i):
        for j in range(nf - 1):
            weight_copy(i, j).start()
        pltpu.make_async_copy(places[i][0], places[i][1], w_loc.at[i]).start()

    def weight_wait(i):
        pltpu.make_async_copy(places[i][0], places[i][1], w_loc.at[i]).wait()
        for j in range(nf - 1):
            weight_copy(i, j).wait()

    weight_start(0)

    def token_copy(s):
        slot = lax.rem(s, 2)
        return pltpu.make_async_copy(tokens.at[s], stage.at[slot], in_sems.at[slot])

    token_copy(0).start()
    quarters = ((tokens, tok_q), (teacher, tea_q), (cot, cot_q))
    for i, (source, target) in enumerate(quarters):
        pltpu.make_async_copy(source.at[:, mine, :], target, q_sems.at[i]).start()

    vec_own[...] = jnp.zeros_like(vec_own)
    rows = ((0, part_bo), (1, part_g2), (2, part_b2), (4, part_bd), (5, part_g1), (6, part_b1))
    for i, part in rows:
        vec_own[i : i + 1, own] = part[...].astype(F32).reshape(1, fs)

    def scatter(part, count):
        wide = part.shape[1]
        unit = wide * nf
        column = lax.broadcasted_iota(jnp.int32, (wide, count * unit), 1)
        inside = lax.broadcasted_iota(jnp.int32, (wide, count * unit), 0) + at.f * wide
        spread = (lax.rem(column, unit) == inside).astype(BF)
        full = matmul(part, spread, 1, 0)
        group = lax.broadcasted_iota(jnp.int32, full.shape, 1) // unit
        owner = lax.broadcasted_iota(jnp.int32, full.shape, 0)
        return jnp.sum(jnp.where(group == owner, full, 0.0), axis=0, keepdims=True)

    vec_own[3:4, :] = scatter(part_up[...], part_up.shape[0])
    for i in range(2):
        columns = pl.ds(i * LOCAL, LOCAL)
        vec_own[7:8, columns] = scatter(part_qv[i], part_qv.shape[1])

    def vec_copy(j):
        pair = (v_sems.at[0, j], v_sems.at[1, j])
        return remote(vec_own, vec_got.at[j], pair, at.peers_f[j])

    for j in range(nf - 1):
        vec_copy(j).start()

    valid = mask[...].astype(F32)
    masks = jnp.concatenate([valid, jnp.zeros_like(valid)], axis=0)
    cnt[0] = jnp.broadcast_to(jnp.sum(masks, keepdims=True), (8, 128))

    def count_z(j):
        pair = (cz_sems.at[0, j], cz_sems.at[1, j])
        return remote(cnt.at[0], cnt.at[1 + j], pair, at.peers_z[j])

    def count_f(j):
        pair = (cf_sems.at[0, j], cf_sems.at[1, j])
        return remote(cnt.at[4], cnt.at[5 + j], pair, at.peers_f[j])

    for j in range(3):
        count_z(j).start()

    turned = jnp.transpose(masks)
    segk[...] = jnp.full(segk.shape, -1.0, F32)
    segk[0:4, 1024:3072] = segs[...].astype(F32)
    seg_turned = jnp.transpose(segk[:, aligned(1024 + at.z * GROUP, GROUP)])
    column = lax.broadcasted_iota(jnp.int32, (1, 128), 1)
    for s in range(SEQS):
        lse[s] = jnp.where(column == 4, turned[:, s : s + 1], seg_turned[:, s : s + 1])
    small[...] = jnp.zeros_like(small)
    @pl.when(at.z < 2)
    def _():
        def clear(s, carry):
            kv[s, 0] = jnp.zeros((GROUP, 2 * LOCAL), BF)
            return carry

        lax.fori_loop(0, SEQS, clear, 0)

    @pl.when(at.z < 1)
    def _():
        def clear(s, carry):
            kv[s, 1] = jnp.zeros((GROUP, 2 * LOCAL), BF)
            return carry

        lax.fori_loop(0, SEQS, clear, 0)

    def near_copy(s, half):
        part = pl.ds(half * HALF, HALF)
        pair = (near_sems.at[0, s, half], near_sems.at[1, s, half])
        return remote(kv.at[s, 2, part], kv.at[s, 1, part], pair, at.up)

    def far_copy(s, half):
        part = pl.ds(half * HALF, HALF)
        pair = (far_sems.at[0, s, half], far_sems.at[1, s, half])
        return remote(kv.at[s, 1, part], kv.at[s, 0, part], pair, at.up)

    def near_start(s):
        for half in range(2):
            near_copy(s, half).start()

    def norm_copy(s):
        return pltpu.make_async_copy(act.at[s], n1_h.at[s], n1_sem.at[s])

    def step_norm(s, carry):
        token_copy(s).wait()

        @pl.when(s < 3)
        def _():
            token_copy(s + 1).start()

        for part in range(2):
            here = pl.ds(part * 256, 256)
            xhat, _ = norm_parts(stage[lax.rem(s, 2), here].astype(F32))
            act[s, here] = (xhat * vec[5:6, :] + vec[6:7, :]).astype(BF)
        norm_copy(s).start()
        return carry

    def step_a(s):
        normed = act[s]
        kv[s, 2, :, 0:LOCAL] = matmul(normed, wqkv[1], 1, 0).astype(BF)
        kv[s, 2, :, LOCAL:] = (matmul(normed, wqkv[2], 1, 0) + vec[7:8, 256:512]).astype(BF)

        @pl.when((at.z < 3) & ((at.z == 0) | (s == 0)))
        def _():
            near_start(s)

    for j in range(nf - 1):
        vec_copy(j).wait()
    whole = vec_own[...]
    for j in range(nf - 1):
        whole = whole + vec_got[j]
    vec[...] = whole
    small[7:8, :] = vec[5:6, :]
    lax.fori_loop(0, SEQS, step_norm, 0)
    weight_wait(0)
    for i in (4, 1, 2, 3):
        weight_start(i)
    for i, (source, target) in enumerate(quarters):
        pltpu.make_async_copy(source.at[:, mine, :], target, q_sems.at[i]).wait()

    def step_count(s):
        for j in range(3):
            count_z(j).wait()
        cnt[4] = cnt[0] + cnt[1] + cnt[2] + cnt[3]
        for j in range(nf - 1):
            count_f(j).start()

    def step_counted(s):
        for j in range(nf - 1):
            count_f(j).wait()
        total_count = cnt[4]
        for j in range(nf - 1):
            total_count = total_count + cnt[5 + j]
        small[6:7, 0:128] = total_count[0:1, :]
        cnt[0] = (SEQS * GROUP * nf * 4) / total_count
        for i in range(SEQS):
            norm_copy(i).wait()
        for copy in block_copies(0):
            copy.start()

    def factor():
        return cnt[0, 0:1, 0:1]

    def block_copies(s):
        return (
            pltpu.make_async_copy(teacher.at[s], stage.at[0], in_sems.at[0]),
            pltpu.make_async_copy(cot.at[s], stage.at[1], in_sems.at[1]),
        )

    def kv_out(s):
        return pltpu.make_async_copy(kv.at[s], kv_h.at[s], res_sem.at[s])

    def head_copies(s):
        pairs = ((att, att_h), (q, q_h), (lse, lse_h))
        return [
            pltpu.make_async_copy(source.at[s], target.at[s], head_sems.at[i, s])
            for i, (source, target) in enumerate(pairs)
        ]

    def mid_copy(s):
        return pltpu.make_async_copy(gblk.at[s], gmid_h.at[s], mid_sems.at[s])

    def mix_copy(s):
        return pltpu.make_async_copy(tok_q.at[s], gmix_h.at[s, mine], mix_sem.at[s])

    def ends(k, s):
        if k == 2:
            return tok_q.at[s], gmix_h
        target = (n2, blk)[k]
        return target.at[s, mine], target

    def step_r(k, s):
        summed = ring.total(s)
        if k == 0:
            middle = tok_q[s].astype(F32) + summed + vec[0:1, :]
            mid[s] = middle
            xhat, _ = norm_parts(middle)
            n2[s, mine] = (xhat * vec[1:2, :] + vec[2:3, :]).astype(BF)
        elif k == 1:
            block = mid[s] + summed + vec[4:5, :]
            blk[s, mine] = block.astype(BF)
            difference = block - tea_q[s].astype(F32)
            masked = lse[s, mine, 4:5] * difference
            small[5:6, :] += column_sum(masked * difference)
            grad = cot_q[s].astype(F32) + masked * factor()
            gblk[s] = grad
            small[0:1, :] += column_sum(grad)
        else:
            xhat, inverse = norm_parts(mid[s])
            small[1:2, :] += column_sum(summed * xhat)
            small[2:3, :] += column_sum(summed)
            grad = gblk[s] + norm_back(summed, xhat, inverse, vec[1:2, :])
            gblk[s] = grad
            mid_copy(s).start()
            small[3:4, :] += column_sum(grad)
            tok_q[s] = grad.astype(BF)
            mix_copy(s).start()
        if k < 2:
            ring.spread(*ends(k, s), s)
        else:

            @pl.when(s < SEQS - 1)
            def _():
                ring.spread(*ends(k, s), s)


    def halo(s):
        for half in range(2):

            @pl.when(at.z > 0)
            def _():
                near_copy(s, half).wait_recv()

            @pl.when((at.z > 0) & (at.z < 3))
            def _():
                far_copy(s, half).start()

        @pl.when((at.z > 0) & (at.z < 3) & (s < 3))
        def _():
            near_start(s + 1)

    def step_p0(s):
        for half in range(2):

            @pl.when(at.z < 3)
            def _():
                near_copy(s, half).wait_send()

            @pl.when((at.z > 0) & (at.z < 3))
            def _():
                far_copy(s, half).wait_send()

            @pl.when(at.z > 1)
            def _():
                far_copy(s, half).wait_recv()

        kv_out(s).start()
        q[s] = ((matmul(act[s], wqkv[0], 1, 0) + vec[7:8, 0:256]) * 0.125).astype(BF)
        lane = lax.broadcasted_iota(jnp.int32, (1, LOCAL), 1) // HD
        slot = lax.broadcasted_iota(jnp.int32, (1, 128), 1)
        keys = kv.at[s].reshape(3 * GROUP, 2 * LOCAL)
        here_segs = segk.at[:, aligned(at.z * GROUP, 3 * GROUP)]
        which = lax.broadcasted_iota(jnp.int32, (8, SPAN), 0) == s

        def block(b, carry):
            start = pl.multiple_of(b * HALF, HALF)
            here = pl.ds(start, HALF)
            span = pl.ds(start, SPAN)
            seg_row = jnp.sum(
                jnp.where(which, here_segs[:, span], 0.0), axis=0, keepdims=True
            )
            columns = lse[s, here]
            bias[...] = allowed_bias(columns[:, 5:6], seg_row)
            query = q[s, here]
            k_block = keys[span, 0:LOCAL]
            v_block = keys[span, LOCAL:]
            mixed = jnp.zeros((HALF, LOCAL), F32)
            logs = columns
            for h in range(LOCAL // HD):
                one = jnp.where(lane == h, query, jnp.zeros_like(query))
                scores = matmul(one, k_block, 1, 1) + bias[...]
                top = jnp.max(scores, axis=-1, keepdims=True)
                weights = jnp.exp(scores - top)
                whole = jnp.sum(weights, axis=-1, keepdims=True)
                part = matmul(weights.astype(BF), v_block, 1, 0) / whole
                mixed = jnp.where(lane == h, part, mixed)
                logs = jnp.where(slot == h, top + jnp.log(whole), logs)
            att[s, here] = mixed.astype(BF)
            lse[s, here] = logs
            return carry

        lax.fori_loop(0, 2, block, 0)
        for copy in head_copies(s):
            copy.start()
        send[s] = matmul(att[s], wout[...], 1, 0).astype(BF)
        ring.rs_core(s).start()

    def step_p1(s):
        ring.step_u(*ends(0, s), s)

        @pl.when(s == 0)
        def _():
            weight_wait(2)

        for part in range(2):
            here = pl.ds(part * 256, 256)
            h = matmul(n2[s, here], wfc1[...], 1, 0) + vec[3:4, :]
            t = jnp.tanh(0.7978845608028654 * (h + 0.044715 * h * h * h))
            act[s, here] = (0.5 * h * (1.0 + t)).astype(BF)
            slope[s, here] = (
                0.5 * (1.0 + t)
                + 0.5 * h * (1.0 - t * t) * (0.7978845608028654 * (1.0 + 0.134145 * h * h))
            ).astype(BF)

        @pl.when(s == 0)
        def _():
            weight_wait(3)

        send[s] = matmul(act[s], wfc2[...], 1, 0).astype(BF)
        ring.rs_core(s).start()

    def step_p2(s):
        ring.step_u(*ends(1, s), s)
        out = pltpu.make_async_copy(blk.at[s], out_h.at[s], out_sem)
        out.start()
        for copy in block_copies(s):
            copy.wait()
        out.wait()
        for part in range(2):
            here = pl.ds(part * 256, 256)
            difference = blk[s, here].astype(F32) - stage[0, here].astype(F32)
            scaled = lse[s, here, 4:5] * factor()
            down = (stage[1, here].astype(F32) + scaled * difference).astype(BF)
            blk[s, here] = down
            up = matmul(down, wfc2[...], 1, 1) * slope[s, here].astype(F32)
            rounded = up.astype(BF)
            slope[s, here] = rounded
            small[4:5, :] += column_sum(rounded.astype(F32))

        @pl.when(s < 3)
        def _():
            for copy in block_copies(s + 1):
                copy.start()

        send[s] = matmul(slope[s], wfc1[...], 1, 1).astype(BF)
        ring.rs_core(s).start()

    deep = lambda ref: ref.reshape(SEQS * GROUP, 1024)

    def down_out():
        return pltpu.make_async_copy(deep(send).at[0:1024], gfc2, in_sems.at[0])

    def up_out():
        return pltpu.make_async_copy(deep(act).at[0:1024], gfc1, in_sems.at[1])

    def step_gdown(s):
        deep(send)[0:1024, :] = matmul(deep(act)[...], deep(blk)[...], 0, 0).astype(BF)
        down_out().start()

    def step_gup(s):
        deep(act)[0:1024, :] = matmul(deep(n2)[...], deep(slope)[...], 0, 0).astype(BF)
        up_out().start()

    actions = {
        "A": step_a,
        "H": halo,
        "C": step_count,
        "D": step_counted,
        "W": lambda s: weight_wait(s),
        "P0": step_p0,
        "P1": step_p1,
        "P2": step_p2,
        "Q": ring.step_q,
        "gdown": step_gdown,
        "gup": step_gup,
    }
    for k in range(3):
        actions[f"R{k}"] = functools.partial(step_r, k)
        actions[f"T{k}"] = lambda s, k=k: ring.step_t(*ends(k, s), s)
    kept = (
        pltpu.make_async_copy(wqkv, wqkv_h, keep_sem.at[0]),
        pltpu.make_async_copy(wout, wout_h, keep_sem.at[1]),
    )

    def step_weights(s):
        for i in (4, 1):
            weight_wait(i)
        for copy in kept:
            copy.start()

    actions["W"] = lambda s: None
    actions["V"] = step_weights
    run_order(actions, FRONT_ORDER)
    for s in range(SEQS):
        if s < SEQS - 1:
            ring.step_u(*ends(2, s), s)
        mix_copy(s).wait()
        kv_out(s).wait()
        mid_copy(s).wait()
        for copy in head_copies(s):
            copy.wait()
    down_out().wait()
    up_out().wait()
    for copy in kept:
        copy.wait()


def front_call(nf, *args):
    anys = pl.BlockSpec(memory_space=pl.ANY)
    vmem = pl.BlockSpec(memory_space=pltpu.VMEM)
    dma = pltpu.SemaphoreType.DMA
    big = lambda *lead: pltpu.VMEM((*lead, GROUP, 1024), BF)
    shape = jax.ShapeDtypeStruct
    return pl.pallas_call(
        functools.partial(front_kernel, nf),
        out_shape=(
            shape((SEQS, GROUP, 1024), BF),
            shape((SEQS, GROUP, 1024), BF),
            shape((SEQS, QUARTER, 1024), F32),
            shape((1024, 1024), BF),
            shape((1024, 1024), BF),
            shape((8, 1024), F32),
            shape((SEQS, GROUP, LOCAL), BF),
            shape((SEQS, GROUP, LOCAL), BF),
            shape((SEQS, 3, GROUP, 2 * LOCAL), BF),
            shape((SEQS, GROUP, 128), F32),
            shape((SEQS, GROUP, 1024), BF),
            shape((3, 1024, LOCAL), BF),
            shape((LOCAL, 1024), BF),
        ),
        in_specs=[anys] * 7 + [vmem] * 10,
        out_specs=(anys, anys, anys, anys, anys, vmem, anys, anys, anys, anys, anys, anys, anys),
        scratch_shapes=[
            pltpu.VMEM((3, 1024, LOCAL), BF),
            pltpu.VMEM((LOCAL, 1024), BF),
            pltpu.VMEM((1024, 1024), BF),
            pltpu.VMEM((1024, 1024), BF),
            big(SEQS),
            big(SEQS),
            big(SEQS),
            big(SEQS),
            big(SEQS),
            pltpu.VMEM((SEQS, HALF, 1024), BF),
            pltpu.VMEM((SEQS, QUARTER, 1024), BF),
            pltpu.VMEM((SEQS, QUARTER, 1024), BF),
            pltpu.VMEM((SEQS, QUARTER, 1024), F32),
            pltpu.VMEM((SEQS, QUARTER, 1024), F32),
            pltpu.VMEM((SEQS, QUARTER, 1024), BF),
            pltpu.VMEM((SEQS, QUARTER, 1024), BF),
            pltpu.VMEM((SEQS, QUARTER, 1024), BF),
            big(2),
            pltpu.VMEM((8, 3072), F32),
            pltpu.VMEM((HALF, SPAN), F32),
            pltpu.VMEM((SEQS, 3, GROUP, 2 * LOCAL), BF),
            pltpu.VMEM((4 + nf, 8, 128), F32),
            dma((5, nf - 1)),
            dma((5, nf - 1)),
            dma((5,)),
            dma((5, 2, SEQS)),
            dma((3,)),
            dma((2,)),
            dma((SEQS,)),
            dma,
            dma((SEQS,)),
            dma((2, SEQS, 2)),
            dma((2, SEQS, 2)),
            dma((2, 3)),
            dma((2, nf - 1)),
            dma((SEQS,)),
            dma((2,)),
            pltpu.VMEM((8, 1024), F32),
            pltpu.VMEM((8, 1024), F32),
            pltpu.VMEM((nf - 1, 8, 1024), F32),
            dma((2, nf - 1)),
            pltpu.VMEM((SEQS, GROUP, LOCAL), BF),
            pltpu.VMEM((SEQS, GROUP, LOCAL), BF),
            pltpu.VMEM((SEQS, GROUP, 128), F32),
            dma((3, SEQS)),
            dma((SEQS,)),
        ],
        compiler_params=pltpu.CompilerParams(
            collective_id=1, has_side_effects=True, vmem_limit_bytes=63 * 2**20
        ),
        cost_estimate=pl.CostEstimate(
            flops=2 * 2048 * 1024 * 1024 * 9, bytes_accessed=30 * 2**20, transcendentals=0
        ),
        name="front",
    )(*args)


class Reduce:
    def __init__(self, at, cut, size, rows, full, arrived, shard, half, quarter, sems):
        self.at, self.cut, self.size, self.rows = at, cut, size, rows
        self.full, self.arrived, self.shard = full, arrived, shard
        self.half, self.quarter = half, quarter
        self.x_sems, self.z_sems = sems
        self.a, self.b = lax.rem(at.z, 2), at.z // 2
        self.side = (at.f, at.z + 1 - 2 * self.a, at.t)
        self.across = (at.f, lax.rem(at.z + 2, 4), at.t)

    def own(self, f):
        return self.cut(self.full, aligned(f * self.size, self.size, math.gcd(self.size, 128)))

    def part(self, ref, start, size):
        where = aligned(start, size, 16)
        return ref.at[:, where, :] if len(ref.shape) == 3 else ref.at[where, :]

    def x_copy(self, j):
        there = lax.rem(self.at.f + 1 + j, self.at.nf)
        pair = (self.x_sems.at[0, j], self.x_sems.at[1, j])
        return remote(self.own(there), self.arrived.at[j], pair, self.at.peers_f[j])

    def z_copy(self, stage):
        h, q = self.rows // 2, self.rows // 4
        pair = (self.z_sems.at[0, stage], self.z_sems.at[1, stage])
        own = self.own(self.at.f)
        if stage == 0:
            return remote(self.part(own, (1 - self.a) * h, h), self.half, pair, self.side)
        if stage == 1:
            src = self.part(own, self.a * h + (1 - self.b) * q, q)
            return remote(src, self.quarter, pair, self.across)
        if stage == 2:
            kept = self.part(self.shard, self.a * h + self.b * q, q)
            return remote(kept, kept, pair, self.across)
        kept = self.part(self.shard, self.a * h, h)
        return remote(kept, kept, pair, self.side)

    def add(self, target, first, others):
        total = first[...].astype(F32)
        for other in others:
            total = total + other[...].astype(F32)
        target[...] = total.astype(BF)

    def run(self, stage):
        h, q = self.rows // 2, self.rows // 4
        peers = range(self.at.nf - 1)
        own = self.own(self.at.f)
        if stage == 0:
            for j in peers:
                self.x_copy(j).start()
            return
        if stage == 1:
            for j in peers:
                self.x_copy(j).wait()
            self.add(own, own, [self.arrived.at[j] for j in peers])
        else:
            self.z_copy(stage - 2).wait()
        if stage == 2:
            kept = self.part(own, self.a * h, h)
            self.add(kept, kept, [self.half])
        elif stage == 3:
            start = self.a * h + self.b * q
            self.add(self.part(self.shard, start, q), self.part(own, start, q), [self.quarter])
        if stage < 5:
            self.z_copy(stage - 1).start()


BACK_ORDER = (
    ("E", 0),
    ("K0", 0),
    ("K0", 1),
    ("K0", 2),
    ("E", 1),
    ("L", 0),
    ("E", 2),
    ("I", 0),
    ("K1", 0),
    ("K1", 1),
    ("I", 1),
    ("K0", 3),
    ("K2", 0),
    ("E", 3),
    ("K3", 0),
    ("K1", 2),
    ("K2", 1),
    ("I", 2),
    ("K4", 0),
    ("F", 0),
    ("K1", 3),
    ("I", 3),
    ("K3", 1),
    ("K2", 2),
    ("Q", 0),
    ("F", 1),
    ("B0", 0),
    ("K4", 1),
    ("K2", 3),
    ("Q", 1),
    ("D1", 0),
    ("R", 0),
    ("F", 2),
    ("D1", 1),
    ("K3", 2),
    ("B1", 0),
    ("F", 3),
    ("Q", 2),
    ("K3", 3),
    ("D1", 2),
    ("C0", 0),
    ("D2", 1),
    ("D1", 3),
    ("B2", 0),
    ("D2", 0),
    ("Q", 3),
    ("K4", 2),
    ("C1", 0),
    ("R", 1),
    ("D1", 4),
    ("R", 2),
    ("D2", 2),
    ("B3", 0),
    ("D3", 1),
    ("D2", 3),
    ("R", 3),
    ("S0", 0),
    ("D3", 0),
    ("C2", 0),
    ("K4", 3),
    ("D1", 5),
    ("T", 2),
    ("D2", 4),
    ("S1", 0),
    ("S2", 0),
    ("D3", 3),
    ("C3", 0),
    ("B4", 0),
    ("D3", 4),
    ("S3", 0),
    ("D1", 7),
    ("D3", 2),
    ("D2", 5),
    ("D1", 6),
    ("C4", 0),
    ("D2", 7),
    ("T", 3),
    ("D2", 6),
    ("S4", 0),
    ("B5", 0),
    ("D3", 7),
    ("T", 0),
    ("D3", 5),
    ("C5", 0),
    ("T", 1),
    ("S5", 0),
    ("D3", 6),
)


class Chain(Reduce):
    def piece(self, ref, half):
        return self.part(ref, half * (self.rows // 2), self.rows // 2)

    def x_half(self, j, half):
        there = lax.rem(self.at.f + 1 + j, self.at.nf)
        pair = (self.x_sems.at[0, j, half], self.x_sems.at[1, j, half])
        src = self.piece(self.own(there), half)
        return remote(src, self.piece(self.arrived.at[j], half), pair, self.at.peers_f[j])

    def up_copy(self, half):
        pair = (self.z_sems.at[0, half], self.z_sems.at[1, half])
        src = self.piece(self.own(self.at.f), half)
        return remote(src, self.piece(self.shard, half), pair, self.at.up)

    def down_copy(self, half, j):
        q = self.rows // 4
        part = self.part(self.shard, half * (self.rows // 2) + j * q, q)
        which = 2 + half * 2 + j
        pair = (self.z_sems.at[0, which], self.z_sems.at[1, which])
        return remote(part, part, pair, self.at.down)

    def climb(self, stage, half):
        own = self.piece(self.own(self.at.f), half)
        peers = range(self.at.nf - 1)
        if stage == 0:
            for j in peers:
                self.x_half(j, half).start()
            return
        if stage == 1:
            for j in peers:
                self.x_half(j, half).wait()
            self.add(own, own, [self.piece(self.arrived.at[j], half) for j in peers])

        @pl.when(self.at.z == stage - 1)
        def _():
            shard = self.piece(self.shard, half)
            if stage > 1:
                self.up_copy(half).wait_recv()
                self.add(own if stage < 4 else shard, own, [shard])
            if stage < 4:
                self.up_copy(half).start()
            else:
                for j in range(2):
                    self.down_copy(half, j).start()

    def hand_down(self, hop, half, j):
        @pl.when(self.at.z == 3 - hop)
        def _():
            self.down_copy(half, j).wait_recv()
            if hop < 3:
                self.down_copy(half, j).start()

    def finish(self):
        for half in range(2):

            @pl.when(self.at.z < 3)
            def _():
                self.up_copy(half).wait_send()

            @pl.when(self.at.z > 0)
            def _():
                for j in range(2):
                    self.down_copy(half, j).wait_send()


def back_kernel(
    nf,
    gmix_h,
    gmid_h,
    gfc1_h,
    gfc2_h,
    att_h,
    q_h,
    kv_h,
    lse_h,
    n1_h,
    tokens,
    wqkv_h,
    wout,
    segs,
    sums_one,
    ig_h,
    small,
    s_qkv,
    s_out,
    s_fc1,
    s_fc2,
    gm,
    gm_last,
    kvs,
    n1s,
    ga,
    dq,
    dots,
    bias,
    segk,
    dkvt,
    dfar,
    dnear,
    down,
    m1,
    m2,
    gq,
    send,
    recv_c,
    send_y,
    recv_y,
    gmid,
    tok_q,
    a_qkv,
    a_out,
    f_qkv,
    f_fc1,
    f_fc2,
    x_qkv,
    x_out,
    x_fc1,
    x_fc2,
    h_qkv,
    h_out,
    k_qkv,
    k_out,
    ring_sems,
    load_sems,
    last_sem,
    first_sems,
    m1_sems,
    m2_sems,
    red_x,
    red_z,
    chain_x,
    chain_z,
    got_core,
    got_y,
    got_f,
    got_z,
    sum_sems,
    sum_f_sems,
    n1e,
    att,
    q,
    lse,
    wqkv,
    head_sems,
    w_sem,
):
    at = Place(nf)
    ring = Ring(at, send, recv_c, send_y, recv_y, ring_sems)
    mine = aligned(at.mine, QUARTER)
    rows_cut = lambda ref, where: ref.at[where, :]
    cols_cut = lambda ref, where: ref.at[:, where]
    deep_cut = lambda ref, where: ref.at[:, where, :]
    fs = 1024 // nf
    f_out = gm.at[0:LOCAL]

    def reducer(i, cut, rows, full, arrived, shard, half, quarter, kind=Reduce):
        sems = (chain_x.at[i - 2], chain_z.at[i - 2]) if kind is Chain else (red_x.at[i], red_z.at[i])
        return kind(at, cut, fs, rows, full, arrived, shard, half, quarter, sems)

    first, rest = pl.ds(0, 1), pl.ds(1, 2)
    red_q = reducer(
        0, deep_cut, fs, f_qkv.at[first], x_qkv.at[:, first], s_qkv.at[first], h_qkv.at[first], k_qkv.at[first]
    )
    red_kv = reducer(
        4, deep_cut, fs, f_qkv.at[rest], x_qkv.at[:, rest], s_qkv.at[rest], h_qkv.at[rest], k_qkv.at[rest]
    )
    red_out = reducer(1, cols_cut, LOCAL, f_out, x_out, s_out, h_out, k_out)
    red_fc1 = reducer(2, rows_cut, fs, f_fc1, x_fc1, s_fc1, None, None, Chain)
    red_fc2 = reducer(3, cols_cut, 1024, f_fc2, x_fc2, s_fc2, None, None, Chain)

    firsts = (
        (gfc1_h, f_fc1),
        (gfc2_h, f_fc2),
        (gmid_h.at[0], gmid),
        (tokens.at[:, mine, :], tok_q),
    )

    def first_copy_of(i):
        return pltpu.make_async_copy(gfc1_h, f_fc1, first_sems.at[i])

    def first_copy(i):
        return pltpu.make_async_copy(firsts[i][0], firsts[i][1], first_sems.at[i])

    def mix_load(s):
        return pltpu.make_async_copy(gmix_h.at[s], gm, load_sems.at[0, 0])

    def kv_load(s):
        return pltpu.make_async_copy(kv_h.at[s], kvs, load_sems.at[1, 0])

    last = SEQS - 1
    over = aligned(at.over_y, QUARTER)
    last_own = pltpu.make_async_copy(gmix_h.at[last, mine], gm_last.at[mine], last_sem)
    last_y = remote(gmix_h.at[last, mine], gm_last.at[mine], ring.pair(2, last), at.mate_y)
    last_c = remote(gmix_h.at[last, mine], gm_last.at[mine], ring.pair(3, last), at.mate_c)
    last_over = remote(gm_last.at[over], gm_last.at[over], ring.pair(4, last), at.mate_c)

    def step_last(s):
        last_y.wait()
        last_over.start()

    def norm_load(s):
        return pltpu.make_async_copy(n1_h.at[s], n1s, load_sems.at[2, 0])

    def norm_early(s):
        return pltpu.make_async_copy(n1_h.at[s], n1e, load_sems.at[0, 1])

    def mid_load(s):
        return pltpu.make_async_copy(gmid_h.at[s], gmid, load_sems.at[2, 1])

    def head_loads(s):
        pairs = ((att_h, att), (q_h, q), (lse_h, lse))
        return [
            pltpu.make_async_copy(source.at[s], target.at[s], head_sems.at[i, s])
            for i, (source, target) in enumerate(pairs)
        ]

    w_load = pltpu.make_async_copy(wqkv_h, wqkv, w_sem)
    mix_load(0).start()
    kv_load(0).start()
    for copy in head_loads(0):
        copy.start()
    at.barrier()
    for copy in (last_own, last_y, last_c):
        copy.start()
    for s in range(1, SEQS):
        for copy in head_loads(s):
            copy.start()
    w_load.start()
    for i in range(4):
        first_copy(i).start()
    norm_load(0).start()
    norm_early(0).start()

    segk[...] = jnp.full(segk.shape, -1.0, F32)
    segk[0:4, 1024:3072] = segs[...].astype(F32)
    small[...] = jnp.zeros_like(small)
    def m1_copy(s):
        return remote(dfar.at[lax.rem(s, 2)], m1.at[s], (m1_sems.at[0, s], m1_sems.at[1, s]), at.down)

    def m2_copy(s):
        return remote(dnear.at[s], m2.at[s], (m2_sems.at[0, s], m2_sems.at[1, s]), at.down)

    def step_e(s):
        kv_load(s).wait()
        for copy in head_loads(s):
            copy.wait()

        @pl.when(s < last)
        def _():
            mix_load(s).wait()

        @pl.when(s == last)
        def _():
            for copy in (last_own, last_c, last_over):
                copy.wait()
            gm[...] = gm_last[...]

        ga[...] = matmul(gm[...], wout[...], 1, 1).astype(BF)
        lane = lax.broadcasted_iota(jnp.int32, (1, LOCAL), 1) // HD
        keys = kvs.reshape(3 * GROUP, 2 * LOCAL)
        here_segs = segk.at[:, aligned(at.z * GROUP, 3 * GROUP)]
        dkvt[...] = jnp.zeros_like(dkvt)

        def pairs(b, low, size, first):
            here, span = pl.ds(b * HALF, HALF), pl.ds(low, size)
            which = lax.broadcasted_iota(jnp.int32, (8, size), 0) == s
            seg_row = jnp.sum(
                jnp.where(which, here_segs[:, span], 0.0), axis=0, keepdims=True
            )
            logs = lse[s, here]
            bias[:, 0:size] = allowed_bias(logs[:, 5:6], seg_row, low - b * HALF, size)
            query = q[s, here]
            grad = ga[here]
            k_block = keys[span, 0:LOCAL]
            v_block = keys[span, LOCAL:]
            dots[0] = jnp.transpose(query)
            dots[1] = jnp.transpose(grad)
            product = grad.astype(F32) * att[s, here].astype(F32)
            grad_query = jnp.zeros((HALF, LOCAL), F32) if first else dq[here]
            for h in range(LOCAL // HD):
                mine_h = lane == h
                one = jnp.where(mine_h, query, jnp.zeros_like(query))
                grad_one = jnp.where(mine_h, grad, jnp.zeros_like(grad))
                delta = jnp.sum(jnp.where(mine_h, product, 0.0), axis=-1, keepdims=True)
                scores = matmul(one, k_block, 1, 1) + bias[:, 0:size]
                probs = jnp.exp(scores - logs[:, h : h + 1])
                dprobs = matmul(grad_one, v_block, 1, 1)
                grad_scores = (probs * (dprobs - delta)).astype(BF)
                part = matmul(grad_scores, k_block, 1, 0)
                grad_query = jnp.where(mine_h, grad_query + part, grad_query)
                k_rows = pl.ds(h * HD, HD)
                v_rows = pl.ds(LOCAL + h * HD, HD)
                dkvt[k_rows, span] += matmul(dots[0, k_rows], grad_scores, 1, 0)
                dkvt[v_rows, span] += matmul(dots[1, k_rows], probs.astype(BF), 1, 0)
            if first:
                dq[here] = grad_query
            else:
                gq[s, here] = (grad_query * 0.125).astype(BF)

        def turned(i):
            return jnp.transpose(dkvt[:, i * GROUP : (i + 1) * GROUP].astype(BF))

        pairs(0, 0, GROUP, True)
        pairs(1, HALF, HALF, True)

        @pl.when((at.z > 1) & (s > 1))
        def _():
            m1_copy(s - 2).wait_send()

        dfar[lax.rem(s, 2)] = turned(0)

        @pl.when(at.z > 1)
        def _():
            m1_copy(s).start()

        @pl.when(s == 0)
        def _():
            a_qkv[...] = jnp.zeros_like(a_qkv)
            a_out[...] = jnp.zeros_like(a_out)

        pairs(0, GROUP, SPAN - GROUP, False)
        pairs(1, GROUP, SPAN - HALF, False)
        dnear[s] = turned(1)
        down[s] = turned(2)
        a_out[...] += matmul(att[s], gm[...], 0, 0)

        @pl.when(s < last)
        def _():
            kv_load(s + 1).start()

        @pl.when(s < last - 1)
        def _():
            mix_load(s + 1).start()

        norm_early(s).wait()
        a_qkv[0] += matmul(n1e[...], gq[s], 0, 0)

        @pl.when(s < 3)
        def _():
            norm_early(s + 1).start()

    def step_i(s):
        @pl.when((at.z > 0) & (at.z < 3))
        def _():
            m1_copy(s).wait_recv()
            dnear[s] = (dnear[s].astype(F32) + m1[s].astype(F32)).astype(BF)

        @pl.when(at.z > 0)
        def _():
            m2_copy(s).start()

    def step_f(s):
        @pl.when(at.z < 3)
        def _():
            m2_copy(s).wait_recv()
            down[s] = (down[s].astype(F32) + m2[s].astype(F32)).astype(BF)

        norm_load(s).wait()
        @pl.when(s == 0)
        def _():
            w_load.wait()

        grads = (gq[s], down[s, :, 0:LOCAL], down[s, :, LOCAL:])
        send[s] = (
            matmul(grads[0], wqkv[0], 1, 1)
            + matmul(grads[1], wqkv[1], 1, 1)
            + matmul(grads[2], wqkv[2], 1, 1)
        ).astype(BF)
        ring.rs_core(s).start()
        normed = n1s[...]
        for i in (1, 2):
            a_qkv[i] += matmul(normed, grads[i], 0, 0)

        @pl.when(s < 3)
        def _():
            norm_load(s + 1).start()

        small[9:10, 0:LOCAL] += column_sum(grads[0].astype(F32))
        small[9:10, LOCAL : 2 * LOCAL] += column_sum(grads[2].astype(F32))

    def ends(s):
        return tok_q.at[s], ig_h

    def ig_copy(s):
        return pltpu.make_async_copy(tok_q.at[s], ig_h.at[s, mine], first_sems.at[s])

    def step_r(s):
        @pl.when(s == 0)
        def _():
            first_copy(2).wait()
            first_copy(3).wait()

        summed = ring.total(s)
        xhat, inverse = norm_parts(tok_q[s].astype(F32))
        small[0:1, :] += column_sum(summed * xhat)
        small[1:2, :] += column_sum(summed)
        @pl.when(s > 0)
        def _():
            mid_load(s).wait()

        grad = gmid[...] + norm_back(summed, xhat, inverse, sums_one[7:8, :])
        tok_q[s] = grad.astype(BF)

        @pl.when(s < 3)
        def _():
            mid_load(s + 1).start()

        ig_copy(s).start()
        ring.spread(*ends(s), s)

    def sum_copy(stage, j=0):
        pair = (sum_sems.at[0, stage], sum_sems.at[1, stage])
        top = small.at[0:8]
        if stage == 0:
            return remote(top, got_core, pair, at.mate_c)
        if stage == 1:
            return remote(top, got_y, pair, at.mate_y)
        if stage == 2:
            pair = (sum_f_sems.at[0, j], sum_f_sems.at[1, j])
            return remote(small, got_f.at[j], pair, at.peers_f[j])
        mate = red_q.side if stage == 3 else red_q.across
        return remote(small, got_z.at[stage - 3], pair, mate)

    def step_sum(stage, s):
        if stage == 0:
            small[2:6, :] = sums_one[0:4, :]
            small[6:7, :] = sums_one[5:6, :]
            small[8:9, :] = sums_one[4:5, :]
        elif stage == 3:
            for j in range(nf - 1):
                sum_copy(2, j).wait()
            for j in range(nf - 1):
                small[...] += got_f[j]
        else:
            sum_copy(stage - 1).wait()
            if stage == 1:
                small[0:8, :] += got_core[...]
            elif stage == 2:
                small[0:8, :] += got_y[...]
            else:
                small[...] += got_z[stage - 4]
        if stage == 2:
            for j in range(nf - 1):
                sum_copy(2, j).start()
        elif stage < 5:
            sum_copy(stage).start()

    def step_group(group, stage, s):
        if stage == 0:
            if group == "B":
                f_out[...] = a_out[...].astype(BF)
                f_qkv[0] = a_qkv[0].astype(BF)
            elif group == "C":
                for i in (1, 2):
                    f_qkv[i] = a_qkv[i].astype(BF)
        for reduce in groups[group]:
            reduce.run(stage)

    groups = {"B": (red_out, red_q), "C": (red_kv,)}
    chains = (red_fc2, red_fc1)
    actions = {
        "E": step_e,
        "L": step_last,
        "I": step_i,
        "F": step_f,
        "Q": ring.step_q,
        "R": step_r,
        "T": lambda s: ring.step_t(*ends(s), s),
    }
    for stage in range(6):
        actions[f"S{stage}"] = functools.partial(step_sum, stage)
        for group in groups:
            actions[f"{group}{stage}"] = functools.partial(step_group, group, stage)

    def step_climb(stage, s):
        if stage == 0:

            @pl.when(lax.rem(s, 2) == 0)
            def _():
                first_copy_of(1 - s // 2).wait()

        for i, chain in enumerate(chains):

            @pl.when(s // 2 == i)
            def _(chain=chain):
                chain.climb(stage, lax.rem(s, 2))

    def step_down(hop, s):
        for i, chain in enumerate(chains):

            @pl.when(s // 4 == i)
            def _(chain=chain):
                chain.hand_down(hop, lax.rem(s // 2, 2), lax.rem(s, 2))

    for stage in range(5):
        actions[f"K{stage}"] = functools.partial(step_climb, stage)
    for hop in (1, 2, 3):
        actions[f"D{hop}"] = functools.partial(step_down, hop)
    run_order(actions, BACK_ORDER)
    for chain in chains:
        chain.finish()
    for s in range(SEQS):
        ring.step_u(*ends(s), s)
        ig_copy(s).wait()

        if s > 1:

            @pl.when(at.z > 1)
            def _():
                m1_copy(s).wait_send()

        @pl.when(at.z > 0)
        def _():
            m2_copy(s).wait_send()


def back_call(nf, *args):
    anys = pl.BlockSpec(memory_space=pl.ANY)
    vmem = pl.BlockSpec(memory_space=pltpu.VMEM)
    dma = pltpu.SemaphoreType.DMA
    big = lambda *lead: pltpu.VMEM((*lead, GROUP, 1024), BF)
    shape = jax.ShapeDtypeStruct
    fs = 1024 // nf
    low = lambda *dims: pltpu.VMEM(dims, BF)
    return pl.pallas_call(
        functools.partial(back_kernel, nf),
        out_shape=(
            shape((SEQS, GROUP, 1024), BF),
            shape((16, 1024), F32),
            shape((3, fs, LOCAL), BF),
            shape((LOCAL, fs), BF),
            shape((fs, 1024), BF),
            shape((1024, fs), BF),
        ),
        in_specs=[anys] * 11 + [vmem, vmem, vmem],
        out_specs=(anys, vmem, vmem, vmem, vmem, vmem),
        scratch_shapes=[
            low(GROUP, 1024),
            low(GROUP, 1024),
            low(3, GROUP, 2 * LOCAL),
            low(GROUP, 1024),
            low(GROUP, LOCAL),
            pltpu.VMEM((GROUP, LOCAL), F32),
            low(2, LOCAL, HALF),
            pltpu.VMEM((HALF, SPAN), F32),
            pltpu.VMEM((8, 3072), F32),
            pltpu.VMEM((2 * LOCAL, 3 * GROUP), F32),
            low(2, GROUP, 2 * LOCAL),
            low(SEQS, GROUP, 2 * LOCAL),
            low(SEQS, GROUP, 2 * LOCAL),
            low(SEQS, GROUP, 2 * LOCAL),
            low(SEQS, GROUP, 2 * LOCAL),
            low(SEQS, GROUP, LOCAL),
            big(SEQS),
            low(SEQS, HALF, 1024),
            low(SEQS, QUARTER, 1024),
            low(SEQS, QUARTER, 1024),
            pltpu.VMEM((QUARTER, 1024), F32),
            low(SEQS, QUARTER, 1024),
            pltpu.VMEM((3, 1024, LOCAL), F32),
            pltpu.VMEM((LOCAL, 1024), F32),
            low(3, 1024, LOCAL),
            low(1024, 1024),
            low(1024, 1024),
            low(nf - 1, 3, fs, LOCAL),
            low(nf - 1, LOCAL, fs),
            low(nf - 1, fs, 1024),
            low(nf - 1, 1024, fs),
            low(3, fs // 2, LOCAL),
            low(LOCAL // 2, fs),
            low(3, fs // 4, LOCAL),
            low(LOCAL // 4, fs),
            dma((5, 2, SEQS)),
            dma((3, 2)),
            dma,
            dma((4,)),
            dma((2, SEQS)),
            dma((2, SEQS)),
            dma((5, 2, nf - 1)),
            dma((5, 2, 4)),
            dma((2, 2, nf - 1, 2)),
            dma((2, 2, 6)),
            pltpu.VMEM((8, 1024), F32),
            pltpu.VMEM((8, 1024), F32),
            pltpu.VMEM((nf - 1, 16, 1024), F32),
            pltpu.VMEM((2, 16, 1024), F32),
            dma((2, 5)),
            dma((2, nf - 1)),
            low(GROUP, 1024),
            low(SEQS, GROUP, LOCAL),
            low(SEQS, GROUP, LOCAL),
            pltpu.VMEM((SEQS, GROUP, 128), F32),
            low(3, 1024, LOCAL),
            dma((3, SEQS)),
            dma,
        ],
        compiler_params=pltpu.CompilerParams(
            collective_id=2, has_side_effects=True, vmem_limit_bytes=63 * 2**20
        ),
        cost_estimate=pl.CostEstimate(
            flops=2 * 2048 * 1024 * 1024 * 6, bytes_accessed=30 * 2**20, transcendentals=0
        ),
        name="back",
    )(*args)


def finish_kernel(
    nf,
    out_in,
    ig_in,
    sums,
    sums_one,
    s_qkv,
    s_out,
    s_fc1,
    s_fc2,
    out,
    loss,
    ig,
    g_g1,
    g_b1,
    g_qkv,
    g_qv,
    g_out,
    g_bo,
    g_g2,
    g_b2,
    g_fc1,
    g_up,
    g_fc2,
    g_bd,
    low,
    wide_qkv,
    wide_out,
    wide_fc1,
    wide_fc2,
    low_qkv,
    low_out,
    low_fc1,
    low_fc2,
    in_sems,
    out_sems,
):
    shards = (
        (s_fc1, low_fc1, wide_fc1, g_fc1),
        (s_fc2, low_fc2, wide_fc2, g_fc2),
        (s_qkv, low_qkv, wide_qkv, g_qkv),
        (s_out, low_out, wide_out, g_out),
    )
    inward, outward = [], []
    for i, (source, kept, widened, target) in enumerate(shards):
        inward.append(pltpu.make_async_copy(source, kept, in_sems.at[i]))
        outward.append(pltpu.make_async_copy(widened, target, out_sems.at[i]))
    for i, (source, target) in enumerate(((out_in, out), (ig_in, ig))):
        for s in range(SEQS):
            which = 4 + i * SEQS + s
            inward.append(
                pltpu.make_async_copy(source.at[s], low.at[i, s], in_sems.at[which])
            )
            outward.append(
                pltpu.make_async_copy(low.at[i, s], target.at[s], out_sems.at[which])
            )
    for copy in inward:
        copy.start()
    for i, (_, kept, widened, _) in enumerate(shards):
        inward[i].wait()
        widened[...] = kept[...].astype(F32)
        outward[i].start()
    for i in range(4, len(inward)):
        inward[i].wait()
        outward[i].start()
    place = lax.axis_index("fsdp")
    fs = g_g1.shape[0]
    here = aligned(place * fs, fs)
    for i, target in enumerate((g_g1, g_b1, g_bd, g_g2, g_b2, g_bo)):
        target[...] = sums[i : i + 1, here].reshape(fs)
    scale = 1.0 / (2.0 * D * sums_one[6:7, 0:1])
    loss[...] = jnp.sum(sums[6:7, :], axis=1, keepdims=True) * scale
    own = sums[8:16, :]
    wide = g_up.shape[1]
    up = pltpu.roll(own, lax.rem(1024 - place * wide, 1024), 1)
    for i in range(g_up.shape[0]):
        g_up[i : i + 1, :] = up[0:1, i * nf * wide : i * nf * wide + wide]
    wide = g_qv.shape[2]
    qv = pltpu.roll(own, lax.rem(1024 - place * wide, 1024), 1)
    for i in range(2):
        for h in range(LOCAL // HD):
            start = i * LOCAL + h * HD
            g_qv[i, h : h + 1, :] = qv[1:2, start : start + wide]
    for copy in outward:
        copy.wait()


def finish_call(nf, *args):
    anys = pl.BlockSpec(memory_space=pl.ANY)
    vmem = pl.BlockSpec(memory_space=pltpu.VMEM)
    shape = jax.ShapeDtypeStruct
    fs = 1024 // nf
    block = shape((SEQS, GROUP, 1024), BF)
    row = shape((fs,), F32)
    return pl.pallas_call(
        functools.partial(finish_kernel, nf),
        out_shape=(
            block,
            shape((1, 1), F32),
            block,
            row,
            row,
            shape((3, fs, LOCAL), F32),
            shape((2, LOCAL // HD, HD // nf), F32),
            shape((LOCAL, fs), F32),
            row,
            row,
            row,
            shape((fs, 1024), F32),
            shape((4, 256 // nf), F32),
            shape((1024, fs), F32),
            row,
        ),
        in_specs=[anys, anys, vmem, vmem] + [anys] * 4,
        out_specs=(anys, vmem, anys, vmem, vmem, anys, vmem, anys)
        + (vmem, vmem, vmem, anys, vmem, anys, vmem),
        scratch_shapes=[
            pltpu.VMEM((2, SEQS, GROUP, 1024), BF),
            pltpu.VMEM((3, fs, LOCAL), F32),
            pltpu.VMEM((LOCAL, fs), F32),
            pltpu.VMEM((fs, 1024), F32),
            pltpu.VMEM((1024, fs), F32),
            pltpu.VMEM((3, fs, LOCAL), BF),
            pltpu.VMEM((LOCAL, fs), BF),
            pltpu.VMEM((fs, 1024), BF),
            pltpu.VMEM((1024, fs), BF),
            pltpu.SemaphoreType.DMA((4 + 2 * SEQS,)),
            pltpu.SemaphoreType.DMA((4 + 2 * SEQS,)),
        ],
        compiler_params=pltpu.CompilerParams(vmem_limit_bytes=63 * 2**20),
        name="finish",
    )(*args)


def local(
    tokens,
    cotangent,
    teacher,
    valid_mask,
    segment_ids,
    ln1_gain,
    ln1_bias,
    w_qkv,
    b_qv,
    w_out,
    b_out,
    ln2_gain,
    ln2_bias,
    w_fc1,
    b_fc1,
    w_fc2,
    b_fc2,
):
    nf = lax.axis_size("fsdp")
    front = front_call(
        nf,
        w_qkv,
        w_out,
        w_fc1,
        w_fc2,
        tokens,
        teacher,
        cotangent,
        b_out,
        ln2_gain,
        ln2_bias,
        b_fc2,
        ln1_gain,
        ln1_bias,
        b_qv,
        b_fc1,
        valid_mask,
        segment_ids,
    )
    (output, grad_mix, grad_middle, gfc1, gfc2, sums_one, att, q, kv, lse, n1, wqkv, wout) = front
    input_grad, everything, s_qkv, s_out, s_fc1, s_fc2 = back_call(
        nf, grad_mix, grad_middle, gfc1, gfc2, att, q, kv, lse, n1, tokens, wqkv, wout, segment_ids, sums_one
    )
    results = finish_call(
        nf, output, input_grad, everything, sums_one, s_qkv, s_out, s_fc1, s_fc2
    )
    return (results[0], results[1].reshape(()), *results[2:])


def solution(mesh):
    return jax.shard_map(
        local,
        mesh=mesh,
        in_specs=(
            P("fsdp", "context", None),
            P("fsdp", "context", None),
            P("fsdp", "context", None),
            P("fsdp", "context"),
            P("fsdp", None),
            P("fsdp"),
            P("fsdp"),
            P(None, "fsdp", "tensor"),
            P(None, "tensor", "fsdp"),
            P("tensor", "fsdp"),
            P("fsdp"),
            P("fsdp"),
            P("fsdp"),
            P("fsdp", "tensor"),
            P("tensor", "fsdp"),
            P("tensor", "fsdp"),
            P("fsdp"),
        ),
        out_specs=(
            P("fsdp", "context", None),
            P(),
            P("fsdp", "context", None),
            P("fsdp"),
            P("fsdp"),
            P(None, "fsdp", "tensor"),
            P(None, "tensor", "fsdp"),
            P("tensor", "fsdp"),
            P("fsdp"),
            P("fsdp"),
            P("fsdp"),
            P("fsdp", "tensor"),
            P("tensor", "fsdp"),
            P("tensor", "fsdp"),
            P("fsdp"),
        ),
        check_vma=False,
    )
```

```python
import functools
import math

import jax
import jax.numpy as jnp
from jax import lax
from jax.experimental import pallas as pl
from jax.experimental.pallas import tpu as pltpu
from jax.sharding import PartitionSpec as P

MESH = pl.DeviceIdType.MESH
BF = jnp.bfloat16
F32 = jnp.float32
D = 1024
HD = 64
WINDOW = 1024
EPSILON = 1e-05
MASKED = -1e30
SEQS = 4
GROUP = 512
QUARTER = 128
HALF = 256
SPAN = 1280
LOCAL = 256


def matmul(left, right, over_left, over_right):
    dims = (((over_left,), (over_right,)), ((), ()))
    return lax.dot_general(left, right, dims, preferred_element_type=F32)


def norm_parts(values):
    mean = jnp.mean(values, axis=-1, keepdims=True)
    center = values - mean
    spread = jnp.mean(center * center, axis=-1, keepdims=True)
    inverse = lax.rsqrt(spread + EPSILON)
    return center * inverse, inverse


def norm_back(grad_normed, xhat, inverse, gain):
    e = grad_normed * gain
    return inverse * (
        e
        - jnp.mean(e, axis=-1, keepdims=True)
        - xhat * jnp.mean(e * xhat, axis=-1, keepdims=True)
    )


def column_sum(values):
    return jnp.sum(values, axis=0, keepdims=True)


def aligned(start, size, unit=128):
    return pl.ds(pl.multiple_of(start, unit), size)


def allowed_bias(query_seg, key_seg, skipped=0, size=SPAN):
    column = lax.broadcasted_iota(jnp.int32, (HALF, size), 1) + skipped
    ahead = column - lax.broadcasted_iota(jnp.int32, (HALF, size), 0)
    allowed = (ahead > 0) & (ahead <= WINDOW) & (query_seg == key_seg)
    return jnp.where(allowed, 0.0, MASKED)


class Place:
    def __init__(self, nf):
        self.nf = nf
        self.f = lax.axis_index("fsdp")
        self.z = lax.axis_index("context")
        self.t = lax.axis_index("tensor")
        self.y, self.c = self.t // 2, lax.rem(self.t, 2)
        self.mate_c = (self.f, self.z, self.t + 1 - 2 * self.c)
        self.mate_y = (self.f, self.z, lax.rem(self.t + 2, 4))
        self.mine = (2 * self.c + self.y) * QUARTER
        self.over_y = (2 * self.c + 1 - self.y) * QUARTER
        self.peers_f = [(lax.rem(self.f + j, nf), self.z, self.t) for j in range(1, nf)]
        self.peers_z = [(self.f, lax.rem(self.z + j, 4), self.t) for j in range(1, 4)]
        self.up = (self.f, lax.rem(self.z + 1, 4), self.t)
        self.down = (self.f, lax.rem(self.z + 3, 4), self.t)

    def barrier(self):
        semaphore = pltpu.get_barrier_semaphore()
        everyone = [self.mate_c, self.mate_y] + self.peers_f + self.peers_z
        for peer in everyone:
            pl.semaphore_signal(semaphore, inc=1, device_id=peer, device_id_type=MESH)
        pl.semaphore_wait(semaphore, len(everyone))


def remote(src, dst, pair, mate):
    return pltpu.make_async_remote_copy(
        src, dst, pair[0], pair[1], device_id=mate, device_id_type=MESH
    )


def run_order(actions, order):
    names = list(actions)
    codes = [names.index(name) * 8 + s for name, s in order]

    def step(i, carry):
        code = jnp.int32(codes[0])
        for j, other in enumerate(codes[1:]):
            code = jnp.where(i == j + 1, other, code)
        kind, s = code // 8, lax.rem(code, 8)
        for j, name in enumerate(names):

            @pl.when(kind == j)
            def _(action=actions[name]):
                action(s)

        return carry

    lax.fori_loop(0, len(order), step, 0)


class Ring:
    def __init__(self, at, send, recv_c, send_y, recv_y, sems):
        self.at, self.send, self.recv_c = at, send, recv_c
        self.send_y, self.recv_y, self.sems = send_y, recv_y, sems

    def pair(self, which, s):
        return self.sems.at[which, 0, s], self.sems.at[which, 1, s]

    def rs_core(self, s):
        half = aligned((1 - self.at.c) * HALF, HALF)
        return remote(self.send.at[s, half], self.recv_c.at[s], self.pair(0, s), self.at.mate_c)

    def rs_y(self, s):
        return remote(self.send_y.at[s], self.recv_y.at[s], self.pair(1, s), self.at.mate_y)

    def back_y(self, src, dst, s):
        return remote(
            src, dst.at[s, aligned(self.at.mine, QUARTER)], self.pair(2, s), self.at.mate_y
        )

    def back_own(self, src, dst, s):
        return remote(
            src, dst.at[s, aligned(self.at.mine, QUARTER)], self.pair(3, s), self.at.mate_c
        )

    def back_over(self, dst, s):
        there = dst.at[s, aligned(self.at.over_y, QUARTER)]
        return remote(there, there, self.pair(4, s), self.at.mate_c)

    def step_q(self, s):
        self.rs_core(s).wait()
        self.send_y[s] = (
            self.send[s, aligned(self.at.over_y, QUARTER)].astype(F32)
            + self.recv_c[s, aligned((1 - self.at.y) * QUARTER, QUARTER)].astype(F32)
        ).astype(BF)
        self.rs_y(s).start()

    def total(self, s):
        self.rs_y(s).wait()
        return (
            self.send[s, aligned(self.at.mine, QUARTER)].astype(F32)
            + self.recv_c[s, aligned(self.at.y * QUARTER, QUARTER)].astype(F32)
            + self.recv_y[s].astype(F32)
        )

    def spread(self, src, dst, s):
        self.back_y(src, dst, s).start()
        self.back_own(src, dst, s).start()

    def step_t(self, src, dst, s):
        self.back_y(src, dst, s).wait()
        self.back_over(dst, s).start()

    def step_u(self, src, dst, s):
        self.back_own(src, dst, s).wait()
        self.back_over(dst, s).wait()


FRONT_ORDER = (
    ("A", 0),
    ("A", 1),
    ("H", 0),
    ("A", 2),
    ("V", 0),
    ("P0", 0),
    ("A", 3),
    ("C", 0),
    ("Q", 0),
    ("H", 1),
    ("R0", 0),
    ("P0", 1),
    ("T0", 0),
    ("H", 2),
    ("Q", 1),
    ("D", 0),
    ("W", 0),
    ("P1", 0),
    ("Q", 0),
    ("R0", 1),
    ("P0", 2),
    ("R1", 0),
    ("T0", 1),
    ("Q", 2),
    ("H", 3),
    ("P1", 1),
    ("Q", 1),
    ("R0", 2),
    ("P0", 3),
    ("R1", 1),
    ("Q", 3),
    ("T0", 2),
    ("P1", 2),
    ("T1", 0),
    ("T1", 1),
    ("Q", 2),
    ("P2", 0),
    ("R0", 3),
    ("P2", 1),
    ("Q", 0),
    ("T0", 3),
    ("R1", 2),
    ("P1", 3),
    ("Q", 3),
    ("T1", 2),
    ("Q", 1),
    ("P2", 2),
    ("R1", 3),
    ("R2", 1),
    ("Q", 2),
    ("T1", 3),
    ("P2", 3),
    ("R2", 0),
    ("Q", 3),
    ("R2", 2),
    ("gdown", 0),
    ("T2", 0),
    ("T2", 1),
    ("gup", 0),
    ("T2", 2),
    ("R2", 3),
)


def front_kernel(
    nf,
    wqkv_s,
    wout_s,
    wfc1_s,
    wfc2_s,
    tokens,
    teacher,
    cot,
    part_bo,
    part_g2,
    part_b2,
    part_bd,
    part_g1,
    part_b1,
    part_qv,
    part_up,
    mask,
    segs,
    out_h,
    gmix_h,
    gmid_h,
    gfc1,
    gfc2,
    small,
    att_h,
    q_h,
    kv_h,
    lse_h,
    n1_h,
    wqkv_h,
    wout_h,
    wqkv,
    wout,
    wfc1,
    wfc2,
    n2,
    blk,
    act,
    slope,
    send,
    recv_c,
    send_y,
    recv_y,
    mid,
    gblk,
    tok_q,
    tea_q,
    cot_q,
    stage,
    segk,
    bias,
    kv,
    cnt,
    w_send,
    w_recv,
    w_loc,
    ring_sems,
    q_sems,
    in_sems,
    n1_sem,
    out_sem,
    mix_sem,
    near_sems,
    far_sems,
    cz_sems,
    cf_sems,
    res_sem,
    keep_sem,
    vec,
    vec_own,
    vec_got,
    v_sems,
    att,
    q,
    lse,
    head_sems,
    mid_sems,
):
    at = Place(nf)
    at.barrier()
    ring = Ring(at, send, recv_c, send_y, recv_y, ring_sems)
    mine = aligned(at.mine, QUARTER)

    fs = wout_s.shape[1]
    own = aligned(at.f * fs, fs)
    query, pair_kv = pl.ds(0, 1), pl.ds(1, 2)
    places = (
        (wqkv_s.at[pair_kv], wqkv.at[pair_kv, own, :]),
        (wout_s, wout.at[:, own]),
        (wfc1_s, wfc1.at[own, :]),
        (wfc2_s, wfc2.at[:, own]),
        (wqkv_s.at[query], wqkv.at[query, own, :]),
    )

    def weight_copy(i, j):
        pair = (w_send.at[i, j], w_recv.at[i, j])
        return remote(places[i][0], places[i][1], pair, at.peers_f[j])

    def weight_start(i):
        for j in range(nf - 1):
            weight_copy(i, j).start()
        pltpu.make_async_copy(places[i][0], places[i][1], w_loc.at[i]).start()

    def weight_wait(i):
        pltpu.make_async_copy(places[i][0], places[i][1], w_loc.at[i]).wait()
        for j in range(nf - 1):
            weight_copy(i, j).wait()

    weight_start(0)

    def token_copy(s):
        slot = lax.rem(s, 2)
        return pltpu.make_async_copy(tokens.at[s], stage.at[slot], in_sems.at[slot])

    token_copy(0).start()
    quarters = ((tokens, tok_q), (teacher, tea_q), (cot, cot_q))
    for i, (source, target) in enumerate(quarters):
        pltpu.make_async_copy(source.at[:, mine, :], target, q_sems.at[i]).start()

    vec_own[...] = jnp.zeros_like(vec_own)
    rows = ((0, part_bo), (1, part_g2), (2, part_b2), (4, part_bd), (5, part_g1), (6, part_b1))
    for i, part in rows:
        vec_own[i : i + 1, own] = part[...].astype(F32).reshape(1, fs)

    def scatter(part, count):
        wide = part.shape[1]
        unit = wide * nf
        column = lax.broadcasted_iota(jnp.int32, (wide, count * unit), 1)
        inside = lax.broadcasted_iota(jnp.int32, (wide, count * unit), 0) + at.f * wide
        spread = (lax.rem(column, unit) == inside).astype(BF)
        full = matmul(part, spread, 1, 0)
        group = lax.broadcasted_iota(jnp.int32, full.shape, 1) // unit
        owner = lax.broadcasted_iota(jnp.int32, full.shape, 0)
        return jnp.sum(jnp.where(group == owner, full, 0.0), axis=0, keepdims=True)

    vec_own[3:4, :] = scatter(part_up[...], part_up.shape[0])
    for i in range(2):
        columns = pl.ds(i * LOCAL, LOCAL)
        vec_own[7:8, columns] = scatter(part_qv[i], part_qv.shape[1])

    def vec_copy(j):
        pair = (v_sems.at[0, j], v_sems.at[1, j])
        return remote(vec_own, vec_got.at[j], pair, at.peers_f[j])

    for j in range(nf - 1):
        vec_copy(j).start()

    valid = mask[...].astype(F32)
    masks = jnp.concatenate([valid, jnp.zeros_like(valid)], axis=0)
    cnt[0] = jnp.broadcast_to(jnp.sum(masks, keepdims=True), (8, 128))

    def count_z(j):
        pair = (cz_sems.at[0, j], cz_sems.at[1, j])
        return remote(cnt.at[0], cnt.at[1 + j], pair, at.peers_z[j])

    def count_f(j):
        pair = (cf_sems.at[0, j], cf_sems.at[1, j])
        return remote(cnt.at[4], cnt.at[5 + j], pair, at.peers_f[j])

    for j in range(3):
        count_z(j).start()

    turned = jnp.transpose(masks)
    segk[...] = jnp.full(segk.shape, -1.0, F32)
    segk[0:4, 1024:3072] = segs[...].astype(F32)
    seg_turned = jnp.transpose(segk[:, aligned(1024 + at.z * GROUP, GROUP)])
    column = lax.broadcasted_iota(jnp.int32, (1, 128), 1)
    for s in range(SEQS):
        lse[s] = jnp.where(column == 4, turned[:, s : s + 1], seg_turned[:, s : s + 1])
    small[...] = jnp.zeros_like(small)
    @pl.when(at.z < 2)
    def _():
        def clear(s, carry):
            kv[s, 0] = jnp.zeros((GROUP, 2 * LOCAL), BF)
            return carry

        lax.fori_loop(0, SEQS, clear, 0)

    @pl.when(at.z < 1)
    def _():
        def clear(s, carry):
            kv[s, 1] = jnp.zeros((GROUP, 2 * LOCAL), BF)
            return carry

        lax.fori_loop(0, SEQS, clear, 0)

    def near_copy(s, half):
        part = pl.ds(half * HALF, HALF)
        pair = (near_sems.at[0, s, half], near_sems.at[1, s, half])
        return remote(kv.at[s, 2, part], kv.at[s, 1, part], pair, at.up)

    def far_copy(s, half):
        part = pl.ds(half * HALF, HALF)
        pair = (far_sems.at[0, s, half], far_sems.at[1, s, half])
        return remote(kv.at[s, 1, part], kv.at[s, 0, part], pair, at.up)

    def near_start(s):
        for half in range(2):
            near_copy(s, half).start()

    def norm_copy(s):
        return pltpu.make_async_copy(act.at[s], n1_h.at[s], n1_sem.at[s])

    def step_norm(s, carry):
        token_copy(s).wait()

        @pl.when(s < 3)
        def _():
            token_copy(s + 1).start()

        for part in range(2):
            here = pl.ds(part * 256, 256)
            xhat, _ = norm_parts(stage[lax.rem(s, 2), here].astype(F32))
            act[s, here] = (xhat * vec[5:6, :] + vec[6:7, :]).astype(BF)
        norm_copy(s).start()
        return carry

    def step_a(s):
        normed = act[s]
        kv[s, 2, :, 0:LOCAL] = matmul(normed, wqkv[1], 1, 0).astype(BF)
        kv[s, 2, :, LOCAL:] = (matmul(normed, wqkv[2], 1, 0) + vec[7:8, 256:512]).astype(BF)

        @pl.when((at.z < 3) & ((at.z == 0) | (s == 0)))
        def _():
            near_start(s)

    for j in range(nf - 1):
        vec_copy(j).wait()
    whole = vec_own[...]
    for j in range(nf - 1):
        whole = whole + vec_got[j]
    vec[...] = whole
    small[7:8, :] = vec[5:6, :]
    lax.fori_loop(0, SEQS, step_norm, 0)
    weight_wait(0)
    for i in (4, 1, 2, 3):
        weight_start(i)
    for i, (source, target) in enumerate(quarters):
        pltpu.make_async_copy(source.at[:, mine, :], target, q_sems.at[i]).wait()

    def step_count(s):
        for j in range(3):
            count_z(j).wait()
        cnt[4] = cnt[0] + cnt[1] + cnt[2] + cnt[3]
        for j in range(nf - 1):
            count_f(j).start()

    def step_counted(s):
        for j in range(nf - 1):
            count_f(j).wait()
        total_count = cnt[4]
        for j in range(nf - 1):
            total_count = total_count + cnt[5 + j]
        small[6:7, 0:128] = total_count[0:1, :]
        cnt[0] = (SEQS * GROUP * nf * 4) / total_count
        for i in range(SEQS):
            norm_copy(i).wait()
        for copy in block_copies(0):
            copy.start()

    def factor():
        return cnt[0, 0:1, 0:1]

    def block_copies(s):
        return (
            pltpu.make_async_copy(teacher.at[s], stage.at[0], in_sems.at[0]),
            pltpu.make_async_copy(cot.at[s], stage.at[1], in_sems.at[1]),
        )

    def kv_out(s):
        return pltpu.make_async_copy(kv.at[s], kv_h.at[s], res_sem.at[s])

    def head_copies(s):
        pairs = ((att, att_h), (q, q_h), (lse, lse_h))
        return [
            pltpu.make_async_copy(source.at[s], target.at[s], head_sems.at[i, s])
            for i, (source, target) in enumerate(pairs)
        ]

    def mid_copy(s):
        return pltpu.make_async_copy(gblk.at[s], gmid_h.at[s], mid_sems.at[s])

    def mix_copy(s):
        return pltpu.make_async_copy(tok_q.at[s], gmix_h.at[s, mine], mix_sem.at[s])

    def ends(k, s):
        if k == 2:
            return tok_q.at[s], gmix_h
        target = (n2, blk)[k]
        return target.at[s, mine], target

    def step_r(k, s):
        summed = ring.total(s)
        if k == 0:
            middle = tok_q[s].astype(F32) + summed + vec[0:1, :]
            mid[s] = middle
            xhat, _ = norm_parts(middle)
            n2[s, mine] = (xhat * vec[1:2, :] + vec[2:3, :]).astype(BF)
        elif k == 1:
            block = mid[s] + summed + vec[4:5, :]
            blk[s, mine] = block.astype(BF)
            difference = block - tea_q[s].astype(F32)
            masked = lse[s, mine, 4:5] * difference
            small[5:6, :] += column_sum(masked * difference)
            grad = cot_q[s].astype(F32) + masked * factor()
            gblk[s] = grad
            small[0:1, :] += column_sum(grad)
        else:
            xhat, inverse = norm_parts(mid[s])
            small[1:2, :] += column_sum(summed * xhat)
            small[2:3, :] += column_sum(summed)
            grad = gblk[s] + norm_back(summed, xhat, inverse, vec[1:2, :])
            gblk[s] = grad
            mid_copy(s).start()
            small[3:4, :] += column_sum(grad)
            tok_q[s] = grad.astype(BF)
            mix_copy(s).start()
        if k < 2:
            ring.spread(*ends(k, s), s)
        else:

            @pl.when(s < SEQS - 1)
            def _():
                ring.spread(*ends(k, s), s)


    def halo(s):
        for half in range(2):

            @pl.when(at.z > 0)
            def _():
                near_copy(s, half).wait_recv()

            @pl.when((at.z > 0) & (at.z < 3))
            def _():
                far_copy(s, half).start()

        @pl.when((at.z > 0) & (at.z < 3) & (s < 3))
        def _():
            near_start(s + 1)

    def step_p0(s):
        for half in range(2):

            @pl.when(at.z < 3)
            def _():
                near_copy(s, half).wait_send()

            @pl.when((at.z > 0) & (at.z < 3))
            def _():
                far_copy(s, half).wait_send()

            @pl.when(at.z > 1)
            def _():
                far_copy(s, half).wait_recv()

        kv_out(s).start()
        q[s] = ((matmul(act[s], wqkv[0], 1, 0) + vec[7:8, 0:256]) * 0.125).astype(BF)
        lane = lax.broadcasted_iota(jnp.int32, (1, LOCAL), 1) // HD
        slot = lax.broadcasted_iota(jnp.int32, (1, 128), 1)
        keys = kv.at[s].reshape(3 * GROUP, 2 * LOCAL)
        here_segs = segk.at[:, aligned(at.z * GROUP, 3 * GROUP)]
        which = lax.broadcasted_iota(jnp.int32, (8, SPAN), 0) == s

        def block(b, carry):
            start = pl.multiple_of(b * HALF, HALF)
            here = pl.ds(start, HALF)
            span = pl.ds(start, SPAN)
            seg_row = jnp.sum(
                jnp.where(which, here_segs[:, span], 0.0), axis=0, keepdims=True
            )
            columns = lse[s, here]
            bias[...] = allowed_bias(columns[:, 5:6], seg_row)
            query = q[s, here]
            k_block = keys[span, 0:LOCAL]
            v_block = keys[span, LOCAL:]
            mixed = jnp.zeros((HALF, LOCAL), F32)
            logs = columns
            for h in range(LOCAL // HD):
                one = jnp.where(lane == h, query, jnp.zeros_like(query))
                scores = matmul(one, k_block, 1, 1) + bias[...]
                top = jnp.max(scores, axis=-1, keepdims=True)
                weights = jnp.exp(scores - top)
                whole = jnp.sum(weights, axis=-1, keepdims=True)
                part = matmul(weights.astype(BF), v_block, 1, 0) / whole
                mixed = jnp.where(lane == h, part, mixed)
                logs = jnp.where(slot == h, top + jnp.log(whole), logs)
            att[s, here] = mixed.astype(BF)
            lse[s, here] = logs
            return carry

        lax.fori_loop(0, 2, block, 0)
        for copy in head_copies(s):
            copy.start()
        send[s] = matmul(att[s], wout[...], 1, 0).astype(BF)
        ring.rs_core(s).start()

    def step_p1(s):
        ring.step_u(*ends(0, s), s)

        @pl.when(s == 0)
        def _():
            weight_wait(2)

        for part in range(2):
            here = pl.ds(part * 256, 256)
            h = matmul(n2[s, here], wfc1[...], 1, 0) + vec[3:4, :]
            t = jnp.tanh(0.7978845608028654 * (h + 0.044715 * h * h * h))
            act[s, here] = (0.5 * h * (1.0 + t)).astype(BF)
            slope[s, here] = (
                0.5 * (1.0 + t)
                + 0.5 * h * (1.0 - t * t) * (0.7978845608028654 * (1.0 + 0.134145 * h * h))
            ).astype(BF)

        @pl.when(s == 0)
        def _():
            weight_wait(3)

        send[s] = matmul(act[s], wfc2[...], 1, 0).astype(BF)
        ring.rs_core(s).start()

    def step_p2(s):
        ring.step_u(*ends(1, s), s)
        out = pltpu.make_async_copy(blk.at[s], out_h.at[s], out_sem)
        out.start()
        for copy in block_copies(s):
            copy.wait()
        out.wait()
        for part in range(2):
            here = pl.ds(part * 256, 256)
            difference = blk[s, here].astype(F32) - stage[0, here].astype(F32)
            scaled = lse[s, here, 4:5] * factor()
            down = (stage[1, here].astype(F32) + scaled * difference).astype(BF)
            blk[s, here] = down
            up = matmul(down, wfc2[...], 1, 1) * slope[s, here].astype(F32)
            rounded = up.astype(BF)
            slope[s, here] = rounded
            small[4:5, :] += column_sum(rounded.astype(F32))

        @pl.when(s < 3)
        def _():
            for copy in block_copies(s + 1):
                copy.start()

        send[s] = matmul(slope[s], wfc1[...], 1, 1).astype(BF)
        ring.rs_core(s).start()

    deep = lambda ref: ref.reshape(SEQS * GROUP, 1024)

    def down_out():
        return pltpu.make_async_copy(deep(send).at[0:1024], gfc2, in_sems.at[0])

    def up_out():
        return pltpu.make_async_copy(deep(act).at[0:1024], gfc1, in_sems.at[1])

    def step_gdown(s):
        deep(send)[0:1024, :] = matmul(deep(act)[...], deep(blk)[...], 0, 0).astype(BF)
        down_out().start()

    def step_gup(s):
        deep(act)[0:1024, :] = matmul(deep(n2)[...], deep(slope)[...], 0, 0).astype(BF)
        up_out().start()

    actions = {
        "A": step_a,
        "H": halo,
        "C": step_count,
        "D": step_counted,
        "W": lambda s: weight_wait(s),
        "P0": step_p0,
        "P1": step_p1,
        "P2": step_p2,
        "Q": ring.step_q,
        "gdown": step_gdown,
        "gup": step_gup,
    }
    for k in range(3):
        actions[f"R{k}"] = functools.partial(step_r, k)
        actions[f"T{k}"] = lambda s, k=k: ring.step_t(*ends(k, s), s)
    kept = (
        pltpu.make_async_copy(wqkv, wqkv_h, keep_sem.at[0]),
        pltpu.make_async_copy(wout, wout_h, keep_sem.at[1]),
    )

    def step_weights(s):
        for i in (4, 1):
            weight_wait(i)
        for copy in kept:
            copy.start()

    actions["W"] = lambda s: None
    actions["V"] = step_weights
    run_order(actions, FRONT_ORDER)
    for s in range(SEQS):
        if s < SEQS - 1:
            ring.step_u(*ends(2, s), s)
        mix_copy(s).wait()
        kv_out(s).wait()
        mid_copy(s).wait()
        for copy in head_copies(s):
            copy.wait()
    down_out().wait()
    up_out().wait()
    for copy in kept:
        copy.wait()


def front_call(nf, *args):
    anys = pl.BlockSpec(memory_space=pl.ANY)
    vmem = pl.BlockSpec(memory_space=pltpu.VMEM)
    dma = pltpu.SemaphoreType.DMA
    big = lambda *lead: pltpu.VMEM((*lead, GROUP, 1024), BF)
    shape = jax.ShapeDtypeStruct
    return pl.pallas_call(
        functools.partial(front_kernel, nf),
        out_shape=(
            shape((SEQS, GROUP, 1024), BF),
            shape((SEQS, GROUP, 1024), BF),
            shape((SEQS, QUARTER, 1024), F32),
            shape((1024, 1024), BF),
            shape((1024, 1024), BF),
            shape((8, 1024), F32),
            shape((SEQS, GROUP, LOCAL), BF),
            shape((SEQS, GROUP, LOCAL), BF),
            shape((SEQS, 3, GROUP, 2 * LOCAL), BF),
            shape((SEQS, GROUP, 128), F32),
            shape((SEQS, GROUP, 1024), BF),
            shape((3, 1024, LOCAL), BF),
            shape((LOCAL, 1024), BF),
        ),
        in_specs=[anys] * 7 + [vmem] * 10,
        out_specs=(anys, anys, anys, anys, anys, vmem, anys, anys, anys, anys, anys, anys, anys),
        scratch_shapes=[
            pltpu.VMEM((3, 1024, LOCAL), BF),
            pltpu.VMEM((LOCAL, 1024), BF),
            pltpu.VMEM((1024, 1024), BF),
            pltpu.VMEM((1024, 1024), BF),
            big(SEQS),
            big(SEQS),
            big(SEQS),
            big(SEQS),
            big(SEQS),
            pltpu.VMEM((SEQS, HALF, 1024), BF),
            pltpu.VMEM((SEQS, QUARTER, 1024), BF),
            pltpu.VMEM((SEQS, QUARTER, 1024), BF),
            pltpu.VMEM((SEQS, QUARTER, 1024), F32),
            pltpu.VMEM((SEQS, QUARTER, 1024), F32),
            pltpu.VMEM((SEQS, QUARTER, 1024), BF),
            pltpu.VMEM((SEQS, QUARTER, 1024), BF),
            pltpu.VMEM((SEQS, QUARTER, 1024), BF),
            big(2),
            pltpu.VMEM((8, 3072), F32),
            pltpu.VMEM((HALF, SPAN), F32),
            pltpu.VMEM((SEQS, 3, GROUP, 2 * LOCAL), BF),
            pltpu.VMEM((4 + nf, 8, 128), F32),
            dma((5, nf - 1)),
            dma((5, nf - 1)),
            dma((5,)),
            dma((5, 2, SEQS)),
            dma((3,)),
            dma((2,)),
            dma((SEQS,)),
            dma,
            dma((SEQS,)),
            dma((2, SEQS, 2)),
            dma((2, SEQS, 2)),
            dma((2, 3)),
            dma((2, nf - 1)),
            dma((SEQS,)),
            dma((2,)),
            pltpu.VMEM((8, 1024), F32),
            pltpu.VMEM((8, 1024), F32),
            pltpu.VMEM((nf - 1, 8, 1024), F32),
            dma((2, nf - 1)),
            pltpu.VMEM((SEQS, GROUP, LOCAL), BF),
            pltpu.VMEM((SEQS, GROUP, LOCAL), BF),
            pltpu.VMEM((SEQS, GROUP, 128), F32),
            dma((3, SEQS)),
            dma((SEQS,)),
        ],
        compiler_params=pltpu.CompilerParams(
            collective_id=1, has_side_effects=True, vmem_limit_bytes=63 * 2**20
        ),
        cost_estimate=pl.CostEstimate(
            flops=2 * 2048 * 1024 * 1024 * 9, bytes_accessed=30 * 2**20, transcendentals=0
        ),
        name="front",
    )(*args)


class Reduce:
    def __init__(self, at, cut, size, rows, full, arrived, shard, half, quarter, sems):
        self.at, self.cut, self.size, self.rows = at, cut, size, rows
        self.full, self.arrived, self.shard = full, arrived, shard
        self.half, self.quarter = half, quarter
        self.x_sems, self.z_sems = sems
        self.a, self.b = lax.rem(at.z, 2), at.z // 2
        self.side = (at.f, at.z + 1 - 2 * self.a, at.t)
        self.across = (at.f, lax.rem(at.z + 2, 4), at.t)

    def own(self, f):
        return self.cut(self.full, aligned(f * self.size, self.size, math.gcd(self.size, 128)))

    def part(self, ref, start, size):
        where = aligned(start, size, 16)
        return ref.at[:, where, :] if len(ref.shape) == 3 else ref.at[where, :]

    def x_copy(self, j):
        there = lax.rem(self.at.f + 1 + j, self.at.nf)
        pair = (self.x_sems.at[0, j], self.x_sems.at[1, j])
        return remote(self.own(there), self.arrived.at[j], pair, self.at.peers_f[j])

    def z_copy(self, stage):
        h, q = self.rows // 2, self.rows // 4
        pair = (self.z_sems.at[0, stage], self.z_sems.at[1, stage])
        own = self.own(self.at.f)
        if stage == 0:
            return remote(self.part(own, (1 - self.a) * h, h), self.half, pair, self.side)
        if stage == 1:
            src = self.part(own, self.a * h + (1 - self.b) * q, q)
            return remote(src, self.quarter, pair, self.across)
        if stage == 2:
            kept = self.part(self.shard, self.a * h + self.b * q, q)
            return remote(kept, kept, pair, self.across)
        kept = self.part(self.shard, self.a * h, h)
        return remote(kept, kept, pair, self.side)

    def add(self, target, first, others):
        total = first[...].astype(F32)
        for other in others:
            total = total + other[...].astype(F32)
        target[...] = total.astype(BF)

    def run(self, stage):
        h, q = self.rows // 2, self.rows // 4
        peers = range(self.at.nf - 1)
        own = self.own(self.at.f)
        if stage == 0:
            for j in peers:
                self.x_copy(j).start()
            return
        if stage == 1:
            for j in peers:
                self.x_copy(j).wait()
            self.add(own, own, [self.arrived.at[j] for j in peers])
        else:
            self.z_copy(stage - 2).wait()
        if stage == 2:
            kept = self.part(own, self.a * h, h)
            self.add(kept, kept, [self.half])
        elif stage == 3:
            start = self.a * h + self.b * q
            self.add(self.part(self.shard, start, q), self.part(own, start, q), [self.quarter])
        if stage < 5:
            self.z_copy(stage - 1).start()


BACK_ORDER = (
    ("E", 0),
    ("K0", 0),
    ("K0", 1),
    ("K0", 2),
    ("E", 1),
    ("L", 0),
    ("E", 2),
    ("I", 0),
    ("K1", 0),
    ("K1", 1),
    ("I", 1),
    ("K0", 3),
    ("K2", 0),
    ("E", 3),
    ("K3", 0),
    ("K1", 2),
    ("K2", 1),
    ("I", 2),
    ("K4", 0),
    ("F", 0),
    ("K1", 3),
    ("I", 3),
    ("K3", 1),
    ("K2", 2),
    ("Q", 0),
    ("F", 1),
    ("B0", 0),
    ("K4", 1),
    ("K2", 3),
    ("Q", 1),
    ("D1", 0),
    ("R", 0),
    ("F", 2),
    ("D1", 1),
    ("K3", 2),
    ("B1", 0),
    ("F", 3),
    ("Q", 2),
    ("K3", 3),
    ("D1", 2),
    ("C0", 0),
    ("D2", 1),
    ("D1", 3),
    ("B2", 0),
    ("D2", 0),
    ("Q", 3),
    ("K4", 2),
    ("C1", 0),
    ("R", 1),
    ("D1", 4),
    ("R", 2),
    ("D2", 2),
    ("B3", 0),
    ("D3", 1),
    ("D2", 3),
    ("R", 3),
    ("S0", 0),
    ("D3", 0),
    ("C2", 0),
    ("K4", 3),
    ("D1", 5),
    ("T", 2),
    ("D2", 4),
    ("S1", 0),
    ("S2", 0),
    ("D3", 3),
    ("C3", 0),
    ("B4", 0),
    ("D3", 4),
    ("S3", 0),
    ("D1", 7),
    ("D3", 2),
    ("D2", 5),
    ("D1", 6),
    ("C4", 0),
    ("D2", 7),
    ("T", 3),
    ("D2", 6),
    ("S4", 0),
    ("B5", 0),
    ("D3", 7),
    ("T", 0),
    ("D3", 5),
    ("C5", 0),
    ("T", 1),
    ("S5", 0),
    ("D3", 6),
)


class Chain(Reduce):
    def piece(self, ref, half):
        return self.part(ref, half * (self.rows // 2), self.rows // 2)

    def x_half(self, j, half):
        there = lax.rem(self.at.f + 1 + j, self.at.nf)
        pair = (self.x_sems.at[0, j, half], self.x_sems.at[1, j, half])
        src = self.piece(self.own(there), half)
        return remote(src, self.piece(self.arrived.at[j], half), pair, self.at.peers_f[j])

    def up_copy(self, half):
        pair = (self.z_sems.at[0, half], self.z_sems.at[1, half])
        src = self.piece(self.own(self.at.f), half)
        return remote(src, self.piece(self.shard, half), pair, self.at.up)

    def down_copy(self, half, j):
        q = self.rows // 4
        part = self.part(self.shard, half * (self.rows // 2) + j * q, q)
        which = 2 + half * 2 + j
        pair = (self.z_sems.at[0, which], self.z_sems.at[1, which])
        return remote(part, part, pair, self.at.down)

    def climb(self, stage, half):
        own = self.piece(self.own(self.at.f), half)
        peers = range(self.at.nf - 1)
        if stage == 0:
            for j in peers:
                self.x_half(j, half).start()
            return
        if stage == 1:
            for j in peers:
                self.x_half(j, half).wait()
            self.add(own, own, [self.piece(self.arrived.at[j], half) for j in peers])

        @pl.when(self.at.z == stage - 1)
        def _():
            shard = self.piece(self.shard, half)
            if stage > 1:
                self.up_copy(half).wait_recv()
                self.add(own if stage < 4 else shard, own, [shard])
            if stage < 4:
                self.up_copy(half).start()
            else:
                for j in range(2):
                    self.down_copy(half, j).start()

    def hand_down(self, hop, half, j):
        @pl.when(self.at.z == 3 - hop)
        def _():
            self.down_copy(half, j).wait_recv()
            if hop < 3:
                self.down_copy(half, j).start()

    def finish(self):
        for half in range(2):

            @pl.when(self.at.z < 3)
            def _():
                self.up_copy(half).wait_send()

            @pl.when(self.at.z > 0)
            def _():
                for j in range(2):
                    self.down_copy(half, j).wait_send()


def back_kernel(
    nf,
    gmix_h,
    gmid_h,
    gfc1_h,
    gfc2_h,
    att_h,
    q_h,
    kv_h,
    lse_h,
    n1_h,
    tokens,
    wqkv_h,
    wout,
    segs,
    sums_one,
    ig_h,
    small,
    s_qkv,
    s_out,
    s_fc1,
    s_fc2,
    gm,
    gm_last,
    kvs,
    n1s,
    ga,
    dq,
    dots,
    bias,
    segk,
    dkvt,
    dfar,
    dnear,
    down,
    m1,
    m2,
    gq,
    send,
    recv_c,
    send_y,
    recv_y,
    gmid,
    tok_q,
    a_qkv,
    a_out,
    f_qkv,
    f_fc1,
    f_fc2,
    x_qkv,
    x_out,
    x_fc1,
    x_fc2,
    h_qkv,
    h_out,
    k_qkv,
    k_out,
    ring_sems,
    load_sems,
    last_sem,
    first_sems,
    m1_sems,
    m2_sems,
    red_x,
    red_z,
    chain_x,
    chain_z,
    got_core,
    got_y,
    got_f,
    got_z,
    sum_sems,
    sum_f_sems,
    n1e,
    att,
    q,
    lse,
    wqkv,
    head_sems,
    w_sem,
):
    at = Place(nf)
    ring = Ring(at, send, recv_c, send_y, recv_y, ring_sems)
    mine = aligned(at.mine, QUARTER)
    rows_cut = lambda ref, where: ref.at[where, :]
    cols_cut = lambda ref, where: ref.at[:, where]
    deep_cut = lambda ref, where: ref.at[:, where, :]
    fs = 1024 // nf
    f_out = gm.at[0:LOCAL]

    def reducer(i, cut, rows, full, arrived, shard, half, quarter, kind=Reduce):
        sems = (chain_x.at[i - 2], chain_z.at[i - 2]) if kind is Chain else (red_x.at[i], red_z.at[i])
        return kind(at, cut, fs, rows, full, arrived, shard, half, quarter, sems)

    first, rest = pl.ds(0, 1), pl.ds(1, 2)
    red_q = reducer(
        0, deep_cut, fs, f_qkv.at[first], x_qkv.at[:, first], s_qkv.at[first], h_qkv.at[first], k_qkv.at[first]
    )
    red_kv = reducer(
        4, deep_cut, fs, f_qkv.at[rest], x_qkv.at[:, rest], s_qkv.at[rest], h_qkv.at[rest], k_qkv.at[rest]
    )
    red_out = reducer(1, cols_cut, LOCAL, f_out, x_out, s_out, h_out, k_out)
    red_fc1 = reducer(2, rows_cut, fs, f_fc1, x_fc1, s_fc1, None, None, Chain)
    red_fc2 = reducer(3, cols_cut, 1024, f_fc2, x_fc2, s_fc2, None, None, Chain)

    firsts = (
        (gfc1_h, f_fc1),
        (gfc2_h, f_fc2),
        (gmid_h.at[0], gmid),
        (tokens.at[:, mine, :], tok_q),
    )

    def first_copy_of(i):
        return pltpu.make_async_copy(gfc1_h, f_fc1, first_sems.at[i])

    def first_copy(i):
        return pltpu.make_async_copy(firsts[i][0], firsts[i][1], first_sems.at[i])

    def mix_load(s):
        return pltpu.make_async_copy(gmix_h.at[s], gm, load_sems.at[0, 0])

    def kv_load(s):
        return pltpu.make_async_copy(kv_h.at[s], kvs, load_sems.at[1, 0])

    last = SEQS - 1
    over = aligned(at.over_y, QUARTER)
    last_own = pltpu.make_async_copy(gmix_h.at[last, mine], gm_last.at[mine], last_sem)
    last_y = remote(gmix_h.at[last, mine], gm_last.at[mine], ring.pair(2, last), at.mate_y)
    last_c = remote(gmix_h.at[last, mine], gm_last.at[mine], ring.pair(3, last), at.mate_c)
    last_over = remote(gm_last.at[over], gm_last.at[over], ring.pair(4, last), at.mate_c)

    def step_last(s):
        last_y.wait()
        last_over.start()

    def norm_load(s):
        return pltpu.make_async_copy(n1_h.at[s], n1s, load_sems.at[2, 0])

    def norm_early(s):
        return pltpu.make_async_copy(n1_h.at[s], n1e, load_sems.at[0, 1])

    def mid_load(s):
        return pltpu.make_async_copy(gmid_h.at[s], gmid, load_sems.at[2, 1])

    def head_loads(s):
        pairs = ((att_h, att), (q_h, q), (lse_h, lse))
        return [
            pltpu.make_async_copy(source.at[s], target.at[s], head_sems.at[i, s])
            for i, (source, target) in enumerate(pairs)
        ]

    w_load = pltpu.make_async_copy(wqkv_h, wqkv, w_sem)
    mix_load(0).start()
    kv_load(0).start()
    for copy in head_loads(0):
        copy.start()
    at.barrier()
    for copy in (last_own, last_y, last_c):
        copy.start()
    for s in range(1, SEQS):
        for copy in head_loads(s):
            copy.start()
    w_load.start()
    for i in range(4):
        first_copy(i).start()
    norm_load(0).start()
    norm_early(0).start()

    segk[...] = jnp.full(segk.shape, -1.0, F32)
    segk[0:4, 1024:3072] = segs[...].astype(F32)
    small[...] = jnp.zeros_like(small)
    def m1_copy(s):
        return remote(dfar.at[lax.rem(s, 2)], m1.at[s], (m1_sems.at[0, s], m1_sems.at[1, s]), at.down)

    def m2_copy(s):
        return remote(dnear.at[s], m2.at[s], (m2_sems.at[0, s], m2_sems.at[1, s]), at.down)

    def step_e(s):
        kv_load(s).wait()
        for copy in head_loads(s):
            copy.wait()

        @pl.when(s < last)
        def _():
            mix_load(s).wait()

        @pl.when(s == last)
        def _():
            for copy in (last_own, last_c, last_over):
                copy.wait()
            gm[...] = gm_last[...]

        ga[...] = matmul(gm[...], wout[...], 1, 1).astype(BF)
        lane = lax.broadcasted_iota(jnp.int32, (1, LOCAL), 1) // HD
        keys = kvs.reshape(3 * GROUP, 2 * LOCAL)
        here_segs = segk.at[:, aligned(at.z * GROUP, 3 * GROUP)]
        dkvt[...] = jnp.zeros_like(dkvt)

        def pairs(b, low, size, first):
            here, span = pl.ds(b * HALF, HALF), pl.ds(low, size)
            which = lax.broadcasted_iota(jnp.int32, (8, size), 0) == s
            seg_row = jnp.sum(
                jnp.where(which, here_segs[:, span], 0.0), axis=0, keepdims=True
            )
            logs = lse[s, here]
            bias[:, 0:size] = allowed_bias(logs[:, 5:6], seg_row, low - b * HALF, size)
            query = q[s, here]
            grad = ga[here]
            k_block = keys[span, 0:LOCAL]
            v_block = keys[span, LOCAL:]
            dots[0] = jnp.transpose(query)
            dots[1] = jnp.transpose(grad)
            product = grad.astype(F32) * att[s, here].astype(F32)
            grad_query = jnp.zeros((HALF, LOCAL), F32) if first else dq[here]
            for h in range(LOCAL // HD):
                mine_h = lane == h
                one = jnp.where(mine_h, query, jnp.zeros_like(query))
                grad_one = jnp.where(mine_h, grad, jnp.zeros_like(grad))
                delta = jnp.sum(jnp.where(mine_h, product, 0.0), axis=-1, keepdims=True)
                scores = matmul(one, k_block, 1, 1) + bias[:, 0:size]
                probs = jnp.exp(scores - logs[:, h : h + 1])
                dprobs = matmul(grad_one, v_block, 1, 1)
                grad_scores = (probs * (dprobs - delta)).astype(BF)
                part = matmul(grad_scores, k_block, 1, 0)
                grad_query = jnp.where(mine_h, grad_query + part, grad_query)
                k_rows = pl.ds(h * HD, HD)
                v_rows = pl.ds(LOCAL + h * HD, HD)
                dkvt[k_rows, span] += matmul(dots[0, k_rows], grad_scores, 1, 0)
                dkvt[v_rows, span] += matmul(dots[1, k_rows], probs.astype(BF), 1, 0)
            if first:
                dq[here] = grad_query
            else:
                gq[s, here] = (grad_query * 0.125).astype(BF)

        def turned(i):
            return jnp.transpose(dkvt[:, i * GROUP : (i + 1) * GROUP].astype(BF))

        pairs(0, 0, GROUP, True)
        pairs(1, HALF, HALF, True)

        @pl.when((at.z > 1) & (s > 1))
        def _():
            m1_copy(s - 2).wait_send()

        dfar[lax.rem(s, 2)] = turned(0)

        @pl.when(at.z > 1)
        def _():
            m1_copy(s).start()

        @pl.when(s == 0)
        def _():
            a_qkv[...] = jnp.zeros_like(a_qkv)
            a_out[...] = jnp.zeros_like(a_out)

        pairs(0, GROUP, SPAN - GROUP, False)
        pairs(1, GROUP, SPAN - HALF, False)
        dnear[s] = turned(1)
        down[s] = turned(2)
        a_out[...] += matmul(att[s], gm[...], 0, 0)

        @pl.when(s < last)
        def _():
            kv_load(s + 1).start()

        @pl.when(s < last - 1)
        def _():
            mix_load(s + 1).start()

        norm_early(s).wait()
        a_qkv[0] += matmul(n1e[...], gq[s], 0, 0)

        @pl.when(s < 3)
        def _():
            norm_early(s + 1).start()

    def step_i(s):
        @pl.when((at.z > 0) & (at.z < 3))
        def _():
            m1_copy(s).wait_recv()
            dnear[s] = (dnear[s].astype(F32) + m1[s].astype(F32)).astype(BF)

        @pl.when(at.z > 0)
        def _():
            m2_copy(s).start()

    def step_f(s):
        @pl.when(at.z < 3)
        def _():
            m2_copy(s).wait_recv()
            down[s] = (down[s].astype(F32) + m2[s].astype(F32)).astype(BF)

        norm_load(s).wait()
        @pl.when(s == 0)
        def _():
            w_load.wait()

        grads = (gq[s], down[s, :, 0:LOCAL], down[s, :, LOCAL:])
        send[s] = (
            matmul(grads[0], wqkv[0], 1, 1)
            + matmul(grads[1], wqkv[1], 1, 1)
            + matmul(grads[2], wqkv[2], 1, 1)
        ).astype(BF)
        ring.rs_core(s).start()
        normed = n1s[...]
        for i in (1, 2):
            a_qkv[i] += matmul(normed, grads[i], 0, 0)

        @pl.when(s < 3)
        def _():
            norm_load(s + 1).start()

        small[9:10, 0:LOCAL] += column_sum(grads[0].astype(F32))
        small[9:10, LOCAL : 2 * LOCAL] += column_sum(grads[2].astype(F32))

    def ends(s):
        return tok_q.at[s], ig_h

    def ig_copy(s):
        return pltpu.make_async_copy(tok_q.at[s], ig_h.at[s, mine], first_sems.at[s])

    def step_r(s):
        @pl.when(s == 0)
        def _():
            first_copy(2).wait()
            first_copy(3).wait()

        summed = ring.total(s)
        xhat, inverse = norm_parts(tok_q[s].astype(F32))
        small[0:1, :] += column_sum(summed * xhat)
        small[1:2, :] += column_sum(summed)
        @pl.when(s > 0)
        def _():
            mid_load(s).wait()

        grad = gmid[...] + norm_back(summed, xhat, inverse, sums_one[7:8, :])
        tok_q[s] = grad.astype(BF)

        @pl.when(s < 3)
        def _():
            mid_load(s + 1).start()

        ig_copy(s).start()
        ring.spread(*ends(s), s)

    def sum_copy(stage, j=0):
        pair = (sum_sems.at[0, stage], sum_sems.at[1, stage])
        top = small.at[0:8]
        if stage == 0:
            return remote(top, got_core, pair, at.mate_c)
        if stage == 1:
            return remote(top, got_y, pair, at.mate_y)
        if stage == 2:
            pair = (sum_f_sems.at[0, j], sum_f_sems.at[1, j])
            return remote(small, got_f.at[j], pair, at.peers_f[j])
        mate = red_q.side if stage == 3 else red_q.across
        return remote(small, got_z.at[stage - 3], pair, mate)

    def step_sum(stage, s):
        if stage == 0:
            small[2:6, :] = sums_one[0:4, :]
            small[6:7, :] = sums_one[5:6, :]
            small[8:9, :] = sums_one[4:5, :]
        elif stage == 3:
            for j in range(nf - 1):
                sum_copy(2, j).wait()
            for j in range(nf - 1):
                small[...] += got_f[j]
        else:
            sum_copy(stage - 1).wait()
            if stage == 1:
                small[0:8, :] += got_core[...]
            elif stage == 2:
                small[0:8, :] += got_y[...]
            else:
                small[...] += got_z[stage - 4]
        if stage == 2:
            for j in range(nf - 1):
                sum_copy(2, j).start()
        elif stage < 5:
            sum_copy(stage).start()

    def step_group(group, stage, s):
        if stage == 0:
            if group == "B":
                f_out[...] = a_out[...].astype(BF)
                f_qkv[0] = a_qkv[0].astype(BF)
            elif group == "C":
                for i in (1, 2):
                    f_qkv[i] = a_qkv[i].astype(BF)
        for reduce in groups[group]:
            reduce.run(stage)

    groups = {"B": (red_out, red_q), "C": (red_kv,)}
    chains = (red_fc2, red_fc1)
    actions = {
        "E": step_e,
        "L": step_last,
        "I": step_i,
        "F": step_f,
        "Q": ring.step_q,
        "R": step_r,
        "T": lambda s: ring.step_t(*ends(s), s),
    }
    for stage in range(6):
        actions[f"S{stage}"] = functools.partial(step_sum, stage)
        for group in groups:
            actions[f"{group}{stage}"] = functools.partial(step_group, group, stage)

    def step_climb(stage, s):
        if stage == 0:

            @pl.when(lax.rem(s, 2) == 0)
            def _():
                first_copy_of(1 - s // 2).wait()

        for i, chain in enumerate(chains):

            @pl.when(s // 2 == i)
            def _(chain=chain):
                chain.climb(stage, lax.rem(s, 2))

    def step_down(hop, s):
        for i, chain in enumerate(chains):

            @pl.when(s // 4 == i)
            def _(chain=chain):
                chain.hand_down(hop, lax.rem(s // 2, 2), lax.rem(s, 2))

    for stage in range(5):
        actions[f"K{stage}"] = functools.partial(step_climb, stage)
    for hop in (1, 2, 3):
        actions[f"D{hop}"] = functools.partial(step_down, hop)
    run_order(actions, BACK_ORDER)
    for chain in chains:
        chain.finish()
    for s in range(SEQS):
        ring.step_u(*ends(s), s)
        ig_copy(s).wait()

        if s > 1:

            @pl.when(at.z > 1)
            def _():
                m1_copy(s).wait_send()

        @pl.when(at.z > 0)
        def _():
            m2_copy(s).wait_send()


def back_call(nf, *args):
    anys = pl.BlockSpec(memory_space=pl.ANY)
    vmem = pl.BlockSpec(memory_space=pltpu.VMEM)
    dma = pltpu.SemaphoreType.DMA
    big = lambda *lead: pltpu.VMEM((*lead, GROUP, 1024), BF)
    shape = jax.ShapeDtypeStruct
    fs = 1024 // nf
    low = lambda *dims: pltpu.VMEM(dims, BF)
    return pl.pallas_call(
        functools.partial(back_kernel, nf),
        out_shape=(
            shape((SEQS, GROUP, 1024), BF),
            shape((16, 1024), F32),
            shape((3, fs, LOCAL), BF),
            shape((LOCAL, fs), BF),
            shape((fs, 1024), BF),
            shape((1024, fs), BF),
        ),
        in_specs=[anys] * 11 + [vmem, vmem, vmem],
        out_specs=(anys, vmem, vmem, vmem, vmem, vmem),
        scratch_shapes=[
            low(GROUP, 1024),
            low(GROUP, 1024),
            low(3, GROUP, 2 * LOCAL),
            low(GROUP, 1024),
            low(GROUP, LOCAL),
            pltpu.VMEM((GROUP, LOCAL), F32),
            low(2, LOCAL, HALF),
            pltpu.VMEM((HALF, SPAN), F32),
            pltpu.VMEM((8, 3072), F32),
            pltpu.VMEM((2 * LOCAL, 3 * GROUP), F32),
            low(2, GROUP, 2 * LOCAL),
            low(SEQS, GROUP, 2 * LOCAL),
            low(SEQS, GROUP, 2 * LOCAL),
            low(SEQS, GROUP, 2 * LOCAL),
            low(SEQS, GROUP, 2 * LOCAL),
            low(SEQS, GROUP, LOCAL),
            big(SEQS),
            low(SEQS, HALF, 1024),
            low(SEQS, QUARTER, 1024),
            low(SEQS, QUARTER, 1024),
            pltpu.VMEM((QUARTER, 1024), F32),
            low(SEQS, QUARTER, 1024),
            pltpu.VMEM((3, 1024, LOCAL), F32),
            pltpu.VMEM((LOCAL, 1024), F32),
            low(3, 1024, LOCAL),
            low(1024, 1024),
            low(1024, 1024),
            low(nf - 1, 3, fs, LOCAL),
            low(nf - 1, LOCAL, fs),
            low(nf - 1, fs, 1024),
            low(nf - 1, 1024, fs),
            low(3, fs // 2, LOCAL),
            low(LOCAL // 2, fs),
            low(3, fs // 4, LOCAL),
            low(LOCAL // 4, fs),
            dma((5, 2, SEQS)),
            dma((3, 2)),
            dma,
            dma((4,)),
            dma((2, SEQS)),
            dma((2, SEQS)),
            dma((5, 2, nf - 1)),
            dma((5, 2, 4)),
            dma((2, 2, nf - 1, 2)),
            dma((2, 2, 6)),
            pltpu.VMEM((8, 1024), F32),
            pltpu.VMEM((8, 1024), F32),
            pltpu.VMEM((nf - 1, 16, 1024), F32),
            pltpu.VMEM((2, 16, 1024), F32),
            dma((2, 5)),
            dma((2, nf - 1)),
            low(GROUP, 1024),
            low(SEQS, GROUP, LOCAL),
            low(SEQS, GROUP, LOCAL),
            pltpu.VMEM((SEQS, GROUP, 128), F32),
            low(3, 1024, LOCAL),
            dma((3, SEQS)),
            dma,
        ],
        compiler_params=pltpu.CompilerParams(
            collective_id=2, has_side_effects=True, vmem_limit_bytes=63 * 2**20
        ),
        cost_estimate=pl.CostEstimate(
            flops=2 * 2048 * 1024 * 1024 * 6, bytes_accessed=30 * 2**20, transcendentals=0
        ),
        name="back",
    )(*args)


def finish_kernel(
    nf,
    out_in,
    ig_in,
    sums,
    sums_one,
    s_qkv,
    s_out,
    s_fc1,
    s_fc2,
    out,
    loss,
    ig,
    g_g1,
    g_b1,
    g_qkv,
    g_qv,
    g_out,
    g_bo,
    g_g2,
    g_b2,
    g_fc1,
    g_up,
    g_fc2,
    g_bd,
    low,
    wide_qkv,
    wide_out,
    wide_fc1,
    wide_fc2,
    low_qkv,
    low_out,
    low_fc1,
    low_fc2,
    in_sems,
    out_sems,
):
    shards = (
        (s_fc1, low_fc1, wide_fc1, g_fc1),
        (s_fc2, low_fc2, wide_fc2, g_fc2),
        (s_qkv, low_qkv, wide_qkv, g_qkv),
        (s_out, low_out, wide_out, g_out),
    )
    inward, outward = [], []
    for i, (source, kept, widened, target) in enumerate(shards):
        inward.append(pltpu.make_async_copy(source, kept, in_sems.at[i]))
        outward.append(pltpu.make_async_copy(widened, target, out_sems.at[i]))
    for i, (source, target) in enumerate(((out_in, out), (ig_in, ig))):
        for s in range(SEQS):
            which = 4 + i * SEQS + s
            inward.append(
                pltpu.make_async_copy(source.at[s], low.at[i, s], in_sems.at[which])
            )
            outward.append(
                pltpu.make_async_copy(low.at[i, s], target.at[s], out_sems.at[which])
            )
    for copy in inward:
        copy.start()
    for i, (_, kept, widened, _) in enumerate(shards):
        inward[i].wait()
        widened[...] = kept[...].astype(F32)
        outward[i].start()
    for i in range(4, len(inward)):
        inward[i].wait()
        outward[i].start()
    place = lax.axis_index("fsdp")
    fs = g_g1.shape[0]
    here = aligned(place * fs, fs)
    for i, target in enumerate((g_g1, g_b1, g_bd, g_g2, g_b2, g_bo)):
        target[...] = sums[i : i + 1, here].reshape(fs)
    scale = 1.0 / (2.0 * D * sums_one[6:7, 0:1])
    loss[...] = jnp.sum(sums[6:7, :], axis=1, keepdims=True) * scale
    own = sums[8:16, :]
    wide = g_up.shape[1]
    up = pltpu.roll(own, lax.rem(1024 - place * wide, 1024), 1)
    for i in range(g_up.shape[0]):
        g_up[i : i + 1, :] = up[0:1, i * nf * wide : i * nf * wide + wide]
    wide = g_qv.shape[2]
    qv = pltpu.roll(own, lax.rem(1024 - place * wide, 1024), 1)
    for i in range(2):
        for h in range(LOCAL // HD):
            start = i * LOCAL + h * HD
            g_qv[i, h : h + 1, :] = qv[1:2, start : start + wide]
    for copy in outward:
        copy.wait()


def finish_call(nf, *args):
    anys = pl.BlockSpec(memory_space=pl.ANY)
    vmem = pl.BlockSpec(memory_space=pltpu.VMEM)
    shape = jax.ShapeDtypeStruct
    fs = 1024 // nf
    block = shape((SEQS, GROUP, 1024), BF)
    row = shape((fs,), F32)
    return pl.pallas_call(
        functools.partial(finish_kernel, nf),
        out_shape=(
            block,
            shape((1, 1), F32),
            block,
            row,
            row,
            shape((3, fs, LOCAL), F32),
            shape((2, LOCAL // HD, HD // nf), F32),
            shape((LOCAL, fs), F32),
            row,
            row,
            row,
            shape((fs, 1024), F32),
            shape((4, 256 // nf), F32),
            shape((1024, fs), F32),
            row,
        ),
        in_specs=[anys, anys, vmem, vmem] + [anys] * 4,
        out_specs=(anys, vmem, anys, vmem, vmem, anys, vmem, anys)
        + (vmem, vmem, vmem, anys, vmem, anys, vmem),
        scratch_shapes=[
            pltpu.VMEM((2, SEQS, GROUP, 1024), BF),
            pltpu.VMEM((3, fs, LOCAL), F32),
            pltpu.VMEM((LOCAL, fs), F32),
            pltpu.VMEM((fs, 1024), F32),
            pltpu.VMEM((1024, fs), F32),
            pltpu.VMEM((3, fs, LOCAL), BF),
            pltpu.VMEM((LOCAL, fs), BF),
            pltpu.VMEM((fs, 1024), BF),
            pltpu.VMEM((1024, fs), BF),
            pltpu.SemaphoreType.DMA((4 + 2 * SEQS,)),
            pltpu.SemaphoreType.DMA((4 + 2 * SEQS,)),
        ],
        compiler_params=pltpu.CompilerParams(vmem_limit_bytes=63 * 2**20),
        name="finish",
    )(*args)


def local(
    tokens,
    cotangent,
    teacher,
    valid_mask,
    segment_ids,
    ln1_gain,
    ln1_bias,
    w_qkv,
    b_qv,
    w_out,
    b_out,
    ln2_gain,
    ln2_bias,
    w_fc1,
    b_fc1,
    w_fc2,
    b_fc2,
):
    nf = lax.axis_size("fsdp")
    front = front_call(
        nf,
        w_qkv,
        w_out,
        w_fc1,
        w_fc2,
        tokens,
        teacher,
        cotangent,
        b_out,
        ln2_gain,
        ln2_bias,
        b_fc2,
        ln1_gain,
        ln1_bias,
        b_qv,
        b_fc1,
        valid_mask,
        segment_ids,
    )
    (output, grad_mix, grad_middle, gfc1, gfc2, sums_one, att, q, kv, lse, n1, wqkv, wout) = front
    input_grad, everything, s_qkv, s_out, s_fc1, s_fc2 = back_call(
        nf, grad_mix, grad_middle, gfc1, gfc2, att, q, kv, lse, n1, tokens, wqkv, wout, segment_ids, sums_one
    )
    results = finish_call(
        nf, output, input_grad, everything, sums_one, s_qkv, s_out, s_fc1, s_fc2
    )
    return (results[0], results[1].reshape(()), *results[2:])


def solution(mesh):
    return jax.shard_map(
        local,
        mesh=mesh,
        in_specs=(
            P("fsdp", "context", None),
            P("fsdp", "context", None),
            P("fsdp", "context", None),
            P("fsdp", "context"),
            P("fsdp", None),
            P("fsdp"),
            P("fsdp"),
            P(None, "fsdp", "tensor"),
            P(None, "tensor", "fsdp"),
            P("tensor", "fsdp"),
            P("fsdp"),
            P("fsdp"),
            P("fsdp"),
            P("fsdp", "tensor"),
            P("tensor", "fsdp"),
            P("tensor", "fsdp"),
            P("fsdp"),
        ),
        out_specs=(
            P("fsdp", "context", None),
            P(),
            P("fsdp", "context", None),
            P("fsdp"),
            P("fsdp"),
            P(None, "fsdp", "tensor"),
            P(None, "tensor", "fsdp"),
            P("tensor", "fsdp"),
            P("fsdp"),
            P("fsdp"),
            P("fsdp"),
            P("fsdp", "tensor"),
            P("tensor", "fsdp"),
            P("tensor", "fsdp"),
            P("fsdp"),
        ),
        check_vma=False,
    )
```
